512 devices in a mesh: ctx: 64 (over z, y), node: 8 (over x, core).
Axes of the slice: x: 4, y: 8, z: 8, core: 2. Of those that a mesh axis runs over, the one named last changes fastest.
Arguments:
- tokens: bfloat16 [131072, 512], P(('ctx', 'node')), may hold values from -64 to 64
- w_query: bfloat16 [512, 512], replicated, may hold values from -0.25 to 0.25
- w_key: bfloat16 [512, 512], replicated, may hold values from -0.25 to 0.25
- w_value: bfloat16 [512, 512], replicated, may hold values from -0.25 to 0.25
- w_out: bfloat16 [512, 512], replicated, may hold values from -0.25 to 0.25
Outputs:
- mixed: bfloat16 [131072, 512], P(('ctx', 'node'))
The draws below stay inside these ranges and needn't reach their ends.
All inputs are finite; a program needn't handle non-finite values.
Results may differ from the reference program's by a relative error of at most 0.012.
Values may be sent and summed in bfloat16 or wider, within the bound.
A program may use at most 64 MiB of HBM per device.

```python
import math
import jax
import jax.numpy as jnp
from jax import lax

D = 512
HEADS = 8
HEAD = 64
BLOCK = 128
LEVELS = 5
TOKENS = 131072


def draw_tokens(key, part):
    key = jax.random.fold_in(key, 11)
    rough_key, phase_key, coef_key = jax.random.split(key, 3)
    places = jnp.arange(TOKENS, dtype=jnp.float32)[:, None]
    smooth = jnp.zeros((TOKENS, D), jnp.float32)
    for term in range(LEVELS + 1):
        period = BLOCK * 2.0 ** term
        phase = jax.random.uniform(jax.random.fold_in(phase_key, term), (1, D), jnp.float32, -math.pi, math.pi)
        weight = jax.random.normal(jax.random.fold_in(coef_key, term), (1, D), jnp.float32)
        smooth = smooth + weight * jnp.sin(places * (2.0 * math.pi / period) + phase)
    smooth = 0.45 * smooth
    rough = jax.random.normal(rough_key, (TOKENS, D), jnp.float32)
    values = rough + smooth
    return jnp.clip(values, -64.0, 64.0).astype(jnp.bfloat16)


def normal_values(key, extent, scale, most, kind=jnp.bfloat16):
    values = jax.random.normal(key, extent, jnp.float32) * scale
    return jnp.minimum(jnp.maximum(values, -most), most).astype(kind)


def setup_inputs(seed: int = 0) -> dict:
    key_list = jax.random.split(jax.random.key(seed), 6)
    return {
        "tokens": draw_tokens(jax.random.fold_in(key_list[5], 71), 0),
        "w_query": normal_values(key_list[1], (D, D), D ** -0.5, 0.25),
        "w_key": normal_values(key_list[2], (D, D), D ** -0.5, 0.25),
        "w_value": normal_values(key_list[3], (D, D), D ** -0.5, 0.25),
        "w_out": normal_values(key_list[4], (D, D), D ** -0.5, 0.25),
    }


def coarse(array, level):
    if level == 0:
        return array
    count = array.shape[0] >> level
    grouped = array.reshape(count, 2 ** level, array.shape[1])
    return lax.optimization_barrier(jnp.mean(grouped.astype(jnp.float32), axis=1)).astype(jnp.bfloat16)

def attend(query_blocks, center, left, right, valid_left, valid_right, heads):
    block_count, query_rows, model_width = query_blocks.shape
    parts = [left]
    masks = [jnp.broadcast_to(valid_left[:, None], (block_count, left.shape[1]))]
    if center is not None:
        parts.append(center)
        masks.append(jnp.ones((block_count, center.shape[1]), dtype=bool))
    parts.append(right)
    masks.append(jnp.broadcast_to(valid_right[:, None], (block_count, right.shape[1])))
    keyset = jnp.concatenate(parts, 1)
    allowed = jnp.concatenate(masks, 1)
    key_rows = keyset.shape[1]
    width = model_width // heads
    query_heads = query_blocks.reshape(block_count, query_rows, heads, width).astype(jnp.float32)
    key_heads = keyset[:, :, :model_width].reshape(block_count, key_rows, heads, width).astype(jnp.float32)
    value_heads = keyset[:, :, model_width:].reshape(block_count, key_rows, heads, width)
    scores = jnp.einsum('bqhd,bkhd->bhqk', query_heads, key_heads) * (1.0 / math.sqrt(width))
    scores = jnp.where(allowed[:, None, None, :], scores, -1e+30)
    highest = lax.optimization_barrier(jnp.max(scores, axis=-1))
    weights = jnp.exp(scores - highest[..., None])
    totals = lax.optimization_barrier(jnp.sum(weights, axis=-1))
    probs = weights.astype(jnp.bfloat16).astype(jnp.float32)
    weighted = jnp.einsum('bhqk,bkhd->bqhd', probs, value_heads.astype(jnp.float32))
    flat = block_count * query_rows
    highest = jnp.transpose(highest, (0, 2, 1)).reshape(flat, heads)
    totals = jnp.transpose(totals, (0, 2, 1)).reshape(flat, heads)
    return (highest, weighted.reshape(flat, heads, width), totals)

def spread(array, level):
    if level == 0:
        return array
    return jnp.repeat(array, 2 ** level, axis=0)

def combine(terms, heads):
    peak = spread(terms[0][0], 0)
    for level in range(1, len(terms)):
        peak = jnp.maximum(peak, spread(terms[level][0], level))
    upper = None
    lower = None
    for level in range(len(terms)):
        factor = 2.0 ** level * jnp.exp(spread(terms[level][0], level) - peak)
        part_up = factor[..., None] * spread(terms[level][1], level)
        part_low = factor * spread(terms[level][2], level)
        upper = part_up if upper is None else upper + part_up
        lower = part_low if lower is None else lower + part_low
    attended = upper / lower[..., None]
    return attended.reshape(attended.shape[0], -1).astype(jnp.bfloat16)

def level_terms(query_level, keyval_level, level):
    count, model_width = query_level.shape
    block_total = count // BLOCK
    group = min(64, block_total)
    zero_block = jnp.zeros((BLOCK, 2 * model_width), keyval_level.dtype)
    padded = jnp.concatenate([zero_block, keyval_level, zero_block], 0)

    def one_group(group_index):
        start = group_index * (group * BLOCK)
        window = lax.dynamic_slice_in_dim(padded, start, (group + 2) * BLOCK, 0)
        window = window.reshape(group + 2, BLOCK, 2 * model_width)
        query_blocks = lax.dynamic_slice_in_dim(query_level, start, group * BLOCK, 0)
        query_blocks = query_blocks.reshape(group, BLOCK, model_width)
        block_ids = group_index * group + jnp.arange(group, dtype=jnp.int32)
        center = window[1:-1] if level == 0 else None
        return attend(query_blocks, center, window[:-2], window[2:], block_ids > 0, block_ids < block_total - 1, HEADS)
    highest, weighted, totals = lax.map(one_group, jnp.arange(block_total // group, dtype=jnp.int32))
    return (highest.reshape(count, HEADS), weighted.reshape(count, HEADS, HEAD), totals.reshape(count, HEADS))

def reference(tokens, w_query, w_key, w_value, w_out):
    query = jnp.dot(tokens, w_query, preferred_element_type=jnp.float32).astype(jnp.bfloat16)
    keys = jnp.dot(tokens, w_key, preferred_element_type=jnp.float32).astype(jnp.bfloat16)
    values = jnp.dot(tokens, w_value, preferred_element_type=jnp.float32).astype(jnp.bfloat16)
    keyval = jnp.concatenate([keys, values], 1)
    terms = []
    for level in range(LEVELS):
        terms.append(level_terms(coarse(query, level), coarse(keyval, level), level))
    attended = combine(terms, HEADS)
    return jnp.dot(attended, w_out, preferred_element_type=jnp.float32).astype(jnp.bfloat16)
```

```python
import functools
import math

import jax
import jax.numpy as jnp
from jax import lax
from jax.experimental import pallas as pl
from jax.experimental.pallas import tpu as pltpu
from jax.sharding import PartitionSpec as P

HEADS = 8
HEAD = 64
WIDTH = HEADS * HEAD
BLOCK = 128
ROWS = 256
NODES = 8
FAR = 1e30
SCALE = math.log2(math.e) / math.sqrt(HEAD)
BF16 = jnp.bfloat16
F32 = jnp.float32
START = {1: 0, 2: 128, 3: 192, 4: 224}
COARSE = 240


def nn(a, b):
    return lax.dot_general(a, b, (((1,), (0,)), ((), ())), preferred_element_type=F32)


def nt(a, b):
    return lax.dot_general(a, b, (((1,), (1,)), ((), ())), preferred_element_type=F32)


def iota(shape, axis):
    return lax.broadcasted_iota(jnp.int32, shape, axis)


def averager(rows, columns, level):
    hit = iota((rows, columns), 0) == iota((rows, columns), 1) >> level
    return jnp.where(hit, 0.5**level, 0.0).astype(BF16)


def spreader(rows, queries, level):
    hit = (iota((rows, ROWS), 0) & (queries - 1)) == iota((rows, ROWS), 1) >> level
    return jnp.where(hit, 1.0, 0.0).astype(BF16)


def spread_exact(values, spread):
    high = values.astype(BF16)
    rest = values - high.astype(F32)
    middle = rest.astype(BF16)
    low = (rest - middle.astype(F32)).astype(BF16)
    count = values.shape[0]
    out = nn(jnp.concatenate([high, middle, low], 0), spread)
    return out[:count] + out[count : 2 * count] + out[2 * count :]


def lane_head(shape, width):
    return iota(shape, 1) // width


def kernel(
    devices, x_hbm, wq_hbm, wk_hbm, wv_hbm, wo_hbm, out_ref,
    x, wq, wk, wv, wo, wvt, t, h01, h2, h3, h4, acc,
    load_sem, send_sem, recv01, recv_far, recv_near,
):
    me = lax.axis_index("ctx") * NODES + lax.axis_index("node")
    core = lax.rem(me, 2)
    chip = lax.div(me, 2)
    pair = lax.div(me, 4)
    group = lax.div(me, 8)

    def place(index):
        index = lax.rem(index + devices, devices)
        return {"ctx": lax.div(index, NODES), "node": lax.rem(index, NODES)}

    twin = me + 1 - 2 * core

    near = [(me + 1, 0), (me - 1, 1)]
    two = [(me + 2, 0), (me - 2, 1)]
    three = [(4 * (pair + s) + 2 * j + core, d) for s, d in ((1, 0), (-1, 1)) for j in range(2)]
    four = [(8 * (group + s) + 2 * j + core, d) for s, d in ((1, 0), (-1, 1)) for j in range(4)]

    barrier = pltpu.get_barrier_semaphore()
    partners = near + two + three + four
    for target, _ in partners:
        pl.semaphore_signal(barrier, inc=1, device_id=place(target), device_id_type=pl.DeviceIdType.MESH)

    loads = []
    for i, (source, kept) in enumerate(((x_hbm, x), (wk_hbm, wk), (wq_hbm, wq), (wv_hbm, wv), (wo_hbm, wo))):
        loads.append(pltpu.make_async_copy(source, kept, load_sem.at[i]))
        loads[-1].start()

    loads[0].wait()
    average = jnp.concatenate([averager(ROWS >> l, ROWS, l) for l in range(1, 5)], 0)
    t[...] = nn(average, x[...]).astype(BF16)

    pl.semaphore_wait(barrier, len(partners))

    sends = []

    def send(source, target, landing, recv):
        copy = pltpu.make_async_remote_copy(
            src_ref=source,
            dst_ref=landing,
            send_sem=send_sem.at[len(sends)],
            recv_sem=recv,
            device_id=place(target),
            device_id_type=pl.DeviceIdType.MESH,
        )
        copy.start()
        sends.append(copy)

    def mine(direction):
        return direction * BLOCK + core * 64

    for target, d in four:
        row = pl.multiple_of(mine(d) + lax.rem(chip, 4) * 16, 16)
        send(t.at[pl.ds(START[4], 16)], target, h4.at[pl.ds(row, 16)], recv_far.at[4 + d])
    for target, d in three:
        row = pl.multiple_of(mine(d) + lax.rem(chip, 2) * 32, 16)
        send(t.at[pl.ds(START[3], 32)], target, h3.at[pl.ds(row, 32)], recv_far.at[2 + d])
    for target, d in two:
        row = pl.multiple_of(mine(d), 16)
        send(t.at[pl.ds(START[2], 64)], target, h2.at[pl.ds(row, 64)], recv_far.at[d])
    for target, d in near:
        send(x.at[pl.ds((1 - d) * BLOCK, BLOCK)], target, h01.at[pl.ds(d * 192, BLOCK)], recv01.at[d])
        send(t.at[pl.ds(d * 64, 64)], target, h01.at[pl.ds(d * 192 + BLOCK, 64)], recv01.at[d])

    def landed(buffer, start, rows, sem):
        region = buffer.at[pl.ds(start, rows)]
        pltpu.make_async_copy(region, region, sem).wait()

    def forward(buffer, which):
        for d in range(2):
            row = pl.multiple_of(mine(d), 16)
            landed(buffer, row, 64, recv_far.at[which + d])
            region = buffer.at[pl.ds(row, 64)]
            send(region, twin, region, recv_near.at[which + d])

    def gather(buffer, which):
        for d in range(2):
            row = pl.multiple_of(d * BLOCK + (1 - core) * 64, 16)
            landed(buffer, row, 64, recv_near.at[which + d])

    ones = jnp.ones((16, ROWS), BF16)
    half = lane_head((1, BLOCK), HEAD)
    pair_masks = [jnp.where(half == h, 1.0, 0.0).astype(BF16) for h in range(2)]

    loads[1].wait()
    k0 = nn(x[...], wk[...]).astype(BF16)
    loads[2].wait()
    q0 = (nn(x[...], wq[...]) * SCALE).astype(BF16)
    ql = nn(average, q0).astype(BF16)
    loads[3].wait()
    eye = jnp.where(iota((WIDTH, WIDTH), 0) == iota((WIDTH, WIDTH), 1), 1.0, 0.0).astype(BF16)
    wvt[...] = nt(eye, wv[...]).astype(BF16)
    v0 = nt(wvt[...], x[...]).astype(BF16)

    def pair_queries(q, j):
        block = q[:, j * BLOCK : (j + 1) * BLOCK]
        return jnp.concatenate([block * pair_masks[0], block * pair_masks[1]], 0)

    def with_ones(v):
        return jnp.concatenate([v, ones[:, : v.shape[1]]], 0)

    state = {}

    def merge(top, total, heads, weight):
        if not state:
            state["peak"], state["den"] = top, total
            for h in range(HEADS):
                acc[h * HEAD : (h + 1) * HEAD, :] = heads(h)
            return
        peak = jnp.maximum(state["peak"], top)
        old = jnp.exp2(state["peak"] - peak)
        new = weight * jnp.exp2(top - peak)
        state["den"] = state["den"] * old + new * total
        state["peak"] = peak
        for h in range(HEADS):
            rows = slice(h * HEAD, (h + 1) * HEAD)
            acc[rows, :] = acc[rows, :] * old[h : h + 1] + heads(h) * new[h : h + 1]

    def base(keys, values, block):
        tops, totals, sums = [], [], []
        q = q0[block * BLOCK : (block + 1) * BLOCK]
        for j in range(HEADS // 2):
            s = nt(keys[:, j * BLOCK : (j + 1) * BLOCK], pair_queries(q, j))
            m = jnp.max(s, axis=0, keepdims=True)
            p = jnp.exp2(s - m).astype(BF16)
            o = nn(with_ones(values[j * BLOCK : (j + 1) * BLOCK]), p)
            for h in range(2):
                lanes = slice(h * BLOCK, (h + 1) * BLOCK)
                tops.append(m[:, lanes])
                totals.append(o[BLOCK : BLOCK + 1, lanes])
                sums.append(o[h * HEAD : (h + 1) * HEAD, lanes])
        return jnp.concatenate(tops, 0), jnp.concatenate(totals, 0), sums

    def both(first, second):
        return (
            jnp.concatenate([first[0], second[0]], 1),
            jnp.concatenate([first[1], second[1]], 1),
            lambda h: jnp.concatenate([first[2][h], second[2][h]], 1),
        )

    merge(*both(base(k0, v0, 0), base(k0, v0, 1)), 1.0)

    def packed(keys, queries, values, off_left, off_right):
        s = nt(keys, queries)
        left, right = s[:BLOCK], s[BLOCK:]
        m = jnp.maximum(
            jnp.max(left, axis=0, keepdims=True) - off_left,
            jnp.max(right, axis=0, keepdims=True) - off_right,
        )
        p = jnp.concatenate(
            [
                jnp.exp2(left - (m + off_left)).astype(BF16),
                jnp.exp2(right - (m + off_right)).astype(BF16),
            ],
            0,
        )
        o = nn(with_ones(values), p)
        return m, o[values.shape[0] : values.shape[0] + 1], o[: values.shape[0]]

    def off(index, count):
        return (
            jnp.where(index == 0, FAR, 0.0).astype(F32),
            jnp.where(index == count - 1, FAR, 0.0).astype(F32),
        )

    def coarse(buffer, level, index, count):
        queries = ROWS >> level
        together = min(HEADS, ROWS // queries)
        features = together * HEAD
        columns = together * queries
        rows = buffer[...]
        keys = nn(rows, wk[...]).astype(BF16)
        values = nt(wvt[...], rows).astype(BF16)
        q = ql[START[level] : START[level] + queries]
        feature_head = lane_head((1, features), HEAD)
        own = iota((features, columns), 0) // HEAD == iota((features, columns), 1) // queries
        spread = spreader(columns, queries, level)
        tops, totals, sums = [], [], []
        for u in range(HEADS // together):
            part = slice(u * features, (u + 1) * features)
            block = q[:, part]
            masked = [block * jnp.where(feature_head == h, 1.0, 0.0).astype(BF16) for h in range(together)]
            m, total, o = packed(keys[:, part], jnp.concatenate(masked, 0), values[part], *off(index, count))
            row_head = iota((together, columns), 0) == iota((together, columns), 1) // queries
            tops.append(jnp.where(row_head, m, 0.0))
            totals.append(jnp.where(row_head, total, 0.0))
            sums.append(nn(jnp.where(own, o, 0.0).astype(BF16), spread))
        stats = spread_exact(jnp.concatenate(tops + totals, 0), spread)

        def heads(h):
            u, inside = divmod(h, together)
            return sums[u][inside * HEAD : (inside + 1) * HEAD]

        merge(stats[:HEADS], stats[HEADS:], heads, 2.0**level)

    forward(h4, 4)
    forward(h3, 2)
    forward(h2, 0)
    gather(h4, 4)
    coarse(h4, 4, group, devices // 8)
    gather(h3, 2)
    coarse(h3, 3, pair, devices // 4)
    gather(h2, 0)
    coarse(h2, 2, chip, devices // 2)

    halve = averager(64, BLOCK, 1)
    k1, v1, outer = [], [], []
    off_left, off_right = off(me, devices)
    for d in range(2):
        landed(h01, d * 192, 192, recv01.at[d])
        rows = h01[d * 192 : (d + 1) * 192, :]
        keys = nn(rows, wk[...]).astype(BF16)
        values = nt(wvt[...], rows).astype(BF16)
        k1 += [keys[BLOCK:], nn(halve, keys[:BLOCK]).astype(BF16)]
        v1 += [values[:, BLOCK:], nt(values[:, :BLOCK], halve).astype(BF16)]
        top, total, sums = base(keys[:BLOCK], values[:, :BLOCK], d)
        outer.append((top - (off_left, off_right)[d], total, sums))
    merge(*both(*outer), 1.0)

    k1 = jnp.concatenate(k1, 0)
    v1 = jnp.concatenate(v1, 1)
    spread = spreader(BLOCK, BLOCK, 1)
    tops, totals, sums = [], [], []
    for j in range(HEADS // 2):
        part = slice(j * BLOCK, (j + 1) * BLOCK)
        m, total, o = packed(k1[:, part], pair_queries(ql[:BLOCK], j), v1[part], off_left, off_right)
        for h in range(2):
            lanes = slice(h * BLOCK, (h + 1) * BLOCK)
            tops.append(m[:, lanes])
            totals.append(total[:, lanes])
            sums.append(o[h * HEAD : (h + 1) * HEAD, lanes].astype(BF16))
    stats = spread_exact(jnp.concatenate(tops + totals, 0), spread)
    spread_sums = nn(jnp.concatenate(sums, 0), spread)
    merge(stats[:HEADS], stats[HEADS:], lambda h: spread_sums[h * HEAD : (h + 1) * HEAD], 2.0)

    inverse = 1.0 / state["den"]
    attended = jnp.concatenate(
        [(acc[h * HEAD : (h + 1) * HEAD, :] * inverse[h : h + 1]).astype(BF16) for h in range(HEADS)], 0
    )
    loads[4].wait()
    turned = nt(eye[:ROWS, :ROWS], attended).astype(BF16)
    out_ref[...] = nn(turned, wo[...]).astype(BF16)

    for copy in sends:
        copy.wait_send()


def solution(mesh):
    devices = mesh.shape["ctx"] * mesh.shape["node"]

    def local(tokens, w_query, w_key, w_value, w_out):
        square = pltpu.VMEM((WIDTH, WIDTH), BF16)
        return pl.pallas_call(
            functools.partial(kernel, devices),
            out_shape=jax.ShapeDtypeStruct((ROWS, WIDTH), BF16),
            in_specs=[pl.BlockSpec(memory_space=pl.ANY)] * 5,
            out_specs=pl.BlockSpec(memory_space=pltpu.VMEM),
            scratch_shapes=[
                pltpu.VMEM((ROWS, WIDTH), BF16),
                square,
                square,
                square,
                square,
                square,
                pltpu.VMEM((COARSE, WIDTH), BF16),
                pltpu.VMEM((384, WIDTH), BF16),
                pltpu.VMEM((ROWS, WIDTH), BF16),
                pltpu.VMEM((ROWS, WIDTH), BF16),
                pltpu.VMEM((ROWS, WIDTH), BF16),
                pltpu.VMEM((WIDTH, ROWS), F32),
                pltpu.SemaphoreType.DMA((5,)),
                pltpu.SemaphoreType.DMA((24,)),
                pltpu.SemaphoreType.DMA((2,)),
                pltpu.SemaphoreType.DMA((6,)),
                pltpu.SemaphoreType.DMA((6,)),
            ],
            compiler_params=pltpu.CompilerParams(
                collective_id=0, has_side_effects=True, vmem_limit_bytes=40 * 2**20
            ),
            name="hierarchical_attention",
        )(tokens, w_query, w_key, w_value, w_out)

    placed = (P(("ctx", "node"), None), P(), P(), P(), P())
    return jax.shard_map(
        local, mesh=mesh, in_specs=placed, out_specs=P(("ctx", "node"), None), check_vma=False
    )
```

```python
import functools
import math

import jax
import jax.numpy as jnp
from jax import lax
from jax.experimental import pallas as pl
from jax.experimental.pallas import tpu as pltpu
from jax.sharding import PartitionSpec as P

HEADS = 8
HEAD = 64
WIDTH = HEADS * HEAD
BLOCK = 128
ROWS = 256
NODES = 8
FAR = 1e30
SCALE = math.log2(math.e) / math.sqrt(HEAD)
BF16 = jnp.bfloat16
F32 = jnp.float32
START = {1: 0, 2: 128, 3: 192, 4: 224}
COARSE = 240


def nn(a, b):
    return lax.dot_general(a, b, (((1,), (0,)), ((), ())), preferred_element_type=F32)


def nt(a, b):
    return lax.dot_general(a, b, (((1,), (1,)), ((), ())), preferred_element_type=F32)


def iota(shape, axis):
    return lax.broadcasted_iota(jnp.int32, shape, axis)


def averager(rows, columns, level):
    hit = iota((rows, columns), 0) == iota((rows, columns), 1) >> level
    return jnp.where(hit, 0.5**level, 0.0).astype(BF16)


def spreader(rows, queries, level):
    hit = (iota((rows, ROWS), 0) & (queries - 1)) == iota((rows, ROWS), 1) >> level
    return jnp.where(hit, 1.0, 0.0).astype(BF16)


def spread_exact(values, spread):
    high = values.astype(BF16)
    rest = values - high.astype(F32)
    middle = rest.astype(BF16)
    low = (rest - middle.astype(F32)).astype(BF16)
    count = values.shape[0]
    out = nn(jnp.concatenate([high, middle, low], 0), spread)
    return out[:count] + out[count : 2 * count] + out[2 * count :]


def lane_head(shape, width):
    return iota(shape, 1) // width


def kernel(
    devices, x_hbm, wq_hbm, wk_hbm, wv_hbm, wo_hbm, out_ref,
    x, wq, wk, wv, wo, wvt, t, hnear, hfar, h2, h3, h4, q0, ql, k0, v0, kh, vh, acc, peak, den,
    load_sem, send_sem, recv01, recv_far, recv_near,
):
    me = lax.axis_index("ctx") * NODES + lax.axis_index("node")
    core = lax.rem(me, 2)
    chip = lax.div(me, 2)
    pair = lax.div(me, 4)
    group = lax.div(me, 8)

    def place(index):
        index = lax.rem(index + devices, devices)
        return {"ctx": lax.div(index, NODES), "node": lax.rem(index, NODES)}

    loads = []
    for i, (source, kept) in enumerate(((x_hbm, x), (wq_hbm, wq), (wk_hbm, wk), (wv_hbm, wv), (wo_hbm, wo))):
        loads.append(pltpu.make_async_copy(source, kept, load_sem.at[i]))
    loads[0].start()

    twin = me + 1 - 2 * core
    beyond = me - 1 + 2 * core
    two = [(me + 2, 0), (me - 2, 1)]
    three = [(4 * (pair + s) + 2 * j + core, d) for s, d in ((1, 0), (-1, 1)) for j in range(2)]
    four = [(8 * (group + s) + 2 * j + core, d) for s, d in ((1, 0), (-1, 1)) for j in range(4)]

    barrier = pltpu.get_barrier_semaphore()
    partners = [target for target, _ in four + three + two] + [beyond, twin]
    for target in partners:
        pl.semaphore_signal(barrier, inc=1, device_id=place(target), device_id_type=pl.DeviceIdType.MESH)
    for load in loads[1:]:
        load.start()

    average = jnp.concatenate([averager(ROWS >> l, ROWS, l) for l in range(1, 5)], 0)
    loads[0].wait()
    t[...] = nn(average, x[...]).astype(BF16)

    pl.semaphore_wait(barrier, len(partners))

    sends = []

    def send(source, target, landing, recv):
        copy = pltpu.make_async_remote_copy(
            src_ref=source,
            dst_ref=landing,
            send_sem=send_sem.at[len(sends)],
            recv_sem=recv,
            device_id=place(target),
            device_id_type=pl.DeviceIdType.MESH,
        )
        copy.start()
        sends.append(copy)

    def mine(direction):
        return direction * BLOCK + core * 64

    def edge(target, side, landing, recv):
        rows = pl.multiple_of(side * BLOCK, BLOCK)
        means = pl.multiple_of((1 - side) * 64, 64)
        send(x.at[pl.ds(rows, BLOCK)], target, landing.at[pl.ds(0, BLOCK)], recv)
        send(t.at[pl.ds(means, 64)], target, landing.at[pl.ds(BLOCK, 64)], recv)

    edge(twin, 1 - core, hnear, recv01.at[0])
    for target, d in four:
        row = pl.multiple_of(mine(d) + lax.rem(chip, 4) * 16, 16)
        send(t.at[pl.ds(START[4], 16)], target, h4.at[pl.ds(row, 16)], recv_far.at[4 + d])
    for target, d in three:
        row = pl.multiple_of(mine(d) + lax.rem(chip, 2) * 32, 16)
        send(t.at[pl.ds(START[3], 32)], target, h3.at[pl.ds(row, 32)], recv_far.at[2 + d])
    for target, d in two:
        row = pl.multiple_of(mine(d), 16)
        send(t.at[pl.ds(START[2], 64)], target, h2.at[pl.ds(row, 64)], recv_far.at[d])
    edge(beyond, core, hfar, recv01.at[1])

    def landed(buffer, start, rows, sem):
        region = buffer.at[pl.ds(start, rows)]
        pltpu.make_async_copy(region, region, sem).wait()

    def forward(buffer, which):
        for d in range(2):
            row = pl.multiple_of(mine(d), 16)
            landed(buffer, row, 64, recv_far.at[which + d])
            region = buffer.at[pl.ds(row, 64)]
            send(region, twin, region, recv_near.at[which + d])

    def gather(buffer, which):
        for d in range(2):
            row = pl.multiple_of(d * BLOCK + (1 - core) * 64, 16)
            landed(buffer, row, 64, recv_near.at[which + d])

    ones = jnp.ones((16, ROWS), BF16)
    half = lane_head((1, BLOCK), HEAD)
    pair_masks = [jnp.where(half == h, 1.0, 0.0).astype(BF16) for h in range(2)]

    def lanes_of(j):
        return slice(j * BLOCK, (j + 1) * BLOCK)

    def head_rows(h):
        return slice(h * HEAD, (h + 1) * HEAD)

    def pair_queries(block):
        return jnp.concatenate([block * pair_masks[0], block * pair_masks[1]], 0)

    def with_ones(v):
        return jnp.concatenate([v, ones[:, : v.shape[1]]], 0)

    def merge(lanes, top, total, heads, weight):
        before = peak[:, lanes]
        after = jnp.maximum(before, top)
        old = jnp.exp2(before - after)
        new = weight * jnp.exp2(top - after)
        den[:, lanes] = den[:, lanes] * old + new * total
        peak[:, lanes] = after
        for h in range(HEADS):
            rows = head_rows(h)
            acc[rows, lanes] = acc[rows, lanes] * old[h : h + 1] + heads(h) * new[h : h + 1]

    loads[1].wait()
    q0[...] = (nn(x[...], wq[...]) * SCALE).astype(BF16)
    ql[...] = nn(average, q0[...]).astype(BF16)
    loads[2].wait()
    k0[...] = nn(x[...], wk[...]).astype(BF16)
    loads[3].wait()
    eye = jnp.where(iota((WIDTH, WIDTH), 0) == iota((WIDTH, WIDTH), 1), 1.0, 0.0).astype(BF16)
    wvt[...] = nt(eye, wv[...]).astype(BF16)
    v0[...] = nt(wvt[...], x[...]).astype(BF16)

    def base_own(h):
        pairs = lanes_of(h // 2)
        s = nt(k0[:, pairs], q0[:, pairs] * pair_masks[h % 2])
        m = jnp.max(s, axis=0, keepdims=True)
        p = jnp.exp2(s - m).astype(BF16)
        o = nn(with_ones(v0[head_rows(h), :]), p)
        peak[h : h + 1, :] = m
        den[h : h + 1, :] = o[HEAD : HEAD + 1]
        acc[head_rows(h), :] = o[:HEAD]

    def side(buffer, slot, block):
        rows = buffer[...]
        halve = averager(64, BLOCK, 1)
        near_k = nn(rows, wk[...]).astype(BF16)
        near_v = nt(wvt[...], rows).astype(BF16)
        kh[slot, :192, :] = near_k
        vh[slot, :, :192] = near_v
        kh[slot, 192:, :] = nn(halve, near_k[:BLOCK]).astype(BF16)
        vh[slot, :, 192:] = nt(near_v[:, :BLOCK], halve).astype(BF16)
        queries = pl.ds(pl.multiple_of(block * BLOCK, BLOCK), BLOCK)
        found = []
        for keys, q in ((slice(0, BLOCK), q0.at[queries]), (slice(BLOCK, 2 * BLOCK), ql.at[pl.ds(0, BLOCK)])):
            tops, totals, sums = [], [], []
            for j in range(HEADS // 2):
                s = nt(kh[slot, keys, lanes_of(j)], pair_queries(q[:, lanes_of(j)]))
                m = jnp.max(s, axis=0, keepdims=True)
                p = jnp.exp2(s - m).astype(BF16)
                o = nn(with_ones(vh[slot, lanes_of(j), keys]), p)
                for h in range(2):
                    tops.append(m[:, lanes_of(h)])
                    totals.append(o[BLOCK : BLOCK + 1, lanes_of(h)])
                    sums.append(o[head_rows(h), lanes_of(h)])
            found.append((jnp.concatenate(tops, 0), jnp.concatenate(totals, 0), sums))
        return queries, found[0], found[1]

    def packed(keys, queries, values, off_left, off_right):
        s = nt(keys, queries)
        left, right = s[:BLOCK], s[BLOCK:]
        m = jnp.maximum(
            jnp.max(left, axis=0, keepdims=True) - off_left,
            jnp.max(right, axis=0, keepdims=True) - off_right,
        )
        p = jnp.concatenate(
            [
                jnp.exp2(left - (m + off_left)).astype(BF16),
                jnp.exp2(right - (m + off_right)).astype(BF16),
            ],
            0,
        )
        o = nn(with_ones(values), p)
        return m, o[values.shape[0] : values.shape[0] + 1], o[: values.shape[0]]

    def off(missing):
        return jnp.where(missing, FAR, 0.0).astype(F32)

    everywhere = slice(0, ROWS)

    def coarse(buffer, level, index, count):
        queries = ROWS >> level
        together = min(HEADS, ROWS // queries)
        features = together * HEAD
        columns = together * queries
        rows = buffer[...]
        kh[0] = nn(rows, wk[...]).astype(BF16)
        vh[0] = nt(wvt[...], rows).astype(BF16)
        feature_head = lane_head((1, features), HEAD)
        own = iota((features, columns), 0) // HEAD == iota((features, columns), 1) // queries
        spread = spreader(columns, queries, level)
        tops, totals, sums = [], [], []
        for u in range(HEADS // together):
            part = slice(u * features, (u + 1) * features)
            block = ql[START[level] : START[level] + queries, part]
            masked = [block * jnp.where(feature_head == h, 1.0, 0.0).astype(BF16) for h in range(together)]
            m, total, o = packed(
                kh[0, :, part], jnp.concatenate(masked, 0), vh[0, part, :], off(index == 0), off(index == count - 1)
            )
            row_head = iota((together, columns), 0) == iota((together, columns), 1) // queries
            tops.append(jnp.where(row_head, m, 0.0))
            totals.append(jnp.where(row_head, total, 0.0))
            sums.append(nn(jnp.where(own, o, 0.0).astype(BF16), spread))
        stats = spread_exact(jnp.concatenate(tops + totals, 0), spread)

        def heads(h):
            u, inside = divmod(h, together)
            return sums[u][head_rows(inside)]

        merge(everywhere, stats[:HEADS], stats[HEADS:], heads, 2.0**level)

    for h in range(4):
        base_own(h)
    forward(h4, 4)
    for h in range(4, HEADS):
        base_own(h)
    landed(hnear, 0, 192, recv01.at[0])
    lanes, (top, total, sums), one_near = side(hnear, 0, 1 - core)
    merge(lanes, top, total, lambda h: sums[h], 1.0)
    forward(h3, 2)
    gather(h4, 4)
    coarse(h4, 4, group, devices // 8)
    forward(h2, 0)
    gather(h3, 2)
    coarse(h3, 3, pair, devices // 4)
    gather(h2, 0)
    coarse(h2, 2, chip, devices // 2)

    landed(hfar, 0, 192, recv01.at[1])
    missing = off(jnp.where(core == 0, me == 0, me == devices - 1))
    lanes, (top, total, sums), one_far = side(hfar, 1, core)
    merge(lanes, top - missing, total, lambda h: sums[h], 1.0)
    top_far = one_far[0] - missing
    top = jnp.maximum(one_near[0], top_far)
    factor_near = jnp.exp2(one_near[0] - top)
    factor_far = jnp.exp2(top_far - top)
    total = one_near[1] * factor_near + one_far[1] * factor_far
    sums = [
        (one_near[2][h] * factor_near[h : h + 1] + one_far[2][h] * factor_far[h : h + 1]).astype(BF16)
        for h in range(HEADS)
    ]
    spread = spreader(BLOCK, BLOCK, 1)
    stats = spread_exact(jnp.concatenate([top, total], 0), spread)
    spread_sums = nn(jnp.concatenate(sums, 0), spread)
    merge(everywhere, stats[:HEADS], stats[HEADS:], lambda h: spread_sums[head_rows(h)], 2.0)

    inverse = 1.0 / den[...]
    attended = jnp.concatenate(
        [(acc[head_rows(h), :] * inverse[h : h + 1]).astype(BF16) for h in range(HEADS)], 0
    )
    loads[4].wait()
    turned = nt(eye[:ROWS, :ROWS], attended).astype(BF16)
    out_ref[...] = nn(turned, wo[...]).astype(BF16)

    for copy in sends:
        copy.wait_send()


def solution(mesh):
    devices = mesh.shape["ctx"] * mesh.shape["node"]

    def local(tokens, w_query, w_key, w_value, w_out):
        square = pltpu.VMEM((WIDTH, WIDTH), BF16)
        tall = pltpu.VMEM((ROWS, WIDTH), BF16)
        return pl.pallas_call(
            functools.partial(kernel, devices),
            out_shape=jax.ShapeDtypeStruct((ROWS, WIDTH), BF16),
            in_specs=[pl.BlockSpec(memory_space=pltpu.HBM)] * 5,
            out_specs=pl.BlockSpec(memory_space=pltpu.VMEM),
            scratch_shapes=[
                tall,
                square,
                square,
                square,
                square,
                square,
                pltpu.VMEM((COARSE, WIDTH), BF16),
                pltpu.VMEM((192, WIDTH), BF16),
                pltpu.VMEM((192, WIDTH), BF16),
                tall,
                tall,
                tall,
                tall,
                pltpu.VMEM((COARSE, WIDTH), BF16),
                tall,
                pltpu.VMEM((WIDTH, ROWS), BF16),
                pltpu.VMEM((2, ROWS, WIDTH), BF16),
                pltpu.VMEM((2, WIDTH, ROWS), BF16),
                pltpu.VMEM((WIDTH, ROWS), F32),
                pltpu.VMEM((HEADS, ROWS), F32),
                pltpu.VMEM((HEADS, ROWS), F32),
                pltpu.SemaphoreType.DMA((5,)),
                pltpu.SemaphoreType.DMA((24,)),
                pltpu.SemaphoreType.DMA((2,)),
                pltpu.SemaphoreType.DMA((6,)),
                pltpu.SemaphoreType.DMA((6,)),
            ],
            compiler_params=pltpu.CompilerParams(
                collective_id=0, has_side_effects=True, vmem_limit_bytes=40 * 2**20
            ),
            name="hierarchical_attention",
        )(*[pltpu.with_memory_space_constraint(a, pltpu.HBM) for a in (tokens, w_query, w_key, w_value, w_out)])

    placed = (P(("ctx", "node"), None), P(), P(), P(), P())
    return jax.shard_map(
        local, mesh=mesh, in_specs=placed, out_specs=P(("ctx", "node"), None), check_vma=False
    )
```

```python
import functools
import math

import jax
import jax.numpy as jnp
from jax import lax
from jax.experimental import pallas as pl
from jax.experimental.pallas import tpu as pltpu
from jax.sharding import PartitionSpec as P

HEADS = 8
HEAD = 64
WIDTH = HEADS * HEAD
BLOCK = 128
ROWS = 256
NODES = 8
FAR = 1e30
SCALE = math.log2(math.e) / math.sqrt(HEAD)
BF16 = jnp.bfloat16
F32 = jnp.float32
START = {1: 0, 2: 128, 3: 192, 4: 224}
COARSE = 240


def nn(a, b):
    return lax.dot_general(a, b, (((1,), (0,)), ((), ())), preferred_element_type=F32)


def nt(a, b):
    return lax.dot_general(a, b, (((1,), (1,)), ((), ())), preferred_element_type=F32)


def iota(shape, axis):
    return lax.broadcasted_iota(jnp.int32, shape, axis)


def averager(rows, columns, level):
    hit = iota((rows, columns), 0) == iota((rows, columns), 1) >> level
    return jnp.where(hit, 0.5**level, 0.0).astype(BF16)


def spreader(rows, queries, level):
    hit = (iota((rows, ROWS), 0) & (queries - 1)) == iota((rows, ROWS), 1) >> level
    return jnp.where(hit, 1.0, 0.0).astype(BF16)


def spread_exact(values, spread):
    high = values.astype(BF16)
    rest = values - high.astype(F32)
    middle = rest.astype(BF16)
    low = (rest - middle.astype(F32)).astype(BF16)
    count = values.shape[0]
    out = nn(jnp.concatenate([high, middle, low], 0), spread)
    return out[:count] + out[count : 2 * count] + out[2 * count :]


def lane_head(shape, width):
    return iota(shape, 1) // width


def kernel(
    devices, x_hbm, wq_hbm, wk_hbm, wv_hbm, wo_hbm, out_ref,
    x, wq, wk, wv, wo, wvt, t, hnear, hfar, h2, h3, h4, q0, ql, k0, v0, kh, vh, acc, peak, den,
    load_sem, send_sem, recv01, recv_far, recv_near,
):
    me = lax.axis_index("ctx") * NODES + lax.axis_index("node")
    core = lax.rem(me, 2)
    chip = lax.div(me, 2)
    pair = lax.div(me, 4)
    group = lax.div(me, 8)

    def place(index):
        index = lax.rem(index + devices, devices)
        return {"ctx": lax.div(index, NODES), "node": lax.rem(index, NODES)}

    loads = []
    for i, (source, kept) in enumerate(((x_hbm, x), (wq_hbm, wq), (wk_hbm, wk), (wv_hbm, wv), (wo_hbm, wo))):
        loads.append(pltpu.make_async_copy(source, kept, load_sem.at[i]))
    loads[0].start()

    twin = me + 1 - 2 * core
    beyond = me - 1 + 2 * core
    two = [(me + 2, 0), (me - 2, 1)]
    three = [(4 * (pair + s) + 2 * j + core, d) for s, d in ((1, 0), (-1, 1)) for j in range(2)]
    four = [(8 * (group + s) + 2 * j + core, d) for s, d in ((1, 0), (-1, 1)) for j in range(4)]

    barrier = pltpu.get_barrier_semaphore()
    partners = [target for target, _ in four + three + two] + [beyond, twin]
    for target in partners:
        pl.semaphore_signal(barrier, inc=1, device_id=place(target), device_id_type=pl.DeviceIdType.MESH)
    for load in loads[1:]:
        load.start()

    average = jnp.concatenate([averager(ROWS >> l, ROWS, l) for l in range(1, 5)], 0)
    loads[0].wait()
    t[...] = nn(average, x[...]).astype(BF16)

    pl.semaphore_wait(barrier, len(partners))

    sends = []

    def send(source, target, landing, recv):
        copy = pltpu.make_async_remote_copy(
            src_ref=source,
            dst_ref=landing,
            send_sem=send_sem.at[len(sends)],
            recv_sem=recv,
            device_id=place(target),
            device_id_type=pl.DeviceIdType.MESH,
        )
        copy.start()
        sends.append(copy)

    def mine(direction):
        return direction * BLOCK + core * 64

    def edge(target, side, landing, recv):
        rows = pl.multiple_of(side * BLOCK, BLOCK)
        means = pl.multiple_of((1 - side) * 64, 64)
        send(x.at[pl.ds(rows, BLOCK)], target, landing.at[pl.ds(0, BLOCK)], recv)
        send(t.at[pl.ds(means, 64)], target, landing.at[pl.ds(BLOCK, 64)], recv)

    edge(twin, 1 - core, hnear, recv01.at[0])
    for target, d in four:
        row = pl.multiple_of(mine(d) + lax.rem(chip, 4) * 16, 16)
        send(t.at[pl.ds(START[4], 16)], target, h4.at[pl.ds(row, 16)], recv_far.at[4 + d])
    for target, d in three:
        row = pl.multiple_of(mine(d) + lax.rem(chip, 2) * 32, 16)
        send(t.at[pl.ds(START[3], 32)], target, h3.at[pl.ds(row, 32)], recv_far.at[2 + d])
    for target, d in two:
        row = pl.multiple_of(mine(d), 16)
        send(t.at[pl.ds(START[2], 64)], target, h2.at[pl.ds(row, 64)], recv_far.at[d])
    edge(beyond, core, hfar, recv01.at[1])

    def landed(buffer, start, rows, sem):
        region = buffer.at[pl.ds(start, rows)]
        pltpu.make_async_copy(region, region, sem).wait()

    def forward(buffer, which):
        for d in range(2):
            row = pl.multiple_of(mine(d), 16)
            landed(buffer, row, 64, recv_far.at[which + d])
            region = buffer.at[pl.ds(row, 64)]
            send(region, twin, region, recv_near.at[which + d])

    def gather(buffer, which):
        for d in range(2):
            row = pl.multiple_of(d * BLOCK + (1 - core) * 64, 16)
            landed(buffer, row, 64, recv_near.at[which + d])

    ones = jnp.ones((16, ROWS), BF16)
    half = lane_head((1, BLOCK), HEAD)
    pair_masks = [jnp.where(half == h, 1.0, 0.0).astype(BF16) for h in range(2)]

    def lanes_of(j):
        return slice(j * BLOCK, (j + 1) * BLOCK)

    def head_rows(h):
        return slice(h * HEAD, (h + 1) * HEAD)

    def pair_queries(block):
        return jnp.concatenate([block * pair_masks[0], block * pair_masks[1]], 0)

    def with_ones(v):
        return jnp.concatenate([v, ones[:, : v.shape[1]]], 0)

    def merge(lanes, top, total, heads, weight):
        before = peak[:, lanes]
        after = jnp.maximum(before, top)
        old = jnp.exp2(before - after)
        new = weight * jnp.exp2(top - after)
        den[:, lanes] = den[:, lanes] * old + new * total
        peak[:, lanes] = after
        for h in range(HEADS):
            rows = head_rows(h)
            acc[rows, lanes] = acc[rows, lanes] * old[h : h + 1] + heads(h) * new[h : h + 1]

    loads[1].wait()
    q0[...] = (nn(x[...], wq[...]) * SCALE).astype(BF16)
    ql[...] = nn(average, q0[...]).astype(BF16)
    loads[2].wait()
    k0[...] = nn(x[...], wk[...]).astype(BF16)
    loads[3].wait()
    eye = jnp.where(iota((WIDTH, WIDTH), 0) == iota((WIDTH, WIDTH), 1), 1.0, 0.0).astype(BF16)
    wvt[...] = nt(eye, wv[...]).astype(BF16)
    v0[...] = nt(wvt[...], x[...]).astype(BF16)

    def run(units):
        waiting, active = list(units), []
        while waiting or active:
            if waiting:
                active.append(waiting.pop(0))
            active = [unit for unit in active if next(unit, None) is not None]

    def attend(keys, queries, values, done):
        s = nt(keys(), queries())
        yield True
        m = jnp.max(s, axis=0, keepdims=True)
        p = jnp.exp2(s - m).astype(BF16)
        yield True
        done(m, nn(with_ones(values()), p))

    def base_own(h):
        pairs = lanes_of(h // 2)

        def done(m, o):
            peak[h : h + 1, :] = m
            den[h : h + 1, :] = o[HEAD : HEAD + 1]
            acc[head_rows(h), :] = o[:HEAD]

        return attend(
            lambda: k0[:, pairs], lambda: q0[:, pairs] * pair_masks[h % 2], lambda: v0[head_rows(h), :], done
        )

    def project(rows, slot, count):
        kh[slot, :count, :] = nn(rows, wk[...]).astype(BF16)
        vh[slot, :, :count] = nt(wvt[...], rows).astype(BF16)

    def project_side(buffer, slot):
        halve = averager(64, BLOCK, 1)
        project(buffer[...], slot, 192)
        kh[slot, 192:, :] = nn(halve, kh[slot, :BLOCK, :]).astype(BF16)
        vh[slot, :, 192:] = nt(vh[slot, :, :BLOCK], halve).astype(BF16)

    def side(slot, block):
        queries = pl.ds(pl.multiple_of(block * BLOCK, BLOCK), BLOCK)
        units, found = [], ([], [])
        for keys, q, part in (
            (slice(0, BLOCK), q0.at[queries], found[0]),
            (slice(BLOCK, 2 * BLOCK), ql.at[pl.ds(0, BLOCK)], found[1]),
        ):
            for j in range(HEADS // 2):
                units.append(
                    attend(
                        lambda keys=keys, j=j: kh[slot, keys, lanes_of(j)],
                        lambda q=q, j=j: pair_queries(q[:, lanes_of(j)]),
                        lambda keys=keys, j=j: vh[slot, lanes_of(j), keys],
                        lambda m, o, part=part: part.append((m, o)),
                    )
                )
        return units, queries, found[0], found[1]

    def by_head(part):
        tops = [m[:, lanes_of(h)] for m, _ in part for h in range(2)]
        totals = [o[BLOCK : BLOCK + 1, lanes_of(h)] for _, o in part for h in range(2)]
        sums = [o[head_rows(h), lanes_of(h)] for _, o in part for h in range(2)]
        return jnp.concatenate(tops, 0), jnp.concatenate(totals, 0), sums

    def off(missing):
        return jnp.where(missing, FAR, 0.0).astype(F32)

    everywhere = slice(0, ROWS)

    def coarse(slot, level, index, count):
        queries = ROWS >> level
        together = min(HEADS, ROWS // queries)
        features = together * HEAD
        columns = together * queries
        off_left, off_right = off(index == 0), off(index == count - 1)
        feature_head = lane_head((1, features), HEAD)
        own = iota((features, columns), 0) // HEAD == iota((features, columns), 1) // queries
        row_head = iota((together, columns), 0) == iota((together, columns), 1) // queries
        spread = spreader(columns, queries, level)
        tops, totals, sums = [], [], []

        def unit(u):
            part = slice(u * features, (u + 1) * features)
            block = ql[START[level] : START[level] + queries, part]
            masked = [block * jnp.where(feature_head == h, 1.0, 0.0).astype(BF16) for h in range(together)]
            s = nt(kh[slot, :, part], jnp.concatenate(masked, 0))
            yield True
            left, right = s[:BLOCK], s[BLOCK:]
            m = jnp.maximum(
                jnp.max(left, axis=0, keepdims=True) - off_left,
                jnp.max(right, axis=0, keepdims=True) - off_right,
            )
            p_left = jnp.exp2(left - (m + off_left)).astype(BF16)
            p_right = jnp.exp2(right - (m + off_right)).astype(BF16)
            yield True
            o = nn(with_ones(vh[slot, part, :]), jnp.concatenate([p_left, p_right], 0))
            yield True
            tops.append(jnp.where(row_head, m, 0.0))
            totals.append(jnp.where(row_head, o[features : features + 1], 0.0))
            sums.append(nn(jnp.where(own, o[:features], 0.0).astype(BF16), spread))

        def finish():
            stats = spread_exact(jnp.concatenate(tops + totals, 0), spread)

            def heads(h):
                u, inside = divmod(h, together)
                return sums[u][head_rows(inside)]

            merge(everywhere, stats[:HEADS], stats[HEADS:], heads, 2.0**level)

        return [unit(u) for u in range(HEADS // together)], finish

    run([base_own(h) for h in range(HEADS)])
    forward(h4, 4)
    landed(hnear, 0, 192, recv01.at[0])
    project_side(hnear, 0)
    units, near_lanes, base_near, one_near = side(0, 1 - core)
    run(units)
    top, total, near_sums = by_head(base_near)
    merge(near_lanes, top, total, lambda h: near_sums[h], 1.0)
    forward(h3, 2)

    gather(h4, 4)
    gather(h3, 2)
    project(h4[...], 2, ROWS)
    project(h3[...], 3, ROWS)
    units4, finish4 = coarse(2, 4, group, devices // 8)
    units3, finish3 = coarse(3, 3, pair, devices // 4)
    run(units4 + units3)
    finish4()
    finish3()
    forward(h2, 0)

    landed(hfar, 0, 192, recv01.at[1])
    gather(h2, 0)
    project_side(hfar, 1)
    project(h2[...], 4, ROWS)
    units, far_lanes, base_far, one_far = side(1, core)
    units2, finish2 = coarse(4, 2, chip, devices // 2)
    run(units + units2)
    finish2()
    missing = off(jnp.where(core == 0, me == 0, me == devices - 1))
    top, total, far_sums = by_head(base_far)
    merge(far_lanes, top - missing, total, lambda h: far_sums[h], 1.0)
    near_top, near_total, near_one = by_head(one_near)
    far_top, far_total, far_one = by_head(one_far)
    far_top = far_top - missing
    top = jnp.maximum(near_top, far_top)
    factor_near = jnp.exp2(near_top - top)
    factor_far = jnp.exp2(far_top - top)
    total = near_total * factor_near + far_total * factor_far
    sums = [
        (near_one[h] * factor_near[h : h + 1] + far_one[h] * factor_far[h : h + 1]).astype(BF16)
        for h in range(HEADS)
    ]
    spread = spreader(BLOCK, BLOCK, 1)
    stats = spread_exact(jnp.concatenate([top, total], 0), spread)
    spread_sums = nn(jnp.concatenate(sums, 0), spread)
    merge(everywhere, stats[:HEADS], stats[HEADS:], lambda h: spread_sums[head_rows(h)], 2.0)

    inverse = 1.0 / den[...]
    attended = jnp.concatenate(
        [(acc[head_rows(h), :] * inverse[h : h + 1]).astype(BF16) for h in range(HEADS)], 0
    )
    loads[4].wait()
    turned = nt(eye[:ROWS, :ROWS], attended).astype(BF16)
    out_ref[...] = nn(turned, wo[...]).astype(BF16)

    for copy in sends:
        copy.wait_send()


def solution(mesh):
    devices = mesh.shape["ctx"] * mesh.shape["node"]

    def local(tokens, w_query, w_key, w_value, w_out):
        square = pltpu.VMEM((WIDTH, WIDTH), BF16)
        tall = pltpu.VMEM((ROWS, WIDTH), BF16)
        return pl.pallas_call(
            functools.partial(kernel, devices),
            out_shape=jax.ShapeDtypeStruct((ROWS, WIDTH), BF16),
            in_specs=[pl.BlockSpec(memory_space=pltpu.HBM)] * 5,
            out_specs=pl.BlockSpec(memory_space=pltpu.VMEM),
            scratch_shapes=[
                tall,
                square,
                square,
                square,
                square,
                square,
                pltpu.VMEM((COARSE, WIDTH), BF16),
                pltpu.VMEM((192, WIDTH), BF16),
                pltpu.VMEM((192, WIDTH), BF16),
                tall,
                tall,
                tall,
                tall,
                pltpu.VMEM((COARSE, WIDTH), BF16),
                tall,
                pltpu.VMEM((WIDTH, ROWS), BF16),
                pltpu.VMEM((5, ROWS, WIDTH), BF16),
                pltpu.VMEM((5, WIDTH, ROWS), BF16),
                pltpu.VMEM((WIDTH, ROWS), F32),
                pltpu.VMEM((HEADS, ROWS), F32),
                pltpu.VMEM((HEADS, ROWS), F32),
                pltpu.SemaphoreType.DMA((5,)),
                pltpu.SemaphoreType.DMA((24,)),
                pltpu.SemaphoreType.DMA((2,)),
                pltpu.SemaphoreType.DMA((6,)),
                pltpu.SemaphoreType.DMA((6,)),
            ],
            compiler_params=pltpu.CompilerParams(
                collective_id=0, has_side_effects=True, vmem_limit_bytes=40 * 2**20
            ),
            name="hierarchical_attention",
        )(*[pltpu.with_memory_space_constraint(a, pltpu.HBM) for a in (tokens, w_query, w_key, w_value, w_out)])

    placed = (P(("ctx", "node"), None), P(), P(), P(), P())
    return jax.shard_map(
        local, mesh=mesh, in_specs=placed, out_specs=P(("ctx", "node"), None), check_vma=False
    )
```

```python
import functools
import math

import jax
import jax.numpy as jnp
from jax import lax
from jax.experimental import pallas as pl
from jax.experimental.pallas import tpu as pltpu
from jax.sharding import PartitionSpec as P

HEADS = 8
HEAD = 64
WIDTH = HEADS * HEAD
BLOCK = 128
ROWS = 256
NODES = 8
FAR = 1e30
SCALE = math.log2(math.e) / math.sqrt(HEAD)
BF16 = jnp.bfloat16
F32 = jnp.float32
START = {1: 0, 2: 128, 3: 192, 4: 224}
COARSE = 240


def nn(a, b):
    return lax.dot_general(a, b, (((1,), (0,)), ((), ())), preferred_element_type=F32)


def nt(a, b):
    return lax.dot_general(a, b, (((1,), (1,)), ((), ())), preferred_element_type=F32)


def iota(shape, axis):
    return lax.broadcasted_iota(jnp.int32, shape, axis)


def averager(rows, columns, level):
    hit = iota((rows, columns), 0) == iota((rows, columns), 1) >> level
    return jnp.where(hit, 0.5**level, 0.0).astype(BF16)


def spreader(rows, queries, level):
    hit = (iota((rows, ROWS), 0) & (queries - 1)) == iota((rows, ROWS), 1) >> level
    return jnp.where(hit, 1.0, 0.0).astype(BF16)


def split(values):
    high = values.astype(BF16)
    rest = values - high.astype(F32)
    middle = rest.astype(BF16)
    return [high, middle, (rest - middle.astype(F32)).astype(BF16)]


def spread_all(sums, tops, totals, spread):
    rows = sums.shape[0]
    out = nn(jnp.concatenate([sums] + split(jnp.concatenate([tops, totals], 0)), 0), spread)
    stats = out[rows : rows + 16] + out[rows + 16 : rows + 32] + out[rows + 32 :]
    return out[:rows], stats[:8], stats[8:]


def lane_head(shape, width):
    return iota(shape, 1) >> (width.bit_length() - 1)


def kernel(
    devices, x_hbm, wq_hbm, wk_hbm, wv_hbm, wo_hbm, out_ref,
    x, wq, wk, wv, wo, wvt, t, hnear, hfar, deep, q0, ql, k0, v0, kh, vh, kd, vd, acc, peak, den,
    average, eye, halve, spread1, spread2, spread3, spread4,
    load_sem, send_sem, recv01, recv_far, recv_near,
):
    me = lax.axis_index("ctx") * NODES + lax.axis_index("node")
    core = lax.rem(me, 2)
    chip = lax.div(me, 2)
    pair = lax.div(me, 4)
    group = lax.div(me, 8)

    def place(index):
        index = lax.rem(index + devices, devices)
        return {"ctx": lax.div(index, NODES), "node": lax.rem(index, NODES)}

    loads = []
    for i, (source, kept) in enumerate(((x_hbm, x), (wq_hbm, wq), (wk_hbm, wk), (wv_hbm, wv), (wo_hbm, wo))):
        loads.append(pltpu.make_async_copy(source, kept, load_sem.at[i]))
    loads[0].start()

    twin = me + 1 - 2 * core
    beyond = me - 1 + 2 * core
    two = [(me + 2, 0), (me - 2, 1)]
    three = [(4 * (pair + s) + 2 * j + core, d) for s, d in ((1, 0), (-1, 1)) for j in range(2)]
    four = [(8 * (group + s) + 2 * j + core, d) for s, d in ((1, 0), (-1, 1)) for j in range(4)]

    barrier = pltpu.get_barrier_semaphore()
    partners = [target for target, _ in four + three + two] + [beyond, twin]
    for target in partners:
        pl.semaphore_signal(barrier, inc=1, device_id=place(target), device_id_type=pl.DeviceIdType.MESH)
    for load in loads[1:]:
        load.start()

    h2, h3, h4 = (deep.at[pl.ds(i * ROWS, ROWS)] for i in range(3))
    for l in range(1, 5):
        average[START[l] : START[l] + (ROWS >> l), :] = averager(ROWS >> l, ROWS, l)
    eye[...] = averager(ROWS, ROWS, 0)
    halve[...] = averager(64, BLOCK, 1)
    spreads = {1: spread1, 2: spread2, 3: spread3, 4: spread4}
    for l in range(1, 5):
        spreads[l][...] = spreader(spreads[l].shape[0], ROWS >> l, l)
    loads[0].wait()
    t[...] = nn(average[...], x[...]).astype(BF16)

    pl.semaphore_wait(barrier, len(partners))

    sends = []

    def send(source, target, landing, recv):
        copy = pltpu.make_async_remote_copy(
            src_ref=source,
            dst_ref=landing,
            send_sem=send_sem.at[len(sends)],
            recv_sem=recv,
            device_id=place(target),
            device_id_type=pl.DeviceIdType.MESH,
        )
        copy.start()
        sends.append(copy)

    def mine(direction):
        return direction * BLOCK + core * 64

    def edge(target, side, landing, recv):
        rows = pl.multiple_of(side * BLOCK, BLOCK)
        means = pl.multiple_of((1 - side) * 64, 64)
        send(x.at[pl.ds(rows, BLOCK)], target, landing.at[pl.ds(0, BLOCK)], recv)
        send(t.at[pl.ds(means, 64)], target, landing.at[pl.ds(BLOCK, 64)], recv)

    edge(twin, 1 - core, hnear, recv01.at[0])
    for target, d in four:
        row = pl.multiple_of(mine(d) + lax.rem(chip, 4) * 16, 16)
        send(t.at[pl.ds(START[4], 16)], target, h4.at[pl.ds(row, 16)], recv_far.at[4 + d])
    for target, d in three:
        row = pl.multiple_of(mine(d) + lax.rem(chip, 2) * 32, 16)
        send(t.at[pl.ds(START[3], 32)], target, h3.at[pl.ds(row, 32)], recv_far.at[2 + d])
    for target, d in two:
        row = pl.multiple_of(mine(d), 16)
        send(t.at[pl.ds(START[2], 64)], target, h2.at[pl.ds(row, 64)], recv_far.at[d])
    edge(beyond, core, hfar, recv01.at[1])

    def landed(buffer, start, rows, sem):
        region = buffer.at[pl.ds(start, rows)]
        pltpu.make_async_copy(region, region, sem).wait()

    def forward(buffer, which):
        for d in range(2):
            row = pl.multiple_of(mine(d), 16)
            landed(buffer, row, 64, recv_far.at[which + d])
            region = buffer.at[pl.ds(row, 64)]
            send(region, twin, region, recv_near.at[which + d])

    def gather(buffer, which):
        for d in range(2):
            row = pl.multiple_of(d * BLOCK + (1 - core) * 64, 16)
            landed(buffer, row, 64, recv_near.at[which + d])

    ones = jnp.ones((16, ROWS), BF16)
    half = lane_head((1, BLOCK), HEAD)
    pair_masks = [jnp.where(half == h, 1.0, 0.0).astype(BF16) for h in range(2)]

    def lanes_of(j):
        return slice(j * BLOCK, (j + 1) * BLOCK)

    def head_rows(h):
        return slice(h * HEAD, (h + 1) * HEAD)

    def pair_queries(block):
        return jnp.concatenate([block * pair_masks[0], block * pair_masks[1]], 0)

    def with_ones(v):
        return jnp.concatenate([v, ones[:, : v.shape[1]]], 0)

    def merge(lanes, top, total, heads, weight):
        before = peak[:, lanes]
        after = jnp.maximum(before, top)
        old = jnp.exp2(before - after)
        new = weight * jnp.exp2(top - after)
        den[:, lanes] = den[:, lanes] * old + new * total
        peak[:, lanes] = after
        for h in range(HEADS):
            rows = head_rows(h)
            acc[rows, lanes] = acc[rows, lanes] * old[h : h + 1] + heads(h) * new[h : h + 1]

    loads[1].wait()
    q0[...] = (nn(x[...], wq[...]) * SCALE).astype(BF16)
    ql[...] = nn(average[...], q0[...]).astype(BF16)
    loads[2].wait()
    k0[...] = nn(x[...], wk[...]).astype(BF16)
    loads[3].wait()
    for i in range(2):
        wvt[i * ROWS : (i + 1) * ROWS, :] = nt(eye[...], wv[:, i * ROWS : (i + 1) * ROWS]).astype(BF16)
    v0[...] = nt(wvt[...], x[...]).astype(BF16)

    def run(units):
        waiting, active = list(units), []
        while waiting or active:
            if waiting:
                active.append(waiting.pop(0))
            active = [unit for unit in active if next(unit, None) is not None]

    def attend(keys, queries, values, done):
        s = nt(keys(), queries())
        yield True
        m = jnp.max(s, axis=0, keepdims=True)
        p = jnp.exp2(s - m).astype(BF16)
        yield True
        done(m, nn(with_ones(values()), p))

    def base_own(h):
        pairs = lanes_of(h // 2)

        def done(m, o):
            peak[h : h + 1, :] = m
            den[h : h + 1, :] = o[HEAD : HEAD + 1]
            acc[head_rows(h), :] = o[:HEAD]

        return attend(
            lambda: k0[:, pairs], lambda: q0[:, pairs] * pair_masks[h % 2], lambda: v0[head_rows(h), :], done
        )

    def project_side(buffer, slot):
        rows = buffer[...]
        kh[slot, :192, :] = nn(rows, wk[...]).astype(BF16)
        vh[slot, :, :192] = nt(wvt[...], rows).astype(BF16)
        kh[slot, 192:, :] = nn(halve[...], kh[slot, :BLOCK, :]).astype(BF16)
        vh[slot, :, 192:] = nt(vh[slot, :, :BLOCK], halve[...]).astype(BF16)

    def side(slot, block):
        queries = pl.ds(pl.multiple_of(block * BLOCK, BLOCK), BLOCK)
        units, found = [], ([], [])
        for keys, q, part in (
            (slice(0, BLOCK), q0.at[queries], found[0]),
            (slice(BLOCK, 2 * BLOCK), ql.at[pl.ds(0, BLOCK)], found[1]),
        ):
            for j in range(HEADS // 2):
                units.append(
                    attend(
                        lambda keys=keys, j=j: kh[slot, keys, lanes_of(j)],
                        lambda q=q, j=j: pair_queries(q[:, lanes_of(j)]),
                        lambda keys=keys, j=j: vh[slot, lanes_of(j), keys],
                        lambda m, o, part=part: part.append((m, o)),
                    )
                )
        return units, queries, found[0], found[1]

    def by_head(part):
        tops = [m[:, lanes_of(h)] for m, _ in part for h in range(2)]
        totals = [o[BLOCK : BLOCK + 1, lanes_of(h)] for _, o in part for h in range(2)]
        sums = [o[head_rows(h), lanes_of(h)] for _, o in part for h in range(2)]
        return jnp.concatenate(tops, 0), jnp.concatenate(totals, 0), sums

    def off(missing):
        return jnp.where(missing, FAR, 0.0).astype(F32)

    everywhere = slice(0, ROWS)

    def coarse(level, index, count):
        queries = ROWS >> level
        together = min(HEADS, ROWS // queries)
        features = together * HEAD
        columns = together * queries
        keys = slice((level - 2) * ROWS, (level - 1) * ROWS)
        off_left, off_right = off(index == 0), off(index == count - 1)
        feature_head = lane_head((1, features), HEAD)
        column_head = lane_head((1, columns), queries)
        spread = spreads[level]
        found = []

        def unit(u):
            part = slice(u * features, (u + 1) * features)
            block = ql[START[level] : START[level] + queries, part]
            masked = [block * jnp.where(feature_head == h, 1.0, 0.0).astype(BF16) for h in range(together)]
            s = nt(kd[keys, part], jnp.concatenate(masked, 0))
            yield True
            left, right = s[:BLOCK], s[BLOCK:]
            m = jnp.maximum(
                jnp.max(left, axis=0, keepdims=True) - off_left,
                jnp.max(right, axis=0, keepdims=True) - off_right,
            )
            p_left = jnp.exp2(left - (m + off_left)).astype(BF16)
            p_right = jnp.exp2(right - (m + off_right)).astype(BF16)
            yield True
            o = nn(with_ones(vd[part, keys]), jnp.concatenate([p_left, p_right], 0))
            yield True
            own = [jnp.where(column_head == h, o[head_rows(h)], 0.0) for h in range(together)]
            row_head = iota((HEADS, columns), 0) == column_head + u * together
            found.append(
                spread_all(
                    jnp.concatenate(own, 0).astype(BF16),
                    jnp.where(row_head, m, 0.0),
                    jnp.where(row_head, o[features : features + 1], 0.0),
                    spread[...],
                )
            )

        def finish():
            def heads(h):
                u, inside = divmod(h, together)
                return found[u][0][head_rows(inside)]

            top = functools.reduce(jnp.add, [f[1] for f in found])
            total = functools.reduce(jnp.add, [f[2] for f in found])
            merge(everywhere, top, total, heads, 2.0**level)

        return [unit(u) for u in range(HEADS // together)], finish

    run([base_own(h) for h in range(HEADS)])
    landed(hnear, 0, 192, recv01.at[0])
    project_side(hnear, 0)
    units, near_lanes, base_near, one_near = side(0, 1 - core)
    run(units)
    top, total, near_sums = by_head(base_near)
    merge(near_lanes, top, total, lambda h: near_sums[h], 1.0)

    forward(h4, 4)
    forward(h3, 2)
    forward(h2, 0)
    gather(h4, 4)
    gather(h3, 2)
    gather(h2, 0)
    kd[...] = nn(deep[...], wk[...]).astype(BF16)
    vd[...] = nt(wvt[...], deep[...]).astype(BF16)
    levels = [coarse(4, group, devices // 8), coarse(3, pair, devices // 4), coarse(2, chip, devices // 2)]
    run([unit for units, _ in levels for unit in units])
    for _, finish in levels:
        finish()

    landed(hfar, 0, 192, recv01.at[1])
    project_side(hfar, 1)
    units, far_lanes, base_far, one_far = side(1, core)
    run(units)
    missing = off(jnp.where(core == 0, me == 0, me == devices - 1))
    top, total, far_sums = by_head(base_far)
    merge(far_lanes, top - missing, total, lambda h: far_sums[h], 1.0)
    near_top, near_total, near_one = by_head(one_near)
    far_top, far_total, far_one = by_head(one_far)
    far_top = far_top - missing
    top = jnp.maximum(near_top, far_top)
    factor_near = jnp.exp2(near_top - top)
    factor_far = jnp.exp2(far_top - top)
    total = near_total * factor_near + far_total * factor_far
    sums = [
        (near_one[h] * factor_near[h : h + 1] + far_one[h] * factor_far[h : h + 1]).astype(BF16)
        for h in range(HEADS)
    ]
    spread_sums, top, total = spread_all(jnp.concatenate(sums, 0), top, total, spread1[...])
    merge(everywhere, top, total, lambda h: spread_sums[head_rows(h)], 2.0)

    inverse = 1.0 / den[...]
    attended = jnp.concatenate(
        [(acc[head_rows(h), :] * inverse[h : h + 1]).astype(BF16) for h in range(HEADS)], 0
    )
    loads[4].wait()
    turned = nt(eye[...], attended).astype(BF16)
    out_ref[...] = nn(turned, wo[...]).astype(BF16)

    for copy in sends:
        copy.wait_send()


def solution(mesh):
    devices = mesh.shape["ctx"] * mesh.shape["node"]

    def local(tokens, w_query, w_key, w_value, w_out):
        square = pltpu.VMEM((WIDTH, WIDTH), BF16)
        tall = pltpu.VMEM((ROWS, WIDTH), BF16)
        return pl.pallas_call(
            functools.partial(kernel, devices),
            out_shape=jax.ShapeDtypeStruct((ROWS, WIDTH), BF16),
            in_specs=[pl.BlockSpec(memory_space=pltpu.HBM)] * 5,
            out_specs=pl.BlockSpec(memory_space=pltpu.VMEM),
            scratch_shapes=[
                tall,
                square,
                square,
                square,
                square,
                square,
                pltpu.VMEM((COARSE, WIDTH), BF16),
                pltpu.VMEM((192, WIDTH), BF16),
                pltpu.VMEM((192, WIDTH), BF16),
                pltpu.VMEM((3 * ROWS, WIDTH), BF16),
                tall,
                pltpu.VMEM((COARSE, WIDTH), BF16),
                tall,
                pltpu.VMEM((WIDTH, ROWS), BF16),
                pltpu.VMEM((2, ROWS, WIDTH), BF16),
                pltpu.VMEM((2, WIDTH, ROWS), BF16),
                pltpu.VMEM((3 * ROWS, WIDTH), BF16),
                pltpu.VMEM((WIDTH, 3 * ROWS), BF16),
                pltpu.VMEM((WIDTH, ROWS), F32),
                pltpu.VMEM((HEADS, ROWS), F32),
                pltpu.VMEM((HEADS, ROWS), F32),
                pltpu.VMEM((COARSE, ROWS), BF16),
                pltpu.VMEM((ROWS, ROWS), BF16),
                pltpu.VMEM((64, BLOCK), BF16),
                pltpu.VMEM((BLOCK, ROWS), BF16),
                pltpu.VMEM((ROWS, ROWS), BF16),
                pltpu.VMEM((ROWS, ROWS), BF16),
                pltpu.VMEM((BLOCK, ROWS), BF16),
                pltpu.SemaphoreType.DMA((5,)),
                pltpu.SemaphoreType.DMA((24,)),
                pltpu.SemaphoreType.DMA((2,)),
                pltpu.SemaphoreType.DMA((6,)),
                pltpu.SemaphoreType.DMA((6,)),
            ],
            compiler_params=pltpu.CompilerParams(
                collective_id=0, has_side_effects=True, vmem_limit_bytes=40 * 2**20
            ),
            name="hierarchical_attention",
        )(*[pltpu.with_memory_space_constraint(a, pltpu.HBM) for a in (tokens, w_query, w_key, w_value, w_out)])

    placed = (P(("ctx", "node"), None), P(), P(), P(), P())
    return jax.shard_map(
        local, mesh=mesh, in_specs=placed, out_specs=P(("ctx", "node"), None), check_vma=False
    )
```

```python
import functools
import math

import jax
import jax.numpy as jnp
from jax import lax
from jax.experimental import pallas as pl
from jax.experimental.pallas import tpu as pltpu
from jax.sharding import PartitionSpec as P

HEADS = 8
HEAD = 64
WIDTH = HEADS * HEAD
BLOCK = 128
ROWS = 256
NODES = 8
FAR = 1e30
SCALE = math.log2(math.e) / math.sqrt(HEAD)
BF16 = jnp.bfloat16
F32 = jnp.float32
START = {1: 0, 2: 128, 3: 192, 4: 224}
COARSE = 240


def nn(a, b):
    return lax.dot_general(a, b, (((1,), (0,)), ((), ())), preferred_element_type=F32)


def nt(a, b):
    return lax.dot_general(a, b, (((1,), (1,)), ((), ())), preferred_element_type=F32)


def iota(shape, axis):
    return lax.broadcasted_iota(jnp.int32, shape, axis)


def averager(rows, columns, level):
    hit = iota((rows, columns), 0) == iota((rows, columns), 1) >> level
    return jnp.where(hit, 0.5**level, 0.0).astype(BF16)


def spreader(rows, queries, level):
    hit = (iota((rows, ROWS), 0) & (queries - 1)) == iota((rows, ROWS), 1) >> level
    return jnp.where(hit, 1.0, 0.0).astype(BF16)


def split(values):
    high = values.astype(BF16)
    rest = values - high.astype(F32)
    middle = rest.astype(BF16)
    return [high, middle, (rest - middle.astype(F32)).astype(BF16)]


def spread_all(sums, tops, totals, spread):
    rows = sums.shape[0]
    out = nn(jnp.concatenate([sums] + split(jnp.concatenate([tops, totals], 0)), 0), spread)
    stats = out[rows : rows + 16] + out[rows + 16 : rows + 32] + out[rows + 32 :]
    return out[:rows], stats[:8], stats[8:]


def lane_head(shape, width):
    return iota(shape, 1) >> (width.bit_length() - 1)


def kernel(
    devices, x_hbm, wq_hbm, wk_hbm, wv_hbm, wo_hbm, out_ref,
    x, wq, wk, wv, wo, wvt, t, hnear, hfar, deep, q0, ql, k0, v0, kh, vh, kd, vd, acc, peak, den,
    average, eye, halve, spread1, spread2, spread3, spread4,
    load_sem, send_sem, recv01, recv_far, recv_near,
):
    me = lax.axis_index("ctx") * NODES + lax.axis_index("node")
    core = lax.rem(me, 2)
    chip = lax.div(me, 2)
    pair = lax.div(me, 4)
    group = lax.div(me, 8)

    def place(index):
        index = lax.rem(index + devices, devices)
        return {"ctx": lax.div(index, NODES), "node": lax.rem(index, NODES)}

    loads = []
    for i, (source, kept) in enumerate(((x_hbm, x), (wq_hbm, wq), (wk_hbm, wk), (wv_hbm, wv), (wo_hbm, wo))):
        loads.append(pltpu.make_async_copy(source, kept, load_sem.at[i]))
    loads[0].start()

    twin = me + 1 - 2 * core
    beyond = me - 1 + 2 * core
    two = [(me + 2, 0), (me - 2, 1)]
    three = [(4 * (pair + s) + 2 * j + core, d) for s, d in ((1, 0), (-1, 1)) for j in range(2)]
    four = [(8 * (group + s) + 2 * j + core, d) for s, d in ((1, 0), (-1, 1)) for j in range(4)]

    barrier = pltpu.get_barrier_semaphore()
    partners = [target for target, _ in four + three + two] + [beyond, twin]
    for target in partners:
        pl.semaphore_signal(barrier, inc=1, device_id=place(target), device_id_type=pl.DeviceIdType.MESH)
    for load in loads[1:]:
        load.start()

    pl.semaphore_wait(barrier, len(partners))

    sends = []

    def send(source, target, landing, recv):
        copy = pltpu.make_async_remote_copy(
            src_ref=source,
            dst_ref=landing,
            send_sem=send_sem.at[len(sends)],
            recv_sem=recv,
            device_id=place(target),
            device_id_type=pl.DeviceIdType.MESH,
        )
        copy.start()
        sends.append(copy)

    def mine(direction):
        return direction * BLOCK + core * 64

    edges = [(beyond, core, hfar, recv01.at[1]), (twin, 1 - core, hnear, recv01.at[0])]
    for target, side, landing, recv in edges:
        rows = pl.multiple_of(side * BLOCK, BLOCK)
        send(x_hbm.at[pl.ds(rows, BLOCK)], target, landing.at[pl.ds(0, BLOCK)], recv)

    h2, h3, h4 = (deep.at[pl.ds(i * ROWS, ROWS)] for i in range(3))
    for l in range(1, 5):
        average[START[l] : START[l] + (ROWS >> l), :] = averager(ROWS >> l, ROWS, l)
    eye[...] = averager(ROWS, ROWS, 0)
    halve[...] = averager(64, BLOCK, 1)
    spreads = {1: spread1, 2: spread2, 3: spread3, 4: spread4}
    for l in range(1, 5):
        spreads[l][...] = spreader(spreads[l].shape[0], ROWS >> l, l)
    loads[0].wait()
    t[...] = nn(average[...], x[...]).astype(BF16)

    for target, side, landing, recv in edges:
        means = pl.multiple_of((1 - side) * 64, 64)
        send(t.at[pl.ds(means, 64)], target, landing.at[pl.ds(BLOCK, 64)], recv)
    for target, d in two:
        row = pl.multiple_of(mine(d), 16)
        send(t.at[pl.ds(START[2], 64)], target, h2.at[pl.ds(row, 64)], recv_far.at[d])
    for target, d in three:
        row = pl.multiple_of(mine(d) + lax.rem(chip, 2) * 32, 16)
        send(t.at[pl.ds(START[3], 32)], target, h3.at[pl.ds(row, 32)], recv_far.at[2 + d])
    for target, d in four:
        row = pl.multiple_of(mine(d) + lax.rem(chip, 4) * 16, 16)
        send(t.at[pl.ds(START[4], 16)], target, h4.at[pl.ds(row, 16)], recv_far.at[4 + d])

    def landed(buffer, start, rows, sem):
        region = buffer.at[pl.ds(start, rows)]
        pltpu.make_async_copy(region, region, sem).wait()

    def forward(buffer, which):
        for d in range(2):
            row = pl.multiple_of(mine(d), 16)
            landed(buffer, row, 64, recv_far.at[which + d])
            region = buffer.at[pl.ds(row, 64)]
            send(region, twin, region, recv_near.at[which + d])

    def gather(buffer, which):
        for d in range(2):
            row = pl.multiple_of(d * BLOCK + (1 - core) * 64, 16)
            landed(buffer, row, 64, recv_near.at[which + d])

    ones = jnp.ones((16, ROWS), BF16)
    half = lane_head((1, BLOCK), HEAD)
    pair_masks = [jnp.where(half == h, 1.0, 0.0).astype(BF16) for h in range(2)]

    def lanes_of(j):
        return slice(j * BLOCK, (j + 1) * BLOCK)

    def head_rows(h):
        return slice(h * HEAD, (h + 1) * HEAD)

    def pair_queries(block):
        return jnp.concatenate([block * pair_masks[0], block * pair_masks[1]], 0)

    def with_ones(v):
        return jnp.concatenate([v, ones[:, : v.shape[1]]], 0)

    def merge(lanes, top, total, heads, weight):
        before = peak[:, lanes]
        after = jnp.maximum(before, top)
        old = jnp.exp2(before - after)
        new = weight * jnp.exp2(top - after)
        den[:, lanes] = den[:, lanes] * old + new * total
        peak[:, lanes] = after
        for h in range(HEADS):
            rows = head_rows(h)
            acc[rows, lanes] = acc[rows, lanes] * old[h : h + 1] + heads(h) * new[h : h + 1]

    loads[1].wait()
    q0[...] = (nn(x[...], wq[...]) * SCALE).astype(BF16)
    ql[...] = nn(average[...], q0[...]).astype(BF16)
    loads[2].wait()
    k0[...] = nn(x[...], wk[...]).astype(BF16)
    loads[3].wait()
    for i in range(2):
        wvt[i * ROWS : (i + 1) * ROWS, :] = nt(eye[...], wv[:, i * ROWS : (i + 1) * ROWS]).astype(BF16)
    v0[...] = nt(wvt[...], x[...]).astype(BF16)

    def run(units):
        waiting, active = list(units), []
        while waiting or active:
            if waiting:
                active.append(waiting.pop(0))
            active = [unit for unit in active if next(unit, None) is not None]

    def attend(keys, queries, values, done):
        s = nt(keys(), queries())
        yield True
        m = jnp.max(s, axis=0, keepdims=True)
        p = jnp.exp2(s - m).astype(BF16)
        yield True
        done(m, nn(with_ones(values()), p))

    def base_own(h):
        pairs = lanes_of(h // 2)

        def done(m, o):
            peak[h : h + 1, :] = m
            den[h : h + 1, :] = o[HEAD : HEAD + 1]
            acc[head_rows(h), :] = o[:HEAD]

        return attend(
            lambda: k0[:, pairs], lambda: q0[:, pairs] * pair_masks[h % 2], lambda: v0[head_rows(h), :], done
        )

    def project_side(buffer, slot):
        rows = buffer[...]
        kh[slot, :192, :] = nn(rows, wk[...]).astype(BF16)
        vh[slot, :, :192] = nt(wvt[...], rows).astype(BF16)
        kh[slot, 192:, :] = nn(halve[...], kh[slot, :BLOCK, :]).astype(BF16)
        vh[slot, :, 192:] = nt(vh[slot, :, :BLOCK], halve[...]).astype(BF16)

    def side(slot, block):
        queries = pl.ds(pl.multiple_of(block * BLOCK, BLOCK), BLOCK)
        units, found = [], ([], [])
        for keys, q, part in (
            (slice(0, BLOCK), q0.at[queries], found[0]),
            (slice(BLOCK, 2 * BLOCK), ql.at[pl.ds(0, BLOCK)], found[1]),
        ):
            for j in range(HEADS // 2):
                units.append(
                    attend(
                        lambda keys=keys, j=j: kh[slot, keys, lanes_of(j)],
                        lambda q=q, j=j: pair_queries(q[:, lanes_of(j)]),
                        lambda keys=keys, j=j: vh[slot, lanes_of(j), keys],
                        lambda m, o, part=part: part.append((m, o)),
                    )
                )
        return units, queries, found[0], found[1]

    def by_head(part):
        tops = [m[:, lanes_of(h)] for m, _ in part for h in range(2)]
        totals = [o[BLOCK : BLOCK + 1, lanes_of(h)] for _, o in part for h in range(2)]
        sums = [o[head_rows(h), lanes_of(h)] for _, o in part for h in range(2)]
        return jnp.concatenate(tops, 0), jnp.concatenate(totals, 0), sums

    def off(missing):
        return jnp.where(missing, FAR, 0.0).astype(F32)

    everywhere = slice(0, ROWS)

    def coarse(level, index, count):
        queries = ROWS >> level
        together = min(HEADS, ROWS // queries)
        features = together * HEAD
        columns = together * queries
        keys = slice((level - 2) * ROWS, (level - 1) * ROWS)
        off_left, off_right = off(index == 0), off(index == count - 1)
        feature_head = lane_head((1, features), HEAD)
        column_head = lane_head((1, columns), queries)
        spread = spreads[level]
        found = []

        def unit(u):
            part = slice(u * features, (u + 1) * features)
            block = ql[START[level] : START[level] + queries, part]
            masked = [block * jnp.where(feature_head == h, 1.0, 0.0).astype(BF16) for h in range(together)]
            s = nt(kd[keys, part], jnp.concatenate(masked, 0))
            yield True
            left, right = s[:BLOCK], s[BLOCK:]
            m = jnp.maximum(
                jnp.max(left, axis=0, keepdims=True) - off_left,
                jnp.max(right, axis=0, keepdims=True) - off_right,
            )
            p_left = jnp.exp2(left - (m + off_left)).astype(BF16)
            p_right = jnp.exp2(right - (m + off_right)).astype(BF16)
            yield True
            o = nn(with_ones(vd[part, keys]), jnp.concatenate([p_left, p_right], 0))
            yield True
            own = [jnp.where(column_head == h, o[head_rows(h)], 0.0) for h in range(together)]
            row_head = iota((HEADS, columns), 0) == column_head + u * together
            found.append(
                spread_all(
                    jnp.concatenate(own, 0).astype(BF16),
                    jnp.where(row_head, m, 0.0),
                    jnp.where(row_head, o[features : features + 1], 0.0),
                    spread[...],
                )
            )

        def finish():
            def heads(h):
                u, inside = divmod(h, together)
                return found[u][0][head_rows(inside)]

            top = functools.reduce(jnp.add, [f[1] for f in found])
            total = functools.reduce(jnp.add, [f[2] for f in found])
            merge(everywhere, top, total, heads, 2.0**level)

        return [unit(u) for u in range(HEADS // together)], finish

    run([base_own(h) for h in range(HEADS)])
    landed(hnear, 0, 192, recv01.at[0])
    project_side(hnear, 0)
    units, near_lanes, base_near, one_near = side(0, 1 - core)
    run(units)
    top, total, near_sums = by_head(base_near)
    merge(near_lanes, top, total, lambda h: near_sums[h], 1.0)

    landed(hfar, 0, 192, recv01.at[1])
    project_side(hfar, 1)
    units, far_lanes, base_far, one_far = side(1, core)
    run(units)
    missing = off(jnp.where(core == 0, me == 0, me == devices - 1))
    top, total, far_sums = by_head(base_far)
    merge(far_lanes, top - missing, total, lambda h: far_sums[h], 1.0)
    near_top, near_total, near_one = by_head(one_near)
    far_top, far_total, far_one = by_head(one_far)
    far_top = far_top - missing
    top = jnp.maximum(near_top, far_top)
    factor_near = jnp.exp2(near_top - top)
    factor_far = jnp.exp2(far_top - top)
    total = near_total * factor_near + far_total * factor_far
    sums = [
        (near_one[h] * factor_near[h : h + 1] + far_one[h] * factor_far[h : h + 1]).astype(BF16)
        for h in range(HEADS)
    ]
    spread_sums, top, total = spread_all(jnp.concatenate(sums, 0), top, total, spread1[...])
    merge(everywhere, top, total, lambda h: spread_sums[head_rows(h)], 2.0)

    forward(h2, 0)
    forward(h3, 2)
    forward(h4, 4)
    gather(h4, 4)
    gather(h3, 2)
    gather(h2, 0)
    kd[...] = nn(deep[...], wk[...]).astype(BF16)
    vd[...] = nt(wvt[...], deep[...]).astype(BF16)
    levels = [coarse(4, group, devices // 8), coarse(3, pair, devices // 4), coarse(2, chip, devices // 2)]
    run([unit for units, _ in levels for unit in units])
    for _, finish in levels:
        finish()

    inverse = 1.0 / den[...]
    attended = jnp.concatenate(
        [(acc[head_rows(h), :] * inverse[h : h + 1]).astype(BF16) for h in range(HEADS)], 0
    )
    loads[4].wait()
    turned = nt(eye[...], attended).astype(BF16)
    out_ref[...] = nn(turned, wo[...]).astype(BF16)

    for copy in sends:
        copy.wait_send()


def solution(mesh):
    devices = mesh.shape["ctx"] * mesh.shape["node"]

    def local(tokens, w_query, w_key, w_value, w_out):
        square = pltpu.VMEM((WIDTH, WIDTH), BF16)
        tall = pltpu.VMEM((ROWS, WIDTH), BF16)
        return pl.pallas_call(
            functools.partial(kernel, devices),
            out_shape=jax.ShapeDtypeStruct((ROWS, WIDTH), BF16),
            in_specs=[pl.BlockSpec(memory_space=pltpu.HBM)] * 5,
            out_specs=pl.BlockSpec(memory_space=pltpu.VMEM),
            scratch_shapes=[
                tall,
                square,
                square,
                square,
                square,
                square,
                pltpu.VMEM((COARSE, WIDTH), BF16),
                pltpu.VMEM((192, WIDTH), BF16),
                pltpu.VMEM((192, WIDTH), BF16),
                pltpu.VMEM((3 * ROWS, WIDTH), BF16),
                tall,
                pltpu.VMEM((COARSE, WIDTH), BF16),
                tall,
                pltpu.VMEM((WIDTH, ROWS), BF16),
                pltpu.VMEM((2, ROWS, WIDTH), BF16),
                pltpu.VMEM((2, WIDTH, ROWS), BF16),
                pltpu.VMEM((3 * ROWS, WIDTH), BF16),
                pltpu.VMEM((WIDTH, 3 * ROWS), BF16),
                pltpu.VMEM((WIDTH, ROWS), F32),
                pltpu.VMEM((HEADS, ROWS), F32),
                pltpu.VMEM((HEADS, ROWS), F32),
                pltpu.VMEM((COARSE, ROWS), BF16),
                pltpu.VMEM((ROWS, ROWS), BF16),
                pltpu.VMEM((64, BLOCK), BF16),
                pltpu.VMEM((BLOCK, ROWS), BF16),
                pltpu.VMEM((ROWS, ROWS), BF16),
                pltpu.VMEM((ROWS, ROWS), BF16),
                pltpu.VMEM((BLOCK, ROWS), BF16),
                pltpu.SemaphoreType.DMA((5,)),
                pltpu.SemaphoreType.DMA((24,)),
                pltpu.SemaphoreType.DMA((2,)),
                pltpu.SemaphoreType.DMA((6,)),
                pltpu.SemaphoreType.DMA((6,)),
            ],
            compiler_params=pltpu.CompilerParams(
                collective_id=0, has_side_effects=True, vmem_limit_bytes=40 * 2**20
            ),
            name="hierarchical_attention",
        )(*[pltpu.with_memory_space_constraint(a, pltpu.HBM) for a in (tokens, w_query, w_key, w_value, w_out)])

    placed = (P(("ctx", "node"), None), P(), P(), P(), P())
    return jax.shard_map(
        local, mesh=mesh, in_specs=placed, out_specs=P(("ctx", "node"), None), check_vma=False
    )
```

```python
import functools
import math

import jax
import jax.numpy as jnp
from jax import lax
from jax.experimental import pallas as pl
from jax.experimental.pallas import tpu as pltpu
from jax.sharding import PartitionSpec as P

HEADS = 8
HEAD = 64
WIDTH = HEADS * HEAD
BLOCK = 128
ROWS = 256
NODES = 8
FAR = 1e30
SCALE = math.log2(math.e) / math.sqrt(HEAD)
BF16 = jnp.bfloat16
F32 = jnp.float32
START = {1: 0, 2: 128, 3: 192, 4: 224}
COARSE = 240


def nn(a, b):
    return lax.dot_general(a, b, (((1,), (0,)), ((), ())), preferred_element_type=F32)


def nt(a, b):
    return lax.dot_general(a, b, (((1,), (1,)), ((), ())), preferred_element_type=F32)


def iota(shape, axis):
    return lax.broadcasted_iota(jnp.int32, shape, axis)


def averager(rows, columns, level):
    hit = iota((rows, columns), 0) == iota((rows, columns), 1) >> level
    return jnp.where(hit, 0.5**level, 0.0).astype(BF16)


def spreader(rows, queries, level):
    hit = (iota((rows, ROWS), 0) & (queries - 1)) == iota((rows, ROWS), 1) >> level
    return jnp.where(hit, 1.0, 0.0).astype(BF16)


def split(values):
    high = values.astype(BF16)
    rest = values - high.astype(F32)
    middle = rest.astype(BF16)
    return [high, middle, (rest - middle.astype(F32)).astype(BF16)]


def spread_all(sums, tops, totals, spread):
    rows = sums.shape[0]
    out = nn(jnp.concatenate([sums] + split(jnp.concatenate([tops, totals], 0)), 0), spread)
    stats = out[rows : rows + 16] + out[rows + 16 : rows + 32] + out[rows + 32 :]
    return out[:rows], stats[:8], stats[8:]


def lane_head(shape, width):
    return iota(shape, 1) >> (width.bit_length() - 1)


def kernel(
    devices, x_hbm, wq_hbm, wk_hbm, wv_hbm, wo_hbm, out_ref,
    x, wq, wk, wv, wo, wvt, t, hnear, hfar, deep, q0, ql, k0, v0, kh, vh, u2, u3, u4, vd, acc, peak, den,
    average, eye, halve, fold, spread1, spread2, spread3, spread4,
    load_sem, send_sem, recv01, recv_far, recv_near,
):
    me = lax.axis_index("ctx") * NODES + lax.axis_index("node")
    core = lax.rem(me, 2)
    chip = lax.div(me, 2)
    pair = lax.div(me, 4)
    group = lax.div(me, 8)

    def place(index):
        index = lax.rem(index + devices, devices)
        return {"ctx": lax.div(index, NODES), "node": lax.rem(index, NODES)}

    loads = []
    for i, (source, kept) in enumerate(((x_hbm, x), (wq_hbm, wq), (wk_hbm, wk), (wv_hbm, wv), (wo_hbm, wo))):
        loads.append(pltpu.make_async_copy(source, kept, load_sem.at[i]))
    loads[0].start()

    twin = me + 1 - 2 * core
    beyond = me - 1 + 2 * core
    odd = lax.rem(chip, 2)
    second = lax.rem(pair, 2)
    step = 1 - 2 * second
    two = me + 3 - 6 * core
    three = [(me + 4 - 8 * odd, odd, 1), (me - 4 + 8 * odd, 1 - odd, 0), (me + 6 - 12 * odd, odd, 0)]
    ahead, behind = 8 * (group + step) + core, 8 * (group - step) + core
    four = [(ahead + 4 * second + 2 * j, second, 1) for j in range(2)]
    four += [(ahead + 4 * (1 - second) + 2 * j, second, 0) for j in range(2)]
    four += [(behind + 4 * second + 2 * j, 1 - second, 0) for j in range(2)]

    barrier = pltpu.get_barrier_semaphore()
    partners = [target for target, _, _ in four + three] + [two, beyond, twin]
    for target in partners:
        pl.semaphore_signal(barrier, inc=1, device_id=place(target), device_id_type=pl.DeviceIdType.MESH)
    for load in loads[1:]:
        load.start()

    pl.semaphore_wait(barrier, len(partners))

    def send(source, target, landing, recv, sent):
        pltpu.make_async_remote_copy(
            src_ref=source,
            dst_ref=landing,
            send_sem=send_sem.at[sent],
            recv_sem=recv,
            device_id=place(target),
            device_id_type=pl.DeviceIdType.MESH,
        ).start()

    def mine(direction):
        return direction * BLOCK + core * 64

    edges = [(beyond, core, hfar, recv01.at[1]), (twin, 1 - core, hnear, recv01.at[0])]
    for target, side, landing, recv in edges:
        rows = pl.multiple_of(side * BLOCK, BLOCK)
        send(x_hbm.at[pl.ds(rows, BLOCK)], target, landing.at[pl.ds(0, BLOCK)], recv, 0)

    h2, h3, h4 = (deep.at[pl.ds(i * ROWS, ROWS)] for i in range(3))
    for l in range(1, 5):
        average[START[l] : START[l] + (ROWS >> l), :] = averager(ROWS >> l, ROWS, l)
    eye[...] = averager(ROWS, ROWS, 0)
    halve[...] = averager(64, BLOCK, 1)
    fold[:32, :] = jnp.concatenate([averager(32, BLOCK, 2), jnp.zeros((32, 64), BF16)], 1)
    fold[32:, :] = jnp.concatenate([jnp.zeros((32, BLOCK), BF16), averager(32, 64, 1)], 1)
    spreads = {1: spread1, 2: spread2, 3: spread3, 4: spread4}
    for l in range(1, 5):
        spreads[l][...] = spreader(spreads[l].shape[0], ROWS >> l, l)
    loads[0].wait()
    t[...] = nn(average[...], x[...]).astype(BF16)

    for target, side, landing, recv in edges:
        means = pl.multiple_of((1 - side) * 64, 64)
        send(t.at[pl.ds(means, 64)], target, landing.at[pl.ds(BLOCK, 64)], recv, 1)
    send(t.at[pl.ds(START[2], 64)], two, h2.at[pl.ds(pl.multiple_of(64 + core * 64, 64), 64)], recv_far.at[0], 1)
    for target, d, short in three:
        row = pl.multiple_of(mine(d) + odd * 32, 32)
        send(t.at[pl.ds(START[3], 32)], target, h3.at[pl.ds(row, 32)], recv_far.at[2 + short], 1)
    for target, d, short in four:
        row = pl.multiple_of(mine(d) + lax.rem(chip, 4) * 16, 16)
        send(t.at[pl.ds(START[4], 16)], target, h4.at[pl.ds(row, 16)], recv_far.at[4 + short], 1)

    def landed(buffer, start, rows, sem):
        region = buffer.at[pl.ds(start, rows)]
        pltpu.make_async_copy(region, region, sem).wait()

    def forward(buffer, which):
        for d in range(2):
            row = pl.multiple_of(mine(d), 16)
            region = buffer.at[pl.ds(row, 64)]
            send(region, twin, region, recv_near.at[which + d], 2)

    def finer(source, d, target, inside):
        rows = source[pl.ds(pl.multiple_of(mine(d), 64), 64), :]
        means = nn(halve[:32, :64], rows).astype(BF16)
        target[pl.ds(pl.multiple_of(mine(d) + inside * 32, 32), 32), :] = means

    def gather(buffer, which):
        for d in range(2):
            row = pl.multiple_of(d * BLOCK + (1 - core) * 64, 16)
            landed(buffer, row, 64, recv_near.at[which + d])

    ones = jnp.ones((16, ROWS), BF16)
    half = lane_head((1, BLOCK), HEAD)
    pair_masks = [jnp.where(half == h, 1.0, 0.0).astype(BF16) for h in range(2)]

    def lanes_of(j):
        return slice(j * BLOCK, (j + 1) * BLOCK)

    def head_rows(h):
        return slice(h * HEAD, (h + 1) * HEAD)

    def pair_queries(block):
        return jnp.concatenate([block * pair_masks[0], block * pair_masks[1]], 0)

    def with_ones(v):
        return jnp.concatenate([v, ones[:, : v.shape[1]]], 0)

    def merge(lanes, top, total, heads):
        before = peak[:, lanes]
        after = jnp.maximum(before, top)
        old = jnp.exp2(before - after)
        new = jnp.exp2(top - after)
        den[:, lanes] = den[:, lanes] * old + new * total
        peak[:, lanes] = after
        for h in range(HEADS):
            rows = head_rows(h)
            acc[rows, lanes] = acc[rows, lanes] * old[h : h + 1] + heads(h) * new[h : h + 1]

    def run(units):
        waiting, active = list(units), []
        while waiting or active:
            if waiting:
                active.append(waiting.pop(0))
            active = [unit for unit in active if next(unit, None) is not None]

    def attend(keys, queries, values, done):
        s = nt(keys(), queries())
        yield True
        m = jnp.max(s, axis=0, keepdims=True)
        p = jnp.exp2(s - m).astype(BF16)
        yield True
        done(m, nn(with_ones(values()), p))

    def base_own(h):
        pairs = lanes_of(h // 2)

        def done(m, o):
            peak[h : h + 1, :] = m
            den[h : h + 1, :] = o[HEAD : HEAD + 1]
            acc[head_rows(h), :] = o[:HEAD]

        return attend(
            lambda: k0[:, pairs], lambda: q0[:, pairs] * pair_masks[h % 2], lambda: v0[head_rows(h), :], done
        )

    def project_side(buffer, slot):
        rows = buffer[...]
        kh[slot, :192, :] = nn(rows, wk[...]).astype(BF16)
        vh[slot, :, :192] = nt(wvt[...], rows).astype(BF16)

    def halve_side(slot):
        kh[slot, 192:, :] = nn(halve[...], kh[slot, :BLOCK, :]).astype(BF16)
        vh[slot, :, 192:] = nt(vh[slot, :, :BLOCK], halve[...]).astype(BF16)

    def side(slot, block):
        queries = pl.ds(pl.multiple_of(block * BLOCK, BLOCK), BLOCK)
        units, found = [], ([], [])
        for keys, q, part in (
            (slice(0, BLOCK), q0.at[queries], found[0]),
            (slice(BLOCK, 2 * BLOCK), ql.at[pl.ds(0, BLOCK)], found[1]),
        ):
            for j in range(HEADS // 2):
                units.append(
                    attend(
                        lambda keys=keys, j=j: kh[slot, keys, lanes_of(j)],
                        lambda q=q, j=j: pair_queries(q[:, lanes_of(j)]),
                        lambda keys=keys, j=j: vh[slot, lanes_of(j), keys],
                        lambda m, o, part=part: part.append((m, o)),
                    )
                )
        return units, queries, found[0], found[1]

    def by_head(part):
        tops = [m[:, lanes_of(h)] for m, _ in part for h in range(2)]
        totals = [o[BLOCK : BLOCK + 1, lanes_of(h)] for _, o in part for h in range(2)]
        sums = [o[head_rows(h), lanes_of(h)] for _, o in part for h in range(2)]
        return jnp.concatenate(tops, 0), jnp.concatenate(totals, 0), sums

    def off(missing):
        return jnp.where(missing, FAR, 0.0).astype(F32)

    everywhere = slice(0, ROWS)

    seen = {2: u2, 3: u3, 4: u4}

    def shape_of(level):
        queries = ROWS >> level
        together = min(HEADS, ROWS // queries)
        return queries, together, together * queries

    def look(level):
        queries = ROWS >> level
        for u in range(2):
            part = slice(u * ROWS, (u + 1) * ROWS)
            block = ql[START[level] : START[level] + queries, part]
            masked = [block * jnp.where(lane_head((1, ROWS), HEAD) == h, 1.0, 0.0).astype(BF16) for h in range(4)]
            rows = slice(u * 4 * queries, (u + 1) * 4 * queries)
            seen[level][rows, :] = nt(jnp.concatenate(masked, 0), wk[:, part]).astype(BF16)

    def coarse(level, index, count):
        queries, together, columns = shape_of(level)
        features = together * HEAD
        keys = slice((level - 2) * ROWS, (level - 1) * ROWS)
        off_left, off_right = off(index == 0), off(index == count - 1)
        column_head = lane_head((1, columns), queries)
        found = []

        def unit(u):
            part = slice(u * features, (u + 1) * features)
            s = nt(deep[keys, :], seen[level][u * columns : (u + 1) * columns, :])
            yield True
            left, right = s[:BLOCK], s[BLOCK:]
            m = jnp.maximum(
                jnp.max(left, axis=0, keepdims=True) - off_left,
                jnp.max(right, axis=0, keepdims=True) - off_right,
            )
            p_left = jnp.exp2(left - (m + off_left)).astype(BF16)
            p_right = jnp.exp2(right - (m + off_right)).astype(BF16)
            yield True
            o = nn(with_ones(vd[part, keys]), jnp.concatenate([p_left, p_right], 0))
            yield True
            own = [jnp.where(column_head == h, o[head_rows(h)], 0.0) for h in range(together)]
            row_head = iota((HEADS, columns), 0) == column_head + u * together
            found.append(
                spread_all(
                    jnp.concatenate(own, 0).astype(BF16),
                    jnp.where(row_head, m, 0.0),
                    jnp.where(row_head, o[features : features + 1], 0.0),
                    spreads[level][...],
                )
            )

        def gathered():
            def heads(h):
                u, inside = divmod(h, together)
                return found[u][0][head_rows(inside)]

            top = functools.reduce(jnp.add, [f[1] for f in found])
            total = functools.reduce(jnp.add, [f[2] for f in found])
            return top, total, heads, 2.0**level

        return [unit(u) for u in range(HEADS // together)], gathered

    for load in loads[1:4]:
        load.wait()
    landed(hnear, 0, 192, recv01.at[0])
    q0[...] = (nn(x[...], wq[...]) * SCALE).astype(BF16)
    k0[...] = nn(x[...], wk[...]).astype(BF16)
    for i in range(2):
        wvt[i * ROWS : (i + 1) * ROWS, :] = nt(eye[...], wv[:, i * ROWS : (i + 1) * ROWS]).astype(BF16)
    ql[...] = nn(average[...], q0[...]).astype(BF16)
    v0[...] = nt(wvt[...], x[...]).astype(BF16)
    project_side(hnear, 0)
    units, near_lanes, base_near, one_near = side(0, 1 - core)
    own_units = [base_own(h) for h in range(HEADS)]
    run(own_units[:4])
    halve_side(0)
    run(own_units[4:] + units)
    top, total, near_sums = by_head(base_near)
    merge(near_lanes, top, total, lambda h: near_sums[h])
    for l in range(2, 5):
        look(l)

    landed(hfar, 0, 192, recv01.at[1])
    h2[pl.ds(pl.multiple_of(mine(core), 64), 64), :] = nn(fold[...], hfar[...]).astype(BF16)
    project_side(hfar, 1)
    landed(h2, pl.multiple_of(mine(1 - core), 64), 64, recv_far.at[0])
    forward(h2, 0)
    finer(h2, odd, h3, 1 - odd)
    halve_side(1)
    landed(h3, pl.multiple_of(mine(1 - odd), 64), 64, recv_far.at[2])
    landed(h3, pl.multiple_of(mine(odd) + odd * 32, 32), 32, recv_far.at[3])
    forward(h3, 2)
    finer(h3, second, h4, 1 - second)
    landed(h4, pl.multiple_of(mine(1 - second), 64), 64, recv_far.at[4])
    landed(h4, pl.multiple_of(mine(second) + second * 32, 32), 32, recv_far.at[5])
    forward(h4, 4)

    units, far_lanes, base_far, one_far = side(1, core)
    run(units)
    missing = off(jnp.where(core == 0, me == 0, me == devices - 1))
    top, total, far_sums = by_head(base_far)
    merge(far_lanes, top - missing, total, lambda h: far_sums[h])
    near_top, near_total, near_one = by_head(one_near)
    far_top, far_total, far_one = by_head(one_far)
    far_top = far_top - missing
    top = jnp.maximum(near_top, far_top)
    factor_near = jnp.exp2(near_top - top)
    factor_far = jnp.exp2(far_top - top)
    total = near_total * factor_near + far_total * factor_far
    sums = [
        (near_one[h] * factor_near[h : h + 1] + far_one[h] * factor_far[h : h + 1]).astype(BF16)
        for h in range(HEADS)
    ]
    one_sums, top, total = spread_all(jnp.concatenate(sums, 0), top, total, spread1[...])
    terms = [(top, total, lambda h: one_sums[head_rows(h)], 2.0)]

    gather(h2, 0)
    gather(h3, 2)
    gather(h4, 4)
    vd[...] = nt(wvt[...], deep[...]).astype(BF16)
    levels = [coarse(4, group, devices // 8), coarse(3, pair, devices // 4), coarse(2, chip, devices // 2)]
    run([unit for units, _ in levels for unit in units])
    terms += [gathered() for _, gathered in levels]

    before = peak[...]
    after = functools.reduce(jnp.maximum, [term[0] for term in terms], before)
    factors = [jnp.exp2(before - after)] + [weight * jnp.exp2(top - after) for top, _, _, weight in terms]
    lower = den[...] * factors[0]
    for factor, term in zip(factors[1:], terms):
        lower = lower + factor * term[1]
    factors = [factor / lower for factor in factors]
    attended = []
    for h in range(HEADS):
        upper = acc[head_rows(h), :] * factors[0][h : h + 1]
        for factor, term in zip(factors[1:], terms):
            upper = upper + term[2](h) * factor[h : h + 1]
        attended.append(upper.astype(BF16))
    loads[4].wait()
    turned = nt(eye[...], jnp.concatenate(attended, 0)).astype(BF16)
    out_ref[...] = nn(turned, wo[...]).astype(BF16)

    landed(deep, 0, 2 * BLOCK, send_sem.at[0])
    landed(deep, 0, 3 * BLOCK, send_sem.at[1])
    landed(deep, 0, 3 * BLOCK, send_sem.at[2])


def solution(mesh):
    devices = mesh.shape["ctx"] * mesh.shape["node"]

    def local(tokens, w_query, w_key, w_value, w_out):
        square = pltpu.VMEM((WIDTH, WIDTH), BF16)
        tall = pltpu.VMEM((ROWS, WIDTH), BF16)
        return pl.pallas_call(
            functools.partial(kernel, devices),
            out_shape=jax.ShapeDtypeStruct((ROWS, WIDTH), BF16),
            in_specs=[pl.BlockSpec(memory_space=pltpu.HBM)] * 5,
            out_specs=pl.BlockSpec(memory_space=pltpu.VMEM),
            scratch_shapes=[
                tall,
                square,
                square,
                square,
                square,
                square,
                pltpu.VMEM((COARSE, WIDTH), BF16),
                pltpu.VMEM((192, WIDTH), BF16),
                pltpu.VMEM((192, WIDTH), BF16),
                pltpu.VMEM((3 * ROWS, WIDTH), BF16),
                tall,
                pltpu.VMEM((COARSE, WIDTH), BF16),
                tall,
                pltpu.VMEM((WIDTH, ROWS), BF16),
                pltpu.VMEM((2, ROWS, WIDTH), BF16),
                pltpu.VMEM((2, WIDTH, ROWS), BF16),
                square,
                tall,
                pltpu.VMEM((BLOCK, WIDTH), BF16),
                pltpu.VMEM((WIDTH, 3 * ROWS), BF16),
                pltpu.VMEM((WIDTH, ROWS), F32),
                pltpu.VMEM((HEADS, ROWS), F32),
                pltpu.VMEM((HEADS, ROWS), F32),
                pltpu.VMEM((COARSE, ROWS), BF16),
                pltpu.VMEM((ROWS, ROWS), BF16),
                pltpu.VMEM((64, BLOCK), BF16),
                pltpu.VMEM((64, 192), BF16),
                pltpu.VMEM((BLOCK, ROWS), BF16),
                pltpu.VMEM((ROWS, ROWS), BF16),
                pltpu.VMEM((ROWS, ROWS), BF16),
                pltpu.VMEM((BLOCK, ROWS), BF16),
                pltpu.SemaphoreType.DMA((5,)),
                pltpu.SemaphoreType.DMA((3,)),
                pltpu.SemaphoreType.DMA((2,)),
                pltpu.SemaphoreType.DMA((6,)),
                pltpu.SemaphoreType.DMA((6,)),
            ],
            compiler_params=pltpu.CompilerParams(
                collective_id=0, has_side_effects=True, vmem_limit_bytes=40 * 2**20
            ),
            name="hierarchical_attention",
        )(*[pltpu.with_memory_space_constraint(a, pltpu.HBM) for a in (tokens, w_query, w_key, w_value, w_out)])

    placed = (P(("ctx", "node"), None), P(), P(), P(), P())
    return jax.shard_map(
        local, mesh=mesh, in_specs=placed, out_specs=P(("ctx", "node"), None), check_vma=False
    )
```

```python
import functools
import math

import jax
import jax.numpy as jnp
from jax import lax
from jax.experimental import pallas as pl
from jax.experimental.pallas import tpu as pltpu
from jax.sharding import PartitionSpec as P

HEADS = 8
HEAD = 64
WIDTH = HEADS * HEAD
BLOCK = 128
ROWS = 256
NODES = 8
FAR = 1e30
SCALE = math.log2(math.e) / math.sqrt(HEAD)
BF16 = jnp.bfloat16
F32 = jnp.float32
START = {1: 0, 2: 128, 3: 192, 4: 224}
COARSE = 240


def nn(a, b):
    return lax.dot_general(a, b, (((1,), (0,)), ((), ())), preferred_element_type=F32)


def nt(a, b):
    return lax.dot_general(a, b, (((1,), (1,)), ((), ())), preferred_element_type=F32)


def iota(shape, axis):
    return lax.broadcasted_iota(jnp.int32, shape, axis)


def averager(rows, columns, level):
    hit = iota((rows, columns), 0) == iota((rows, columns), 1) >> level
    return jnp.where(hit, 0.5**level, 0.0).astype(BF16)


def spreader(rows, queries, level):
    hit = (iota((rows, ROWS), 0) & (queries - 1)) == iota((rows, ROWS), 1) >> level
    return jnp.where(hit, 1.0, 0.0).astype(BF16)


def split(values):
    high = values.astype(BF16)
    rest = values - high.astype(F32)
    middle = rest.astype(BF16)
    return [high, middle, (rest - middle.astype(F32)).astype(BF16)]


def spread_all(sums, tops, totals, spread):
    rows = sums.shape[0]
    out = nn(jnp.concatenate([sums] + split(jnp.concatenate([tops, totals], 0)), 0), spread)
    stats = out[rows : rows + 16] + out[rows + 16 : rows + 32] + out[rows + 32 :]
    return out[:rows], stats[:8], stats[8:]


def lane_head(shape, width):
    return iota(shape, 1) >> (width.bit_length() - 1)


def kernel(
    devices, x_hbm, wq_hbm, wk_hbm, wv_hbm, wo_hbm, out_ref,
    x, wq, wk, wv, wo, wvt, t, hedge, deep, q0, ql, k0, v0, kh, vh, u2, u3, u4, vd, acc, peak, den,
    average, eye, halve, fold, spread1, spread2, spread3, spread4,
    load_sem, send_sem, recv01, recv_far, recv_near, ready,
):
    me = lax.axis_index("ctx") * NODES + lax.axis_index("node")
    core = lax.rem(me, 2)
    chip = lax.div(me, 2)
    pair = lax.div(me, 4)
    group = lax.div(me, 8)

    def place(index):
        index = lax.rem(index + devices, devices)
        return {"ctx": lax.div(index, NODES), "node": lax.rem(index, NODES)}

    loads = []
    for i, (source, kept) in enumerate(((x_hbm, x), (wq_hbm, wq), (wk_hbm, wk), (wv_hbm, wv), (wo_hbm, wo))):
        loads.append(pltpu.make_async_copy(source, kept, load_sem.at[i]))
    loads[0].start()

    twin = me + 1 - 2 * core
    odd = lax.rem(chip, 2)
    second = lax.rem(pair, 2)

    def signal(semaphore, target):
        pl.semaphore_signal(semaphore, inc=1, device_id=place(target), device_id_type=pl.DeviceIdType.MESH)

    def for_each_above(act):
        act(me + 1)
        act(me + 4)
        for j in (2, 3):
            act(8 * (group + 1) + 2 * j + core)
        pl.when(core == 0)(lambda: act(me + 3))
        pl.when(odd == 0)(lambda: act(me + 6))

        @pl.when(second == 0)
        def _():
            for j in (0, 1):
                act(8 * (group + 1) + 2 * j + core)

    def for_each_below(act):
        act(me - 1)
        act(me - 4)
        for j in (0, 1):
            act(8 * (group - 1) + 2 * j + core)
        pl.when(core == 1)(lambda: act(me - 3))
        pl.when(odd == 1)(lambda: act(me - 6))

        @pl.when(second == 1)
        def _():
            for j in (2, 3):
                act(8 * (group - 1) + 2 * j + core)

    barrier = pltpu.get_barrier_semaphore()
    for_each_below(functools.partial(signal, barrier))
    for load in loads[1:]:
        load.start()

    pl.semaphore_wait(barrier, 4 + (1 - core) + (1 - odd) + 2 * (1 - second))

    def send(source, target, landing, recv, sent):
        pltpu.make_async_remote_copy(
            src_ref=source,
            dst_ref=landing,
            send_sem=send_sem.at[sent],
            recv_sem=recv,
            device_id=place(target),
            device_id_type=pl.DeviceIdType.MESH,
        ).start()

    def mine(direction):
        return direction * BLOCK + core * 64

    hnear, hfar = (hedge.at[pl.ds(i * 192, 192)] for i in range(2))

    def send_edge(up):
        target, to_far = (me + 1, core) if up else (me - 1, 1 - core)
        landing = hedge.at[pl.ds(pl.multiple_of(to_far * 192, 64), BLOCK)]
        send(x_hbm.at[pl.ds(up * BLOCK, BLOCK)], target, landing, recv01.at[to_far], 0)

    send_edge(1)
    for_each_above(functools.partial(signal, ready))

    h2, h3, h4 = (deep.at[pl.ds(i * ROWS, ROWS)] for i in range(3))
    for l in range(1, 5):
        average[START[l] : START[l] + (ROWS >> l), :] = averager(ROWS >> l, ROWS, l)
    eye[...] = averager(ROWS, ROWS, 0)
    halve[...] = averager(64, BLOCK, 1)
    fold[:32, :] = jnp.concatenate([averager(32, BLOCK, 2), jnp.zeros((32, 64), BF16)], 1)
    fold[32:, :] = jnp.concatenate([jnp.zeros((32, BLOCK), BF16), averager(32, 64, 1)], 1)
    spreads = {1: spread1, 2: spread2, 3: spread3, 4: spread4}
    for l in range(1, 5):
        spreads[l][...] = spreader(spreads[l].shape[0], ROWS >> l, l)
    loads[0].wait()
    t[...] = nn(average[...], x[...]).astype(BF16)

    def send_means(up):
        target, to_far = (me + 1, core) if up else (me - 1, 1 - core)
        landing = hedge.at[pl.ds(pl.multiple_of(to_far * 192 + BLOCK, 64), 64)]
        send(t.at[pl.ds((1 - up) * 64, 64)], target, landing, recv01.at[to_far], 1)
        d = 1 - up
        sign = 1 if up else -1

        @pl.when(core == d)
        def _():
            landing = h2.at[pl.ds(pl.multiple_of(64 + core * 64, 64), 64)]
            send(t.at[pl.ds(START[2], 64)], me + 3 * sign, landing, recv_far.at[0], 1)

        def three(target, recv):
            landing = h3.at[pl.ds(pl.multiple_of(mine(d) + odd * 32, 32), 32)]
            send(t.at[pl.ds(START[3], 32)], target, landing, recv, 1)

        three(me + 4 * sign, recv_far.at[3 - odd if up else 2 + odd])
        pl.when(odd == d)(lambda: three(me + 6 * sign, recv_far.at[2]))

        def four(j, recv):
            landing = h4.at[pl.ds(pl.multiple_of(mine(d) + lax.rem(chip, 4) * 16, 16), 16)]
            send(t.at[pl.ds(START[4], 16)], 8 * (group + sign) + 2 * j + core, landing, recv, 1)

        for j in (2, 3) if up else (0, 1):
            four(j, recv_far.at[4])

        @pl.when(second == d)
        def _():
            for j in (0, 1) if up else (2, 3):
                four(j, recv_far.at[5])

    send_means(1)

    def landed(buffer, start, rows, sem):
        region = buffer.at[pl.ds(start, rows)]
        pltpu.make_async_copy(region, region, sem).wait()

    def forward(buffer, which):
        for d in range(2):
            row = pl.multiple_of(mine(d), 16)
            region = buffer.at[pl.ds(row, 64)]
            send(region, twin, region, recv_near.at[which + d], 2)

    def finer(source, d, target, inside):
        rows = source[pl.ds(pl.multiple_of(mine(d), 64), 64), :]
        means = nn(halve[:32, :64], rows).astype(BF16)
        target[pl.ds(pl.multiple_of(mine(d) + inside * 32, 32), 32), :] = means

    def gather(buffer, which):
        for d in range(2):
            row = pl.multiple_of(d * BLOCK + (1 - core) * 64, 16)
            landed(buffer, row, 64, recv_near.at[which + d])

    ones = jnp.ones((16, ROWS), BF16)
    half = lane_head((1, BLOCK), HEAD)
    pair_masks = [jnp.where(half == h, 1.0, 0.0).astype(BF16) for h in range(2)]

    def lanes_of(j):
        return slice(j * BLOCK, (j + 1) * BLOCK)

    def head_rows(h):
        return slice(h * HEAD, (h + 1) * HEAD)

    def pair_queries(block):
        return jnp.concatenate([block * pair_masks[0], block * pair_masks[1]], 0)

    def with_ones(v):
        return jnp.concatenate([v, ones[:, : v.shape[1]]], 0)

    def merge(lanes, top, total, heads):
        before = peak[:, lanes]
        after = jnp.maximum(before, top)
        old = jnp.exp2(before - after)
        new = jnp.exp2(top - after)
        den[:, lanes] = den[:, lanes] * old + new * total
        peak[:, lanes] = after
        for h in range(HEADS):
            rows = head_rows(h)
            acc[rows, lanes] = acc[rows, lanes] * old[h : h + 1] + heads(h) * new[h : h + 1]

    def run(units):
        waiting, active = list(units), []
        while waiting or active:
            if waiting:
                active.append(waiting.pop(0))
            active = [unit for unit in active if next(unit, None) is not None]

    def attend(keys, queries, values, done):
        s = nt(keys(), queries())
        yield True
        m = jnp.max(s, axis=0, keepdims=True)
        p = jnp.exp2(s - m).astype(BF16)
        yield True
        done(m, nn(with_ones(values()), p))

    def base_own(h):
        pairs = lanes_of(h // 2)

        def done(m, o):
            peak[h : h + 1, :] = m
            den[h : h + 1, :] = o[HEAD : HEAD + 1]
            acc[head_rows(h), :] = o[:HEAD]

        return attend(
            lambda: k0[:, pairs], lambda: q0[:, pairs] * pair_masks[h % 2], lambda: v0[head_rows(h), :], done
        )

    def project_side(buffer, slot):
        rows = buffer[...]
        kh[slot, :192, :] = nn(rows, wk[...]).astype(BF16)
        vh[slot, :, :192] = nt(wvt[...], rows).astype(BF16)

    def halve_side(slot):
        kh[slot, 192:, :] = nn(halve[...], kh[slot, :BLOCK, :]).astype(BF16)
        vh[slot, :, 192:] = nt(vh[slot, :, :BLOCK], halve[...]).astype(BF16)

    def side(slot, block):
        queries = pl.ds(pl.multiple_of(block * BLOCK, BLOCK), BLOCK)
        units, found = [], ([], [])
        for keys, q, part in (
            (slice(0, BLOCK), q0.at[queries], found[0]),
            (slice(BLOCK, 2 * BLOCK), ql.at[pl.ds(0, BLOCK)], found[1]),
        ):
            for j in range(HEADS // 2):
                units.append(
                    attend(
                        lambda keys=keys, j=j: kh[slot, keys, lanes_of(j)],
                        lambda q=q, j=j: pair_queries(q[:, lanes_of(j)]),
                        lambda keys=keys, j=j: vh[slot, lanes_of(j), keys],
                        lambda m, o, part=part: part.append((m, o)),
                    )
                )
        return units, queries, found[0], found[1]

    def by_head(part):
        tops = [m[:, lanes_of(h)] for m, _ in part for h in range(2)]
        totals = [o[BLOCK : BLOCK + 1, lanes_of(h)] for _, o in part for h in range(2)]
        sums = [o[head_rows(h), lanes_of(h)] for _, o in part for h in range(2)]
        return jnp.concatenate(tops, 0), jnp.concatenate(totals, 0), sums

    def off(missing):
        return jnp.where(missing, FAR, 0.0).astype(F32)

    everywhere = slice(0, ROWS)

    seen = {2: u2, 3: u3, 4: u4}

    def shape_of(level):
        queries = ROWS >> level
        together = min(HEADS, ROWS // queries)
        return queries, together, together * queries

    def look(level):
        queries = ROWS >> level
        for u in range(2):
            part = slice(u * ROWS, (u + 1) * ROWS)
            block = ql[START[level] : START[level] + queries, part]
            masked = [block * jnp.where(lane_head((1, ROWS), HEAD) == h, 1.0, 0.0).astype(BF16) for h in range(4)]
            rows = slice(u * 4 * queries, (u + 1) * 4 * queries)
            seen[level][rows, :] = nt(jnp.concatenate(masked, 0), wk[:, part]).astype(BF16)

    def coarse(level, index, count):
        queries, together, columns = shape_of(level)
        features = together * HEAD
        keys = slice((level - 2) * ROWS, (level - 1) * ROWS)
        off_left, off_right = off(index == 0), off(index == count - 1)
        column_head = lane_head((1, columns), queries)
        found = []

        def unit(u):
            part = slice(u * features, (u + 1) * features)
            s = nt(deep[keys, :], seen[level][u * columns : (u + 1) * columns, :])
            yield True
            left, right = s[:BLOCK], s[BLOCK:]
            m = jnp.maximum(
                jnp.max(left, axis=0, keepdims=True) - off_left,
                jnp.max(right, axis=0, keepdims=True) - off_right,
            )
            p_left = jnp.exp2(left - (m + off_left)).astype(BF16)
            p_right = jnp.exp2(right - (m + off_right)).astype(BF16)
            yield True
            o = nn(with_ones(vd[part, keys]), jnp.concatenate([p_left, p_right], 0))
            yield True
            own = [jnp.where(column_head == h, o[head_rows(h)], 0.0) for h in range(together)]
            row_head = iota((HEADS, columns), 0) == column_head + u * together
            found.append(
                spread_all(
                    jnp.concatenate(own, 0).astype(BF16),
                    jnp.where(row_head, m, 0.0),
                    jnp.where(row_head, o[features : features + 1], 0.0),
                    spreads[level][...],
                )
            )

        def gathered():
            def heads(h):
                u, inside = divmod(h, together)
                return found[u][0][head_rows(inside)]

            top = functools.reduce(jnp.add, [f[1] for f in found])
            total = functools.reduce(jnp.add, [f[2] for f in found])
            return top, total, heads, 2.0**level

        return [unit(u) for u in range(HEADS // together)], gathered

    for load in loads[1:4]:
        load.wait()
    q0[...] = (nn(x[...], wq[...]) * SCALE).astype(BF16)
    k0[...] = nn(x[...], wk[...]).astype(BF16)
    for i in range(2):
        wvt[i * ROWS : (i + 1) * ROWS, :] = nt(eye[...], wv[:, i * ROWS : (i + 1) * ROWS]).astype(BF16)
    ql[...] = nn(average[...], q0[...]).astype(BF16)
    v0[...] = nt(wvt[...], x[...]).astype(BF16)

    pl.semaphore_wait(ready, 4 + core + odd + 2 * second)
    send_edge(0)
    send_means(0)

    landed(hnear, 0, 192, recv01.at[0])
    project_side(hnear, 0)
    units, near_lanes, base_near, one_near = side(0, 1 - core)
    own_units = [base_own(h) for h in range(HEADS)]
    run(own_units[:4])
    halve_side(0)
    run(own_units[4:] + units)
    top, total, near_sums = by_head(base_near)
    merge(near_lanes, top, total, lambda h: near_sums[h])
    for l in range(2, 5):
        look(l)

    landed(hfar, 0, 192, recv01.at[1])
    h2[pl.ds(pl.multiple_of(mine(core), 64), 64), :] = nn(fold[...], hfar[...]).astype(BF16)
    project_side(hfar, 1)
    landed(h2, pl.multiple_of(mine(1 - core), 64), 64, recv_far.at[0])
    forward(h2, 0)
    finer(h2, odd, h3, 1 - odd)
    halve_side(1)
    landed(h3, pl.multiple_of(mine(1 - odd), 64), 64, recv_far.at[2])
    landed(h3, pl.multiple_of(mine(odd) + odd * 32, 32), 32, recv_far.at[3])
    forward(h3, 2)
    finer(h3, second, h4, 1 - second)
    landed(h4, pl.multiple_of(mine(1 - second), 64), 64, recv_far.at[4])
    landed(h4, pl.multiple_of(mine(second) + second * 32, 32), 32, recv_far.at[5])
    forward(h4, 4)

    units, far_lanes, base_far, one_far = side(1, core)
    run(units)
    missing = off(jnp.where(core == 0, me == 0, me == devices - 1))
    top, total, far_sums = by_head(base_far)
    merge(far_lanes, top - missing, total, lambda h: far_sums[h])
    near_top, near_total, near_one = by_head(one_near)
    far_top, far_total, far_one = by_head(one_far)
    far_top = far_top - missing
    top = jnp.maximum(near_top, far_top)
    factor_near = jnp.exp2(near_top - top)
    factor_far = jnp.exp2(far_top - top)
    total = near_total * factor_near + far_total * factor_far
    sums = [
        (near_one[h] * factor_near[h : h + 1] + far_one[h] * factor_far[h : h + 1]).astype(BF16)
        for h in range(HEADS)
    ]
    one_sums, top, total = spread_all(jnp.concatenate(sums, 0), top, total, spread1[...])
    terms = [(top, total, lambda h: one_sums[head_rows(h)], 2.0)]

    gather(h2, 0)
    gather(h3, 2)
    gather(h4, 4)
    vd[...] = nt(wvt[...], deep[...]).astype(BF16)
    levels = [coarse(4, group, devices // 8), coarse(3, pair, devices // 4), coarse(2, chip, devices // 2)]
    run([unit for units, _ in levels for unit in units])
    terms += [gathered() for _, gathered in levels]

    before = peak[...]
    after = functools.reduce(jnp.maximum, [term[0] for term in terms], before)
    factors = [jnp.exp2(before - after)] + [weight * jnp.exp2(top - after) for top, _, _, weight in terms]
    lower = den[...] * factors[0]
    for factor, term in zip(factors[1:], terms):
        lower = lower + factor * term[1]
    factors = [factor / lower for factor in factors]
    attended = []
    for h in range(HEADS):
        upper = acc[head_rows(h), :] * factors[0][h : h + 1]
        for factor, term in zip(factors[1:], terms):
            upper = upper + term[2](h) * factor[h : h + 1]
        attended.append(upper.astype(BF16))
    loads[4].wait()
    turned = nt(eye[...], jnp.concatenate(attended, 0)).astype(BF16)
    out_ref[...] = nn(turned, wo[...]).astype(BF16)

    landed(deep, 0, 2 * BLOCK, send_sem.at[0])
    landed(deep, 0, 3 * BLOCK, send_sem.at[1])
    landed(deep, 0, 3 * BLOCK, send_sem.at[2])


def solution(mesh):
    devices = mesh.shape["ctx"] * mesh.shape["node"]

    def local(tokens, w_query, w_key, w_value, w_out):
        square = pltpu.VMEM((WIDTH, WIDTH), BF16)
        tall = pltpu.VMEM((ROWS, WIDTH), BF16)
        return pl.pallas_call(
            functools.partial(kernel, devices),
            out_shape=jax.ShapeDtypeStruct((ROWS, WIDTH), BF16),
            in_specs=[pl.BlockSpec(memory_space=pltpu.HBM)] * 5,
            out_specs=pl.BlockSpec(memory_space=pltpu.VMEM),
            scratch_shapes=[
                tall,
                square,
                square,
                square,
                square,
                square,
                pltpu.VMEM((COARSE, WIDTH), BF16),
                pltpu.VMEM((2 * 192, WIDTH), BF16),
                pltpu.VMEM((3 * ROWS, WIDTH), BF16),
                tall,
                pltpu.VMEM((COARSE, WIDTH), BF16),
                tall,
                pltpu.VMEM((WIDTH, ROWS), BF16),
                pltpu.VMEM((2, ROWS, WIDTH), BF16),
                pltpu.VMEM((2, WIDTH, ROWS), BF16),
                square,
                tall,
                pltpu.VMEM((BLOCK, WIDTH), BF16),
                pltpu.VMEM((WIDTH, 3 * ROWS), BF16),
                pltpu.VMEM((WIDTH, ROWS), F32),
                pltpu.VMEM((HEADS, ROWS), F32),
                pltpu.VMEM((HEADS, ROWS), F32),
                pltpu.VMEM((COARSE, ROWS), BF16),
                pltpu.VMEM((ROWS, ROWS), BF16),
                pltpu.VMEM((64, BLOCK), BF16),
                pltpu.VMEM((64, 192), BF16),
                pltpu.VMEM((BLOCK, ROWS), BF16),
                pltpu.VMEM((ROWS, ROWS), BF16),
                pltpu.VMEM((ROWS, ROWS), BF16),
                pltpu.VMEM((BLOCK, ROWS), BF16),
                pltpu.SemaphoreType.DMA((5,)),
                pltpu.SemaphoreType.DMA((3,)),
                pltpu.SemaphoreType.DMA((2,)),
                pltpu.SemaphoreType.DMA((6,)),
                pltpu.SemaphoreType.DMA((6,)),
                pltpu.SemaphoreType.REGULAR,
            ],
            compiler_params=pltpu.CompilerParams(
                collective_id=0, has_side_effects=True, vmem_limit_bytes=40 * 2**20
            ),
            name="hierarchical_attention",
        )(*[pltpu.with_memory_space_constraint(a, pltpu.HBM) for a in (tokens, w_query, w_key, w_value, w_out)])

    placed = (P(("ctx", "node"), None), P(), P(), P(), P())
    return jax.shard_map(
        local, mesh=mesh, in_specs=placed, out_specs=P(("ctx", "node"), None), check_vma=False
    )
```

```python
import functools
import math

import jax
import jax.numpy as jnp
from jax import lax
from jax.experimental import pallas as pl
from jax.experimental.pallas import tpu as pltpu
from jax.sharding import PartitionSpec as P

HEADS = 8
HEAD = 64
WIDTH = HEADS * HEAD
BLOCK = 128
ROWS = 256
NODES = 8
FAR = 1e30
SCALE = math.log2(math.e) / math.sqrt(HEAD)
BF16 = jnp.bfloat16
F32 = jnp.float32
START = {1: 0, 2: 128, 3: 192, 4: 224}
COARSE = 240


def nn(a, b):
    return lax.dot_general(a, b, (((1,), (0,)), ((), ())), preferred_element_type=F32)


def nt(a, b):
    return lax.dot_general(a, b, (((1,), (1,)), ((), ())), preferred_element_type=F32)


def iota(shape, axis):
    return lax.broadcasted_iota(jnp.int32, shape, axis)


def averager(rows, columns, level):
    hit = iota((rows, columns), 0) == iota((rows, columns), 1) >> level
    return jnp.where(hit, 0.5**level, 0.0).astype(BF16)


def spreader(rows, queries, level):
    hit = (iota((rows, ROWS), 0) & (queries - 1)) == iota((rows, ROWS), 1) >> level
    return jnp.where(hit, 1.0, 0.0).astype(BF16)


def split(values):
    high = values.astype(BF16)
    rest = values - high.astype(F32)
    middle = rest.astype(BF16)
    return [high, middle, (rest - middle.astype(F32)).astype(BF16)]


def spread_all(sums, tops, totals, spread):
    rows = sums.shape[0]
    out = nn(jnp.concatenate([sums] + split(jnp.concatenate([tops, totals], 0)), 0), spread)
    stats = out[rows : rows + 16] + out[rows + 16 : rows + 32] + out[rows + 32 :]
    return out[:rows], stats[:8], stats[8:]


def lane_head(shape, width):
    return iota(shape, 1) >> (width.bit_length() - 1)


def kernel(
    devices, x_hbm, wq_hbm, wk_hbm, wv_hbm, wo_hbm, out_ref,
    x, wq, wk, wv, wo, wvt, t, hedge, deep, q0, ql, k0, v0, kh, vh, u2, u3, u4, vd, acc, peak, den,
    average, eye, halve, fold, spread1, spread2, spread3, spread4,
    load_sem, send_sem, recv01, recv_far, recv_near, ready,
):
    me = lax.axis_index("ctx") * NODES + lax.axis_index("node")
    core = lax.rem(me, 2)
    chip = lax.div(me, 2)
    pair = lax.div(me, 4)
    group = lax.div(me, 8)

    def place(index):
        index = lax.rem(index + devices, devices)
        return {"ctx": lax.div(index, NODES), "node": lax.rem(index, NODES)}

    loads = []
    for i, (source, kept) in enumerate(((x_hbm, x), (wq_hbm, wq), (wk_hbm, wk), (wv_hbm, wv), (wo_hbm, wo))):
        loads.append(pltpu.make_async_copy(source, kept, load_sem.at[i]))
    loads[0].start()

    twin = me + 1 - 2 * core
    odd = lax.rem(chip, 2)
    second = lax.rem(pair, 2)

    def signal(semaphore, target):
        pl.semaphore_signal(semaphore, inc=1, device_id=place(target), device_id_type=pl.DeviceIdType.MESH)

    def elsewhere(target):
        return jnp.where(lax.div(target + devices, NODES) == group + devices // NODES, 0, 1)

    node = lax.rem(me, NODES)

    def for_each_above(act):
        act(me + 1)
        act(me + 4)
        for j in (2, 3):
            act(8 * (group + 1) + 2 * j + core)
        pl.when(core == 0)(lambda: act(me + 3))
        pl.when(odd == 0)(lambda: act(me + 6))

        @pl.when(second == 0)
        def _():
            for j in (0, 1):
                act(8 * (group + 1) + 2 * j + core)

    def for_each_below(act):
        act(me - 1)
        act(me - 4)
        for j in (0, 1):
            act(8 * (group - 1) + 2 * j + core)
        pl.when(core == 1)(lambda: act(me - 3))
        pl.when(odd == 1)(lambda: act(me - 6))

        @pl.when(second == 1)
        def _():
            for j in (2, 3):
                act(8 * (group - 1) + 2 * j + core)

    barrier = pltpu.get_barrier_semaphore()
    for_each_below(functools.partial(signal, barrier))
    for load in loads[1:]:
        load.start()

    pl.semaphore_wait(barrier, 4 + (1 - core) + (1 - odd) + 2 * (1 - second))

    def send(source, target, landing, recv, sent):
        pltpu.make_async_remote_copy(
            src_ref=source,
            dst_ref=landing,
            send_sem=send_sem.at[sent],
            recv_sem=recv,
            device_id=place(target),
            device_id_type=pl.DeviceIdType.MESH,
        ).start()

    def mine(direction):
        return direction * BLOCK + core * 64

    hnear, hfar = (hedge.at[pl.ds(i * 192, 192)] for i in range(2))

    def send_edge(up):
        target, to_far = (me + 1, core) if up else (me - 1, 1 - core)
        landing = hedge.at[pl.ds(pl.multiple_of(to_far * 192, 64), BLOCK)]
        send(x_hbm.at[pl.ds(up * BLOCK, BLOCK)], target, landing, recv01.at[to_far], 0)

    send_edge(1)
    for_each_above(lambda target: signal(ready.at[elsewhere(target)], target))

    h2, h3, h4 = (deep.at[pl.ds(i * ROWS, ROWS)] for i in range(3))
    for l in range(1, 5):
        average[START[l] : START[l] + (ROWS >> l), :] = averager(ROWS >> l, ROWS, l)
    eye[...] = averager(ROWS, ROWS, 0)
    halve[...] = averager(64, BLOCK, 1)
    fold[:32, :] = jnp.concatenate([averager(32, BLOCK, 2), jnp.zeros((32, 64), BF16)], 1)
    fold[32:, :] = jnp.concatenate([jnp.zeros((32, BLOCK), BF16), averager(32, 64, 1)], 1)
    spreads = {1: spread1, 2: spread2, 3: spread3, 4: spread4}
    for l in range(1, 5):
        spreads[l][...] = spreader(spreads[l].shape[0], ROWS >> l, l)
    loads[0].wait()
    t[...] = nn(average[...], x[...]).astype(BF16)

    def send_one_means(up):
        target, to_far = (me + 1, core) if up else (me - 1, 1 - core)
        landing = hedge.at[pl.ds(pl.multiple_of(to_far * 192 + BLOCK, 64), 64)]
        send(t.at[pl.ds((1 - up) * 64, 64)], target, landing, recv01.at[to_far], 1)

    def send_two(up):
        landing = h2.at[pl.ds(pl.multiple_of(64 + core * 64, 64), 64)]
        send(t.at[pl.ds(START[2], 64)], me + (3 if up else -3), landing, recv_far.at[0], 1)

    def send_three(up, target, recv):
        landing = h3.at[pl.ds(pl.multiple_of(mine(1 - up) + odd * 32, 32), 32)]
        send(t.at[pl.ds(START[3], 32)], target, landing, recv, 1)

    def send_four(up):
        def one(j, recv):
            landing = h4.at[pl.ds(pl.multiple_of(mine(1 - up) + lax.rem(chip, 4) * 16, 16), 16)]
            target = 8 * (group + (1 if up else -1)) + 2 * j + core
            send(t.at[pl.ds(START[4], 16)], target, landing, recv, 1)

        for j in (2, 3) if up else (0, 1):
            one(j, recv_far.at[4])

        @pl.when(second == 1 - up)
        def _():
            for j in (0, 1) if up else (2, 3):
                one(j, recv_far.at[5])

    def send_down(out):
        @pl.when(elsewhere(me - 1) == out)
        def _():
            send_edge(0)
            send_one_means(0)

        pl.when(jnp.logical_and(core == 1, elsewhere(me - 3) == out))(lambda: send_two(0))
        pl.when(elsewhere(me - 4) == out)(lambda: send_three(0, me - 4, recv_far.at[2 + odd]))
        pl.when(jnp.logical_and(odd == 1, elsewhere(me - 6) == out))(lambda: send_three(0, me - 6, recv_far.at[2]))
        if out:
            send_four(0)

    send_one_means(1)
    pl.when(core == 0)(lambda: send_two(1))
    send_three(1, me + 4, recv_far.at[3 - odd])
    pl.when(odd == 0)(lambda: send_three(1, me + 6, recv_far.at[2]))
    send_four(1)

    def landed(buffer, start, rows, sem):
        region = buffer.at[pl.ds(start, rows)]
        pltpu.make_async_copy(region, region, sem).wait()

    def forward(buffer, which):
        for d in range(2):
            row = pl.multiple_of(mine(d), 16)
            region = buffer.at[pl.ds(row, 64)]
            send(region, twin, region, recv_near.at[which + d], 2)

    def finer(source, d, target, inside):
        rows = source[pl.ds(pl.multiple_of(mine(d), 64), 64), :]
        means = nn(halve[:32, :64], rows).astype(BF16)
        target[pl.ds(pl.multiple_of(mine(d) + inside * 32, 32), 32), :] = means

    def gather(buffer, which):
        for d in range(2):
            row = pl.multiple_of(d * BLOCK + (1 - core) * 64, 16)
            landed(buffer, row, 64, recv_near.at[which + d])

    ones = jnp.ones((16, ROWS), BF16)
    half = lane_head((1, BLOCK), HEAD)
    pair_masks = [jnp.where(half == h, 1.0, 0.0).astype(BF16) for h in range(2)]

    def lanes_of(j):
        return slice(j * BLOCK, (j + 1) * BLOCK)

    def head_rows(h):
        return slice(h * HEAD, (h + 1) * HEAD)

    def pair_queries(block):
        return jnp.concatenate([block * pair_masks[0], block * pair_masks[1]], 0)

    def with_ones(v):
        return jnp.concatenate([v, ones[:, : v.shape[1]]], 0)

    def merge(lanes, top, total, heads):
        before = peak[:, lanes]
        after = jnp.maximum(before, top)
        old = jnp.exp2(before - after)
        new = jnp.exp2(top - after)
        den[:, lanes] = den[:, lanes] * old + new * total
        peak[:, lanes] = after
        for h in range(HEADS):
            rows = head_rows(h)
            acc[rows, lanes] = acc[rows, lanes] * old[h : h + 1] + heads(h) * new[h : h + 1]

    def run(units):
        waiting, active = list(units), []
        while waiting or active:
            if waiting:
                active.append(waiting.pop(0))
            active = [unit for unit in active if next(unit, None) is not None]

    def attend(keys, queries, values, done):
        s = nt(keys(), queries())
        yield True
        m = jnp.max(s, axis=0, keepdims=True)
        p = jnp.exp2(s - m).astype(BF16)
        yield True
        done(m, nn(with_ones(values()), p))

    def base_own(h):
        pairs = lanes_of(h // 2)

        def done(m, o):
            peak[h : h + 1, :] = m
            den[h : h + 1, :] = o[HEAD : HEAD + 1]
            acc[head_rows(h), :] = o[:HEAD]

        return attend(
            lambda: k0[:, pairs], lambda: q0[:, pairs] * pair_masks[h % 2], lambda: v0[head_rows(h), :], done
        )

    def project_side(buffer, slot):
        rows = buffer[...]
        kh[slot, :192, :] = nn(rows, wk[...]).astype(BF16)
        vh[slot, :, :192] = nt(wvt[...], rows).astype(BF16)

    def halve_side(slot):
        kh[slot, 192:, :] = nn(halve[...], kh[slot, :BLOCK, :]).astype(BF16)
        vh[slot, :, 192:] = nt(vh[slot, :, :BLOCK], halve[...]).astype(BF16)

    def side(slot, block):
        queries = pl.ds(pl.multiple_of(block * BLOCK, BLOCK), BLOCK)
        units, found = [], ([], [])
        for keys, q, part in (
            (slice(0, BLOCK), q0.at[queries], found[0]),
            (slice(BLOCK, 2 * BLOCK), ql.at[pl.ds(0, BLOCK)], found[1]),
        ):
            for j in range(HEADS // 2):
                units.append(
                    attend(
                        lambda keys=keys, j=j: kh[slot, keys, lanes_of(j)],
                        lambda q=q, j=j: pair_queries(q[:, lanes_of(j)]),
                        lambda keys=keys, j=j: vh[slot, lanes_of(j), keys],
                        lambda m, o, part=part: part.append((m, o)),
                    )
                )
        return units, queries, found[0], found[1]

    def by_head(part):
        tops = [m[:, lanes_of(h)] for m, _ in part for h in range(2)]
        totals = [o[BLOCK : BLOCK + 1, lanes_of(h)] for _, o in part for h in range(2)]
        sums = [o[head_rows(h), lanes_of(h)] for _, o in part for h in range(2)]
        return jnp.concatenate(tops, 0), jnp.concatenate(totals, 0), sums

    def off(missing):
        return jnp.where(missing, FAR, 0.0).astype(F32)

    everywhere = slice(0, ROWS)

    seen = {2: u2, 3: u3, 4: u4}

    def shape_of(level):
        queries = ROWS >> level
        together = min(HEADS, ROWS // queries)
        return queries, together, together * queries

    def look(level):
        queries = ROWS >> level
        for u in range(2):
            part = slice(u * ROWS, (u + 1) * ROWS)
            block = ql[START[level] : START[level] + queries, part]
            masked = [block * jnp.where(lane_head((1, ROWS), HEAD) == h, 1.0, 0.0).astype(BF16) for h in range(4)]
            rows = slice(u * 4 * queries, (u + 1) * 4 * queries)
            seen[level][rows, :] = nt(jnp.concatenate(masked, 0), wk[:, part]).astype(BF16)

    def coarse(level, index, count):
        queries, together, columns = shape_of(level)
        features = together * HEAD
        keys = slice((level - 2) * ROWS, (level - 1) * ROWS)
        off_left, off_right = off(index == 0), off(index == count - 1)
        column_head = lane_head((1, columns), queries)
        found = []

        def unit(u):
            part = slice(u * features, (u + 1) * features)
            s = nt(deep[keys, :], seen[level][u * columns : (u + 1) * columns, :])
            yield True
            left, right = s[:BLOCK], s[BLOCK:]
            m = jnp.maximum(
                jnp.max(left, axis=0, keepdims=True) - off_left,
                jnp.max(right, axis=0, keepdims=True) - off_right,
            )
            p_left = jnp.exp2(left - (m + off_left)).astype(BF16)
            p_right = jnp.exp2(right - (m + off_right)).astype(BF16)
            yield True
            o = nn(with_ones(vd[part, keys]), jnp.concatenate([p_left, p_right], 0))
            yield True
            own = [jnp.where(column_head == h, o[head_rows(h)], 0.0) for h in range(together)]
            row_head = iota((HEADS, columns), 0) == column_head + u * together
            found.append(
                spread_all(
                    jnp.concatenate(own, 0).astype(BF16),
                    jnp.where(row_head, m, 0.0),
                    jnp.where(row_head, o[features : features + 1], 0.0),
                    spreads[level][...],
                )
            )

        def gathered():
            def heads(h):
                u, inside = divmod(h, together)
                return found[u][0][head_rows(inside)]

            top = functools.reduce(jnp.add, [f[1] for f in found])
            total = functools.reduce(jnp.add, [f[2] for f in found])
            return top, total, heads, 2.0**level

        return [unit(u) for u in range(HEADS // together)], gathered

    for load in loads[1:4]:
        load.wait()
    q0[...] = (nn(x[...], wq[...]) * SCALE).astype(BF16)
    k0[...] = nn(x[...], wk[...]).astype(BF16)
    for i in range(2):
        wvt[i * ROWS : (i + 1) * ROWS, :] = nt(eye[...], wv[:, i * ROWS : (i + 1) * ROWS]).astype(BF16)
    ql[...] = nn(average[...], q0[...]).astype(BF16)
    v0[...] = nt(wvt[...], x[...]).astype(BF16)

    inside = (
        jnp.where(node >= 1, 1, 0)
        + jnp.where(node >= 4, 1, 0)
        + jnp.where(jnp.logical_and(core == 1, node >= 3), 1, 0)
        + jnp.where(jnp.logical_and(odd == 1, node >= 6), 1, 0)
    )
    pl.when(inside > 0)(lambda: pl.semaphore_wait(ready.at[0], inside))
    send_down(0)

    run([base_own(h) for h in range(HEADS)])
    for l in range(2, 5):
        look(l)

    landed(hnear, 0, 192, recv01.at[0])
    project_side(hnear, 0)
    halve_side(0)
    units, near_lanes, base_near, one_near = side(0, 1 - core)
    run(units)
    top, total, near_sums = by_head(base_near)
    merge(near_lanes, top, total, lambda h: near_sums[h])

    pl.semaphore_wait(ready.at[1], 4 + core + odd + 2 * second - inside)
    send_down(1)

    landed(hfar, 0, 192, recv01.at[1])
    h2[pl.ds(pl.multiple_of(mine(core), 64), 64), :] = nn(fold[...], hfar[...]).astype(BF16)
    project_side(hfar, 1)
    halve_side(1)
    units, far_lanes, base_far, one_far = side(1, core)
    run(units)
    missing = off(jnp.where(core == 0, me == 0, me == devices - 1))
    top, total, far_sums = by_head(base_far)
    merge(far_lanes, top - missing, total, lambda h: far_sums[h])
    near_top, near_total, near_one = by_head(one_near)
    far_top, far_total, far_one = by_head(one_far)
    far_top = far_top - missing
    top = jnp.maximum(near_top, far_top)
    factor_near = jnp.exp2(near_top - top)
    factor_far = jnp.exp2(far_top - top)
    total = near_total * factor_near + far_total * factor_far
    sums = [
        (near_one[h] * factor_near[h : h + 1] + far_one[h] * factor_far[h : h + 1]).astype(BF16)
        for h in range(HEADS)
    ]
    one_sums, top, total = spread_all(jnp.concatenate(sums, 0), top, total, spread1[...])
    terms = [(top, total, lambda h: one_sums[head_rows(h)], 2.0)]

    landed(h2, pl.multiple_of(mine(1 - core), 64), 64, recv_far.at[0])
    forward(h2, 0)
    finer(h2, odd, h3, 1 - odd)
    landed(h3, pl.multiple_of(mine(1 - odd), 64), 64, recv_far.at[2])
    landed(h3, pl.multiple_of(mine(odd) + odd * 32, 32), 32, recv_far.at[3])
    forward(h3, 2)
    finer(h3, second, h4, 1 - second)
    landed(h4, pl.multiple_of(mine(1 - second), 64), 64, recv_far.at[4])
    landed(h4, pl.multiple_of(mine(second) + second * 32, 32), 32, recv_far.at[5])
    forward(h4, 4)

    gather(h2, 0)
    gather(h3, 2)
    gather(h4, 4)
    vd[...] = nt(wvt[...], deep[...]).astype(BF16)
    levels = [coarse(4, group, devices // 8), coarse(3, pair, devices // 4), coarse(2, chip, devices // 2)]
    run([unit for units, _ in levels for unit in units])
    terms += [gathered() for _, gathered in levels]

    before = peak[...]
    after = functools.reduce(jnp.maximum, [term[0] for term in terms], before)
    factors = [jnp.exp2(before - after)] + [weight * jnp.exp2(top - after) for top, _, _, weight in terms]
    lower = den[...] * factors[0]
    for factor, term in zip(factors[1:], terms):
        lower = lower + factor * term[1]
    factors = [factor / lower for factor in factors]
    attended = []
    for h in range(HEADS):
        upper = acc[head_rows(h), :] * factors[0][h : h + 1]
        for factor, term in zip(factors[1:], terms):
            upper = upper + term[2](h) * factor[h : h + 1]
        attended.append(upper.astype(BF16))
    loads[4].wait()
    turned = nt(eye[...], jnp.concatenate(attended, 0)).astype(BF16)
    out_ref[...] = nn(turned, wo[...]).astype(BF16)

    landed(deep, 0, 2 * BLOCK, send_sem.at[0])
    landed(deep, 0, 3 * BLOCK, send_sem.at[1])
    landed(deep, 0, 3 * BLOCK, send_sem.at[2])


def solution(mesh):
    devices = mesh.shape["ctx"] * mesh.shape["node"]

    def local(tokens, w_query, w_key, w_value, w_out):
        square = pltpu.VMEM((WIDTH, WIDTH), BF16)
        tall = pltpu.VMEM((ROWS, WIDTH), BF16)
        return pl.pallas_call(
            functools.partial(kernel, devices),
            out_shape=jax.ShapeDtypeStruct((ROWS, WIDTH), BF16),
            in_specs=[pl.BlockSpec(memory_space=pltpu.HBM)] * 5,
            out_specs=pl.BlockSpec(memory_space=pltpu.VMEM),
            scratch_shapes=[
                tall,
                square,
                square,
                square,
                square,
                square,
                pltpu.VMEM((COARSE, WIDTH), BF16),
                pltpu.VMEM((2 * 192, WIDTH), BF16),
                pltpu.VMEM((3 * ROWS, WIDTH), BF16),
                tall,
                pltpu.VMEM((COARSE, WIDTH), BF16),
                tall,
                pltpu.VMEM((WIDTH, ROWS), BF16),
                pltpu.VMEM((2, ROWS, WIDTH), BF16),
                pltpu.VMEM((2, WIDTH, ROWS), BF16),
                square,
                tall,
                pltpu.VMEM((BLOCK, WIDTH), BF16),
                pltpu.VMEM((WIDTH, 3 * ROWS), BF16),
                pltpu.VMEM((WIDTH, ROWS), F32),
                pltpu.VMEM((HEADS, ROWS), F32),
                pltpu.VMEM((HEADS, ROWS), F32),
                pltpu.VMEM((COARSE, ROWS), BF16),
                pltpu.VMEM((ROWS, ROWS), BF16),
                pltpu.VMEM((64, BLOCK), BF16),
                pltpu.VMEM((64, 192), BF16),
                pltpu.VMEM((BLOCK, ROWS), BF16),
                pltpu.VMEM((ROWS, ROWS), BF16),
                pltpu.VMEM((ROWS, ROWS), BF16),
                pltpu.VMEM((BLOCK, ROWS), BF16),
                pltpu.SemaphoreType.DMA((5,)),
                pltpu.SemaphoreType.DMA((3,)),
                pltpu.SemaphoreType.DMA((2,)),
                pltpu.SemaphoreType.DMA((6,)),
                pltpu.SemaphoreType.DMA((6,)),
                pltpu.SemaphoreType.REGULAR((2,)),
            ],
            compiler_params=pltpu.CompilerParams(
                collective_id=0, has_side_effects=True, vmem_limit_bytes=40 * 2**20
            ),
            name="hierarchical_attention",
        )(*[pltpu.with_memory_space_constraint(a, pltpu.HBM) for a in (tokens, w_query, w_key, w_value, w_out)])

    placed = (P(("ctx", "node"), None), P(), P(), P(), P())
    return jax.shard_map(
        local, mesh=mesh, in_specs=placed, out_specs=P(("ctx", "node"), None), check_vma=False
    )
```

```python
import functools
import math

import jax
import jax.numpy as jnp
from jax import lax
from jax.experimental import pallas as pl
from jax.experimental.pallas import tpu as pltpu
from jax.sharding import PartitionSpec as P

HEADS = 8
HEAD = 64
WIDTH = HEADS * HEAD
BLOCK = 128
ROWS = 256
NODES = 8
FAR = 1e30
SCALE = math.log2(math.e) / math.sqrt(HEAD)
BF16 = jnp.bfloat16
F32 = jnp.float32
START = {1: 0, 2: 128, 3: 192, 4: 224}
COARSE = 240


def nn(a, b):
    return lax.dot_general(a, b, (((1,), (0,)), ((), ())), preferred_element_type=F32)


def nt(a, b):
    return lax.dot_general(a, b, (((1,), (1,)), ((), ())), preferred_element_type=F32)


def iota(shape, axis):
    return lax.broadcasted_iota(jnp.int32, shape, axis)


def averager(rows, columns, level):
    hit = iota((rows, columns), 0) == iota((rows, columns), 1) >> level
    return jnp.where(hit, 0.5**level, 0.0).astype(BF16)


def spreader(rows, queries, level):
    hit = (iota((rows, ROWS), 0) & (queries - 1)) == iota((rows, ROWS), 1) >> level
    return jnp.where(hit, 1.0, 0.0).astype(BF16)


def split(values):
    high = values.astype(BF16)
    rest = values - high.astype(F32)
    middle = rest.astype(BF16)
    return [high, middle, (rest - middle.astype(F32)).astype(BF16)]


def spread_all(sums, tops, totals, spread):
    rows = sums.shape[0]
    out = nn(jnp.concatenate([sums] + split(jnp.concatenate([tops, totals], 0)), 0), spread)
    stats = out[rows : rows + 16] + out[rows + 16 : rows + 32] + out[rows + 32 :]
    return out[:rows], stats[:8], stats[8:]


def lane_head(shape, width):
    return iota(shape, 1) >> (width.bit_length() - 1)


def kernel(
    devices, x_hbm, wq_hbm, wk_hbm, wv_hbm, wo_hbm, out_ref,
    x, wq, wk, wv, wo, wvt, t, hedge, deep, q0, ql, k0, v0, kh, vh, u2, u3, u4, vd, acc, peak, den,
    average, eye, halve, fold, spread1, spread2, spread3, spread4,
    load_sem, send_sem, recv01, recv_far, recv_near, ready,
):
    me = lax.axis_index("ctx") * NODES + lax.axis_index("node")
    core = lax.rem(me, 2)
    chip = lax.div(me, 2)
    pair = lax.div(me, 4)
    group = lax.div(me, 8)

    def place(index):
        index = lax.rem(index + devices, devices)
        return {"ctx": lax.div(index, NODES), "node": lax.rem(index, NODES)}

    loads = []
    for i, (source, kept) in enumerate(((x_hbm, x), (wq_hbm, wq), (wk_hbm, wk), (wv_hbm, wv), (wo_hbm, wo))):
        loads.append(pltpu.make_async_copy(source, kept, load_sem.at[i]))
    loads[0].start()

    twin = me + 1 - 2 * core
    odd = lax.rem(chip, 2)
    second = lax.rem(pair, 2)

    def signal(semaphore, target):
        pl.semaphore_signal(semaphore, inc=1, device_id=place(target), device_id_type=pl.DeviceIdType.MESH)

    def elsewhere(target):
        return jnp.where(lax.div(target + devices, NODES) == group + devices // NODES, 0, 1)

    node = lax.rem(me, NODES)

    def for_each_above(act):
        act(me + 1)
        act(me + 4)
        for j in (2, 3):
            act(8 * (group + 1) + 2 * j + core)
        pl.when(core == 0)(lambda: act(me + 3))
        pl.when(odd == 0)(lambda: act(me + 6))

        @pl.when(second == 0)
        def _():
            for j in (0, 1):
                act(8 * (group + 1) + 2 * j + core)

    def for_each_below(act):
        act(me - 1)
        act(me - 4)
        for j in (0, 1):
            act(8 * (group - 1) + 2 * j + core)
        pl.when(core == 1)(lambda: act(me - 3))
        pl.when(odd == 1)(lambda: act(me - 6))

        @pl.when(second == 1)
        def _():
            for j in (2, 3):
                act(8 * (group - 1) + 2 * j + core)

    barrier = pltpu.get_barrier_semaphore()
    for_each_below(functools.partial(signal, barrier))
    for load in loads[1:]:
        load.start()

    pl.semaphore_wait(barrier, 4 + (1 - core) + (1 - odd) + 2 * (1 - second))

    def send(source, target, landing, recv, sent):
        pltpu.make_async_remote_copy(
            src_ref=source,
            dst_ref=landing,
            send_sem=send_sem.at[sent],
            recv_sem=recv,
            device_id=place(target),
            device_id_type=pl.DeviceIdType.MESH,
        ).start()

    def mine(direction):
        return core * BLOCK + direction * 64

    hnear, hfar = (hedge.at[pl.ds(i * 192, 192)] for i in range(2))

    def send_edge(up):
        target, to_far = (me + 1, core) if up else (me - 1, 1 - core)
        landing = hedge.at[pl.ds(pl.multiple_of(to_far * 192, 64), BLOCK)]
        send(x_hbm.at[pl.ds(up * BLOCK, BLOCK)], target, landing, recv01.at[to_far], 0)

    send_edge(1)
    for_each_above(lambda target: signal(ready.at[elsewhere(target)], target))

    h2, h3, h4 = (deep.at[pl.ds(i * ROWS, ROWS)] for i in range(3))
    for l in range(1, 5):
        average[START[l] : START[l] + (ROWS >> l), :] = averager(ROWS >> l, ROWS, l)
    loads[0].wait()
    t[...] = nn(average[...], x[...]).astype(BF16)

    def send_one_means(up):
        target, to_far = (me + 1, core) if up else (me - 1, 1 - core)
        landing = hedge.at[pl.ds(pl.multiple_of(to_far * 192 + BLOCK, 64), 64)]
        send(t.at[pl.ds((1 - up) * 64, 64)], target, landing, recv01.at[to_far], 1)

    def send_two(up):
        landing = h2.at[pl.ds(pl.multiple_of(BLOCK - core * 64, 64), 64)]
        send(t.at[pl.ds(START[2], 64)], me + (3 if up else -3), landing, recv_far.at[0], 1)

    def send_three(up, target, recv):
        landing = h3.at[pl.ds(pl.multiple_of(mine(1 - up) + odd * 32, 32), 32)]
        send(t.at[pl.ds(START[3], 32)], target, landing, recv, 1)

    def send_four(up):
        def one(j, recv):
            landing = h4.at[pl.ds(pl.multiple_of(mine(1 - up) + lax.rem(chip, 4) * 16, 16), 16)]
            target = 8 * (group + (1 if up else -1)) + 2 * j + core
            send(t.at[pl.ds(START[4], 16)], target, landing, recv, 1)

        for j in (2, 3) if up else (0, 1):
            one(j, recv_far.at[4])

        @pl.when(second == 1 - up)
        def _():
            for j in (0, 1) if up else (2, 3):
                one(j, recv_far.at[5])

    def send_down(out):
        @pl.when(elsewhere(me - 1) == out)
        def _():
            send_edge(0)
            send_one_means(0)

        pl.when(jnp.logical_and(core == 1, elsewhere(me - 3) == out))(lambda: send_two(0))
        pl.when(elsewhere(me - 4) == out)(lambda: send_three(0, me - 4, recv_far.at[2 + odd]))
        pl.when(jnp.logical_and(odd == 1, elsewhere(me - 6) == out))(lambda: send_three(0, me - 6, recv_far.at[2]))
        if out:
            send_four(0)

    send_one_means(1)
    pl.when(core == 0)(lambda: send_two(1))
    send_three(1, me + 4, recv_far.at[3 - odd])
    pl.when(odd == 0)(lambda: send_three(1, me + 6, recv_far.at[2]))
    send_four(1)

    def landed(buffer, start, rows, sem):
        region = buffer.at[pl.ds(start, rows)]
        pltpu.make_async_copy(region, region, sem).wait()

    def half_of(buffer, whose):
        return buffer.at[pl.ds(pl.multiple_of(whose * BLOCK, BLOCK), BLOCK)]

    def forward(buffer, which):
        region = half_of(buffer, core)
        send(region, twin, region, recv_near.at[which], 2)

    def finer(source, d, target, inside):
        rows = source[pl.ds(pl.multiple_of(mine(d), 64), 64), :]
        means = nn(halve[:32, :64], rows).astype(BF16)
        target[pl.ds(pl.multiple_of(mine(d) + inside * 32, 32), 32), :] = means

    ones = jnp.ones((16, ROWS), BF16)
    half = lane_head((1, BLOCK), HEAD)
    pair_masks = [jnp.where(half == h, 1.0, 0.0).astype(BF16) for h in range(2)]

    def lanes_of(j):
        return slice(j * BLOCK, (j + 1) * BLOCK)

    def head_rows(h):
        return slice(h * HEAD, (h + 1) * HEAD)

    def pair_queries(block):
        return jnp.concatenate([block * pair_masks[0], block * pair_masks[1]], 0)

    def with_ones(v):
        return jnp.concatenate([v, ones[:, : v.shape[1]]], 0)

    def merge(lanes, top, total, heads):
        before = peak[:, lanes]
        after = jnp.maximum(before, top)
        old = jnp.exp2(before - after)
        new = jnp.exp2(top - after)
        den[:, lanes] = den[:, lanes] * old + new * total
        peak[:, lanes] = after
        for h in range(HEADS):
            rows = head_rows(h)
            acc[rows, lanes] = acc[rows, lanes] * old[h : h + 1] + heads(h) * new[h : h + 1]

    def run(units):
        waiting, active = list(units), []
        while waiting or active:
            if waiting:
                active.append(waiting.pop(0))
            active = [unit for unit in active if next(unit, None) is not None]

    def attend(keys, queries, values, done):
        s = nt(keys(), queries())
        yield True
        m = jnp.max(s, axis=0, keepdims=True)
        p = jnp.exp2(s - m).astype(BF16)
        yield True
        done(m, nn(with_ones(values()), p))

    def base_own(h):
        pairs = lanes_of(h // 2)

        def done(m, o):
            peak[h : h + 1, :] = m
            den[h : h + 1, :] = o[HEAD : HEAD + 1]
            acc[head_rows(h), :] = o[:HEAD]

        return attend(
            lambda: k0[:, pairs], lambda: q0[:, pairs] * pair_masks[h % 2], lambda: v0[head_rows(h), :], done
        )

    def project_side(buffer, slot):
        rows = buffer[...]
        kh[slot, :192, :] = nn(rows, wk[...]).astype(BF16)
        vh[slot, :, :192] = nt(wvt[...], rows).astype(BF16)

    def halve_side(slot):
        kh[slot, 192:, :] = nn(halve[...], kh[slot, :BLOCK, :]).astype(BF16)
        vh[slot, :, 192:] = nt(vh[slot, :, :BLOCK], halve[...]).astype(BF16)

    def side(slot, block):
        queries = pl.ds(pl.multiple_of(block * BLOCK, BLOCK), BLOCK)
        units, found = [], ([], [])
        for keys, q, part in (
            (slice(0, BLOCK), q0.at[queries], found[0]),
            (slice(BLOCK, 2 * BLOCK), ql.at[pl.ds(0, BLOCK)], found[1]),
        ):
            for j in range(HEADS // 2):
                units.append(
                    attend(
                        lambda keys=keys, j=j: kh[slot, keys, lanes_of(j)],
                        lambda q=q, j=j: pair_queries(q[:, lanes_of(j)]),
                        lambda keys=keys, j=j: vh[slot, lanes_of(j), keys],
                        lambda m, o, part=part: part.append((m, o)),
                    )
                )
        return units, queries, found[0], found[1]

    def by_head(part):
        tops = [m[:, lanes_of(h)] for m, _ in part for h in range(2)]
        totals = [o[BLOCK : BLOCK + 1, lanes_of(h)] for _, o in part for h in range(2)]
        sums = [o[head_rows(h), lanes_of(h)] for _, o in part for h in range(2)]
        return jnp.concatenate(tops, 0), jnp.concatenate(totals, 0), sums

    def off(missing):
        return jnp.where(missing, FAR, 0.0).astype(F32)

    everywhere = slice(0, ROWS)

    seen = {2: u2, 3: u3, 4: u4}

    def shape_of(level):
        queries = ROWS >> level
        together = min(HEADS, ROWS // queries)
        return queries, together, together * queries

    def look(level):
        queries = ROWS >> level
        for u in range(2):
            part = slice(u * ROWS, (u + 1) * ROWS)
            block = ql[START[level] : START[level] + queries, part]
            masked = [block * jnp.where(lane_head((1, ROWS), HEAD) == h, 1.0, 0.0).astype(BF16) for h in range(4)]
            rows = slice(u * 4 * queries, (u + 1) * 4 * queries)
            seen[level][rows, :] = nt(jnp.concatenate(masked, 0), wk[:, part]).astype(BF16)

    def rows_of(level, whose):
        return half_of((h2, h3, h4)[level - 2], whose)[...]

    def values_of(whose):
        return nt(wvt[...], jnp.concatenate([rows_of(l, whose) for l in range(2, 5)], 0)).astype(BF16)

    scores = {}

    def coarse(level, index, count):
        queries, together, columns = shape_of(level)
        features = together * HEAD
        lanes = lanes_of(level - 2)
        off_left, off_right = off(index == 0), off(index == count - 1)
        column_head = lane_head((1, columns), queries)
        found = []

        def unit(u):
            part = slice(u * features, (u + 1) * features)
            s = [scores[level, u], nt(rows_of(level, 1 - core), seen[level][u * columns : (u + 1) * columns, :])]
            yield True
            left = [half[:64] for half in s]
            right = [half[64:] for half in s]
            m = jnp.maximum(
                jnp.max(jnp.maximum(*left), axis=0, keepdims=True) - off_left,
                jnp.max(jnp.maximum(*right), axis=0, keepdims=True) - off_right,
            )
            p = []
            for half in range(2):
                p.append(jnp.exp2(left[half] - (m + off_left)).astype(BF16))
                p.append(jnp.exp2(right[half] - (m + off_right)).astype(BF16))
            yield True
            values = jnp.concatenate([vd[0, part, lanes], vd[1, part, lanes]], 1)
            o = nn(with_ones(values), jnp.concatenate(p, 0))
            yield True
            own = [jnp.where(column_head == h, o[head_rows(h)], 0.0) for h in range(together)]
            row_head = iota((HEADS, columns), 0) == column_head + u * together
            found.append(
                spread_all(
                    jnp.concatenate(own, 0).astype(BF16),
                    jnp.where(row_head, m, 0.0),
                    jnp.where(row_head, o[features : features + 1], 0.0),
                    spreads[level][...],
                )
            )

        def gathered():
            def heads(h):
                u, inside = divmod(h, together)
                return found[u][0][head_rows(inside)]

            top = functools.reduce(jnp.add, [f[1] for f in found])
            total = functools.reduce(jnp.add, [f[2] for f in found])
            return top, total, heads, 2.0**level

        return [unit(u) for u in range(HEADS // together)], gathered

    eye[...] = averager(ROWS, ROWS, 0)
    halve[...] = averager(64, BLOCK, 1)
    fold[:32, :] = jnp.concatenate([averager(32, BLOCK, 2), jnp.zeros((32, 64), BF16)], 1)
    fold[32:, :] = jnp.concatenate([jnp.zeros((32, BLOCK), BF16), averager(32, 64, 1)], 1)
    spreads = {1: spread1, 2: spread2, 3: spread3, 4: spread4}
    for l in range(1, 5):
        spreads[l][...] = spreader(spreads[l].shape[0], ROWS >> l, l)
    for load in loads[1:4]:
        load.wait()
    q0[...] = (nn(x[...], wq[...]) * SCALE).astype(BF16)
    k0[...] = nn(x[...], wk[...]).astype(BF16)
    for i in range(2):
        wvt[i * ROWS : (i + 1) * ROWS, :] = nt(eye[...], wv[:, i * ROWS : (i + 1) * ROWS]).astype(BF16)
    ql[...] = nn(average[...], q0[...]).astype(BF16)
    v0[...] = nt(wvt[...], x[...]).astype(BF16)

    inside = (
        jnp.where(node >= 1, 1, 0)
        + jnp.where(node >= 4, 1, 0)
        + jnp.where(jnp.logical_and(core == 1, node >= 3), 1, 0)
        + jnp.where(jnp.logical_and(odd == 1, node >= 6), 1, 0)
    )
    pl.when(inside > 0)(lambda: pl.semaphore_wait(ready.at[0], inside))
    send_down(0)

    run([base_own(h) for h in range(HEADS)])
    for l in range(2, 5):
        look(l)

    landed(hnear, 0, 192, recv01.at[0])
    project_side(hnear, 0)
    halve_side(0)
    units, near_lanes, base_near, one_near = side(0, 1 - core)
    run(units)
    top, total, near_sums = by_head(base_near)
    merge(near_lanes, top, total, lambda h: near_sums[h])

    pl.semaphore_wait(ready.at[1], 4 + core + odd + 2 * second - inside)
    send_down(1)

    landed(hfar, 0, 192, recv01.at[1])
    h2[pl.ds(pl.multiple_of(mine(core), 64), 64), :] = nn(fold[...], hfar[...]).astype(BF16)
    landed(h2, pl.multiple_of(mine(1 - core), 64), 64, recv_far.at[0])
    forward(h2, 0)
    finer(h2, odd, h3, 1 - odd)
    project_side(hfar, 1)
    landed(h3, pl.multiple_of(mine(1 - odd), 64), 64, recv_far.at[2])
    landed(h3, pl.multiple_of(mine(odd) + odd * 32, 32), 32, recv_far.at[3])
    forward(h3, 1)
    finer(h3, second, h4, 1 - second)
    halve_side(1)
    landed(h4, pl.multiple_of(mine(1 - second), 64), 64, recv_far.at[4])
    landed(h4, pl.multiple_of(mine(second) + second * 32, 32), 32, recv_far.at[5])
    forward(h4, 2)

    units, far_lanes, base_far, one_far = side(1, core)
    run(units)
    missing = off(jnp.where(core == 0, me == 0, me == devices - 1))
    top, total, far_sums = by_head(base_far)
    merge(far_lanes, top - missing, total, lambda h: far_sums[h])
    near_top, near_total, near_one = by_head(one_near)
    far_top, far_total, far_one = by_head(one_far)
    far_top = far_top - missing
    top = jnp.maximum(near_top, far_top)
    factor_near = jnp.exp2(near_top - top)
    factor_far = jnp.exp2(far_top - top)
    total = near_total * factor_near + far_total * factor_far
    sums = [
        (near_one[h] * factor_near[h : h + 1] + far_one[h] * factor_far[h : h + 1]).astype(BF16)
        for h in range(HEADS)
    ]
    one_sums, top, total = spread_all(jnp.concatenate(sums, 0), top, total, spread1[...])
    terms = [(top, total, lambda h: one_sums[head_rows(h)], 2.0)]

    vd[0] = values_of(core)
    for l in range(4, 1, -1):
        _, together, columns = shape_of(l)
        for u in range(HEADS // together):
            scores[l, u] = nt(rows_of(l, core), seen[l][u * columns : (u + 1) * columns, :])
    for i, buffer in enumerate((h2, h3, h4)):
        landed(buffer, pl.multiple_of((1 - core) * BLOCK, BLOCK), BLOCK, recv_near.at[i])
    vd[1] = values_of(1 - core)
    levels = [coarse(4, group, devices // 8), coarse(3, pair, devices // 4), coarse(2, chip, devices // 2)]
    run([unit for units, _ in levels for unit in units])
    terms += [gathered() for _, gathered in levels]

    before = peak[...]
    after = functools.reduce(jnp.maximum, [term[0] for term in terms], before)
    factors = [jnp.exp2(before - after)] + [weight * jnp.exp2(top - after) for top, _, _, weight in terms]
    lower = den[...] * factors[0]
    for factor, term in zip(factors[1:], terms):
        lower = lower + factor * term[1]
    factors = [factor / lower for factor in factors]
    attended = []
    for h in range(HEADS):
        upper = acc[head_rows(h), :] * factors[0][h : h + 1]
        for factor, term in zip(factors[1:], terms):
            upper = upper + term[2](h) * factor[h : h + 1]
        attended.append(upper.astype(BF16))
    loads[4].wait()
    turned = nt(eye[...], jnp.concatenate(attended, 0)).astype(BF16)
    out_ref[...] = nn(turned, wo[...]).astype(BF16)

    landed(deep, 0, 2 * BLOCK, send_sem.at[0])
    landed(deep, 0, 3 * BLOCK, send_sem.at[1])
    landed(deep, 0, 3 * BLOCK, send_sem.at[2])


def solution(mesh):
    devices = mesh.shape["ctx"] * mesh.shape["node"]

    def local(tokens, w_query, w_key, w_value, w_out):
        square = pltpu.VMEM((WIDTH, WIDTH), BF16)
        tall = pltpu.VMEM((ROWS, WIDTH), BF16)
        return pl.pallas_call(
            functools.partial(kernel, devices),
            out_shape=jax.ShapeDtypeStruct((ROWS, WIDTH), BF16),
            in_specs=[pl.BlockSpec(memory_space=pltpu.HBM)] * 5,
            out_specs=pl.BlockSpec(memory_space=pltpu.VMEM),
            scratch_shapes=[
                tall,
                square,
                square,
                square,
                square,
                square,
                pltpu.VMEM((COARSE, WIDTH), BF16),
                pltpu.VMEM((2 * 192, WIDTH), BF16),
                pltpu.VMEM((3 * ROWS, WIDTH), BF16),
                tall,
                pltpu.VMEM((COARSE, WIDTH), BF16),
                tall,
                pltpu.VMEM((WIDTH, ROWS), BF16),
                pltpu.VMEM((2, ROWS, WIDTH), BF16),
                pltpu.VMEM((2, WIDTH, ROWS), BF16),
                square,
                tall,
                pltpu.VMEM((BLOCK, WIDTH), BF16),
                pltpu.VMEM((2, WIDTH, 3 * BLOCK), BF16),
                pltpu.VMEM((WIDTH, ROWS), F32),
                pltpu.VMEM((HEADS, ROWS), F32),
                pltpu.VMEM((HEADS, ROWS), F32),
                pltpu.VMEM((COARSE, ROWS), BF16),
                pltpu.VMEM((ROWS, ROWS), BF16),
                pltpu.VMEM((64, BLOCK), BF16),
                pltpu.VMEM((64, 192), BF16),
                pltpu.VMEM((BLOCK, ROWS), BF16),
                pltpu.VMEM((ROWS, ROWS), BF16),
                pltpu.VMEM((ROWS, ROWS), BF16),
                pltpu.VMEM((BLOCK, ROWS), BF16),
                pltpu.SemaphoreType.DMA((5,)),
                pltpu.SemaphoreType.DMA((3,)),
                pltpu.SemaphoreType.DMA((2,)),
                pltpu.SemaphoreType.DMA((6,)),
                pltpu.SemaphoreType.DMA((3,)),
                pltpu.SemaphoreType.REGULAR((2,)),
            ],
            compiler_params=pltpu.CompilerParams(
                collective_id=0, has_side_effects=True, vmem_limit_bytes=40 * 2**20
            ),
            name="hierarchical_attention",
        )(*[pltpu.with_memory_space_constraint(a, pltpu.HBM) for a in (tokens, w_query, w_key, w_value, w_out)])

    placed = (P(("ctx", "node"), None), P(), P(), P(), P())
    return jax.shard_map(
        local, mesh=mesh, in_specs=placed, out_specs=P(("ctx", "node"), None), check_vma=False
    )
```

```python
import functools
import math

import jax
import jax.numpy as jnp
from jax import lax
from jax.experimental import pallas as pl
from jax.experimental.pallas import tpu as pltpu
from jax.sharding import PartitionSpec as P

HEADS = 8
HEAD = 64
WIDTH = HEADS * HEAD
BLOCK = 128
ROWS = 256
NODES = 8
FAR = 1e30
SCALE = math.log2(math.e) / math.sqrt(HEAD)
BF16 = jnp.bfloat16
F32 = jnp.float32
START = {1: 0, 2: 128, 3: 192, 4: 224}
COARSE = 240


def nn(a, b):
    return lax.dot_general(a, b, (((1,), (0,)), ((), ())), preferred_element_type=F32)


def nt(a, b):
    return lax.dot_general(a, b, (((1,), (1,)), ((), ())), preferred_element_type=F32)


def iota(shape, axis):
    return lax.broadcasted_iota(jnp.int32, shape, axis)


def averager(rows, columns, level):
    hit = iota((rows, columns), 0) == iota((rows, columns), 1) >> level
    return jnp.where(hit, 0.5**level, 0.0).astype(BF16)


def spreader(rows, queries, level):
    hit = (iota((rows, ROWS), 0) & (queries - 1)) == iota((rows, ROWS), 1) >> level
    return jnp.where(hit, 1.0, 0.0).astype(BF16)


def split(values):
    high = values.astype(BF16)
    rest = values - high.astype(F32)
    middle = rest.astype(BF16)
    return [high, middle, (rest - middle.astype(F32)).astype(BF16)]


def spread_all(sums, tops, totals, spread):
    rows = sums.shape[0]
    out = nn(jnp.concatenate([sums] + split(jnp.concatenate([tops, totals], 0)), 0), spread)
    stats = out[rows : rows + 16] + out[rows + 16 : rows + 32] + out[rows + 32 :]
    return out[:rows], stats[:8], stats[8:]


def lane_head(shape, width):
    return iota(shape, 1) >> (width.bit_length() - 1)


def kernel(
    devices, x_hbm, wq_hbm, wk_hbm, wv_hbm, wo_hbm, out_ref,
    x, wq, wk, wv, wo, wvt, t, hedge, deep, q0, ql, k0, v0, kh, vh, u2, u3, u4, vd, acc, peak, den,
    near_one, near_top, near_total, one_acc, one_top, one_total,
    average, eye, halve, fold, spread1, spread2, spread3, spread4,
    load_sem, send_sem, recv01, recv_far, recv_near, ready,
):
    me = lax.axis_index("ctx") * NODES + lax.axis_index("node")
    core = lax.rem(me, 2)
    chip = lax.div(me, 2)
    pair = lax.div(me, 4)
    group = lax.div(me, 8)

    def place(index):
        index = lax.rem(index + devices, devices)
        return {"ctx": lax.div(index, NODES), "node": lax.rem(index, NODES)}

    loads = []
    for i, (source, kept) in enumerate(((x_hbm, x), (wq_hbm, wq), (wk_hbm, wk), (wv_hbm, wv), (wo_hbm, wo))):
        loads.append(pltpu.make_async_copy(source, kept, load_sem.at[i]))
    loads[0].start()

    twin = me + 1 - 2 * core
    odd = lax.rem(chip, 2)
    second = lax.rem(pair, 2)

    def signal(semaphore, target):
        pl.semaphore_signal(semaphore, inc=1, device_id=place(target), device_id_type=pl.DeviceIdType.MESH)

    def elsewhere(target):
        return jnp.where(lax.div(target + devices, NODES) == group + devices // NODES, 0, 1)

    node = lax.rem(me, NODES)

    def for_each_above(act):
        act(me + 1)
        act(me + 4)
        for j in (2, 3):
            act(8 * (group + 1) + 2 * j + core)
        pl.when(core == 0)(lambda: act(me + 3))
        pl.when(odd == 0)(lambda: act(me + 6))

        @pl.when(second == 0)
        def _():
            for j in (0, 1):
                act(8 * (group + 1) + 2 * j + core)

    def for_each_below(act):
        act(me - 1)
        act(me - 4)
        for j in (0, 1):
            act(8 * (group - 1) + 2 * j + core)
        pl.when(core == 1)(lambda: act(me - 3))
        pl.when(odd == 1)(lambda: act(me - 6))

        @pl.when(second == 1)
        def _():
            for j in (2, 3):
                act(8 * (group - 1) + 2 * j + core)

    barrier = pltpu.get_barrier_semaphore()
    for_each_below(functools.partial(signal, barrier))
    for load in loads[1:]:
        load.start()

    h2, h3, h4 = (deep.at[pl.ds(i * ROWS, ROWS)] for i in range(3))
    for l in range(1, 5):
        average[START[l] : START[l] + (ROWS >> l), :] = averager(ROWS >> l, ROWS, l)
    loads[0].wait()
    t[...] = nn(average[...], x[...]).astype(BF16)

    pl.semaphore_wait(barrier, 4 + (1 - core) + (1 - odd) + 2 * (1 - second))

    def send(source, target, landing, recv, sent):
        pltpu.make_async_remote_copy(
            src_ref=source,
            dst_ref=landing,
            send_sem=send_sem.at[sent],
            recv_sem=recv,
            device_id=place(target),
            device_id_type=pl.DeviceIdType.MESH,
        ).start()

    def mine(direction):
        return core * BLOCK + direction * 64

    hnear, hfar = (hedge.at[pl.ds(i * 192, 192)] for i in range(2))

    def send_edge(up):
        target, to_far = (me + 1, core) if up else (me - 1, 1 - core)
        landing = hedge.at[pl.ds(pl.multiple_of(to_far * 192, 64), BLOCK)]
        send(x_hbm.at[pl.ds(up * BLOCK, BLOCK)], target, landing, recv01.at[to_far], 0)

    send_edge(1)
    for_each_above(lambda target: signal(ready.at[elsewhere(target)], target))

    def send_one_means(up):
        target, to_far = (me + 1, core) if up else (me - 1, 1 - core)
        landing = hedge.at[pl.ds(pl.multiple_of(to_far * 192 + BLOCK, 64), 64)]
        send(t.at[pl.ds((1 - up) * 64, 64)], target, landing, recv01.at[to_far], 1)

    def send_two(up):
        landing = h2.at[pl.ds(pl.multiple_of(BLOCK - core * 64, 64), 64)]
        send(t.at[pl.ds(START[2], 64)], me + (3 if up else -3), landing, recv_far.at[0], 1)

    def send_three(up, target, recv):
        landing = h3.at[pl.ds(pl.multiple_of(mine(1 - up) + odd * 32, 32), 32)]
        send(t.at[pl.ds(START[3], 32)], target, landing, recv, 1)

    def send_four(up):
        def one(j, recv):
            landing = h4.at[pl.ds(pl.multiple_of(mine(1 - up) + lax.rem(chip, 4) * 16, 16), 16)]
            target = 8 * (group + (1 if up else -1)) + 2 * j + core
            send(t.at[pl.ds(START[4], 16)], target, landing, recv, 1)

        for j in (2, 3) if up else (0, 1):
            one(j, recv_far.at[4])

        @pl.when(second == 1 - up)
        def _():
            for j in (0, 1) if up else (2, 3):
                one(j, recv_far.at[5])

    def send_down(out):
        @pl.when(elsewhere(me - 1) == out)
        def _():
            send_edge(0)
            send_one_means(0)

        pl.when(jnp.logical_and(core == 1, elsewhere(me - 3) == out))(lambda: send_two(0))
        pl.when(elsewhere(me - 4) == out)(lambda: send_three(0, me - 4, recv_far.at[2 + odd]))
        pl.when(jnp.logical_and(odd == 1, elsewhere(me - 6) == out))(lambda: send_three(0, me - 6, recv_far.at[2]))
        if out:
            send_four(0)

    send_one_means(1)
    pl.when(core == 0)(lambda: send_two(1))
    send_three(1, me + 4, recv_far.at[3 - odd])
    pl.when(odd == 0)(lambda: send_three(1, me + 6, recv_far.at[2]))
    send_four(1)

    def landed(buffer, start, rows, sem):
        region = buffer.at[pl.ds(start, rows)]
        pltpu.make_async_copy(region, region, sem).wait()

    def half_of(buffer, whose):
        return buffer.at[pl.ds(pl.multiple_of(whose * BLOCK, BLOCK), BLOCK)]

    def forward(buffer, which):
        region = half_of(buffer, core)
        send(region, twin, region, recv_near.at[which], 2)

    def finer(source, d, target, inside):
        rows = source[pl.ds(pl.multiple_of(mine(d), 64), 64), :]
        means = nn(halve[:32, :64], rows).astype(BF16)
        target[pl.ds(pl.multiple_of(mine(d) + inside * 32, 32), 32), :] = means

    ones = jnp.ones((16, ROWS), BF16)
    half = lane_head((1, BLOCK), HEAD)
    pair_masks = [jnp.where(half == h, 1.0, 0.0).astype(BF16) for h in range(2)]

    def lanes_of(j):
        return slice(j * BLOCK, (j + 1) * BLOCK)

    def head_rows(h):
        return slice(h * HEAD, (h + 1) * HEAD)

    def pair_queries(block):
        return jnp.concatenate([block * pair_masks[0], block * pair_masks[1]], 0)

    def with_ones(v):
        return jnp.concatenate([v, ones[:, : v.shape[1]]], 0)

    def merge(lanes, top, total, heads):
        before = peak[:, lanes]
        after = jnp.maximum(before, top)
        old = jnp.exp2(before - after)
        new = jnp.exp2(top - after)
        den[:, lanes] = den[:, lanes] * old + new * total
        peak[:, lanes] = after
        for h in range(HEADS):
            rows = head_rows(h)
            acc[rows, lanes] = acc[rows, lanes] * old[h : h + 1] + heads(h) * new[h : h + 1]

    def run(units):
        waiting, active = list(units), []
        while waiting or active:
            if waiting:
                active.append(waiting.pop(0))
            active = [unit for unit in active if next(unit, None) is not None]

    def attend(keys, queries, values, done):
        s = nt(keys(), queries())
        yield True
        m = jnp.max(s, axis=0, keepdims=True)
        p = jnp.exp2(s - m).astype(BF16)
        yield True
        done(m, nn(with_ones(values()), p))

    def base_own(h):
        pairs = lanes_of(h // 2)

        def done(m, o):
            peak[h : h + 1, :] = m
            den[h : h + 1, :] = o[HEAD : HEAD + 1]
            acc[head_rows(h), :] = o[:HEAD]

        return attend(
            lambda: k0[:, pairs], lambda: q0[:, pairs] * pair_masks[h % 2], lambda: v0[head_rows(h), :], done
        )

    def project_side(buffer, slot):
        rows = buffer[...]
        kh[slot, :192, :] = nn(rows, wk[...]).astype(BF16)
        vh[slot, :, :192] = nt(wvt[...], rows).astype(BF16)

    def halve_side(slot):
        kh[slot, 192:, :] = nn(halve[...], kh[slot, :BLOCK, :]).astype(BF16)
        vh[slot, :, 192:] = nt(vh[slot, :, :BLOCK], halve[...]).astype(BF16)

    def side(slot, block):
        queries = pl.ds(pl.multiple_of(block * BLOCK, BLOCK), BLOCK)
        units, found = [], ([], [])
        for keys, q, part in (
            (slice(0, BLOCK), q0.at[queries], found[0]),
            (slice(BLOCK, 2 * BLOCK), ql.at[pl.ds(0, BLOCK)], found[1]),
        ):
            for j in range(HEADS // 2):
                units.append(
                    attend(
                        lambda keys=keys, j=j: kh[slot, keys, lanes_of(j)],
                        lambda q=q, j=j: pair_queries(q[:, lanes_of(j)]),
                        lambda keys=keys, j=j: vh[slot, lanes_of(j), keys],
                        lambda m, o, part=part: part.append((m, o)),
                    )
                )
        return units, queries, found[0], found[1]

    def by_head(part):
        tops = [m[:, lanes_of(h)] for m, _ in part for h in range(2)]
        totals = [o[BLOCK : BLOCK + 1, lanes_of(h)] for _, o in part for h in range(2)]
        sums = [o[head_rows(h), lanes_of(h)] for _, o in part for h in range(2)]
        return jnp.concatenate(tops, 0), jnp.concatenate(totals, 0), sums

    def off(missing):
        return jnp.where(missing, FAR, 0.0).astype(F32)

    everywhere = slice(0, ROWS)

    seen = {2: u2, 3: u3, 4: u4}

    def shape_of(level):
        queries = ROWS >> level
        together = min(HEADS, ROWS // queries)
        return queries, together, together * queries

    def look(level):
        queries = ROWS >> level
        for u in range(2):
            part = slice(u * ROWS, (u + 1) * ROWS)
            block = ql[START[level] : START[level] + queries, part]
            masked = [block * jnp.where(lane_head((1, ROWS), HEAD) == h, 1.0, 0.0).astype(BF16) for h in range(4)]
            rows = slice(u * 4 * queries, (u + 1) * 4 * queries)
            seen[level][rows, :] = nt(jnp.concatenate(masked, 0), wk[:, part]).astype(BF16)

    def rows_of(level, whose):
        return half_of((h2, h3, h4)[level - 2], whose)[...]

    def values_of(whose):
        return nt(wvt[...], jnp.concatenate([rows_of(l, whose) for l in range(2, 5)], 0)).astype(BF16)

    scores = {}

    def coarse(level, index, count):
        queries, together, columns = shape_of(level)
        features = together * HEAD
        lanes = lanes_of(level - 2)
        off_left, off_right = off(index == 0), off(index == count - 1)
        column_head = lane_head((1, columns), queries)
        found = []

        def unit(u):
            part = slice(u * features, (u + 1) * features)
            s = [scores[level, u], nt(rows_of(level, 1 - core), seen[level][u * columns : (u + 1) * columns, :])]
            yield True
            left = [half[:64] for half in s]
            right = [half[64:] for half in s]
            m = jnp.maximum(
                jnp.max(jnp.maximum(*left), axis=0, keepdims=True) - off_left,
                jnp.max(jnp.maximum(*right), axis=0, keepdims=True) - off_right,
            )
            p = []
            for half in range(2):
                p.append(jnp.exp2(left[half] - (m + off_left)).astype(BF16))
                p.append(jnp.exp2(right[half] - (m + off_right)).astype(BF16))
            yield True
            values = jnp.concatenate([vd[0, part, lanes], vd[1, part, lanes]], 1)
            o = nn(with_ones(values), jnp.concatenate(p, 0))
            yield True
            own = [jnp.where(column_head == h, o[head_rows(h)], 0.0) for h in range(together)]
            row_head = iota((HEADS, columns), 0) == column_head + u * together
            found.append(
                spread_all(
                    jnp.concatenate(own, 0).astype(BF16),
                    jnp.where(row_head, m, 0.0),
                    jnp.where(row_head, o[features : features + 1], 0.0),
                    spreads[level][...],
                )
            )

        def gathered():
            def heads(h):
                u, inside = divmod(h, together)
                return found[u][0][head_rows(inside)]

            top = functools.reduce(jnp.add, [f[1] for f in found])
            total = functools.reduce(jnp.add, [f[2] for f in found])
            return top, total, heads, 2.0**level

        return [unit(u) for u in range(HEADS // together)], gathered

    eye[...] = averager(ROWS, ROWS, 0)
    halve[...] = averager(64, BLOCK, 1)
    fold[:32, :] = jnp.concatenate([averager(32, BLOCK, 2), jnp.zeros((32, 64), BF16)], 1)
    fold[32:, :] = jnp.concatenate([jnp.zeros((32, BLOCK), BF16), averager(32, 64, 1)], 1)
    spreads = {1: spread1, 2: spread2, 3: spread3, 4: spread4}
    for l in range(1, 5):
        spreads[l][...] = spreader(spreads[l].shape[0], ROWS >> l, l)
    for load in loads[1:4]:
        load.wait()
    q0[...] = (nn(x[...], wq[...]) * SCALE).astype(BF16)
    k0[...] = nn(x[...], wk[...]).astype(BF16)
    for i in range(2):
        wvt[i * ROWS : (i + 1) * ROWS, :] = nt(eye[...], wv[:, i * ROWS : (i + 1) * ROWS]).astype(BF16)
    ql[...] = nn(average[...], q0[...]).astype(BF16)
    v0[...] = nt(wvt[...], x[...]).astype(BF16)

    inside = (
        jnp.where(node >= 1, 1, 0)
        + jnp.where(node >= 4, 1, 0)
        + jnp.where(jnp.logical_and(core == 1, node >= 3), 1, 0)
        + jnp.where(jnp.logical_and(odd == 1, node >= 6), 1, 0)
    )
    pl.when(inside > 0)(lambda: pl.semaphore_wait(ready.at[0], inside))
    send_down(0)

    run([base_own(h) for h in range(HEADS)])
    for l in range(2, 5):
        look(l)

    landed(hnear, 0, 192, recv01.at[0])
    project_side(hnear, 0)
    halve_side(0)
    units, near_lanes, base_near, one_near = side(0, 1 - core)
    run(units)
    top, total, near_sums = by_head(base_near)
    merge(near_lanes, top, total, lambda h: near_sums[h])
    top, total, near_sums = by_head(one_near)
    near_top[...] = top
    near_total[...] = total
    near_one[...] = jnp.concatenate(near_sums, 0)

    pl.semaphore_wait(ready.at[1], 4 + core + odd + 2 * second - inside)
    send_down(1)

    def far_side():
        project_side(hfar, 1)
        halve_side(1)
        units, far_lanes, base_far, one_far = side(1, core)
        run(units)
        missing = off(jnp.where(core == 0, me == 0, me == devices - 1))
        top, total, far_sums = by_head(base_far)
        merge(far_lanes, top - missing, total, lambda h: far_sums[h])
        far_top, far_total, far_one = by_head(one_far)
        far_top = far_top - missing
        top = jnp.maximum(near_top[...], far_top)
        factor_near = jnp.exp2(near_top[...] - top)
        factor_far = jnp.exp2(far_top - top)
        total = near_total[...] * factor_near + far_total * factor_far
        sums = [
            (near_one[head_rows(h), :] * factor_near[h : h + 1] + far_one[h] * factor_far[h : h + 1]).astype(BF16)
            for h in range(HEADS)
        ]
        one_acc[...], one_top[...], one_total[...] = spread_all(jnp.concatenate(sums, 0), top, total, spread1[...])

    within = jnp.logical_and(node > 0, node < NODES - 1)
    landed(hfar, 0, 192, recv01.at[1])
    h2[pl.ds(pl.multiple_of(mine(core), 64), 64), :] = nn(fold[...], hfar[...]).astype(BF16)
    pl.when(within)(far_side)

    landed(h2, pl.multiple_of(mine(1 - core), 64), 64, recv_far.at[0])
    forward(h2, 0)
    finer(h2, odd, h3, 1 - odd)
    landed(h3, pl.multiple_of(mine(1 - odd), 64), 64, recv_far.at[2])
    landed(h3, pl.multiple_of(mine(odd) + odd * 32, 32), 32, recv_far.at[3])
    forward(h3, 1)
    finer(h3, second, h4, 1 - second)
    landed(h4, pl.multiple_of(mine(1 - second), 64), 64, recv_far.at[4])
    landed(h4, pl.multiple_of(mine(second) + second * 32, 32), 32, recv_far.at[5])
    forward(h4, 2)

    pl.when(jnp.logical_not(within))(far_side)
    vd[0] = values_of(core)
    for l in range(4, 1, -1):
        _, together, columns = shape_of(l)
        for u in range(HEADS // together):
            scores[l, u] = nt(rows_of(l, core), seen[l][u * columns : (u + 1) * columns, :])
    for i, buffer in enumerate((h2, h3, h4)):
        landed(buffer, pl.multiple_of((1 - core) * BLOCK, BLOCK), BLOCK, recv_near.at[i])
    vd[1] = values_of(1 - core)
    levels = [coarse(4, group, devices // 8), coarse(3, pair, devices // 4), coarse(2, chip, devices // 2)]
    run([unit for units, _ in levels for unit in units])
    terms = [(one_top[...], one_total[...], lambda h: one_acc[head_rows(h), :], 2.0)]
    terms += [gathered() for _, gathered in levels]

    before = peak[...]
    after = functools.reduce(jnp.maximum, [term[0] for term in terms], before)
    factors = [jnp.exp2(before - after)] + [weight * jnp.exp2(top - after) for top, _, _, weight in terms]
    lower = den[...] * factors[0]
    for factor, term in zip(factors[1:], terms):
        lower = lower + factor * term[1]
    factors = [factor / lower for factor in factors]
    attended = []
    for h in range(HEADS):
        upper = acc[head_rows(h), :] * factors[0][h : h + 1]
        for factor, term in zip(factors[1:], terms):
            upper = upper + term[2](h) * factor[h : h + 1]
        attended.append(upper.astype(BF16))
    loads[4].wait()
    turned = nt(eye[...], jnp.concatenate(attended, 0)).astype(BF16)
    out_ref[...] = nn(turned, wo[...]).astype(BF16)

    landed(deep, 0, 2 * BLOCK, send_sem.at[0])
    landed(deep, 0, 3 * BLOCK, send_sem.at[1])
    landed(deep, 0, 3 * BLOCK, send_sem.at[2])


def solution(mesh):
    devices = mesh.shape["ctx"] * mesh.shape["node"]

    def local(tokens, w_query, w_key, w_value, w_out):
        square = pltpu.VMEM((WIDTH, WIDTH), BF16)
        tall = pltpu.VMEM((ROWS, WIDTH), BF16)
        return pl.pallas_call(
            functools.partial(kernel, devices),
            out_shape=jax.ShapeDtypeStruct((ROWS, WIDTH), BF16),
            in_specs=[pl.BlockSpec(memory_space=pltpu.HBM)] * 5,
            out_specs=pl.BlockSpec(memory_space=pltpu.VMEM),
            scratch_shapes=[
                tall,
                square,
                square,
                square,
                square,
                square,
                pltpu.VMEM((COARSE, WIDTH), BF16),
                pltpu.VMEM((2 * 192, WIDTH), BF16),
                pltpu.VMEM((3 * ROWS, WIDTH), BF16),
                tall,
                pltpu.VMEM((COARSE, WIDTH), BF16),
                tall,
                pltpu.VMEM((WIDTH, ROWS), BF16),
                pltpu.VMEM((2, ROWS, WIDTH), BF16),
                pltpu.VMEM((2, WIDTH, ROWS), BF16),
                square,
                tall,
                pltpu.VMEM((BLOCK, WIDTH), BF16),
                pltpu.VMEM((2, WIDTH, 3 * BLOCK), BF16),
                pltpu.VMEM((WIDTH, ROWS), F32),
                pltpu.VMEM((HEADS, ROWS), F32),
                pltpu.VMEM((HEADS, ROWS), F32),
                pltpu.VMEM((WIDTH, BLOCK), F32),
                pltpu.VMEM((HEADS, BLOCK), F32),
                pltpu.VMEM((HEADS, BLOCK), F32),
                pltpu.VMEM((WIDTH, ROWS), F32),
                pltpu.VMEM((HEADS, ROWS), F32),
                pltpu.VMEM((HEADS, ROWS), F32),
                pltpu.VMEM((COARSE, ROWS), BF16),
                pltpu.VMEM((ROWS, ROWS), BF16),
                pltpu.VMEM((64, BLOCK), BF16),
                pltpu.VMEM((64, 192), BF16),
                pltpu.VMEM((BLOCK, ROWS), BF16),
                pltpu.VMEM((ROWS, ROWS), BF16),
                pltpu.VMEM((ROWS, ROWS), BF16),
                pltpu.VMEM((BLOCK, ROWS), BF16),
                pltpu.SemaphoreType.DMA((5,)),
                pltpu.SemaphoreType.DMA((3,)),
                pltpu.SemaphoreType.DMA((2,)),
                pltpu.SemaphoreType.DMA((6,)),
                pltpu.SemaphoreType.DMA((3,)),
                pltpu.SemaphoreType.REGULAR((2,)),
            ],
            compiler_params=pltpu.CompilerParams(
                collective_id=0, has_side_effects=True, vmem_limit_bytes=40 * 2**20
            ),
            name="hierarchical_attention",
        )(*[pltpu.with_memory_space_constraint(a, pltpu.HBM) for a in (tokens, w_query, w_key, w_value, w_out)])

    placed = (P(("ctx", "node"), None), P(), P(), P(), P())
    return jax.shard_map(
        local, mesh=mesh, in_specs=placed, out_specs=P(("ctx", "node"), None), check_vma=False
    )
```

```python
import functools
import math

import jax
import jax.numpy as jnp
from jax import lax
from jax.experimental import pallas as pl
from jax.experimental.pallas import tpu as pltpu
from jax.sharding import PartitionSpec as P

HEADS = 8
HEAD = 64
WIDTH = HEADS * HEAD
BLOCK = 128
ROWS = 256
NODES = 8
FAR = 1e30
SCALE = math.log2(math.e) / math.sqrt(HEAD)
BF16 = jnp.bfloat16
F32 = jnp.float32
START = {1: 0, 2: 128, 3: 192, 4: 224}
COARSE = 240


def nn(a, b):
    return lax.dot_general(a, b, (((1,), (0,)), ((), ())), preferred_element_type=F32)


def nt(a, b):
    return lax.dot_general(a, b, (((1,), (1,)), ((), ())), preferred_element_type=F32)


def iota(shape, axis):
    return lax.broadcasted_iota(jnp.int32, shape, axis)


def averager(rows, columns, level):
    hit = iota((rows, columns), 0) == iota((rows, columns), 1) >> level
    return jnp.where(hit, 0.5**level, 0.0).astype(BF16)


def spreader(rows, queries, level):
    hit = (iota((rows, ROWS), 0) & (queries - 1)) == iota((rows, ROWS), 1) >> level
    return jnp.where(hit, 1.0, 0.0).astype(BF16)


def split(values):
    high = values.astype(BF16)
    rest = values - high.astype(F32)
    middle = rest.astype(BF16)
    return [high, middle, (rest - middle.astype(F32)).astype(BF16)]


def spread_all(sums, tops, totals, spread):
    rows = sums.shape[0]
    out = nn(jnp.concatenate([sums] + split(jnp.concatenate([tops, totals], 0)), 0), spread)
    stats = out[rows : rows + 16] + out[rows + 16 : rows + 32] + out[rows + 32 :]
    return out[:rows], stats[:8], stats[8:]


def lane_head(shape, width):
    return iota(shape, 1) >> (width.bit_length() - 1)


def kernel(
    devices, x_hbm, wq_hbm, wk_hbm, wv_hbm, wo_hbm, out_ref,
    x, wq, wk, wv, wo, wvt, t, hedge, deep, q0, ql, k0, v0, kh, vh, u2, u3, u4, vd, acc, peak, den,
    one_sums, one_top, one_total,
    average, eye, halve, spread1, spread2, spread3, spread4,
    load_sem, send_sem, recv01, recv_far, recv_near, ready,
):
    me = lax.axis_index("ctx") * NODES + lax.axis_index("node")
    core = lax.rem(me, 2)
    chip = lax.div(me, 2)
    pair = lax.div(me, 4)
    group = lax.div(me, 8)

    def place(index):
        index = lax.rem(index + devices, devices)
        return {"ctx": lax.div(index, NODES), "node": lax.rem(index, NODES)}

    loads = []
    for i, (source, kept) in enumerate(((x_hbm, x), (wq_hbm, wq), (wk_hbm, wk), (wv_hbm, wv), (wo_hbm, wo))):
        loads.append(pltpu.make_async_copy(source, kept, load_sem.at[i]))
    loads[0].start()

    twin = me + 1 - 2 * core
    odd = lax.rem(chip, 2)
    second = lax.rem(pair, 2)

    def signal(semaphore, target):
        pl.semaphore_signal(semaphore, inc=1, device_id=place(target), device_id_type=pl.DeviceIdType.MESH)

    def elsewhere(target):
        return jnp.where(lax.div(target + devices, NODES) == group + devices // NODES, 0, 1)

    node = lax.rem(me, NODES)

    def for_each_above(act):
        act(me + 1)
        act(me + 2)
        act(me + 4)
        for j in (2, 3):
            act(8 * (group + 1) + 2 * j + core)
        pl.when(odd == 0)(lambda: act(me + 6))

        @pl.when(second == 0)
        def _():
            for j in (0, 1):
                act(8 * (group + 1) + 2 * j + core)

    def for_each_below(act):
        act(me - 1)
        act(me - 2)
        act(me - 4)
        for j in (0, 1):
            act(8 * (group - 1) + 2 * j + core)
        pl.when(odd == 1)(lambda: act(me - 6))

        @pl.when(second == 1)
        def _():
            for j in (2, 3):
                act(8 * (group - 1) + 2 * j + core)

    barrier = pltpu.get_barrier_semaphore()
    for_each_below(functools.partial(signal, barrier))
    for load in loads[1:]:
        load.start()

    h2, h3, h4 = (deep.at[pl.ds(i * ROWS, ROWS)] for i in range(3))
    for l in range(1, 5):
        average[START[l] : START[l] + (ROWS >> l), :] = averager(ROWS >> l, ROWS, l)
    loads[0].wait()
    t[...] = nn(average[...], x[...]).astype(BF16)

    pl.semaphore_wait(barrier, 5 + (1 - odd) + 2 * (1 - second))

    def send(source, target, landing, recv, sent):
        pltpu.make_async_remote_copy(
            src_ref=source,
            dst_ref=landing,
            send_sem=send_sem.at[sent],
            recv_sem=recv,
            device_id=place(target),
            device_id_type=pl.DeviceIdType.MESH,
        ).start()

    def mine(direction):
        return core * BLOCK + direction * 64


    def send_edge(up):
        target, to_far = (me + 1, core) if up else (me - 1, 1 - core)
        landing = hedge.at[pl.ds(pl.multiple_of(to_far * 192, 64), BLOCK)]
        send(x_hbm.at[pl.ds(up * BLOCK, BLOCK)], target, landing, recv01.at[to_far], 0)

    for_each_above(lambda target: signal(ready.at[elsewhere(target)], target))

    def send_one_means(up):
        target, to_far = (me + 1, core) if up else (me - 1, 1 - core)
        landing = hedge.at[pl.ds(pl.multiple_of(to_far * 192 + BLOCK, 64), 64)]
        send(t.at[pl.ds((1 - up) * 64, 64)], target, landing, recv01.at[to_far], 1)

    def send_two(up):
        landing = h2.at[pl.ds(pl.multiple_of(mine(1 - up), 64), 64)]
        send(t.at[pl.ds(START[2], 64)], me + (2 if up else -2), landing, recv_far.at[1 - up], 1)

    def send_three(up, target, recv):
        landing = h3.at[pl.ds(pl.multiple_of(mine(1 - up) + odd * 32, 32), 32)]
        send(t.at[pl.ds(START[3], 32)], target, landing, recv, 1)

    def send_four(up):
        def one(j, recv):
            landing = h4.at[pl.ds(pl.multiple_of(mine(1 - up) + lax.rem(chip, 4) * 16, 16), 16)]
            target = 8 * (group + (1 if up else -1)) + 2 * j + core
            send(t.at[pl.ds(START[4], 16)], target, landing, recv, 1)

        for j in (2, 3) if up else (0, 1):
            one(j, recv_far.at[4])

        @pl.when(second == 1 - up)
        def _():
            for j in (0, 1) if up else (2, 3):
                one(j, recv_far.at[5])

    def send_down(out):
        if out:
            send_four(0)
        pl.when(elsewhere(me - 4) == out)(lambda: send_three(0, me - 4, recv_far.at[2 + odd]))
        pl.when(jnp.logical_and(odd == 1, elsewhere(me - 6) == out))(lambda: send_three(0, me - 6, recv_far.at[2]))
        pl.when(elsewhere(me - 2) == out)(lambda: send_two(0))

        @pl.when(elsewhere(me - 1) == out)
        def _():
            send_one_means(0)
            send_edge(0)

    send_four(1)
    send_three(1, me + 4, recv_far.at[3 - odd])
    pl.when(odd == 0)(lambda: send_three(1, me + 6, recv_far.at[2]))
    send_two(1)
    send_one_means(1)
    send_edge(1)

    def landed(buffer, start, rows, sem):
        region = buffer.at[pl.ds(start, rows)]
        pltpu.make_async_copy(region, region, sem).wait()

    def half_of(buffer, whose):
        return buffer.at[pl.ds(pl.multiple_of(whose * BLOCK, BLOCK), BLOCK)]

    def forward(buffer, which):
        region = half_of(buffer, core)
        send(region, twin, region, recv_near.at[which], 2)

    def finer(source, d, target, inside):
        rows = source[pl.ds(pl.multiple_of(mine(d), 64), 64), :]
        means = nn(halve[:32, :64], rows).astype(BF16)
        target[pl.ds(pl.multiple_of(mine(d) + inside * 32, 32), 32), :] = means

    ones = jnp.ones((16, ROWS), BF16)
    half = lane_head((1, BLOCK), HEAD)
    pair_masks = [jnp.where(half == h, 1.0, 0.0).astype(BF16) for h in range(2)]

    def lanes_of(j):
        return slice(j * BLOCK, (j + 1) * BLOCK)

    def head_rows(h):
        return slice(h * HEAD, (h + 1) * HEAD)

    def pair_queries(block):
        return jnp.concatenate([block * pair_masks[0], block * pair_masks[1]], 0)

    def with_ones(v):
        return jnp.concatenate([v, ones[:, : v.shape[1]]], 0)

    def merge(lanes, top, total, heads):
        before = peak[:, lanes]
        after = jnp.maximum(before, top)
        old = jnp.exp2(before - after)
        new = jnp.exp2(top - after)
        den[:, lanes] = den[:, lanes] * old + new * total
        peak[:, lanes] = after
        for h in range(HEADS):
            rows = head_rows(h)
            acc[rows, lanes] = acc[rows, lanes] * old[h : h + 1] + heads(h) * new[h : h + 1]

    def run(units):
        waiting, active = list(units), []
        while waiting or active:
            if waiting:
                active.append(waiting.pop(0))
            active = [unit for unit in active if next(unit, None) is not None]

    def attend(keys, queries, values, done):
        s = nt(keys(), queries())
        yield True
        m = jnp.max(s, axis=0, keepdims=True)
        p = jnp.exp2(s - m).astype(BF16)
        yield True
        done(m, nn(with_ones(values()), p))

    def base_own(h):
        pairs = lanes_of(h // 2)

        def done(m, o):
            peak[h : h + 1, :] = m
            den[h : h + 1, :] = o[HEAD : HEAD + 1]
            acc[head_rows(h), :] = o[:HEAD]

        return attend(
            lambda: k0[:, pairs], lambda: q0[:, pairs] * pair_masks[h % 2], lambda: v0[head_rows(h), :], done
        )

    def side(slot, carry):
        start = pl.multiple_of(slot * 192, 64)
        landed(hedge, start, 192, recv01.at[slot])
        rows = hedge[pl.ds(start, 192), :]
        keys, values = kh.at[slot], vh.at[slot]
        keys[:192, :] = nn(rows, wk[...]).astype(BF16)
        values[:, :192] = nt(wvt[...], rows).astype(BF16)
        keys[192:, :] = nn(halve[...], keys[:BLOCK, :]).astype(BF16)
        values[:, 192:] = nt(values[:, :BLOCK], halve[...]).astype(BF16)
        queries = pl.ds(pl.multiple_of(jnp.where(slot == 0, 1 - core, core) * BLOCK, BLOCK), BLOCK)
        units, found = [], ([], [])
        for level, q, part in ((0, q0.at[queries], found[0]), (1, ql.at[pl.ds(0, BLOCK)], found[1])):
            for j in range(HEADS // 2):
                units.append(
                    attend(
                        lambda level=level, j=j: keys[lanes_of(level), lanes_of(j)],
                        lambda q=q, j=j: pair_queries(q[:, lanes_of(j)]),
                        lambda level=level, j=j: values[lanes_of(j), lanes_of(level)],
                        lambda m, o, part=part: part.append((m, o)),
                    )
                )
        run(units)
        missing = off(jnp.logical_and(slot == 1, jnp.where(core == 0, me == 0, me == devices - 1)))
        top, total, sums = by_head(found[0])
        merge(queries, top - missing, total, lambda h: sums[h])
        top, one_total[slot], sums = by_head(found[1])
        one_top[slot] = top - missing
        one_sums[slot] = jnp.concatenate(sums, 0)
        return carry

    def by_head(part):
        tops = [m[:, lanes_of(h)] for m, _ in part for h in range(2)]
        totals = [o[BLOCK : BLOCK + 1, lanes_of(h)] for _, o in part for h in range(2)]
        sums = [o[head_rows(h), lanes_of(h)] for _, o in part for h in range(2)]
        return jnp.concatenate(tops, 0), jnp.concatenate(totals, 0), sums

    def off(missing):
        return jnp.where(missing, FAR, 0.0).astype(F32)

    everywhere = slice(0, ROWS)

    seen = {2: u2, 3: u3, 4: u4}

    def shape_of(level):
        queries = ROWS >> level
        together = min(HEADS, ROWS // queries)
        return queries, together, together * queries

    def look(level):
        queries = ROWS >> level
        for u in range(2):
            part = slice(u * ROWS, (u + 1) * ROWS)
            block = ql[START[level] : START[level] + queries, part]
            masked = [block * jnp.where(lane_head((1, ROWS), HEAD) == h, 1.0, 0.0).astype(BF16) for h in range(4)]
            rows = slice(u * 4 * queries, (u + 1) * 4 * queries)
            seen[level][rows, :] = nt(jnp.concatenate(masked, 0), wk[:, part]).astype(BF16)

    def rows_of(level, whose):
        return half_of((h2, h3, h4)[level - 2], whose)[...]

    def values_of(whose):
        return nt(wvt[...], jnp.concatenate([rows_of(l, whose) for l in range(2, 5)], 0)).astype(BF16)

    scores = {}

    def coarse(level, index, count):
        queries, together, columns = shape_of(level)
        features = together * HEAD
        lanes = lanes_of(level - 2)
        off_left, off_right = off(index == 0), off(index == count - 1)
        column_head = lane_head((1, columns), queries)
        found = []

        def unit(u):
            part = slice(u * features, (u + 1) * features)
            s = [scores[level, u], nt(rows_of(level, 1 - core), seen[level][u * columns : (u + 1) * columns, :])]
            yield True
            left = [half[:64] for half in s]
            right = [half[64:] for half in s]
            m = jnp.maximum(
                jnp.max(jnp.maximum(*left), axis=0, keepdims=True) - off_left,
                jnp.max(jnp.maximum(*right), axis=0, keepdims=True) - off_right,
            )
            p = []
            for half in range(2):
                p.append(jnp.exp2(left[half] - (m + off_left)).astype(BF16))
                p.append(jnp.exp2(right[half] - (m + off_right)).astype(BF16))
            yield True
            values = jnp.concatenate([vd[0, part, lanes], vd[1, part, lanes]], 1)
            o = nn(with_ones(values), jnp.concatenate(p, 0))
            yield True
            own = [jnp.where(column_head == h, o[head_rows(h)], 0.0) for h in range(together)]
            row_head = iota((HEADS, columns), 0) == column_head + u * together
            found.append(
                spread_all(
                    jnp.concatenate(own, 0).astype(BF16),
                    jnp.where(row_head, m, 0.0),
                    jnp.where(row_head, o[features : features + 1], 0.0),
                    spreads[level][...],
                )
            )

        def gathered():
            def heads(h):
                u, inside = divmod(h, together)
                return found[u][0][head_rows(inside)]

            top = functools.reduce(jnp.add, [f[1] for f in found])
            total = functools.reduce(jnp.add, [f[2] for f in found])
            return top, total, heads, 2.0**level

        return [unit(u) for u in range(HEADS // together)], gathered

    eye[...] = averager(ROWS, ROWS, 0)
    halve[...] = averager(64, BLOCK, 1)
    spreads = {1: spread1, 2: spread2, 3: spread3, 4: spread4}
    for l in range(1, 5):
        spreads[l][...] = spreader(spreads[l].shape[0], ROWS >> l, l)
    for load in loads[1:4]:
        load.wait()
    q0[...] = (nn(x[...], wq[...]) * SCALE).astype(BF16)
    k0[...] = nn(x[...], wk[...]).astype(BF16)
    for i in range(2):
        wvt[i * ROWS : (i + 1) * ROWS, :] = nt(eye[...], wv[:, i * ROWS : (i + 1) * ROWS]).astype(BF16)
    ql[...] = nn(average[...], q0[...]).astype(BF16)
    v0[...] = nt(wvt[...], x[...]).astype(BF16)

    inside = (
        jnp.where(node >= 1, 1, 0)
        + jnp.where(node >= 4, 1, 0)
        + jnp.where(node >= 2, 1, 0)
        + jnp.where(jnp.logical_and(odd == 1, node >= 6), 1, 0)
    )
    pl.when(inside > 0)(lambda: pl.semaphore_wait(ready.at[0], inside))
    send_down(0)

    run([base_own(h) for h in range(HEADS)])
    for l in range(2, 5):
        look(l)

    early = jnp.where(jnp.logical_and(node > 0, node < NODES - 1), 2, 1)
    lax.fori_loop(0, early, side, 0)

    pl.semaphore_wait(ready.at[1], 5 + odd + 2 * second - inside)
    send_down(1)

    for d in range(2):
        landed(h2, pl.multiple_of(mine(d), 64), 64, recv_far.at[d])
    forward(h2, 0)
    finer(h2, odd, h3, 1 - odd)
    landed(h3, pl.multiple_of(mine(1 - odd), 64), 64, recv_far.at[2])
    landed(h3, pl.multiple_of(mine(odd) + odd * 32, 32), 32, recv_far.at[3])
    forward(h3, 1)
    finer(h3, second, h4, 1 - second)
    landed(h4, pl.multiple_of(mine(1 - second), 64), 64, recv_far.at[4])
    landed(h4, pl.multiple_of(mine(second) + second * 32, 32), 32, recv_far.at[5])
    forward(h4, 2)

    lax.fori_loop(early, 2, side, 0)

    top = jnp.maximum(one_top[0], one_top[1])
    parts = [jnp.exp2(one_top[slot] - top) for slot in range(2)]
    total = one_total[0] * parts[0] + one_total[1] * parts[1]
    sums = [
        (
            one_sums[0, head_rows(h), :] * parts[0][h : h + 1] + one_sums[1, head_rows(h), :] * parts[1][h : h + 1]
        ).astype(BF16)
        for h in range(HEADS)
    ]
    spread_sums, top, total = spread_all(jnp.concatenate(sums, 0), top, total, spread1[...])
    terms = [(top, total, lambda h: spread_sums[head_rows(h)], 2.0)]
    vd[0] = values_of(core)
    for l in range(4, 1, -1):
        _, together, columns = shape_of(l)
        for u in range(HEADS // together):
            scores[l, u] = nt(rows_of(l, core), seen[l][u * columns : (u + 1) * columns, :])
    for i, buffer in enumerate((h2, h3, h4)):
        landed(buffer, pl.multiple_of((1 - core) * BLOCK, BLOCK), BLOCK, recv_near.at[i])
    vd[1] = values_of(1 - core)
    levels = [coarse(4, group, devices // 8), coarse(3, pair, devices // 4), coarse(2, chip, devices // 2)]
    run([unit for units, _ in levels for unit in units])
    terms += [gathered() for _, gathered in levels]

    before = peak[...]
    after = functools.reduce(jnp.maximum, [term[0] for term in terms], before)
    factors = [jnp.exp2(before - after)] + [weight * jnp.exp2(top - after) for top, _, _, weight in terms]
    lower = den[...] * factors[0]
    for factor, term in zip(factors[1:], terms):
        lower = lower + factor * term[1]
    factors = [factor / lower for factor in factors]
    attended = []
    for h in range(HEADS):
        upper = acc[head_rows(h), :] * factors[0][h : h + 1]
        for factor, term in zip(factors[1:], terms):
            upper = upper + term[2](h) * factor[h : h + 1]
        attended.append(upper.astype(BF16))
    loads[4].wait()
    turned = nt(eye[...], jnp.concatenate(attended, 0)).astype(BF16)
    out_ref[...] = nn(turned, wo[...]).astype(BF16)

    landed(deep, 0, 2 * BLOCK, send_sem.at[0])
    landed(deep, 0, 3 * BLOCK + 64, send_sem.at[1])
    landed(deep, 0, 3 * BLOCK, send_sem.at[2])


def solution(mesh):
    devices = mesh.shape["ctx"] * mesh.shape["node"]

    def local(tokens, w_query, w_key, w_value, w_out):
        square = pltpu.VMEM((WIDTH, WIDTH), BF16)
        tall = pltpu.VMEM((ROWS, WIDTH), BF16)
        return pl.pallas_call(
            functools.partial(kernel, devices),
            out_shape=jax.ShapeDtypeStruct((ROWS, WIDTH), BF16),
            in_specs=[pl.BlockSpec(memory_space=pltpu.HBM)] * 5,
            out_specs=pl.BlockSpec(memory_space=pltpu.VMEM),
            scratch_shapes=[
                tall,
                square,
                square,
                square,
                square,
                square,
                pltpu.VMEM((COARSE, WIDTH), BF16),
                pltpu.VMEM((2 * 192, WIDTH), BF16),
                pltpu.VMEM((3 * ROWS, WIDTH), BF16),
                tall,
                pltpu.VMEM((COARSE, WIDTH), BF16),
                tall,
                pltpu.VMEM((WIDTH, ROWS), BF16),
                pltpu.VMEM((2, ROWS, WIDTH), BF16),
                pltpu.VMEM((2, WIDTH, ROWS), BF16),
                square,
                tall,
                pltpu.VMEM((BLOCK, WIDTH), BF16),
                pltpu.VMEM((2, WIDTH, 3 * BLOCK), BF16),
                pltpu.VMEM((WIDTH, ROWS), F32),
                pltpu.VMEM((HEADS, ROWS), F32),
                pltpu.VMEM((HEADS, ROWS), F32),
                pltpu.VMEM((2, WIDTH, BLOCK), F32),
                pltpu.VMEM((2, HEADS, BLOCK), F32),
                pltpu.VMEM((2, HEADS, BLOCK), F32),
                pltpu.VMEM((COARSE, ROWS), BF16),
                pltpu.VMEM((ROWS, ROWS), BF16),
                pltpu.VMEM((64, BLOCK), BF16),
                pltpu.VMEM((BLOCK, ROWS), BF16),
                pltpu.VMEM((ROWS, ROWS), BF16),
                pltpu.VMEM((ROWS, ROWS), BF16),
                pltpu.VMEM((BLOCK, ROWS), BF16),
                pltpu.SemaphoreType.DMA((5,)),
                pltpu.SemaphoreType.DMA((3,)),
                pltpu.SemaphoreType.DMA((2,)),
                pltpu.SemaphoreType.DMA((6,)),
                pltpu.SemaphoreType.DMA((3,)),
                pltpu.SemaphoreType.REGULAR((2,)),
            ],
            compiler_params=pltpu.CompilerParams(
                collective_id=0, has_side_effects=True, vmem_limit_bytes=40 * 2**20
            ),
            name="hierarchical_attention",
        )(*[pltpu.with_memory_space_constraint(a, pltpu.HBM) for a in (tokens, w_query, w_key, w_value, w_out)])

    placed = (P(("ctx", "node"), None), P(), P(), P(), P())
    return jax.shard_map(
        local, mesh=mesh, in_specs=placed, out_specs=P(("ctx", "node"), None), check_vma=False
    )
```

```python
import functools
import math

import jax
import jax.numpy as jnp
from jax import lax
from jax.experimental import pallas as pl
from jax.experimental.pallas import tpu as pltpu
from jax.sharding import PartitionSpec as P

HEADS = 8
HEAD = 64
WIDTH = HEADS * HEAD
BLOCK = 128
ROWS = 256
NODES = 8
FAR = 1e30
SCALE = math.log2(math.e) / math.sqrt(HEAD)
BF16 = jnp.bfloat16
F32 = jnp.float32
START = {1: 0, 2: 128, 3: 192, 4: 224}
COARSE = 240


def nn(a, b):
    return lax.dot_general(a, b, (((1,), (0,)), ((), ())), preferred_element_type=F32)


def nt(a, b):
    return lax.dot_general(a, b, (((1,), (1,)), ((), ())), preferred_element_type=F32)


def iota(shape, axis):
    return lax.broadcasted_iota(jnp.int32, shape, axis)


def averager(rows, columns, level):
    hit = iota((rows, columns), 0) == iota((rows, columns), 1) >> level
    return jnp.where(hit, 0.5**level, 0.0).astype(BF16)


def spreader(rows, queries, level):
    hit = (iota((rows, ROWS), 0) & (queries - 1)) == iota((rows, ROWS), 1) >> level
    return jnp.where(hit, 1.0, 0.0).astype(BF16)


def split(values):
    high = values.astype(BF16)
    rest = values - high.astype(F32)
    middle = rest.astype(BF16)
    return [high, middle, (rest - middle.astype(F32)).astype(BF16)]


def spread_all(sums, tops, totals, spread):
    rows = sums.shape[0]
    out = nn(jnp.concatenate([sums] + split(jnp.concatenate([tops, totals], 0)), 0), spread)
    stats = out[rows : rows + 16] + out[rows + 16 : rows + 32] + out[rows + 32 :]
    return out[:rows], stats[:8], stats[8:]


def lane_head(shape, width):
    return iota(shape, 1) >> (width.bit_length() - 1)


def kernel(
    devices, x_hbm, wq_hbm, wk_hbm, wv_hbm, wo_hbm, out_ref,
    x, wq, wk, wv, wo, wvt, t, hnear, hfar, deep, q0, ql, k0, v0, kh, vh, u2, u3, u4, vd, acc, peak, den,
    average, eye, halve, fold, spread1, spread2, spread3, spread4,
    load_sem, send_sem, recv01, recv_far, recv_near,
):
    me = lax.axis_index("ctx") * NODES + lax.axis_index("node")
    core = lax.rem(me, 2)
    chip = lax.div(me, 2)
    pair = lax.div(me, 4)
    group = lax.div(me, 8)

    def place(index):
        return {"ctx": lax.div(index, NODES), "node": lax.rem(index, NODES)}

    def exists(index):
        return jnp.logical_and(index >= 0, index < devices)

    loads = []
    for i, (source, kept) in enumerate(((x_hbm, x), (wq_hbm, wq), (wk_hbm, wk), (wv_hbm, wv), (wo_hbm, wo))):
        loads.append(pltpu.make_async_copy(source, kept, load_sem.at[i]))
    loads[0].start()

    twin = me + 1 - 2 * core
    beyond = me - 1 + 2 * core
    odd = lax.rem(chip, 2)
    second = lax.rem(pair, 2)
    two = me + 3 - 6 * core
    three_ahead = [(me + 4 - 8 * odd, odd, 1), (me + 6 - 12 * odd, odd, 0)]
    three_behind = [(me - 4 + 8 * odd, 1 - odd, 0)]
    ahead = 8 * (group + 1 - 2 * second) + core
    behind = 8 * (group - 1 + 2 * second) + core
    four_ahead = [(ahead + 4 * second + 2 * j, second, 1) for j in range(2)]
    four_ahead += [(ahead + 4 * (1 - second) + 2 * j, second, 0) for j in range(2)]
    four_behind = [(behind + 4 * second + 2 * j, 1 - second, 0) for j in range(2)]
    there = [exists(beyond), exists(two), exists(three_ahead[0][0]), exists(three_behind[0][0])]
    there += [exists(ahead), exists(behind)]
    parties = [[beyond], [two]] + [[p[0] for p in ps] for ps in (three_ahead, three_behind, four_ahead, four_behind)]

    barrier = pltpu.get_barrier_semaphore()

    def signal(target):
        pl.semaphore_signal(barrier, inc=1, device_id=place(target), device_id_type=pl.DeviceIdType.MESH)

    expected = 1
    for here, targets in zip(there, parties):
        expected = expected + jnp.where(here, len(targets), 0)
        pl.when(here)(lambda targets=targets: [signal(target) for target in targets] and None)
    signal(twin)
    for load in loads[1:]:
        load.start()

    pl.semaphore_wait(barrier, expected)

    def send(source, target, landing, recv, sent):
        pltpu.make_async_remote_copy(
            src_ref=source,
            dst_ref=landing,
            send_sem=send_sem.at[sent],
            recv_sem=recv,
            device_id=place(target),
            device_id_type=pl.DeviceIdType.MESH,
        ).start()

    def mine(direction):
        return core * BLOCK + direction * 64

    def send_edge(target, half, landing, recv, sent):
        rows = pl.multiple_of(half * BLOCK, BLOCK)
        send(x_hbm.at[pl.ds(rows, BLOCK)], target, landing.at[pl.ds(0, BLOCK)], recv, sent)

    pl.when(there[0])(lambda: send_edge(beyond, core, hfar, recv01.at[1], 1))
    send_edge(twin, 1 - core, hnear, recv01.at[0], 0)

    h2, h3, h4 = (deep.at[pl.ds(i * ROWS, ROWS)] for i in range(3))
    for l in range(1, 5):
        average[START[l] : START[l] + (ROWS >> l), :] = averager(ROWS >> l, ROWS, l)
    loads[0].wait()
    t[...] = nn(average[...], x[...]).astype(BF16)

    def send_one_means(target, half, landing, recv, sent):
        means = pl.multiple_of((1 - half) * 64, 64)
        send(t.at[pl.ds(means, 64)], target, landing.at[pl.ds(BLOCK, 64)], recv, sent)

    @pl.when(there[0])
    def _():
        send_one_means(beyond, core, hfar, recv01.at[1], 1)

    @pl.when(there[1])
    def _():
        landing = h2.at[pl.ds(pl.multiple_of(BLOCK - core * 64, 64), 64)]
        send(t.at[pl.ds(START[2], 64)], two, landing, recv_far.at[0], 2)

    def send_three(targets, sent):
        for target, d, short in targets:
            landing = h3.at[pl.ds(pl.multiple_of(mine(d) + odd * 32, 32), 32)]
            send(t.at[pl.ds(START[3], 32)], target, landing, recv_far.at[2 + short], sent)

    def send_four(targets, sent):
        for target, d, short in targets:
            landing = h4.at[pl.ds(pl.multiple_of(mine(d) + lax.rem(chip, 4) * 16, 16), 16)]
            send(t.at[pl.ds(START[4], 16)], target, landing, recv_far.at[4 + short], sent)

    pl.when(there[2])(lambda: send_three(three_ahead, 3))
    pl.when(there[3])(lambda: send_three(three_behind, 4))
    pl.when(there[4])(lambda: send_four(four_ahead, 5))
    pl.when(there[5])(lambda: send_four(four_behind, 6))
    send_one_means(twin, 1 - core, hnear, recv01.at[0], 0)

    def landed(buffer, start, rows, sem):
        region = buffer.at[pl.ds(start, rows)]
        pltpu.make_async_copy(region, region, sem).wait()

    def landed_or_zero(here, buffer, start, rows, sem):
        pl.when(here)(lambda: landed(buffer, start, rows, sem))

        @pl.when(jnp.logical_not(here))
        def _():
            buffer[pl.ds(start, rows), :] = jnp.zeros((rows, WIDTH), BF16)

    def half_of(buffer, whose):
        return buffer.at[pl.ds(pl.multiple_of(whose * BLOCK, BLOCK), BLOCK)]

    def forward(buffer, which):
        region = half_of(buffer, core)
        send(region, twin, region, recv_near.at[which], 0)

    def finer(source, d, target, inside):
        rows = source[pl.ds(pl.multiple_of(mine(d), 64), 64), :]
        means = nn(halve[:32, :64], rows).astype(BF16)
        target[pl.ds(pl.multiple_of(mine(d) + inside * 32, 32), 32), :] = means

    ones = jnp.ones((16, ROWS), BF16)
    half = lane_head((1, BLOCK), HEAD)
    pair_masks = [jnp.where(half == h, 1.0, 0.0).astype(BF16) for h in range(2)]

    def lanes_of(j):
        return slice(j * BLOCK, (j + 1) * BLOCK)

    def head_rows(h):
        return slice(h * HEAD, (h + 1) * HEAD)

    def pair_queries(block):
        return jnp.concatenate([block * pair_masks[0], block * pair_masks[1]], 0)

    def with_ones(v):
        return jnp.concatenate([v, ones[:, : v.shape[1]]], 0)

    def merge(lanes, top, total, heads):
        before = peak[:, lanes]
        after = jnp.maximum(before, top)
        old = jnp.exp2(before - after)
        new = jnp.exp2(top - after)
        den[:, lanes] = den[:, lanes] * old + new * total
        peak[:, lanes] = after
        for h in range(HEADS):
            rows = head_rows(h)
            acc[rows, lanes] = acc[rows, lanes] * old[h : h + 1] + heads(h) * new[h : h + 1]

    def run(units):
        waiting, active = list(units), []
        while waiting or active:
            if waiting:
                active.append(waiting.pop(0))
            active = [unit for unit in active if next(unit, None) is not None]

    def attend(keys, queries, values, done):
        s = nt(keys(), queries())
        yield True
        m = jnp.max(s, axis=0, keepdims=True)
        p = jnp.exp2(s - m).astype(BF16)
        yield True
        done(m, nn(with_ones(values()), p))

    def base_own(h):
        pairs = lanes_of(h // 2)

        def done(m, o):
            peak[h : h + 1, :] = m
            den[h : h + 1, :] = o[HEAD : HEAD + 1]
            acc[head_rows(h), :] = o[:HEAD]

        return attend(
            lambda: k0[:, pairs], lambda: q0[:, pairs] * pair_masks[h % 2], lambda: v0[head_rows(h), :], done
        )

    def project_side(buffer, slot):
        rows = buffer[...]
        kh[slot, :192, :] = nn(rows, wk[...]).astype(BF16)
        vh[slot, :, :192] = nt(wvt[...], rows).astype(BF16)

    def halve_side(slot):
        kh[slot, 192:, :] = nn(halve[...], kh[slot, :BLOCK, :]).astype(BF16)
        vh[slot, :, 192:] = nt(vh[slot, :, :BLOCK], halve[...]).astype(BF16)

    def side(slot, block):
        queries = pl.ds(pl.multiple_of(block * BLOCK, BLOCK), BLOCK)
        units, found = [], ([], [])
        for keys, q, part in (
            (slice(0, BLOCK), q0.at[queries], found[0]),
            (slice(BLOCK, 2 * BLOCK), ql.at[pl.ds(0, BLOCK)], found[1]),
        ):
            for j in range(HEADS // 2):
                units.append(
                    attend(
                        lambda keys=keys, j=j: kh[slot, keys, lanes_of(j)],
                        lambda q=q, j=j: pair_queries(q[:, lanes_of(j)]),
                        lambda keys=keys, j=j: vh[slot, lanes_of(j), keys],
                        lambda m, o, part=part: part.append((m, o)),
                    )
                )
        return units, queries, found[0], found[1]

    def by_head(part):
        tops = [m[:, lanes_of(h)] for m, _ in part for h in range(2)]
        totals = [o[BLOCK : BLOCK + 1, lanes_of(h)] for _, o in part for h in range(2)]
        sums = [o[head_rows(h), lanes_of(h)] for _, o in part for h in range(2)]
        return jnp.concatenate(tops, 0), jnp.concatenate(totals, 0), sums

    def off(missing):
        return jnp.where(missing, FAR, 0.0).astype(F32)

    everywhere = slice(0, ROWS)

    seen = {2: u2, 3: u3, 4: u4}

    def shape_of(level):
        queries = ROWS >> level
        together = min(HEADS, ROWS // queries)
        return queries, together, together * queries

    def look(level):
        queries = ROWS >> level
        for u in range(2):
            part = slice(u * ROWS, (u + 1) * ROWS)
            block = ql[START[level] : START[level] + queries, part]
            masked = [block * jnp.where(lane_head((1, ROWS), HEAD) == h, 1.0, 0.0).astype(BF16) for h in range(4)]
            rows = slice(u * 4 * queries, (u + 1) * 4 * queries)
            seen[level][rows, :] = nt(jnp.concatenate(masked, 0), wk[:, part]).astype(BF16)

    def rows_of(level, whose):
        return half_of((h2, h3, h4)[level - 2], whose)[...]

    def values_of(whose):
        return nt(wvt[...], jnp.concatenate([rows_of(l, whose) for l in range(2, 5)], 0)).astype(BF16)

    scores = {}

    def coarse(level, index, count):
        queries, together, columns = shape_of(level)
        features = together * HEAD
        lanes = lanes_of(level - 2)
        off_left, off_right = off(index == 0), off(index == count - 1)
        column_head = lane_head((1, columns), queries)
        found = []

        def unit(u):
            part = slice(u * features, (u + 1) * features)
            s = [scores[level, u], nt(rows_of(level, 1 - core), seen[level][u * columns : (u + 1) * columns, :])]
            yield True
            left = [half[:64] for half in s]
            right = [half[64:] for half in s]
            m = jnp.maximum(
                jnp.max(jnp.maximum(*left), axis=0, keepdims=True) - off_left,
                jnp.max(jnp.maximum(*right), axis=0, keepdims=True) - off_right,
            )
            p = []
            for half in range(2):
                p.append(jnp.exp2(left[half] - (m + off_left)).astype(BF16))
                p.append(jnp.exp2(right[half] - (m + off_right)).astype(BF16))
            yield True
            values = jnp.concatenate([vd[0, part, lanes], vd[1, part, lanes]], 1)
            o = nn(with_ones(values), jnp.concatenate(p, 0))
            yield True
            own = [jnp.where(column_head == h, o[head_rows(h)], 0.0) for h in range(together)]
            row_head = iota((HEADS, columns), 0) == column_head + u * together
            found.append(
                spread_all(
                    jnp.concatenate(own, 0).astype(BF16),
                    jnp.where(row_head, m, 0.0),
                    jnp.where(row_head, o[features : features + 1], 0.0),
                    spreads[level][...],
                )
            )

        def gathered():
            def heads(h):
                u, inside = divmod(h, together)
                return found[u][0][head_rows(inside)]

            top = functools.reduce(jnp.add, [f[1] for f in found])
            total = functools.reduce(jnp.add, [f[2] for f in found])
            return top, total, heads, 2.0**level

        return [unit(u) for u in range(HEADS // together)], gathered

    eye[...] = averager(ROWS, ROWS, 0)
    halve[...] = averager(64, BLOCK, 1)
    fold[:32, :] = jnp.concatenate([averager(32, BLOCK, 2), jnp.zeros((32, 64), BF16)], 1)
    fold[32:, :] = jnp.concatenate([jnp.zeros((32, BLOCK), BF16), averager(32, 64, 1)], 1)
    spreads = {1: spread1, 2: spread2, 3: spread3, 4: spread4}
    for l in range(1, 5):
        spreads[l][...] = spreader(spreads[l].shape[0], ROWS >> l, l)
    for load in loads[1:4]:
        load.wait()
    q0[...] = (nn(x[...], wq[...]) * SCALE).astype(BF16)
    k0[...] = nn(x[...], wk[...]).astype(BF16)
    for i in range(2):
        wvt[i * ROWS : (i + 1) * ROWS, :] = nt(eye[...], wv[:, i * ROWS : (i + 1) * ROWS]).astype(BF16)
    ql[...] = nn(average[...], q0[...]).astype(BF16)
    v0[...] = nt(wvt[...], x[...]).astype(BF16)

    landed(hnear, 0, 192, recv01.at[0])
    project_side(hnear, 0)
    units, near_lanes, base_near, one_near = side(0, 1 - core)
    own_units = [base_own(h) for h in range(HEADS)]
    run(own_units[:4])
    halve_side(0)
    run(own_units[4:] + units)
    top, total, near_sums = by_head(base_near)
    merge(near_lanes, top, total, lambda h: near_sums[h])
    for l in range(2, 5):
        look(l)

    landed_or_zero(there[0], hfar, 0, 192, recv01.at[1])
    h2[pl.ds(pl.multiple_of(mine(core), 64), 64), :] = nn(fold[...], hfar[...]).astype(BF16)
    landed_or_zero(there[1], h2, pl.multiple_of(mine(1 - core), 64), 64, recv_far.at[0])
    forward(h2, 0)
    finer(h2, odd, h3, 1 - odd)
    project_side(hfar, 1)
    landed_or_zero(there[2], h3, pl.multiple_of(mine(1 - odd), 64), 64, recv_far.at[2])
    landed_or_zero(there[3], h3, pl.multiple_of(mine(odd) + odd * 32, 32), 32, recv_far.at[3])
    forward(h3, 1)
    finer(h3, second, h4, 1 - second)
    halve_side(1)
    landed_or_zero(there[4], h4, pl.multiple_of(mine(1 - second), 64), 64, recv_far.at[4])
    landed_or_zero(there[5], h4, pl.multiple_of(mine(second) + second * 32, 32), 32, recv_far.at[5])
    forward(h4, 2)

    units, far_lanes, base_far, one_far = side(1, core)
    run(units)
    missing = off(jnp.where(core == 0, me == 0, me == devices - 1))
    top, total, far_sums = by_head(base_far)
    merge(far_lanes, top - missing, total, lambda h: far_sums[h])
    near_top, near_total, near_one = by_head(one_near)
    far_top, far_total, far_one = by_head(one_far)
    far_top = far_top - missing
    top = jnp.maximum(near_top, far_top)
    factor_near = jnp.exp2(near_top - top)
    factor_far = jnp.exp2(far_top - top)
    total = near_total * factor_near + far_total * factor_far
    sums = [
        (near_one[h] * factor_near[h : h + 1] + far_one[h] * factor_far[h : h + 1]).astype(BF16)
        for h in range(HEADS)
    ]
    one_sums, top, total = spread_all(jnp.concatenate(sums, 0), top, total, spread1[...])
    terms = [(top, total, lambda h: one_sums[head_rows(h)], 2.0)]

    vd[0] = values_of(core)
    for l in range(4, 1, -1):
        _, together, columns = shape_of(l)
        for u in range(HEADS // together):
            scores[l, u] = nt(rows_of(l, core), seen[l][u * columns : (u + 1) * columns, :])
    for i, buffer in enumerate((h2, h3, h4)):
        landed(buffer, pl.multiple_of((1 - core) * BLOCK, BLOCK), BLOCK, recv_near.at[i])
    vd[1] = values_of(1 - core)
    levels = [coarse(4, group, devices // 8), coarse(3, pair, devices // 4), coarse(2, chip, devices // 2)]
    run([unit for units, _ in levels for unit in units])
    terms += [gathered() for _, gathered in levels]

    before = peak[...]
    after = functools.reduce(jnp.maximum, [term[0] for term in terms], before)
    factors = [jnp.exp2(before - after)] + [weight * jnp.exp2(top - after) for top, _, _, weight in terms]
    lower = den[...] * factors[0]
    for factor, term in zip(factors[1:], terms):
        lower = lower + factor * term[1]
    factors = [factor / lower for factor in factors]
    attended = []
    for h in range(HEADS):
        upper = acc[head_rows(h), :] * factors[0][h : h + 1]
        for factor, term in zip(factors[1:], terms):
            upper = upper + term[2](h) * factor[h : h + 1]
        attended.append(upper.astype(BF16))
    loads[4].wait()
    turned = nt(eye[...], jnp.concatenate(attended, 0)).astype(BF16)
    out_ref[...] = nn(turned, wo[...]).astype(BF16)

    landed(deep, 0, 192 + 3 * BLOCK, send_sem.at[0])
    for i, (here, rows) in enumerate(zip(there, (192, 64, 64, 32, 64, 32))):
        pl.when(here)(lambda i=i, rows=rows: landed(deep, 0, rows, send_sem.at[i + 1]))


def solution(mesh):
    devices = mesh.shape["ctx"] * mesh.shape["node"]

    def local(tokens, w_query, w_key, w_value, w_out):
        square = pltpu.VMEM((WIDTH, WIDTH), BF16)
        tall = pltpu.VMEM((ROWS, WIDTH), BF16)
        return pl.pallas_call(
            functools.partial(kernel, devices),
            out_shape=jax.ShapeDtypeStruct((ROWS, WIDTH), BF16),
            in_specs=[pl.BlockSpec(memory_space=pltpu.HBM)] * 5,
            out_specs=pl.BlockSpec(memory_space=pltpu.VMEM),
            scratch_shapes=[
                tall,
                square,
                square,
                square,
                square,
                square,
                pltpu.VMEM((COARSE, WIDTH), BF16),
                pltpu.VMEM((192, WIDTH), BF16),
                pltpu.VMEM((192, WIDTH), BF16),
                pltpu.VMEM((3 * ROWS, WIDTH), BF16),
                tall,
                pltpu.VMEM((COARSE, WIDTH), BF16),
                tall,
                pltpu.VMEM((WIDTH, ROWS), BF16),
                pltpu.VMEM((2, ROWS, WIDTH), BF16),
                pltpu.VMEM((2, WIDTH, ROWS), BF16),
                square,
                tall,
                pltpu.VMEM((BLOCK, WIDTH), BF16),
                pltpu.VMEM((2, WIDTH, 3 * BLOCK), BF16),
                pltpu.VMEM((WIDTH, ROWS), F32),
                pltpu.VMEM((HEADS, ROWS), F32),
                pltpu.VMEM((HEADS, ROWS), F32),
                pltpu.VMEM((COARSE, ROWS), BF16),
                pltpu.VMEM((ROWS, ROWS), BF16),
                pltpu.VMEM((64, BLOCK), BF16),
                pltpu.VMEM((64, 192), BF16),
                pltpu.VMEM((BLOCK, ROWS), BF16),
                pltpu.VMEM((ROWS, ROWS), BF16),
                pltpu.VMEM((ROWS, ROWS), BF16),
                pltpu.VMEM((BLOCK, ROWS), BF16),
                pltpu.SemaphoreType.DMA((5,)),
                pltpu.SemaphoreType.DMA((7,)),
                pltpu.SemaphoreType.DMA((2,)),
                pltpu.SemaphoreType.DMA((6,)),
                pltpu.SemaphoreType.DMA((3,)),
            ],
            compiler_params=pltpu.CompilerParams(
                collective_id=0, has_side_effects=True, vmem_limit_bytes=40 * 2**20
            ),
            name="hierarchical_attention",
        )(*[pltpu.with_memory_space_constraint(a, pltpu.HBM) for a in (tokens, w_query, w_key, w_value, w_out)])

    placed = (P(("ctx", "node"), None), P(), P(), P(), P())
    return jax.shard_map(
        local, mesh=mesh, in_specs=placed, out_specs=P(("ctx", "node"), None), check_vma=False
    )
```

```python
import functools
import math

import jax
import jax.numpy as jnp
from jax import lax
from jax.experimental import pallas as pl
from jax.experimental.pallas import tpu as pltpu
from jax.sharding import PartitionSpec as P

HEADS = 8
HEAD = 64
WIDTH = HEADS * HEAD
BLOCK = 128
ROWS = 256
NODES = 8
FAR = 1e30
SCALE = math.log2(math.e) / math.sqrt(HEAD)
BF16 = jnp.bfloat16
F32 = jnp.float32
START = {1: 0, 2: 128, 3: 192, 4: 224}
COARSE = 240


def nn(a, b):
    return lax.dot_general(a, b, (((1,), (0,)), ((), ())), preferred_element_type=F32)


def nt(a, b):
    return lax.dot_general(a, b, (((1,), (1,)), ((), ())), preferred_element_type=F32)


def iota(shape, axis):
    return lax.broadcasted_iota(jnp.int32, shape, axis)


def averager(rows, columns, level):
    hit = iota((rows, columns), 0) == iota((rows, columns), 1) >> level
    return jnp.where(hit, 0.5**level, 0.0).astype(BF16)


def spreader(rows, queries, level):
    hit = (iota((rows, ROWS), 0) & (queries - 1)) == iota((rows, ROWS), 1) >> level
    return jnp.where(hit, 1.0, 0.0).astype(BF16)


def split(values):
    high = values.astype(BF16)
    rest = values - high.astype(F32)
    middle = rest.astype(BF16)
    return [high, middle, (rest - middle.astype(F32)).astype(BF16)]


def spread_all(sums, tops, totals, spread):
    rows = sums.shape[0]
    out = nn(jnp.concatenate([sums] + split(jnp.concatenate([tops, totals], 0)), 0), spread)
    stats = out[rows : rows + 16] + out[rows + 16 : rows + 32] + out[rows + 32 :]
    return out[:rows], stats[:8], stats[8:]


def lane_head(shape, width):
    return iota(shape, 1) >> (width.bit_length() - 1)


def kernel(
    devices, x_hbm, wq_hbm, wk_hbm, wv_hbm, wo_hbm, out_ref,
    x, wq, wk, wv, wo, wvt, t, hnear, hfar, deep, q0, ql, k0, v0, kh, vh, u2, u3, u4, vd, acc, peak, den,
    average, eye, halve, fold, spread1, spread2, spread3, spread4,
    load_sem, send_sem, recv01, recv_far, recv_near,
):
    me = lax.axis_index("ctx") * NODES + lax.axis_index("node")
    core = lax.rem(me, 2)
    chip = lax.div(me, 2)
    pair = lax.div(me, 4)
    group = lax.div(me, 8)

    def place(index):
        return {"ctx": lax.div(index, NODES), "node": lax.rem(index, NODES)}

    def exists(index):
        return jnp.logical_and(index >= 0, index < devices)

    loads = []
    for i, (source, kept) in enumerate(((x_hbm, x), (wq_hbm, wq), (wk_hbm, wk), (wv_hbm, wv), (wo_hbm, wo))):
        loads.append(pltpu.make_async_copy(source, kept, load_sem.at[i]))
    loads[0].start()

    twin = me + 1 - 2 * core
    beyond = me - 1 + 2 * core
    odd = lax.rem(chip, 2)
    second = lax.rem(pair, 2)
    two = me + 3 - 6 * core
    three_ahead = [(me + 4 - 8 * odd, odd, 1), (me + 6 - 12 * odd, odd, 0)]
    three_behind = [(me - 4 + 8 * odd, 1 - odd, 0)]
    ahead = 8 * (group + 1 - 2 * second) + core
    behind = 8 * (group - 1 + 2 * second) + core
    four_ahead = [(ahead + 4 * second + 2 * j, second, 1) for j in range(2)]
    four_ahead += [(ahead + 4 * (1 - second) + 2 * j, second, 0) for j in range(2)]
    four_behind = [(behind + 4 * second + 2 * j, 1 - second, 0) for j in range(2)]
    there = [exists(beyond), exists(two), exists(three_ahead[0][0]), exists(three_behind[0][0])]
    there += [exists(ahead), exists(behind)]
    parties = [[beyond], [two]] + [[p[0] for p in ps] for ps in (three_ahead, three_behind, four_ahead, four_behind)]

    barrier = pltpu.get_barrier_semaphore()

    def signal(target):
        pl.semaphore_signal(barrier, inc=1, device_id=place(target), device_id_type=pl.DeviceIdType.MESH)

    expected = 1
    for here, targets in zip(there, parties):
        expected = expected + jnp.where(here, len(targets), 0)
        pl.when(here)(lambda targets=targets: [signal(target) for target in targets] and None)
    signal(twin)
    for load in loads[1:]:
        load.start()

    h2, h3, h4 = (deep.at[pl.ds(i * ROWS, ROWS)] for i in range(3))
    for l in range(1, 5):
        average[START[l] : START[l] + (ROWS >> l), :] = averager(ROWS >> l, ROWS, l)
    loads[0].wait()
    t[...] = nn(average[...], x[...]).astype(BF16)

    pl.semaphore_wait(barrier, expected)

    def send(source, target, landing, recv, sent):
        pltpu.make_async_remote_copy(
            src_ref=source,
            dst_ref=landing,
            send_sem=send_sem.at[sent],
            recv_sem=recv,
            device_id=place(target),
            device_id_type=pl.DeviceIdType.MESH,
        ).start()

    def mine(direction):
        return core * BLOCK + direction * 64

    def send_edge(target, half, landing, recv, sent):
        rows = pl.multiple_of(half * BLOCK, BLOCK)
        send(x_hbm.at[pl.ds(rows, BLOCK)], target, landing.at[pl.ds(0, BLOCK)], recv, sent)

    pl.when(there[0])(lambda: send_edge(beyond, core, hfar, recv01.at[1], 1))
    send_edge(twin, 1 - core, hnear, recv01.at[0], 0)

    def send_one_means(target, half, landing, recv, sent):
        means = pl.multiple_of((1 - half) * 64, 64)
        send(t.at[pl.ds(means, 64)], target, landing.at[pl.ds(BLOCK, 64)], recv, sent)

    @pl.when(there[0])
    def _():
        send_one_means(beyond, core, hfar, recv01.at[1], 1)

    @pl.when(there[1])
    def _():
        landing = h2.at[pl.ds(pl.multiple_of(BLOCK - core * 64, 64), 64)]
        send(t.at[pl.ds(START[2], 64)], two, landing, recv_far.at[0], 2)

    def send_three(targets, sent):
        for target, d, short in targets:
            landing = h3.at[pl.ds(pl.multiple_of(mine(d) + odd * 32, 32), 32)]
            send(t.at[pl.ds(START[3], 32)], target, landing, recv_far.at[2 + short], sent)

    def send_four(targets, sent):
        for target, d, short in targets:
            landing = h4.at[pl.ds(pl.multiple_of(mine(d) + lax.rem(chip, 4) * 16, 16), 16)]
            send(t.at[pl.ds(START[4], 16)], target, landing, recv_far.at[4 + short], sent)

    pl.when(there[2])(lambda: send_three(three_ahead, 3))
    pl.when(there[3])(lambda: send_three(three_behind, 4))
    pl.when(there[4])(lambda: send_four(four_ahead, 5))
    pl.when(there[5])(lambda: send_four(four_behind, 6))
    send_one_means(twin, 1 - core, hnear, recv01.at[0], 0)

    def landed(buffer, start, rows, sem):
        region = buffer.at[pl.ds(start, rows)]
        pltpu.make_async_copy(region, region, sem).wait()

    def landed_or_zero(here, buffer, start, rows, sem):
        pl.when(here)(lambda: landed(buffer, start, rows, sem))

        @pl.when(jnp.logical_not(here))
        def _():
            buffer[pl.ds(start, rows), :] = jnp.zeros((rows, WIDTH), BF16)

    def half_of(buffer, whose):
        return buffer.at[pl.ds(pl.multiple_of(whose * BLOCK, BLOCK), BLOCK)]

    def forward(buffer, which):
        region = half_of(buffer, core)
        send(region, twin, region, recv_near.at[which], 0)

    def finer(source, d, target, inside):
        rows = source[pl.ds(pl.multiple_of(mine(d), 64), 64), :]
        means = nn(halve[:32, :64], rows).astype(BF16)
        target[pl.ds(pl.multiple_of(mine(d) + inside * 32, 32), 32), :] = means

    ones = jnp.ones((16, ROWS), BF16)
    half = lane_head((1, BLOCK), HEAD)
    pair_masks = [jnp.where(half == h, 1.0, 0.0).astype(BF16) for h in range(2)]

    def lanes_of(j):
        return slice(j * BLOCK, (j + 1) * BLOCK)

    def head_rows(h):
        return slice(h * HEAD, (h + 1) * HEAD)

    def pair_queries(block):
        return jnp.concatenate([block * pair_masks[0], block * pair_masks[1]], 0)

    def with_ones(v):
        return jnp.concatenate([v, ones[:, : v.shape[1]]], 0)

    def merge(lanes, top, total, heads):
        before = peak[:, lanes]
        after = jnp.maximum(before, top)
        old = jnp.exp2(before - after)
        new = jnp.exp2(top - after)
        den[:, lanes] = den[:, lanes] * old + new * total
        peak[:, lanes] = after
        for h in range(HEADS):
            rows = head_rows(h)
            acc[rows, lanes] = acc[rows, lanes] * old[h : h + 1] + heads(h) * new[h : h + 1]

    def run(units):
        waiting, active = list(units), []
        while waiting or active:
            if waiting:
                active.append(waiting.pop(0))
            active = [unit for unit in active if next(unit, None) is not None]

    def attend(keys, queries, values, done):
        s = nt(keys(), queries())
        yield True
        m = jnp.max(s, axis=0, keepdims=True)
        p = jnp.exp2(s - m).astype(BF16)
        yield True
        done(m, nn(with_ones(values()), p))

    def base_own(h):
        pairs = lanes_of(h // 2)

        def done(m, o):
            peak[h : h + 1, :] = m
            den[h : h + 1, :] = o[HEAD : HEAD + 1]
            acc[head_rows(h), :] = o[:HEAD]

        return attend(
            lambda: k0[:, pairs], lambda: q0[:, pairs] * pair_masks[h % 2], lambda: v0[head_rows(h), :], done
        )

    def project_side(buffer, slot):
        buffer[192:, :] = nn(halve[...], buffer[:BLOCK, :]).astype(BF16)
        kh[slot] = nn(buffer[...], wk[...]).astype(BF16)
        vh[slot] = nt(wvt[...], buffer[...]).astype(BF16)

    def side(slot, block):
        queries = pl.ds(pl.multiple_of(block * BLOCK, BLOCK), BLOCK)
        found = []
        units = [
            attend(
                lambda j=j: kh[slot, :BLOCK, lanes_of(j)],
                lambda j=j: pair_queries(q0[queries, lanes_of(j)]),
                lambda j=j: vh[slot, lanes_of(j), :BLOCK],
                lambda m, o: found.append((m, o)),
            )
            for j in range(HEADS // 2)
        ]
        return units, queries, found

    def level_one(j, missing, found):
        queries = pair_queries(ql[:BLOCK, lanes_of(j)])
        s = nt(kh[:, BLOCK:, lanes_of(j)].reshape(ROWS, BLOCK), queries)
        yield True
        near, far = s[:BLOCK], s[BLOCK:]
        m = jnp.maximum(jnp.max(near, axis=0, keepdims=True), jnp.max(far, axis=0, keepdims=True) - missing)
        p = jnp.concatenate([jnp.exp2(near - m).astype(BF16), jnp.exp2(far - (m + missing)).astype(BF16)], 0)
        yield True
        values = jnp.concatenate([vh[0, lanes_of(j), BLOCK:], vh[1, lanes_of(j), BLOCK:]], 1)
        found.append((m, nn(with_ones(values), p)))

    def by_head(part):
        tops = [m[:, lanes_of(h)] for m, _ in part for h in range(2)]
        totals = [o[BLOCK : BLOCK + 1, lanes_of(h)] for _, o in part for h in range(2)]
        sums = [o[head_rows(h), lanes_of(h)] for _, o in part for h in range(2)]
        return jnp.concatenate(tops, 0), jnp.concatenate(totals, 0), sums

    def off(missing):
        return jnp.where(missing, FAR, 0.0).astype(F32)

    everywhere = slice(0, ROWS)

    seen = {2: u2, 3: u3, 4: u4}

    def shape_of(level):
        queries = ROWS >> level
        together = min(HEADS, ROWS // queries)
        return queries, together, together * queries

    def look(level):
        queries = ROWS >> level
        for u in range(2):
            part = slice(u * ROWS, (u + 1) * ROWS)
            block = ql[START[level] : START[level] + queries, part]
            masked = [block * jnp.where(lane_head((1, ROWS), HEAD) == h, 1.0, 0.0).astype(BF16) for h in range(4)]
            rows = slice(u * 4 * queries, (u + 1) * 4 * queries)
            seen[level][rows, :] = nt(jnp.concatenate(masked, 0), wk[:, part]).astype(BF16)
            yield True

    def rows_of(level, whose):
        return half_of((h2, h3, h4)[level - 2], whose)[...]

    def values_of(whose):
        return nt(wvt[...], jnp.concatenate([rows_of(l, whose) for l in range(2, 5)], 0)).astype(BF16)

    scores = {}

    def coarse(level, index, count):
        queries, together, columns = shape_of(level)
        features = together * HEAD
        lanes = lanes_of(level - 2)
        off_left, off_right = off(index == 0), off(index == count - 1)
        column_head = lane_head((1, columns), queries)
        found = []

        def unit(u):
            part = slice(u * features, (u + 1) * features)
            s = [scores[level, u], nt(rows_of(level, 1 - core), seen[level][u * columns : (u + 1) * columns, :])]
            yield True
            left = [half[:64] for half in s]
            right = [half[64:] for half in s]
            m = jnp.maximum(
                jnp.max(jnp.maximum(*left), axis=0, keepdims=True) - off_left,
                jnp.max(jnp.maximum(*right), axis=0, keepdims=True) - off_right,
            )
            p = []
            for half in range(2):
                p.append(jnp.exp2(left[half] - (m + off_left)).astype(BF16))
                p.append(jnp.exp2(right[half] - (m + off_right)).astype(BF16))
            yield True
            values = jnp.concatenate([vd[0, part, lanes], vd[1, part, lanes]], 1)
            o = nn(with_ones(values), jnp.concatenate(p, 0))
            yield True
            own = [jnp.where(column_head == h, o[head_rows(h)], 0.0) for h in range(together)]
            row_head = iota((HEADS, columns), 0) == column_head + u * together
            found.append(
                spread_all(
                    jnp.concatenate(own, 0).astype(BF16),
                    jnp.where(row_head, m, 0.0),
                    jnp.where(row_head, o[features : features + 1], 0.0),
                    spreads[level][...],
                )
            )

        def gathered():
            def heads(h):
                u, inside = divmod(h, together)
                return found[u][0][head_rows(inside)]

            top = functools.reduce(jnp.add, [f[1] for f in found])
            total = functools.reduce(jnp.add, [f[2] for f in found])
            return top, total, heads, 2.0**level

        return [unit(u) for u in range(HEADS // together)], gathered

    eye[...] = averager(ROWS, ROWS, 0)
    halve[...] = averager(64, BLOCK, 1)
    fold[:32, :] = jnp.concatenate([averager(32, BLOCK, 2), jnp.zeros((32, 64), BF16)], 1)
    fold[32:, :] = jnp.concatenate([jnp.zeros((32, BLOCK), BF16), averager(32, 64, 1)], 1)
    spreads = {1: spread1, 2: spread2, 3: spread3, 4: spread4}
    for l in range(1, 5):
        spreads[l][...] = spreader(spreads[l].shape[0], ROWS >> l, l)
    for load in loads[1:4]:
        load.wait()
    q0[...] = (nn(x[...], wq[...]) * SCALE).astype(BF16)
    k0[...] = nn(x[...], wk[...]).astype(BF16)
    for i in range(2):
        wvt[i * ROWS : (i + 1) * ROWS, :] = nt(eye[...], wv[:, i * ROWS : (i + 1) * ROWS]).astype(BF16)
    ql[...] = nn(average[...], q0[...]).astype(BF16)
    v0[...] = nt(wvt[...], x[...]).astype(BF16)

    landed(hnear, 0, 192, recv01.at[0])
    project_side(hnear, 0)
    units, near_lanes, base_near = side(0, 1 - core)
    mixed = [base_own(h) for h in range(HEADS)] + units
    for place_in_line, level in ((9, 4), (6, 3), (3, 2)):
        mixed.insert(place_in_line, look(level))
    run(mixed)
    top, total, near_sums = by_head(base_near)
    merge(near_lanes, top, total, lambda h: near_sums[h])

    landed_or_zero(there[0], hfar, 0, 192, recv01.at[1])
    h2[pl.ds(pl.multiple_of(mine(core), 64), 64), :] = nn(fold[...], hfar[:192, :]).astype(BF16)
    landed_or_zero(there[1], h2, pl.multiple_of(mine(1 - core), 64), 64, recv_far.at[0])
    forward(h2, 0)
    finer(h2, odd, h3, 1 - odd)
    landed_or_zero(there[2], h3, pl.multiple_of(mine(1 - odd), 64), 64, recv_far.at[2])
    landed_or_zero(there[3], h3, pl.multiple_of(mine(odd) + odd * 32, 32), 32, recv_far.at[3])
    forward(h3, 1)
    finer(h3, second, h4, 1 - second)
    project_side(hfar, 1)
    landed_or_zero(there[4], h4, pl.multiple_of(mine(1 - second), 64), 64, recv_far.at[4])
    landed_or_zero(there[5], h4, pl.multiple_of(mine(second) + second * 32, 32), 32, recv_far.at[5])
    forward(h4, 2)

    missing = off(jnp.logical_not(there[0]))
    units, far_lanes, base_far = side(1, core)
    one = []
    run(units + [level_one(j, missing, one) for j in range(HEADS // 2)])
    top, total, far_sums = by_head(base_far)
    merge(far_lanes, top - missing, total, lambda h: far_sums[h])
    top, total, sums = by_head(one)
    one_sums, top, total = spread_all(jnp.concatenate(sums, 0).astype(BF16), top, total, spread1[...])
    terms = [(top, total, lambda h: one_sums[head_rows(h)], 2.0)]

    vd[0] = values_of(core)
    for l in range(4, 1, -1):
        _, together, columns = shape_of(l)
        for u in range(HEADS // together):
            scores[l, u] = nt(rows_of(l, core), seen[l][u * columns : (u + 1) * columns, :])
    for i, buffer in enumerate((h2, h3, h4)):
        landed(buffer, pl.multiple_of((1 - core) * BLOCK, BLOCK), BLOCK, recv_near.at[i])
    loads[4].wait()
    landed(deep, 0, 192 + 3 * BLOCK, send_sem.at[0])
    for i, (here, rows) in enumerate(zip(there, (192, 64, 64, 32, 64, 32))):
        pl.when(here)(lambda i=i, rows=rows: landed(deep, 0, rows, send_sem.at[i + 1]))

    vd[1] = values_of(1 - core)
    levels = [coarse(4, group, devices // 8), coarse(3, pair, devices // 4), coarse(2, chip, devices // 2)]
    run([unit for units, _ in levels for unit in units])
    terms += [gathered() for _, gathered in levels]

    before = peak[...]
    after = functools.reduce(jnp.maximum, [term[0] for term in terms], before)
    factors = [jnp.exp2(before - after)] + [weight * jnp.exp2(top - after) for top, _, _, weight in terms]
    lower = den[...] * factors[0]
    for factor, term in zip(factors[1:], terms):
        lower = lower + factor * term[1]
    inverse = 1.0 / lower
    factors = [factor * inverse for factor in factors]
    attended = []
    for h in range(HEADS):
        upper = acc[head_rows(h), :] * factors[0][h : h + 1]
        for factor, term in zip(factors[1:], terms):
            upper = upper + term[2](h) * factor[h : h + 1]
        attended.append(upper.astype(BF16))
    turned = nt(eye[...], jnp.concatenate(attended, 0)).astype(BF16)
    out_ref[...] = nn(turned, wo[...]).astype(BF16)


def solution(mesh):
    devices = mesh.shape["ctx"] * mesh.shape["node"]

    def local(tokens, w_query, w_key, w_value, w_out):
        square = pltpu.VMEM((WIDTH, WIDTH), BF16)
        tall = pltpu.VMEM((ROWS, WIDTH), BF16)
        return pl.pallas_call(
            functools.partial(kernel, devices),
            out_shape=jax.ShapeDtypeStruct((ROWS, WIDTH), BF16),
            in_specs=[pl.BlockSpec(memory_space=pltpu.HBM)] * 5,
            out_specs=pl.BlockSpec(memory_space=pltpu.VMEM),
            scratch_shapes=[
                tall,
                square,
                square,
                square,
                square,
                square,
                pltpu.VMEM((COARSE, WIDTH), BF16),
                tall,
                tall,
                pltpu.VMEM((3 * ROWS, WIDTH), BF16),
                tall,
                pltpu.VMEM((COARSE, WIDTH), BF16),
                tall,
                pltpu.VMEM((WIDTH, ROWS), BF16),
                pltpu.VMEM((2, ROWS, WIDTH), BF16),
                pltpu.VMEM((2, WIDTH, ROWS), BF16),
                square,
                tall,
                pltpu.VMEM((BLOCK, WIDTH), BF16),
                pltpu.VMEM((2, WIDTH, 3 * BLOCK), BF16),
                pltpu.VMEM((WIDTH, ROWS), F32),
                pltpu.VMEM((HEADS, ROWS), F32),
                pltpu.VMEM((HEADS, ROWS), F32),
                pltpu.VMEM((COARSE, ROWS), BF16),
                pltpu.VMEM((ROWS, ROWS), BF16),
                pltpu.VMEM((64, BLOCK), BF16),
                pltpu.VMEM((64, 192), BF16),
                pltpu.VMEM((BLOCK, ROWS), BF16),
                pltpu.VMEM((ROWS, ROWS), BF16),
                pltpu.VMEM((ROWS, ROWS), BF16),
                pltpu.VMEM((BLOCK, ROWS), BF16),
                pltpu.SemaphoreType.DMA((5,)),
                pltpu.SemaphoreType.DMA((7,)),
                pltpu.SemaphoreType.DMA((2,)),
                pltpu.SemaphoreType.DMA((6,)),
                pltpu.SemaphoreType.DMA((3,)),
            ],
            compiler_params=pltpu.CompilerParams(
                collective_id=0, has_side_effects=True, vmem_limit_bytes=40 * 2**20
            ),
            name="hierarchical_attention",
        )(*[pltpu.with_memory_space_constraint(a, pltpu.HBM) for a in (tokens, w_query, w_key, w_value, w_out)])

    placed = (P(("ctx", "node"), None), P(), P(), P(), P())
    return jax.shard_map(
        local, mesh=mesh, in_specs=placed, out_specs=P(("ctx", "node"), None), check_vma=False
    )
```

```python
import functools
import math

import jax
import jax.numpy as jnp
from jax import lax
from jax.experimental import pallas as pl
from jax.experimental.pallas import tpu as pltpu
from jax.sharding import PartitionSpec as P

HEADS = 8
HEAD = 64
WIDTH = HEADS * HEAD
BLOCK = 128
ROWS = 256
NODES = 8
FAR = 1e30
SCALE = math.log2(math.e) / math.sqrt(HEAD)
BF16 = jnp.bfloat16
F32 = jnp.float32
START = {1: 0, 2: 128, 3: 192, 4: 224}
COARSE = 240


def nn(a, b):
    return lax.dot_general(a, b, (((1,), (0,)), ((), ())), preferred_element_type=F32)


def nt(a, b):
    return lax.dot_general(a, b, (((1,), (1,)), ((), ())), preferred_element_type=F32)


def iota(shape, axis):
    return lax.broadcasted_iota(jnp.int32, shape, axis)


def averager(rows, columns, level):
    hit = iota((rows, columns), 0) == iota((rows, columns), 1) >> level
    return jnp.where(hit, 0.5**level, 0.0).astype(BF16)


def spreader(rows, queries, level):
    hit = (iota((rows, ROWS), 0) & (queries - 1)) == iota((rows, ROWS), 1) >> level
    return jnp.where(hit, 1.0, 0.0).astype(BF16)


def split(values):
    high = values.astype(BF16)
    rest = values - high.astype(F32)
    middle = rest.astype(BF16)
    return [high, middle, (rest - middle.astype(F32)).astype(BF16)]


def spread_all(sums, tops, totals, spread):
    rows = sums.shape[0]
    out = nn(jnp.concatenate([sums] + split(jnp.concatenate([tops, totals], 0)), 0), spread)
    stats = out[rows : rows + 16] + out[rows + 16 : rows + 32] + out[rows + 32 :]
    return out[:rows], stats[:8], stats[8:]


def lane_head(shape, width):
    return iota(shape, 1) >> (width.bit_length() - 1)


def kernel(
    devices, x_hbm, wq_hbm, wk_hbm, wv_hbm, wo_hbm, out_ref,
    x, wq, wk, wv, wo, wvt, t, hnear, hfar, deep, q0, ql, k0, v0, kh, vh, u2, u3, u4, vd, acc, peak, den,
    average, eye, halve, fold, spread1, spread2, spread3, spread4,
    load_sem, send_sem, recv01, recv_far, recv_near,
):
    me = lax.axis_index("ctx") * NODES + lax.axis_index("node")
    core = lax.rem(me, 2)
    chip = lax.div(me, 2)
    pair = lax.div(me, 4)
    group = lax.div(me, 8)

    def place(index):
        return {"ctx": lax.div(index, NODES), "node": lax.rem(index, NODES)}

    def exists(index):
        return jnp.logical_and(index >= 0, index < devices)

    loads = []
    for i, (source, kept) in enumerate(((x_hbm, x), (wq_hbm, wq), (wk_hbm, wk), (wv_hbm, wv), (wo_hbm, wo))):
        loads.append(pltpu.make_async_copy(source, kept, load_sem.at[i]))
    loads[0].start()

    twin = me + 1 - 2 * core
    beyond = me - 1 + 2 * core
    odd = lax.rem(chip, 2)
    second = lax.rem(pair, 2)
    two = me + 3 - 6 * core
    three_ahead = [(me + 4 - 8 * odd, odd, 1), (me + 6 - 12 * odd, odd, 0)]
    three_behind = [(me - 4 + 8 * odd, 1 - odd, 0)]
    ahead = 8 * (group + 1 - 2 * second) + core
    behind = 8 * (group - 1 + 2 * second) + core
    four_ahead = [(ahead + 4 * second + 2 * j, second, 1) for j in range(2)]
    four_ahead += [(ahead + 4 * (1 - second) + 2 * j, second, 0) for j in range(2)]
    four_behind = [(behind + 4 * second + 2 * j, 1 - second, 0) for j in range(2)]
    there = [exists(beyond), exists(two), exists(three_ahead[0][0]), exists(three_behind[0][0])]
    there += [exists(ahead), exists(behind)]
    parties = [[beyond], [two]] + [[p[0] for p in ps] for ps in (three_ahead, three_behind, four_ahead, four_behind)]

    barrier = pltpu.get_barrier_semaphore()

    def signal(target):
        pl.semaphore_signal(barrier, inc=1, device_id=place(target), device_id_type=pl.DeviceIdType.MESH)

    expected = 1
    for here, targets in zip(there, parties):
        expected = expected + jnp.where(here, len(targets), 0)
        pl.when(here)(lambda targets=targets: [signal(target) for target in targets] and None)
    signal(twin)
    for load in loads[1:]:
        load.start()

    h2, h3, h4 = (deep.at[pl.ds(i * ROWS, ROWS)] for i in range(3))
    for l in range(1, 5):
        average[START[l] : START[l] + (ROWS >> l), :] = averager(ROWS >> l, ROWS, l)
    pl.semaphore_wait(barrier, expected)

    def send(source, target, landing, recv, sent):
        pltpu.make_async_remote_copy(
            src_ref=source,
            dst_ref=landing,
            send_sem=send_sem.at[sent],
            recv_sem=recv,
            device_id=place(target),
            device_id_type=pl.DeviceIdType.MESH,
        ).start()

    def mine(direction):
        return core * BLOCK + direction * 64

    def send_edge(target, half, landing, recv, sent):
        rows = pl.multiple_of(half * BLOCK, BLOCK)
        send(x_hbm.at[pl.ds(rows, BLOCK)], target, landing.at[pl.ds(0, BLOCK)], recv, sent)

    pl.when(there[0])(lambda: send_edge(beyond, core, hfar, recv01.at[1], 1))
    send_edge(twin, 1 - core, hnear, recv01.at[0], 0)

    loads[0].wait()
    t[...] = nn(average[...], x[...]).astype(BF16)

    def send_one_means(target, half, landing, recv, sent):
        means = pl.multiple_of((1 - half) * 64, 64)
        send(t.at[pl.ds(means, 64)], target, landing.at[pl.ds(BLOCK, 64)], recv, sent)

    @pl.when(there[0])
    def _():
        send_one_means(beyond, core, hfar, recv01.at[1], 1)

    @pl.when(there[1])
    def _():
        landing = h2.at[pl.ds(pl.multiple_of(BLOCK - core * 64, 64), 64)]
        send(t.at[pl.ds(START[2], 64)], two, landing, recv_far.at[0], 2)

    def send_three(targets, sent):
        for target, d, short in targets:
            landing = h3.at[pl.ds(pl.multiple_of(mine(d) + odd * 32, 32), 32)]
            send(t.at[pl.ds(START[3], 32)], target, landing, recv_far.at[2 + short], sent)

    def send_four(targets, sent):
        for target, d, short in targets:
            landing = h4.at[pl.ds(pl.multiple_of(mine(d) + lax.rem(chip, 4) * 16, 16), 16)]
            send(t.at[pl.ds(START[4], 16)], target, landing, recv_far.at[4 + short], sent)

    pl.when(there[2])(lambda: send_three(three_ahead, 3))
    pl.when(there[3])(lambda: send_three(three_behind, 4))
    pl.when(there[4])(lambda: send_four(four_ahead, 5))
    pl.when(there[5])(lambda: send_four(four_behind, 6))
    send_one_means(twin, 1 - core, hnear, recv01.at[0], 0)

    def landed(buffer, start, rows, sem):
        region = buffer.at[pl.ds(start, rows)]
        pltpu.make_async_copy(region, region, sem).wait()

    def landed_or_zero(here, buffer, start, rows, sem):
        pl.when(here)(lambda: landed(buffer, start, rows, sem))

        @pl.when(jnp.logical_not(here))
        def _():
            buffer[pl.ds(start, rows), :] = jnp.zeros((rows, WIDTH), BF16)

    def half_of(buffer, whose):
        return buffer.at[pl.ds(pl.multiple_of(whose * BLOCK, BLOCK), BLOCK)]

    def forward(buffer, which):
        region = half_of(buffer, core)
        send(region, twin, region, recv_near.at[which], 0)

    def finer(source, d, target, inside):
        rows = source[pl.ds(pl.multiple_of(mine(d), 64), 64), :]
        means = nn(halve[:32, :64], rows).astype(BF16)
        target[pl.ds(pl.multiple_of(mine(d) + inside * 32, 32), 32), :] = means

    ones = jnp.ones((16, ROWS), BF16)
    half = lane_head((1, BLOCK), HEAD)
    pair_masks = [jnp.where(half == h, 1.0, 0.0).astype(BF16) for h in range(2)]

    def lanes_of(j):
        return slice(j * BLOCK, (j + 1) * BLOCK)

    def head_rows(h):
        return slice(h * HEAD, (h + 1) * HEAD)

    def pair_queries(block):
        return jnp.concatenate([block * pair_masks[0], block * pair_masks[1]], 0)

    def with_ones(v):
        return jnp.concatenate([v, ones[:, : v.shape[1]]], 0)

    def merge(lanes, top, total, heads):
        before = peak[:, lanes]
        after = jnp.maximum(before, top)
        old = jnp.exp2(before - after)
        new = jnp.exp2(top - after)
        den[:, lanes] = den[:, lanes] * old + new * total
        peak[:, lanes] = after
        for h in range(HEADS):
            rows = head_rows(h)
            acc[rows, lanes] = acc[rows, lanes] * old[h : h + 1] + heads(h) * new[h : h + 1]

    def run(units):
        waiting, active = list(units), []
        while waiting or active:
            if waiting:
                active.append(waiting.pop(0))
            active = [unit for unit in active if next(unit, None) is not None]

    def attend(keys, queries, values, done):
        s = nt(keys(), queries())
        yield True
        m = jnp.max(s, axis=0, keepdims=True)
        p = jnp.exp2(s - m).astype(BF16)
        yield True
        done(m, nn(with_ones(values()), p))

    def base_own(h):
        pairs = lanes_of(h // 2)

        def done(m, o):
            peak[h : h + 1, :] = m
            den[h : h + 1, :] = o[HEAD : HEAD + 1]
            acc[head_rows(h), :] = o[:HEAD]

        return attend(
            lambda: k0[:, pairs], lambda: q0[:, pairs] * pair_masks[h % 2], lambda: v0[head_rows(h), :], done
        )

    def project_side(buffer, slot):
        buffer[192:, :] = nn(halve[...], buffer[:BLOCK, :]).astype(BF16)
        kh[slot] = nn(buffer[...], wk[...]).astype(BF16)
        vh[slot] = nt(wvt[...], buffer[...]).astype(BF16)

    def side(slot, block):
        queries = pl.ds(pl.multiple_of(block * BLOCK, BLOCK), BLOCK)
        found = []
        units = [
            attend(
                lambda j=j: kh[slot, :BLOCK, lanes_of(j)],
                lambda j=j: pair_queries(q0[queries, lanes_of(j)]),
                lambda j=j: vh[slot, lanes_of(j), :BLOCK],
                lambda m, o: found.append((m, o)),
            )
            for j in range(HEADS // 2)
        ]
        return units, queries, found

    def level_one(j, missing, found):
        queries = pair_queries(ql[:BLOCK, lanes_of(j)])
        s = nt(kh[:, BLOCK:, lanes_of(j)].reshape(ROWS, BLOCK), queries)
        yield True
        near, far = s[:BLOCK], s[BLOCK:]
        m = jnp.maximum(jnp.max(near, axis=0, keepdims=True), jnp.max(far, axis=0, keepdims=True) - missing)
        p = jnp.concatenate([jnp.exp2(near - m).astype(BF16), jnp.exp2(far - (m + missing)).astype(BF16)], 0)
        yield True
        values = jnp.concatenate([vh[0, lanes_of(j), BLOCK:], vh[1, lanes_of(j), BLOCK:]], 1)
        found.append((m, nn(with_ones(values), p)))

    def by_head(part):
        tops = [m[:, lanes_of(h)] for m, _ in part for h in range(2)]
        totals = [o[BLOCK : BLOCK + 1, lanes_of(h)] for _, o in part for h in range(2)]
        sums = [o[head_rows(h), lanes_of(h)] for _, o in part for h in range(2)]
        return jnp.concatenate(tops, 0), jnp.concatenate(totals, 0), sums

    def off(missing):
        return jnp.where(missing, FAR, 0.0).astype(F32)

    everywhere = slice(0, ROWS)

    seen = {2: u2, 3: u3, 4: u4}

    def shape_of(level):
        queries = ROWS >> level
        together = min(HEADS, ROWS // queries)
        return queries, together, together * queries

    def look(level):
        queries = ROWS >> level
        for u in range(2):
            part = slice(u * ROWS, (u + 1) * ROWS)
            block = ql[START[level] : START[level] + queries, part]
            masked = [block * jnp.where(lane_head((1, ROWS), HEAD) == h, 1.0, 0.0).astype(BF16) for h in range(4)]
            rows = slice(u * 4 * queries, (u + 1) * 4 * queries)
            seen[level][rows, :] = nt(jnp.concatenate(masked, 0), wk[:, part]).astype(BF16)
            yield True

    def rows_of(level, whose):
        return half_of((h2, h3, h4)[level - 2], whose)[...]

    def values_of(whose):
        return nt(wvt[...], jnp.concatenate([rows_of(l, whose) for l in range(2, 5)], 0)).astype(BF16)

    scores = {}

    def coarse(level, index, count):
        queries, together, columns = shape_of(level)
        features = together * HEAD
        lanes = lanes_of(level - 2)
        off_left, off_right = off(index == 0), off(index == count - 1)
        column_head = lane_head((1, columns), queries)
        found = []

        def unit(u):
            part = slice(u * features, (u + 1) * features)
            s = [scores[level, u], nt(rows_of(level, 1 - core), seen[level][u * columns : (u + 1) * columns, :])]
            yield True
            left = [half[:64] for half in s]
            right = [half[64:] for half in s]
            m = jnp.maximum(
                jnp.max(jnp.maximum(*left), axis=0, keepdims=True) - off_left,
                jnp.max(jnp.maximum(*right), axis=0, keepdims=True) - off_right,
            )
            p = []
            for half in range(2):
                p.append(jnp.exp2(left[half] - (m + off_left)).astype(BF16))
                p.append(jnp.exp2(right[half] - (m + off_right)).astype(BF16))
            yield True
            values = jnp.concatenate([vd[0, part, lanes], vd[1, part, lanes]], 1)
            o = nn(with_ones(values), jnp.concatenate(p, 0))
            yield True
            own = [jnp.where(column_head == h, o[head_rows(h)], 0.0) for h in range(together)]
            row_head = iota((HEADS, columns), 0) == column_head + u * together
            found.append(
                spread_all(
                    jnp.concatenate(own, 0).astype(BF16),
                    jnp.where(row_head, m, 0.0),
                    jnp.where(row_head, o[features : features + 1], 0.0),
                    spreads[level][...],
                )
            )

        def gathered():
            def heads(h):
                u, inside = divmod(h, together)
                return found[u][0][head_rows(inside)]

            top = functools.reduce(jnp.add, [f[1] for f in found])
            total = functools.reduce(jnp.add, [f[2] for f in found])
            return top, total, heads, 2.0**level

        return [unit(u) for u in range(HEADS // together)], gathered

    eye[...] = averager(ROWS, ROWS, 0)
    halve[...] = averager(64, BLOCK, 1)
    fold[:32, :] = jnp.concatenate([averager(32, BLOCK, 2), jnp.zeros((32, 64), BF16)], 1)
    fold[32:, :] = jnp.concatenate([jnp.zeros((32, BLOCK), BF16), averager(32, 64, 1)], 1)
    spreads = {1: spread1, 2: spread2, 3: spread3, 4: spread4}
    for l in range(1, 5):
        spreads[l][...] = spreader(spreads[l].shape[0], ROWS >> l, l)
    for load in loads[1:4]:
        load.wait()
    q0[...] = (nn(x[...], wq[...]) * SCALE).astype(BF16)
    k0[...] = nn(x[...], wk[...]).astype(BF16)
    for i in range(2):
        wvt[i * ROWS : (i + 1) * ROWS, :] = nt(eye[...], wv[:, i * ROWS : (i + 1) * ROWS]).astype(BF16)
    ql[...] = nn(average[...], q0[...]).astype(BF16)
    v0[...] = nt(wvt[...], x[...]).astype(BF16)

    landed(hnear, 0, 192, recv01.at[0])
    project_side(hnear, 0)
    units, near_lanes, base_near = side(0, 1 - core)
    mixed = [base_own(h) for h in range(HEADS)] + units
    for place_in_line, level in ((9, 4), (6, 3), (3, 2)):
        mixed.insert(place_in_line, look(level))
    run(mixed)
    top, total, near_sums = by_head(base_near)
    merge(near_lanes, top, total, lambda h: near_sums[h])

    landed_or_zero(there[0], hfar, 0, 192, recv01.at[1])
    h2[pl.ds(pl.multiple_of(mine(core), 64), 64), :] = nn(fold[...], hfar[:192, :]).astype(BF16)
    landed_or_zero(there[1], h2, pl.multiple_of(mine(1 - core), 64), 64, recv_far.at[0])
    forward(h2, 0)
    finer(h2, odd, h3, 1 - odd)
    landed_or_zero(there[2], h3, pl.multiple_of(mine(1 - odd), 64), 64, recv_far.at[2])
    landed_or_zero(there[3], h3, pl.multiple_of(mine(odd) + odd * 32, 32), 32, recv_far.at[3])
    forward(h3, 1)
    finer(h3, second, h4, 1 - second)
    project_side(hfar, 1)
    landed_or_zero(there[4], h4, pl.multiple_of(mine(1 - second), 64), 64, recv_far.at[4])
    landed_or_zero(there[5], h4, pl.multiple_of(mine(second) + second * 32, 32), 32, recv_far.at[5])
    forward(h4, 2)

    missing = off(jnp.logical_not(there[0]))
    units, far_lanes, base_far = side(1, core)
    one = []
    run(units + [level_one(j, missing, one) for j in range(HEADS // 2)])
    top, total, far_sums = by_head(base_far)
    merge(far_lanes, top - missing, total, lambda h: far_sums[h])
    top, total, sums = by_head(one)
    one_sums, top, total = spread_all(jnp.concatenate(sums, 0).astype(BF16), top, total, spread1[...])
    terms = [(top, total, lambda h: one_sums[head_rows(h)], 2.0)]

    vd[0] = values_of(core)
    for l in range(4, 1, -1):
        _, together, columns = shape_of(l)
        for u in range(HEADS // together):
            scores[l, u] = nt(rows_of(l, core), seen[l][u * columns : (u + 1) * columns, :])
    for i, buffer in enumerate((h2, h3, h4)):
        landed(buffer, pl.multiple_of((1 - core) * BLOCK, BLOCK), BLOCK, recv_near.at[i])
    loads[4].wait()
    landed(deep, 0, 192 + 3 * BLOCK, send_sem.at[0])
    for i, (here, rows) in enumerate(zip(there, (192, 64, 64, 32, 64, 32))):
        pl.when(here)(lambda i=i, rows=rows: landed(deep, 0, rows, send_sem.at[i + 1]))

    vd[1] = values_of(1 - core)
    levels = [coarse(4, group, devices // 8), coarse(3, pair, devices // 4), coarse(2, chip, devices // 2)]
    run([unit for units, _ in levels for unit in units])
    terms += [gathered() for _, gathered in levels]

    before = peak[...]
    after = functools.reduce(jnp.maximum, [term[0] for term in terms], before)
    factors = [jnp.exp2(before - after)] + [weight * jnp.exp2(top - after) for top, _, _, weight in terms]
    lower = den[...] * factors[0]
    for factor, term in zip(factors[1:], terms):
        lower = lower + factor * term[1]
    inverse = 1.0 / lower
    factors = [factor * inverse for factor in factors]
    attended = []
    for h in range(HEADS):
        upper = acc[head_rows(h), :] * factors[0][h : h + 1]
        for factor, term in zip(factors[1:], terms):
            upper = upper + term[2](h) * factor[h : h + 1]
        attended.append(upper.astype(BF16))
    turned = nt(eye[...], jnp.concatenate(attended, 0)).astype(BF16)
    out_ref[...] = nn(turned, wo[...]).astype(BF16)


def solution(mesh):
    devices = mesh.shape["ctx"] * mesh.shape["node"]

    def local(tokens, w_query, w_key, w_value, w_out):
        square = pltpu.VMEM((WIDTH, WIDTH), BF16)
        tall = pltpu.VMEM((ROWS, WIDTH), BF16)
        return pl.pallas_call(
            functools.partial(kernel, devices),
            out_shape=jax.ShapeDtypeStruct((ROWS, WIDTH), BF16),
            in_specs=[pl.BlockSpec(memory_space=pltpu.HBM)] * 5,
            out_specs=pl.BlockSpec(memory_space=pltpu.VMEM),
            scratch_shapes=[
                tall,
                square,
                square,
                square,
                square,
                square,
                pltpu.VMEM((COARSE, WIDTH), BF16),
                tall,
                tall,
                pltpu.VMEM((3 * ROWS, WIDTH), BF16),
                tall,
                pltpu.VMEM((COARSE, WIDTH), BF16),
                tall,
                pltpu.VMEM((WIDTH, ROWS), BF16),
                pltpu.VMEM((2, ROWS, WIDTH), BF16),
                pltpu.VMEM((2, WIDTH, ROWS), BF16),
                square,
                tall,
                pltpu.VMEM((BLOCK, WIDTH), BF16),
                pltpu.VMEM((2, WIDTH, 3 * BLOCK), BF16),
                pltpu.VMEM((WIDTH, ROWS), F32),
                pltpu.VMEM((HEADS, ROWS), F32),
                pltpu.VMEM((HEADS, ROWS), F32),
                pltpu.VMEM((COARSE, ROWS), BF16),
                pltpu.VMEM((ROWS, ROWS), BF16),
                pltpu.VMEM((64, BLOCK), BF16),
                pltpu.VMEM((64, 192), BF16),
                pltpu.VMEM((BLOCK, ROWS), BF16),
                pltpu.VMEM((ROWS, ROWS), BF16),
                pltpu.VMEM((ROWS, ROWS), BF16),
                pltpu.VMEM((BLOCK, ROWS), BF16),
                pltpu.SemaphoreType.DMA((5,)),
                pltpu.SemaphoreType.DMA((7,)),
                pltpu.SemaphoreType.DMA((2,)),
                pltpu.SemaphoreType.DMA((6,)),
                pltpu.SemaphoreType.DMA((3,)),
            ],
            compiler_params=pltpu.CompilerParams(
                collective_id=0, has_side_effects=True, vmem_limit_bytes=40 * 2**20
            ),
            name="hierarchical_attention",
        )(*[pltpu.with_memory_space_constraint(a, pltpu.HBM) for a in (tokens, w_query, w_key, w_value, w_out)])

    placed = (P(("ctx", "node"), None), P(), P(), P(), P())
    return jax.shard_map(
        local, mesh=mesh, in_specs=placed, out_specs=P(("ctx", "node"), None), check_vma=False
    )
```

```python
import functools
import math

import jax
import jax.numpy as jnp
from jax import lax
from jax.experimental import pallas as pl
from jax.experimental.pallas import tpu as pltpu
from jax.sharding import PartitionSpec as P

HEADS = 8
HEAD = 64
WIDTH = HEADS * HEAD
BLOCK = 128
ROWS = 256
NODES = 8
FAR = 1e30
SCALE = math.log2(math.e) / math.sqrt(HEAD)
BF16 = jnp.bfloat16
F32 = jnp.float32
START = {1: 0, 2: 128, 3: 192, 4: 224}
COARSE = 240


def nn(a, b):
    return lax.dot_general(a, b, (((1,), (0,)), ((), ())), preferred_element_type=F32)


def nt(a, b):
    return lax.dot_general(a, b, (((1,), (1,)), ((), ())), preferred_element_type=F32)


def iota(shape, axis):
    return lax.broadcasted_iota(jnp.int32, shape, axis)


def averager(rows, columns, level):
    hit = iota((rows, columns), 0) == iota((rows, columns), 1) >> level
    return jnp.where(hit, 0.5**level, 0.0).astype(BF16)


def spreader(rows, queries, level):
    hit = (iota((rows, ROWS), 0) & (queries - 1)) == iota((rows, ROWS), 1) >> level
    return jnp.where(hit, 1.0, 0.0).astype(BF16)


def split(values):
    high = values.astype(BF16)
    rest = values - high.astype(F32)
    middle = rest.astype(BF16)
    return [high, middle, (rest - middle.astype(F32)).astype(BF16)]


def spread_all(sums, tops, totals, spread):
    rows = sums.shape[0]
    out = nn(jnp.concatenate([sums] + split(jnp.concatenate([tops, totals], 0)), 0), spread)
    stats = out[rows : rows + 16] + out[rows + 16 : rows + 32] + out[rows + 32 :]
    return out[:rows], stats[:8], stats[8:]


def lane_head(shape, width):
    return iota(shape, 1) >> (width.bit_length() - 1)


def kernel(
    devices, x_hbm, wq_hbm, wk_hbm, wv_hbm, wo_hbm, out_ref, wo,
    x, wq, wk, wv, wvt, t, hnear, hfar, deep, q0, ql, k0, v0, kh, vh, u2, u3, u4, vd, acc, peak, den,
    average, eye, halve, fold, spread1, spread2, spread3, spread4,
    load_sem, send_sem, recv01, recv_far, recv_near,
):
    me = lax.axis_index("ctx") * NODES + lax.axis_index("node")
    core = lax.rem(me, 2)
    chip = lax.div(me, 2)
    pair = lax.div(me, 4)
    group = lax.div(me, 8)

    def place(index):
        return {"ctx": lax.div(index, NODES), "node": lax.rem(index, NODES)}

    def exists(index):
        return jnp.logical_and(index >= 0, index < devices)

    loads = []
    for i, (source, kept) in enumerate(((x_hbm, x), (wq_hbm, wq), (wk_hbm, wk), (wv_hbm, wv), (wo_hbm, wo))):
        loads.append(pltpu.make_async_copy(source, kept, load_sem.at[i]))
    loads[0].start()

    twin = me + 1 - 2 * core
    beyond = me - 1 + 2 * core
    odd = lax.rem(chip, 2)
    second = lax.rem(pair, 2)
    two = me + 3 - 6 * core
    three_ahead = [(me + 4 - 8 * odd, odd, 1), (me + 6 - 12 * odd, odd, 0)]
    three_behind = [(me - 4 + 8 * odd, 1 - odd, 0)]
    ahead = 8 * (group + 1 - 2 * second) + core
    behind = 8 * (group - 1 + 2 * second) + core
    four_ahead = [(ahead + 4 * second + 2 * j, second, 1) for j in range(2)]
    four_ahead += [(ahead + 4 * (1 - second) + 2 * j, second, 0) for j in range(2)]
    four_behind = [(behind + 4 * second + 2 * j, 1 - second, 0) for j in range(2)]
    there = [exists(beyond), exists(two), exists(three_ahead[0][0]), exists(three_behind[0][0])]
    there += [exists(ahead), exists(behind)]
    parties = [[beyond], [two]] + [[p[0] for p in ps] for ps in (three_ahead, three_behind, four_ahead, four_behind)]

    barrier = pltpu.get_barrier_semaphore()

    def signal(target):
        pl.semaphore_signal(barrier, inc=1, device_id=place(target), device_id_type=pl.DeviceIdType.MESH)

    expected = 1
    for here, targets in reversed(list(zip(there, parties))):
        expected = expected + jnp.where(here, len(targets), 0)
        pl.when(here)(lambda targets=targets: [signal(target) for target in targets] and None)
    signal(twin)
    for load in loads[1:]:
        load.start()

    h2, h3, h4 = (deep.at[pl.ds(i * ROWS, ROWS)] for i in range(3))
    for l in range(1, 5):
        average[START[l] : START[l] + (ROWS >> l), :] = averager(ROWS >> l, ROWS, l)
    pl.semaphore_wait(barrier, expected)

    def send(source, target, landing, recv, sent):
        pltpu.make_async_remote_copy(
            src_ref=source,
            dst_ref=landing,
            send_sem=send_sem.at[sent],
            recv_sem=recv,
            device_id=place(target),
            device_id_type=pl.DeviceIdType.MESH,
        ).start()

    def mine(direction):
        return core * BLOCK + direction * 64

    def send_edge(target, half, landing, recv, sent):
        rows = pl.multiple_of(half * BLOCK, BLOCK)
        send(x_hbm.at[pl.ds(rows, BLOCK)], target, landing.at[pl.ds(0, BLOCK)], recv, sent)

    pl.when(there[0])(lambda: send_edge(beyond, core, hfar, recv01.at[1], 1))
    send_edge(twin, 1 - core, hnear, recv01.at[0], 0)

    loads[0].wait()
    t[...] = nn(average[...], x[...]).astype(BF16)

    def send_one_means(target, half, landing, recv, sent):
        means = pl.multiple_of((1 - half) * 64, 64)
        send(t.at[pl.ds(means, 64)], target, landing.at[pl.ds(BLOCK, 64)], recv, sent)

    @pl.when(there[0])
    def _():
        send_one_means(beyond, core, hfar, recv01.at[1], 1)

    @pl.when(there[1])
    def _():
        landing = h2.at[pl.ds(pl.multiple_of(BLOCK - core * 64, 64), 64)]
        send(t.at[pl.ds(START[2], 64)], two, landing, recv_far.at[0], 2)

    def send_three(targets, sent):
        for target, d, short in targets:
            landing = h3.at[pl.ds(pl.multiple_of(mine(d) + odd * 32, 32), 32)]
            send(t.at[pl.ds(START[3], 32)], target, landing, recv_far.at[2 + short], sent)

    def send_four(targets, sent):
        for target, d, short in targets:
            landing = h4.at[pl.ds(pl.multiple_of(mine(d) + lax.rem(chip, 4) * 16, 16), 16)]
            send(t.at[pl.ds(START[4], 16)], target, landing, recv_far.at[4 + short], sent)

    pl.when(there[2])(lambda: send_three(three_ahead, 3))
    pl.when(there[3])(lambda: send_three(three_behind, 4))
    pl.when(there[4])(lambda: send_four(four_ahead, 5))
    pl.when(there[5])(lambda: send_four(four_behind, 6))
    send_one_means(twin, 1 - core, hnear, recv01.at[0], 0)

    def landed(buffer, start, rows, sem):
        region = buffer.at[pl.ds(start, rows)]
        pltpu.make_async_copy(region, region, sem).wait()

    def landed_or_zero(here, buffer, start, rows, sem):
        pl.when(here)(lambda: landed(buffer, start, rows, sem))

        @pl.when(jnp.logical_not(here))
        def _():
            buffer[pl.ds(start, rows), :] = jnp.zeros((rows, WIDTH), BF16)

    def half_of(buffer, whose):
        return buffer.at[pl.ds(pl.multiple_of(whose * BLOCK, BLOCK), BLOCK)]

    def forward(buffer, which):
        region = half_of(buffer, core)
        send(region, twin, region, recv_near.at[which], 0)

    def finer(source, d, target, inside):
        rows = source[pl.ds(pl.multiple_of(mine(d), 64), 64), :]
        means = nn(halve[:32, :64], rows).astype(BF16)
        target[pl.ds(pl.multiple_of(mine(d) + inside * 32, 32), 32), :] = means

    ones = jnp.ones((16, ROWS), BF16)
    half = lane_head((1, BLOCK), HEAD)
    pair_masks = [jnp.where(half == h, 1.0, 0.0).astype(BF16) for h in range(2)]

    def lanes_of(j):
        return slice(j * BLOCK, (j + 1) * BLOCK)

    def head_rows(h):
        return slice(h * HEAD, (h + 1) * HEAD)

    def pair_queries(block):
        return jnp.concatenate([block * pair_masks[0], block * pair_masks[1]], 0)

    def with_ones(v):
        return jnp.concatenate([v, ones[:, : v.shape[1]]], 0)

    def merge(lanes, top, total, heads):
        before = peak[:, lanes]
        after = jnp.maximum(before, top)
        old = jnp.exp2(before - after)
        new = jnp.exp2(top - after)
        den[:, lanes] = den[:, lanes] * old + new * total
        peak[:, lanes] = after
        for h in range(HEADS):
            rows = head_rows(h)
            acc[rows, lanes] = acc[rows, lanes] * old[h : h + 1] + heads(h) * new[h : h + 1]

    def run(units):
        waiting, active = list(units), []
        while waiting or active:
            if waiting:
                active.append(waiting.pop(0))
            active = [unit for unit in active if next(unit, None) is not None]

    def attend(keys, queries, values, done):
        s = nt(keys(), queries())
        yield True
        m = jnp.max(s, axis=0, keepdims=True)
        p = jnp.exp2(s - m).astype(BF16)
        yield True
        done(m, nn(with_ones(values()), p))

    def base_own(h):
        pairs = lanes_of(h // 2)

        def done(m, o):
            peak[h : h + 1, :] = m
            den[h : h + 1, :] = o[HEAD : HEAD + 1]
            acc[head_rows(h), :] = o[:HEAD]

        return attend(
            lambda: k0[:, pairs], lambda: q0[:, pairs] * pair_masks[h % 2], lambda: v0[head_rows(h), :], done
        )

    def project_side(buffer, slot):
        buffer[192:, :] = nn(halve[...], buffer[:BLOCK, :]).astype(BF16)
        kh[slot] = nn(buffer[...], wk[...]).astype(BF16)
        vh[slot] = nt(wvt[...], buffer[...]).astype(BF16)

    def side(slot, block):
        queries = pl.ds(pl.multiple_of(block * BLOCK, BLOCK), BLOCK)
        found = []
        units = [
            attend(
                lambda j=j: kh[slot, :BLOCK, lanes_of(j)],
                lambda j=j: pair_queries(q0[queries, lanes_of(j)]),
                lambda j=j: vh[slot, lanes_of(j), :BLOCK],
                lambda m, o: found.append((m, o)),
            )
            for j in range(HEADS // 2)
        ]
        return units, queries, found

    def level_one(j, missing, found):
        queries = pair_queries(ql[:BLOCK, lanes_of(j)])
        s = nt(kh[:, BLOCK:, lanes_of(j)].reshape(ROWS, BLOCK), queries)
        yield True
        near, far = s[:BLOCK], s[BLOCK:]
        m = jnp.maximum(jnp.max(near, axis=0, keepdims=True), jnp.max(far, axis=0, keepdims=True) - missing)
        p = jnp.concatenate([jnp.exp2(near - m).astype(BF16), jnp.exp2(far - (m + missing)).astype(BF16)], 0)
        yield True
        values = jnp.concatenate([vh[0, lanes_of(j), BLOCK:], vh[1, lanes_of(j), BLOCK:]], 1)
        found.append((m, nn(with_ones(values), p)))

    def by_head(part):
        tops = [m[:, lanes_of(h)] for m, _ in part for h in range(2)]
        totals = [o[BLOCK : BLOCK + 1, lanes_of(h)] for _, o in part for h in range(2)]
        sums = [o[head_rows(h), lanes_of(h)] for _, o in part for h in range(2)]
        return jnp.concatenate(tops, 0), jnp.concatenate(totals, 0), sums

    def off(missing):
        return jnp.where(missing, FAR, 0.0).astype(F32)

    everywhere = slice(0, ROWS)

    seen = {2: u2, 3: u3, 4: u4}

    def shape_of(level):
        queries = ROWS >> level
        together = min(HEADS, ROWS // queries)
        return queries, together, together * queries

    def look(level):
        queries = ROWS >> level
        for u in range(2):
            part = slice(u * ROWS, (u + 1) * ROWS)
            block = ql[START[level] : START[level] + queries, part]
            masked = [block * jnp.where(lane_head((1, ROWS), HEAD) == h, 1.0, 0.0).astype(BF16) for h in range(4)]
            rows = slice(u * 4 * queries, (u + 1) * 4 * queries)
            seen[level][rows, :] = nt(jnp.concatenate(masked, 0), wk[:, part]).astype(BF16)
            yield True

    def rows_of(level, whose):
        return half_of((h2, h3, h4)[level - 2], whose)[...]

    def values_of(whose):
        return nt(wvt[...], jnp.concatenate([rows_of(l, whose) for l in range(2, 5)], 0)).astype(BF16)

    scores = {}

    def coarse(level, index, count):
        queries, together, columns = shape_of(level)
        features = together * HEAD
        lanes = lanes_of(level - 2)
        off_left, off_right = off(index == 0), off(index == count - 1)
        column_head = lane_head((1, columns), queries)
        found = []

        def unit(u):
            part = slice(u * features, (u + 1) * features)
            s = [scores[level, u], nt(rows_of(level, 1 - core), seen[level][u * columns : (u + 1) * columns, :])]
            yield True
            left = [half[:64] for half in s]
            right = [half[64:] for half in s]
            m = jnp.maximum(
                jnp.max(jnp.maximum(*left), axis=0, keepdims=True) - off_left,
                jnp.max(jnp.maximum(*right), axis=0, keepdims=True) - off_right,
            )
            p = []
            for half in range(2):
                p.append(jnp.exp2(left[half] - (m + off_left)).astype(BF16))
                p.append(jnp.exp2(right[half] - (m + off_right)).astype(BF16))
            yield True
            values = jnp.concatenate([vd[0, part, lanes], vd[1, part, lanes]], 1)
            o = nn(with_ones(values), jnp.concatenate(p, 0))
            yield True
            own = [jnp.where(column_head == h, o[head_rows(h)], 0.0) for h in range(together)]
            row_head = iota((HEADS, columns), 0) == column_head + u * together
            found.append(
                spread_all(
                    jnp.concatenate(own, 0).astype(BF16),
                    jnp.where(row_head, m, 0.0),
                    jnp.where(row_head, o[features : features + 1], 0.0),
                    spreads[level][...],
                )
            )

        def gathered():
            def heads(h):
                u, inside = divmod(h, together)
                return found[u][0][head_rows(inside)]

            top = functools.reduce(jnp.add, [f[1] for f in found])
            total = functools.reduce(jnp.add, [f[2] for f in found])
            return top, total, heads, 2.0**level

        return [unit(u) for u in range(HEADS // together)], gathered

    eye[...] = averager(ROWS, ROWS, 0)
    halve[...] = averager(64, BLOCK, 1)
    fold[:32, :] = jnp.concatenate([averager(32, BLOCK, 2), jnp.zeros((32, 64), BF16)], 1)
    fold[32:, :] = jnp.concatenate([jnp.zeros((32, BLOCK), BF16), averager(32, 64, 1)], 1)
    spreads = {1: spread1, 2: spread2, 3: spread3, 4: spread4}
    for l in range(1, 5):
        spreads[l][...] = spreader(spreads[l].shape[0], ROWS >> l, l)
    for load in loads[1:4]:
        load.wait()
    q0[...] = (nn(x[...], wq[...]) * SCALE).astype(BF16)
    k0[...] = nn(x[...], wk[...]).astype(BF16)
    for i in range(2):
        wvt[i * ROWS : (i + 1) * ROWS, :] = nt(eye[...], wv[:, i * ROWS : (i + 1) * ROWS]).astype(BF16)
    ql[...] = nn(average[...], q0[...]).astype(BF16)
    v0[...] = nt(wvt[...], x[...]).astype(BF16)

    landed(hnear, 0, 192, recv01.at[0])
    project_side(hnear, 0)
    units, near_lanes, base_near = side(0, 1 - core)
    mixed = [base_own(h) for h in range(HEADS)] + units
    for place_in_line, level in ((9, 4), (6, 3), (3, 2)):
        mixed.insert(place_in_line, look(level))
    run(mixed)
    top, total, near_sums = by_head(base_near)
    merge(near_lanes, top, total, lambda h: near_sums[h])

    landed_or_zero(there[0], hfar, 0, 192, recv01.at[1])
    h2[pl.ds(pl.multiple_of(mine(core), 64), 64), :] = nn(fold[...], hfar[:192, :]).astype(BF16)
    project_side(hfar, 1)
    missing = off(jnp.logical_not(there[0]))
    units, far_lanes, base_far = side(1, core)
    run(units)
    top, total, far_sums = by_head(base_far)
    merge(far_lanes, top - missing, total, lambda h: far_sums[h])

    landed_or_zero(there[1], h2, pl.multiple_of(mine(1 - core), 64), 64, recv_far.at[0])
    forward(h2, 0)
    finer(h2, odd, h3, 1 - odd)
    landed_or_zero(there[2], h3, pl.multiple_of(mine(1 - odd), 64), 64, recv_far.at[2])
    landed_or_zero(there[3], h3, pl.multiple_of(mine(odd) + odd * 32, 32), 32, recv_far.at[3])
    forward(h3, 1)
    finer(h3, second, h4, 1 - second)
    landed_or_zero(there[4], h4, pl.multiple_of(mine(1 - second), 64), 64, recv_far.at[4])
    landed_or_zero(there[5], h4, pl.multiple_of(mine(second) + second * 32, 32), 32, recv_far.at[5])
    forward(h4, 2)

    one = []
    run([level_one(j, missing, one) for j in range(HEADS // 2)])
    vd[0] = values_of(core)
    for l in range(4, 1, -1):
        _, together, columns = shape_of(l)
        for u in range(HEADS // together):
            scores[l, u] = nt(rows_of(l, core), seen[l][u * columns : (u + 1) * columns, :])
    top, total, sums = by_head(one)
    one_sums, top, total = spread_all(jnp.concatenate(sums, 0).astype(BF16), top, total, spread1[...])
    terms = [(top, total, lambda h: one_sums[head_rows(h)], 2.0)]
    for i, buffer in enumerate((h2, h3, h4)):
        landed(buffer, pl.multiple_of((1 - core) * BLOCK, BLOCK), BLOCK, recv_near.at[i])
    loads[4].wait()
    landed(deep, 0, 192 + 3 * BLOCK, send_sem.at[0])
    for i, (here, rows) in enumerate(zip(there, (192, 64, 64, 32, 64, 32))):
        pl.when(here)(lambda i=i, rows=rows: landed(deep, 0, rows, send_sem.at[i + 1]))

    vd[1] = values_of(1 - core)
    levels = [coarse(4, group, devices // 8), coarse(3, pair, devices // 4), coarse(2, chip, devices // 2)]
    run([unit for units, _ in levels for unit in units])
    terms += [gathered() for _, gathered in levels]

    before = peak[...]
    after = functools.reduce(jnp.maximum, [term[0] for term in terms], before)
    factors = [jnp.exp2(before - after)] + [weight * jnp.exp2(top - after) for top, _, _, weight in terms]
    lower = den[...] * factors[0]
    for factor, term in zip(factors[1:], terms):
        lower = lower + factor * term[1]
    inverse = 1.0 / lower
    factors = [factor * inverse for factor in factors]
    attended = []
    for h in range(HEADS):
        upper = acc[head_rows(h), :] * factors[0][h : h + 1]
        for factor, term in zip(factors[1:], terms):
            upper = upper + term[2](h) * factor[h : h + 1]
        attended.append(upper.astype(BF16))
    out_ref[...] = jnp.concatenate(attended, 0)


def project_out(attended, wo, out_hbm, out, sems):
    eye = averager(BLOCK, BLOCK, 0)
    copies = []
    for i in range(2):
        rows = pl.ds(i * BLOCK, BLOCK)
        turned = nt(eye, attended[:, i * BLOCK : (i + 1) * BLOCK]).astype(BF16)
        out[rows, :] = nn(turned, wo[...]).astype(BF16)
        copies.append(pltpu.make_async_copy(out.at[rows], out_hbm.at[rows], sems.at[i]))
        copies[-1].start()
    for copy in copies:
        copy.wait()


def solution(mesh):
    devices = mesh.shape["ctx"] * mesh.shape["node"]

    def local(tokens, w_query, w_key, w_value, w_out):
        square = pltpu.VMEM((WIDTH, WIDTH), BF16)
        tall = pltpu.VMEM((ROWS, WIDTH), BF16)
        attended, out_weights = pl.pallas_call(
            functools.partial(kernel, devices),
            out_shape=(jax.ShapeDtypeStruct((WIDTH, ROWS), BF16), jax.ShapeDtypeStruct((WIDTH, WIDTH), BF16)),
            in_specs=[pl.BlockSpec(memory_space=pltpu.HBM)] * 5,
            out_specs=(pl.BlockSpec(memory_space=pltpu.VMEM),) * 2,
            scratch_shapes=[
                tall,
                square,
                square,
                square,
                square,
                pltpu.VMEM((COARSE, WIDTH), BF16),
                tall,
                tall,
                pltpu.VMEM((3 * ROWS, WIDTH), BF16),
                tall,
                pltpu.VMEM((COARSE, WIDTH), BF16),
                tall,
                pltpu.VMEM((WIDTH, ROWS), BF16),
                pltpu.VMEM((2, ROWS, WIDTH), BF16),
                pltpu.VMEM((2, WIDTH, ROWS), BF16),
                square,
                tall,
                pltpu.VMEM((BLOCK, WIDTH), BF16),
                pltpu.VMEM((2, WIDTH, 3 * BLOCK), BF16),
                pltpu.VMEM((WIDTH, ROWS), F32),
                pltpu.VMEM((HEADS, ROWS), F32),
                pltpu.VMEM((HEADS, ROWS), F32),
                pltpu.VMEM((COARSE, ROWS), BF16),
                pltpu.VMEM((ROWS, ROWS), BF16),
                pltpu.VMEM((64, BLOCK), BF16),
                pltpu.VMEM((64, 192), BF16),
                pltpu.VMEM((BLOCK, ROWS), BF16),
                pltpu.VMEM((ROWS, ROWS), BF16),
                pltpu.VMEM((ROWS, ROWS), BF16),
                pltpu.VMEM((BLOCK, ROWS), BF16),
                pltpu.SemaphoreType.DMA((5,)),
                pltpu.SemaphoreType.DMA((7,)),
                pltpu.SemaphoreType.DMA((2,)),
                pltpu.SemaphoreType.DMA((6,)),
                pltpu.SemaphoreType.DMA((3,)),
            ],
            compiler_params=pltpu.CompilerParams(
                collective_id=0, has_side_effects=True, vmem_limit_bytes=40 * 2**20
            ),
            name="hierarchical_attention",
        )(*[pltpu.with_memory_space_constraint(a, pltpu.HBM) for a in (tokens, w_query, w_key, w_value, w_out)])
        return pl.pallas_call(
            project_out,
            out_shape=jax.ShapeDtypeStruct((ROWS, WIDTH), BF16),
            in_specs=[pl.BlockSpec(memory_space=pltpu.VMEM)] * 2,
            out_specs=pl.BlockSpec(memory_space=pltpu.HBM),
            scratch_shapes=[tall, pltpu.SemaphoreType.DMA((2,))],
            name="output_projection",
        )(attended, out_weights)

    placed = (P(("ctx", "node"), None), P(), P(), P(), P())
    return jax.shard_map(
        local, mesh=mesh, in_specs=placed, out_specs=P(("ctx", "node"), None), check_vma=False
    )
```

```python
import functools
import math

import jax
import jax.numpy as jnp
from jax import lax
from jax.experimental import pallas as pl
from jax.experimental.pallas import tpu as pltpu
from jax.sharding import PartitionSpec as P

HEADS = 8
HEAD = 64
WIDTH = HEADS * HEAD
BLOCK = 128
ROWS = 256
NODES = 8
FAR = 1e30
SCALE = math.log2(math.e) / math.sqrt(HEAD)
BF16 = jnp.bfloat16
F32 = jnp.float32
START = {1: 0, 2: 128, 3: 192, 4: 224}
COARSE = 240


def nn(a, b):
    return lax.dot_general(a, b, (((1,), (0,)), ((), ())), preferred_element_type=F32)


def nt(a, b):
    return lax.dot_general(a, b, (((1,), (1,)), ((), ())), preferred_element_type=F32)


def iota(shape, axis):
    return lax.broadcasted_iota(jnp.int32, shape, axis)


def averager(rows, columns, level):
    hit = iota((rows, columns), 0) == iota((rows, columns), 1) >> level
    return jnp.where(hit, 0.5**level, 0.0).astype(BF16)


def spreader(rows, queries, level):
    hit = (iota((rows, ROWS), 0) & (queries - 1)) == iota((rows, ROWS), 1) >> level
    return jnp.where(hit, 1.0, 0.0).astype(BF16)


def split(values):
    high = values.astype(BF16)
    rest = values - high.astype(F32)
    middle = rest.astype(BF16)
    return [high, middle, (rest - middle.astype(F32)).astype(BF16)]


def spread_all(sums, tops, totals, spread):
    rows = sums.shape[0]
    out = nn(jnp.concatenate([sums] + split(jnp.concatenate([tops, totals], 0)), 0), spread)
    stats = out[rows : rows + 16] + out[rows + 16 : rows + 32] + out[rows + 32 :]
    return out[:rows], stats[:8], stats[8:]


def lane_head(shape, width):
    return iota(shape, 1) >> (width.bit_length() - 1)


def kernel(
    devices, x_hbm, wq_hbm, wk_hbm, wv_hbm, wo_hbm, out_ref,
    x, wq, wk, wv, wo, wvt, t, hnear, hfar, deep, q0, ql, k0, v0, kh, vh, u2, u3, u4, vd, acc, peak, den,
    average, eye, halve, fold, spread1, spread2, spread3, spread4,
    load_sem, send_sem, recv01, recv_far, recv_near,
):
    me = lax.axis_index("ctx") * NODES + lax.axis_index("node")
    core = lax.rem(me, 2)
    chip = lax.div(me, 2)
    pair = lax.div(me, 4)
    group = lax.div(me, 8)

    def place(index):
        return {"ctx": lax.div(index, NODES), "node": lax.rem(index, NODES)}

    def exists(index):
        return jnp.logical_and(index >= 0, index < devices)

    loads = []
    for i, (source, kept) in enumerate(((x_hbm, x), (wq_hbm, wq), (wk_hbm, wk), (wv_hbm, wv), (wo_hbm, wo))):
        loads.append(pltpu.make_async_copy(source, kept, load_sem.at[i]))
    loads[0].start()

    twin = me + 1 - 2 * core
    beyond = me - 1 + 2 * core
    odd = lax.rem(chip, 2)
    second = lax.rem(pair, 2)
    two = me + 3 - 6 * core
    three_ahead = [(me + 4 - 8 * odd, odd, 1), (me + 6 - 12 * odd, odd, 0)]
    three_behind = [(me - 4 + 8 * odd, 1 - odd, 0)]
    ahead = 8 * (group + 1 - 2 * second) + core
    behind = 8 * (group - 1 + 2 * second) + core
    four_ahead = [(ahead + 4 * second + 2 * j, second, 1) for j in range(2)]
    four_ahead += [(ahead + 4 * (1 - second) + 2 * j, second, 0) for j in range(2)]
    four_behind = [(behind + 4 * second + 2 * j, 1 - second, 0) for j in range(2)]
    there = [exists(beyond), exists(two), exists(three_ahead[0][0]), exists(three_behind[0][0])]
    there += [exists(ahead), exists(behind)]
    parties = [[beyond], [two]] + [[p[0] for p in ps] for ps in (three_ahead, three_behind, four_ahead, four_behind)]

    barrier = pltpu.get_barrier_semaphore()

    def signal(target):
        pl.semaphore_signal(barrier, inc=1, device_id=place(target), device_id_type=pl.DeviceIdType.MESH)

    expected = 1
    for here, targets in reversed(list(zip(there, parties))):
        expected = expected + jnp.where(here, len(targets), 0)
        pl.when(here)(lambda targets=targets: [signal(target) for target in targets] and None)
    signal(twin)
    for load in loads[1:]:
        load.start()

    h2, h3, h4 = (deep.at[pl.ds(i * ROWS, ROWS)] for i in range(3))
    for l in range(1, 5):
        average[START[l] : START[l] + (ROWS >> l), :] = averager(ROWS >> l, ROWS, l)
    loads[0].wait()
    t[...] = nn(average[...], x[...]).astype(BF16)

    eye[...] = averager(ROWS, ROWS, 0)
    halve[...] = averager(64, BLOCK, 1)
    fold[:32, :] = jnp.concatenate([averager(32, BLOCK, 2), jnp.zeros((32, 64), BF16)], 1)
    fold[32:, :] = jnp.concatenate([jnp.zeros((32, BLOCK), BF16), averager(32, 64, 1)], 1)
    spreads = {1: spread1, 2: spread2, 3: spread3, 4: spread4}
    for l in range(1, 5):
        spreads[l][...] = spreader(spreads[l].shape[0], ROWS >> l, l)
    for load in loads[1:4]:
        load.wait()
    q0[...] = (nn(x[...], wq[...]) * SCALE).astype(BF16)
    k0[...] = nn(x[...], wk[...]).astype(BF16)
    for i in range(2):
        wvt[i * ROWS : (i + 1) * ROWS, :] = nt(eye[...], wv[:, i * ROWS : (i + 1) * ROWS]).astype(BF16)
    ql[...] = nn(average[...], q0[...]).astype(BF16)
    v0[...] = nt(wvt[...], x[...]).astype(BF16)


    pl.semaphore_wait(barrier, expected)

    def send(source, target, landing, recv, sent):
        pltpu.make_async_remote_copy(
            src_ref=source,
            dst_ref=landing,
            send_sem=send_sem.at[sent],
            recv_sem=recv,
            device_id=place(target),
            device_id_type=pl.DeviceIdType.MESH,
        ).start()

    def mine(direction):
        return core * BLOCK + direction * 64

    def send_edge(target, half, landing, recv, sent):
        rows = pl.multiple_of(half * BLOCK, BLOCK)
        send(x_hbm.at[pl.ds(rows, BLOCK)], target, landing.at[pl.ds(0, BLOCK)], recv, sent)

    pl.when(there[0])(lambda: send_edge(beyond, core, hfar, recv01.at[1], 1))
    send_edge(twin, 1 - core, hnear, recv01.at[0], 0)

    def send_one_means(target, half, landing, recv, sent):
        means = pl.multiple_of((1 - half) * 64, 64)
        send(t.at[pl.ds(means, 64)], target, landing.at[pl.ds(BLOCK, 64)], recv, sent)

    @pl.when(there[0])
    def _():
        send_one_means(beyond, core, hfar, recv01.at[1], 1)

    @pl.when(there[1])
    def _():
        landing = h2.at[pl.ds(pl.multiple_of(BLOCK - core * 64, 64), 64)]
        send(t.at[pl.ds(START[2], 64)], two, landing, recv_far.at[0], 2)

    def send_three(targets, sent):
        for target, d, short in targets:
            landing = h3.at[pl.ds(pl.multiple_of(mine(d) + odd * 32, 32), 32)]
            send(t.at[pl.ds(START[3], 32)], target, landing, recv_far.at[2 + short], sent)

    def send_four(targets, sent):
        for target, d, short in targets:
            landing = h4.at[pl.ds(pl.multiple_of(mine(d) + lax.rem(chip, 4) * 16, 16), 16)]
            send(t.at[pl.ds(START[4], 16)], target, landing, recv_far.at[4 + short], sent)

    pl.when(there[2])(lambda: send_three(three_ahead, 3))
    pl.when(there[3])(lambda: send_three(three_behind, 4))
    pl.when(there[4])(lambda: send_four(four_ahead, 5))
    pl.when(there[5])(lambda: send_four(four_behind, 6))
    send_one_means(twin, 1 - core, hnear, recv01.at[0], 0)

    def landed(buffer, start, rows, sem):
        region = buffer.at[pl.ds(start, rows)]
        pltpu.make_async_copy(region, region, sem).wait()

    def landed_or_zero(here, buffer, start, rows, sem):
        pl.when(here)(lambda: landed(buffer, start, rows, sem))

        @pl.when(jnp.logical_not(here))
        def _():
            buffer[pl.ds(start, rows), :] = jnp.zeros((rows, WIDTH), BF16)

    def half_of(buffer, whose):
        return buffer.at[pl.ds(pl.multiple_of(whose * BLOCK, BLOCK), BLOCK)]

    def forward(buffer, which):
        region = half_of(buffer, core)
        send(region, twin, region, recv_near.at[which], 0)

    def finer(source, d, target, inside):
        rows = source[pl.ds(pl.multiple_of(mine(d), 64), 64), :]
        means = nn(halve[:32, :64], rows).astype(BF16)
        target[pl.ds(pl.multiple_of(mine(d) + inside * 32, 32), 32), :] = means

    ones = jnp.ones((16, ROWS), BF16)
    half = lane_head((1, BLOCK), HEAD)
    pair_masks = [jnp.where(half == h, 1.0, 0.0).astype(BF16) for h in range(2)]

    def lanes_of(j):
        return slice(j * BLOCK, (j + 1) * BLOCK)

    def head_rows(h):
        return slice(h * HEAD, (h + 1) * HEAD)

    def pair_queries(block):
        return jnp.concatenate([block * pair_masks[0], block * pair_masks[1]], 0)

    def with_ones(v):
        return jnp.concatenate([v, ones[:, : v.shape[1]]], 0)

    def merge(lanes, top, total, heads):
        before = peak[:, lanes]
        after = jnp.maximum(before, top)
        old = jnp.exp2(before - after)
        new = jnp.exp2(top - after)
        den[:, lanes] = den[:, lanes] * old + new * total
        peak[:, lanes] = after
        for h in range(HEADS):
            rows = head_rows(h)
            acc[rows, lanes] = acc[rows, lanes] * old[h : h + 1] + heads(h) * new[h : h + 1]

    def run(units):
        waiting, active = list(units), []
        while waiting or active:
            if waiting:
                active.append(waiting.pop(0))
            active = [unit for unit in active if next(unit, None) is not None]

    def attend(keys, queries, values, done):
        s = nt(keys(), queries())
        yield True
        m = jnp.max(s, axis=0, keepdims=True)
        p = jnp.exp2(s - m).astype(BF16)
        yield True
        done(m, nn(with_ones(values()), p))

    def base_own(h):
        pairs = lanes_of(h // 2)

        def done(m, o):
            peak[h : h + 1, :] = m
            den[h : h + 1, :] = o[HEAD : HEAD + 1]
            acc[head_rows(h), :] = o[:HEAD]

        return attend(
            lambda: k0[:, pairs], lambda: q0[:, pairs] * pair_masks[h % 2], lambda: v0[head_rows(h), :], done
        )

    def project_side(buffer, slot):
        buffer[192:, :] = nn(halve[...], buffer[:BLOCK, :]).astype(BF16)
        kh[slot] = nn(buffer[...], wk[...]).astype(BF16)
        vh[slot] = nt(wvt[...], buffer[...]).astype(BF16)

    def side(slot, block):
        queries = pl.ds(pl.multiple_of(block * BLOCK, BLOCK), BLOCK)
        found = []
        units = [
            attend(
                lambda j=j: kh[slot, :BLOCK, lanes_of(j)],
                lambda j=j: pair_queries(q0[queries, lanes_of(j)]),
                lambda j=j: vh[slot, lanes_of(j), :BLOCK],
                lambda m, o: found.append((m, o)),
            )
            for j in range(HEADS // 2)
        ]
        return units, queries, found

    def level_one(j, missing, found):
        queries = pair_queries(ql[:BLOCK, lanes_of(j)])
        s = nt(kh[:, BLOCK:, lanes_of(j)].reshape(ROWS, BLOCK), queries)
        yield True
        near, far = s[:BLOCK], s[BLOCK:]
        m = jnp.maximum(jnp.max(near, axis=0, keepdims=True), jnp.max(far, axis=0, keepdims=True) - missing)
        p = jnp.concatenate([jnp.exp2(near - m).astype(BF16), jnp.exp2(far - (m + missing)).astype(BF16)], 0)
        yield True
        values = jnp.concatenate([vh[0, lanes_of(j), BLOCK:], vh[1, lanes_of(j), BLOCK:]], 1)
        found.append((m, nn(with_ones(values), p)))

    def by_head(part):
        tops = [m[:, lanes_of(h)] for m, _ in part for h in range(2)]
        totals = [o[BLOCK : BLOCK + 1, lanes_of(h)] for _, o in part for h in range(2)]
        sums = [o[head_rows(h), lanes_of(h)] for _, o in part for h in range(2)]
        return jnp.concatenate(tops, 0), jnp.concatenate(totals, 0), sums

    def off(missing):
        return jnp.where(missing, FAR, 0.0).astype(F32)

    everywhere = slice(0, ROWS)

    seen = {2: u2, 3: u3, 4: u4}

    def shape_of(level):
        queries = ROWS >> level
        together = min(HEADS, ROWS // queries)
        return queries, together, together * queries

    def look(level):
        queries = ROWS >> level
        for u in range(2):
            part = slice(u * ROWS, (u + 1) * ROWS)
            block = ql[START[level] : START[level] + queries, part]
            masked = [block * jnp.where(lane_head((1, ROWS), HEAD) == h, 1.0, 0.0).astype(BF16) for h in range(4)]
            rows = slice(u * 4 * queries, (u + 1) * 4 * queries)
            seen[level][rows, :] = nt(jnp.concatenate(masked, 0), wk[:, part]).astype(BF16)
            yield True

    def rows_of(level, whose):
        return half_of((h2, h3, h4)[level - 2], whose)[...]

    def values_of(whose):
        return nt(wvt[...], jnp.concatenate([rows_of(l, whose) for l in range(2, 5)], 0)).astype(BF16)

    scores = {}

    def coarse(level, index, count):
        queries, together, columns = shape_of(level)
        features = together * HEAD
        lanes = lanes_of(level - 2)
        off_left, off_right = off(index == 0), off(index == count - 1)
        column_head = lane_head((1, columns), queries)
        found = []

        def unit(u):
            part = slice(u * features, (u + 1) * features)
            s = [scores[level, u], nt(rows_of(level, 1 - core), seen[level][u * columns : (u + 1) * columns, :])]
            yield True
            left = [half[:64] for half in s]
            right = [half[64:] for half in s]
            m = jnp.maximum(
                jnp.max(jnp.maximum(*left), axis=0, keepdims=True) - off_left,
                jnp.max(jnp.maximum(*right), axis=0, keepdims=True) - off_right,
            )
            p = []
            for half in range(2):
                p.append(jnp.exp2(left[half] - (m + off_left)).astype(BF16))
                p.append(jnp.exp2(right[half] - (m + off_right)).astype(BF16))
            yield True
            values = jnp.concatenate([vd[0, part, lanes], vd[1, part, lanes]], 1)
            o = nn(with_ones(values), jnp.concatenate(p, 0))
            yield True
            own = [jnp.where(column_head == h, o[head_rows(h)], 0.0) for h in range(together)]
            row_head = iota((HEADS, columns), 0) == column_head + u * together
            found.append(
                spread_all(
                    jnp.concatenate(own, 0).astype(BF16),
                    jnp.where(row_head, m, 0.0),
                    jnp.where(row_head, o[features : features + 1], 0.0),
                    spreads[level][...],
                )
            )

        def gathered():
            def heads(h):
                u, inside = divmod(h, together)
                return found[u][0][head_rows(inside)]

            top = functools.reduce(jnp.add, [f[1] for f in found])
            total = functools.reduce(jnp.add, [f[2] for f in found])
            return top, total, heads, 2.0**level

        return [unit(u) for u in range(HEADS // together)], gathered

    landed(hnear, 0, 192, recv01.at[0])
    project_side(hnear, 0)
    units, near_lanes, base_near = side(0, 1 - core)
    mixed = [base_own(h) for h in range(HEADS)] + units
    for place_in_line, level in ((9, 4), (6, 3), (3, 2)):
        mixed.insert(place_in_line, look(level))
    run(mixed)
    top, total, near_sums = by_head(base_near)
    merge(near_lanes, top, total, lambda h: near_sums[h])

    landed_or_zero(there[0], hfar, 0, 192, recv01.at[1])
    h2[pl.ds(pl.multiple_of(mine(core), 64), 64), :] = nn(fold[...], hfar[:192, :]).astype(BF16)
    project_side(hfar, 1)
    missing = off(jnp.logical_not(there[0]))
    units, far_lanes, base_far = side(1, core)
    run(units)
    top, total, far_sums = by_head(base_far)
    merge(far_lanes, top - missing, total, lambda h: far_sums[h])

    landed_or_zero(there[1], h2, pl.multiple_of(mine(1 - core), 64), 64, recv_far.at[0])
    forward(h2, 0)
    finer(h2, odd, h3, 1 - odd)
    landed_or_zero(there[2], h3, pl.multiple_of(mine(1 - odd), 64), 64, recv_far.at[2])
    landed_or_zero(there[3], h3, pl.multiple_of(mine(odd) + odd * 32, 32), 32, recv_far.at[3])
    forward(h3, 1)
    finer(h3, second, h4, 1 - second)
    landed_or_zero(there[4], h4, pl.multiple_of(mine(1 - second), 64), 64, recv_far.at[4])
    landed_or_zero(there[5], h4, pl.multiple_of(mine(second) + second * 32, 32), 32, recv_far.at[5])
    forward(h4, 2)

    one = []
    run([level_one(j, missing, one) for j in range(HEADS // 2)])
    vd[0] = values_of(core)
    for l in range(4, 1, -1):
        _, together, columns = shape_of(l)
        for u in range(HEADS // together):
            scores[l, u] = nt(rows_of(l, core), seen[l][u * columns : (u + 1) * columns, :])
    top, total, sums = by_head(one)
    one_sums, top, total = spread_all(jnp.concatenate(sums, 0).astype(BF16), top, total, spread1[...])
    terms = [(top, total, lambda h: one_sums[head_rows(h)], 2.0)]
    for i, buffer in enumerate((h2, h3, h4)):
        landed(buffer, pl.multiple_of((1 - core) * BLOCK, BLOCK), BLOCK, recv_near.at[i])
    loads[4].wait()
    landed(deep, 0, 192 + 3 * BLOCK, send_sem.at[0])
    for i, (here, rows) in enumerate(zip(there, (192, 64, 64, 32, 64, 32))):
        pl.when(here)(lambda i=i, rows=rows: landed(deep, 0, rows, send_sem.at[i + 1]))

    vd[1] = values_of(1 - core)
    levels = [coarse(4, group, devices // 8), coarse(3, pair, devices // 4), coarse(2, chip, devices // 2)]
    run([unit for units, _ in levels for unit in units])
    terms += [gathered() for _, gathered in levels]

    before = peak[...]
    after = functools.reduce(jnp.maximum, [term[0] for term in terms], before)
    factors = [jnp.exp2(before - after)] + [weight * jnp.exp2(top - after) for top, _, _, weight in terms]
    lower = den[...] * factors[0]
    for factor, term in zip(factors[1:], terms):
        lower = lower + factor * term[1]
    inverse = 1.0 / lower
    factors = [factor * inverse for factor in factors]
    attended = []
    for h in range(HEADS):
        upper = acc[head_rows(h), :] * factors[0][h : h + 1]
        for factor, term in zip(factors[1:], terms):
            upper = upper + term[2](h) * factor[h : h + 1]
        attended.append(upper.astype(BF16))
    turned = nt(eye[...], jnp.concatenate(attended, 0)).astype(BF16)
    out_ref[...] = nn(turned, wo[...]).astype(BF16)


def solution(mesh):
    devices = mesh.shape["ctx"] * mesh.shape["node"]

    def local(tokens, w_query, w_key, w_value, w_out):
        square = pltpu.VMEM((WIDTH, WIDTH), BF16)
        tall = pltpu.VMEM((ROWS, WIDTH), BF16)
        return pl.pallas_call(
            functools.partial(kernel, devices),
            out_shape=jax.ShapeDtypeStruct((ROWS, WIDTH), BF16),
            in_specs=[pl.BlockSpec(memory_space=pltpu.HBM)] * 5,
            out_specs=pl.BlockSpec(memory_space=pltpu.VMEM),
            scratch_shapes=[
                tall,
                square,
                square,
                square,
                square,
                square,
                pltpu.VMEM((COARSE, WIDTH), BF16),
                tall,
                tall,
                pltpu.VMEM((3 * ROWS, WIDTH), BF16),
                tall,
                pltpu.VMEM((COARSE, WIDTH), BF16),
                tall,
                pltpu.VMEM((WIDTH, ROWS), BF16),
                pltpu.VMEM((2, ROWS, WIDTH), BF16),
                pltpu.VMEM((2, WIDTH, ROWS), BF16),
                square,
                tall,
                pltpu.VMEM((BLOCK, WIDTH), BF16),
                pltpu.VMEM((2, WIDTH, 3 * BLOCK), BF16),
                pltpu.VMEM((WIDTH, ROWS), F32),
                pltpu.VMEM((HEADS, ROWS), F32),
                pltpu.VMEM((HEADS, ROWS), F32),
                pltpu.VMEM((COARSE, ROWS), BF16),
                pltpu.VMEM((ROWS, ROWS), BF16),
                pltpu.VMEM((64, BLOCK), BF16),
                pltpu.VMEM((64, 192), BF16),
                pltpu.VMEM((BLOCK, ROWS), BF16),
                pltpu.VMEM((ROWS, ROWS), BF16),
                pltpu.VMEM((ROWS, ROWS), BF16),
                pltpu.VMEM((BLOCK, ROWS), BF16),
                pltpu.SemaphoreType.DMA((5,)),
                pltpu.SemaphoreType.DMA((7,)),
                pltpu.SemaphoreType.DMA((2,)),
                pltpu.SemaphoreType.DMA((6,)),
                pltpu.SemaphoreType.DMA((3,)),
            ],
            compiler_params=pltpu.CompilerParams(
                collective_id=0, has_side_effects=True, vmem_limit_bytes=40 * 2**20
            ),
            name="hierarchical_attention",
        )(*[pltpu.with_memory_space_constraint(a, pltpu.HBM) for a in (tokens, w_query, w_key, w_value, w_out)])

    placed = (P(("ctx", "node"), None), P(), P(), P(), P())
    return jax.shard_map(
        local, mesh=mesh, in_specs=placed, out_specs=P(("ctx", "node"), None), check_vma=False
    )
```

```python
import functools
import math

import jax
import jax.numpy as jnp
from jax import lax
from jax.experimental import pallas as pl
from jax.experimental.pallas import tpu as pltpu
from jax.sharding import PartitionSpec as P

HEADS = 8
HEAD = 64
WIDTH = HEADS * HEAD
BLOCK = 128
ROWS = 256
NODES = 8
FAR = 1e30
SCALE = math.log2(math.e) / math.sqrt(HEAD)
BF16 = jnp.bfloat16
F32 = jnp.float32
START = {1: 0, 2: 128, 3: 192, 4: 224}
COARSE = 240


def nn(a, b):
    return lax.dot_general(a, b, (((1,), (0,)), ((), ())), preferred_element_type=F32)


def nt(a, b):
    return lax.dot_general(a, b, (((1,), (1,)), ((), ())), preferred_element_type=F32)


def iota(shape, axis):
    return lax.broadcasted_iota(jnp.int32, shape, axis)


def averager(rows, columns, level):
    hit = iota((rows, columns), 0) == iota((rows, columns), 1) >> level
    return jnp.where(hit, 0.5**level, 0.0).astype(BF16)


def spreader(rows, queries, level):
    hit = (iota((rows, ROWS), 0) & (queries - 1)) == iota((rows, ROWS), 1) >> level
    return jnp.where(hit, 1.0, 0.0).astype(BF16)


def split(values):
    high = values.astype(BF16)
    rest = values - high.astype(F32)
    middle = rest.astype(BF16)
    return [high, middle, (rest - middle.astype(F32)).astype(BF16)]


def spread_all(sums, tops, totals, spread):
    rows = sums.shape[0]
    out = nn(jnp.concatenate([sums] + split(jnp.concatenate([tops, totals], 0)), 0), spread)
    stats = out[rows : rows + 16] + out[rows + 16 : rows + 32] + out[rows + 32 :]
    return out[:rows], stats[:8], stats[8:]


def lane_head(shape, width):
    return iota(shape, 1) >> (width.bit_length() - 1)


def kernel(
    devices, x_hbm, wq_hbm, wk_hbm, wv_hbm, wo_hbm, out_ref,
    x, wq, wk, wv, wo, wvt, t, hnear, hfar, deep, q0, ql, k0, v0, kh, vh, u2, u3, u4, vd, acc, peak, den,
    average, eye, halve, fold, spread1, spread2, spread3, spread4,
    load_sem, send_sem, recv01, recv_far, recv_near,
):
    me = lax.axis_index("ctx") * NODES + lax.axis_index("node")
    core = lax.rem(me, 2)
    chip = lax.div(me, 2)
    pair = lax.div(me, 4)
    group = lax.div(me, 8)

    def place(index):
        return {"ctx": lax.div(index, NODES), "node": lax.rem(index, NODES)}

    def exists(index):
        return jnp.logical_and(index >= 0, index < devices)

    loads = []
    for i, (source, kept) in enumerate(((x_hbm, x), (wq_hbm, wq), (wk_hbm, wk), (wv_hbm, wv), (wo_hbm, wo))):
        loads.append(pltpu.make_async_copy(source, kept, load_sem.at[i]))
    loads[0].start()

    twin = me + 1 - 2 * core
    beyond = me - 1 + 2 * core
    odd = lax.rem(chip, 2)
    second = lax.rem(pair, 2)
    two = me + 3 - 6 * core
    three_ahead = [(me + 4 - 8 * odd, odd, 1), (me + 6 - 12 * odd, odd, 0)]
    three_behind = [(me - 4 + 8 * odd, 1 - odd, 0)]
    ahead = 8 * (group + 1 - 2 * second) + core
    behind = 8 * (group - 1 + 2 * second) + core
    four_ahead = [(ahead + 4 * second + 2 * j, second, 1) for j in range(2)]
    four_ahead += [(ahead + 4 * (1 - second) + 2 * j, second, 0) for j in range(2)]
    four_behind = [(behind + 4 * second + 2 * j, 1 - second, 0) for j in range(2)]
    there = [exists(beyond), exists(two), exists(three_ahead[0][0]), exists(three_behind[0][0])]
    there += [exists(ahead), exists(behind)]
    parties = [[beyond], [two]] + [[p[0] for p in ps] for ps in (three_ahead, three_behind, four_ahead, four_behind)]

    barrier = pltpu.get_barrier_semaphore()

    def signal(target):
        pl.semaphore_signal(barrier, inc=1, device_id=place(target), device_id_type=pl.DeviceIdType.MESH)

    expected = 1
    for here, targets in reversed(list(zip(there, parties))):
        expected = expected + jnp.where(here, len(targets), 0)
        pl.when(here)(lambda targets=targets: [signal(target) for target in targets] and None)
    signal(twin)
    for load in loads[1:]:
        load.start()

    h2, h3, h4 = (deep.at[pl.ds(i * ROWS, ROWS)] for i in range(3))
    for l in range(1, 5):
        average[START[l] : START[l] + (ROWS >> l), :] = averager(ROWS >> l, ROWS, l)
    loads[0].wait()
    t[...] = nn(average[...], x[...]).astype(BF16)

    eye[...] = averager(ROWS, ROWS, 0)
    halve[...] = averager(64, BLOCK, 1)
    fold[:32, :] = jnp.concatenate([averager(32, BLOCK, 2), jnp.zeros((32, 64), BF16)], 1)
    fold[32:, :] = jnp.concatenate([jnp.zeros((32, BLOCK), BF16), averager(32, 64, 1)], 1)
    spreads = {1: spread1, 2: spread2, 3: spread3, 4: spread4}
    for l in range(1, 5):
        spreads[l][...] = spreader(spreads[l].shape[0], ROWS >> l, l)
    for load in loads[1:4]:
        load.wait()
    q0[...] = (nn(x[...], wq[...]) * SCALE).astype(BF16)
    k0[...] = nn(x[...], wk[...]).astype(BF16)
    for i in range(2):
        wvt[i * ROWS : (i + 1) * ROWS, :] = nt(eye[...], wv[:, i * ROWS : (i + 1) * ROWS]).astype(BF16)
    ql[...] = nn(average[...], q0[...]).astype(BF16)
    v0[...] = nt(wvt[...], x[...]).astype(BF16)


    pl.semaphore_wait(barrier, expected)

    def send(source, target, landing, recv, sent, pieces=1):
        rows = source.shape[0] // pieces
        for i in range(pieces):
            piece = pl.ds(i * rows, rows)
            pltpu.make_async_remote_copy(
                src_ref=source.at[piece],
                dst_ref=landing.at[piece],
                send_sem=send_sem.at[sent],
                recv_sem=recv,
                device_id=place(target),
                device_id_type=pl.DeviceIdType.MESH,
            ).start()

    def mine(direction):
        return core * BLOCK + direction * 64

    def send_edge(target, half, landing, recv, sent):
        rows = pl.multiple_of(half * BLOCK, BLOCK)
        send(x_hbm.at[pl.ds(rows, BLOCK)], target, landing.at[pl.ds(0, BLOCK)], recv, sent, 4)

    pl.when(there[0])(lambda: send_edge(beyond, core, hfar, recv01.at[1], 1))
    send_edge(twin, 1 - core, hnear, recv01.at[0], 0)

    def send_one_means(target, half, landing, recv, sent):
        means = pl.multiple_of((1 - half) * 64, 64)
        send(t.at[pl.ds(means, 64)], target, landing.at[pl.ds(BLOCK, 64)], recv, sent, 2)

    @pl.when(there[0])
    def _():
        send_one_means(beyond, core, hfar, recv01.at[1], 1)

    @pl.when(there[1])
    def _():
        landing = h2.at[pl.ds(pl.multiple_of(BLOCK - core * 64, 64), 64)]
        send(t.at[pl.ds(START[2], 64)], two, landing, recv_far.at[0], 2, 2)

    def send_three(targets, sent):
        for target, d, short in targets:
            landing = h3.at[pl.ds(pl.multiple_of(mine(d) + odd * 32, 32), 32)]
            send(t.at[pl.ds(START[3], 32)], target, landing, recv_far.at[2 + short], sent)

    def send_four(targets, sent):
        for target, d, short in targets:
            landing = h4.at[pl.ds(pl.multiple_of(mine(d) + lax.rem(chip, 4) * 16, 16), 16)]
            send(t.at[pl.ds(START[4], 16)], target, landing, recv_far.at[4 + short], sent)

    pl.when(there[2])(lambda: send_three(three_ahead, 3))
    pl.when(there[3])(lambda: send_three(three_behind, 4))
    pl.when(there[4])(lambda: send_four(four_ahead, 5))
    pl.when(there[5])(lambda: send_four(four_behind, 6))
    send_one_means(twin, 1 - core, hnear, recv01.at[0], 0)

    def landed(buffer, start, rows, sem):
        region = buffer.at[pl.ds(start, rows)]
        pltpu.make_async_copy(region, region, sem).wait()

    def landed_or_zero(here, buffer, start, rows, sem):
        pl.when(here)(lambda: landed(buffer, start, rows, sem))

        @pl.when(jnp.logical_not(here))
        def _():
            buffer[pl.ds(start, rows), :] = jnp.zeros((rows, WIDTH), BF16)

    def half_of(buffer, whose):
        return buffer.at[pl.ds(pl.multiple_of(whose * BLOCK, BLOCK), BLOCK)]

    def forward(buffer, which):
        region = half_of(buffer, core)
        send(region, twin, region, recv_near.at[which], 0)

    def finer(source, d, target, inside):
        rows = source[pl.ds(pl.multiple_of(mine(d), 64), 64), :]
        means = nn(halve[:32, :64], rows).astype(BF16)
        target[pl.ds(pl.multiple_of(mine(d) + inside * 32, 32), 32), :] = means

    ones = jnp.ones((16, ROWS), BF16)
    half = lane_head((1, BLOCK), HEAD)
    pair_masks = [jnp.where(half == h, 1.0, 0.0).astype(BF16) for h in range(2)]

    def lanes_of(j):
        return slice(j * BLOCK, (j + 1) * BLOCK)

    def head_rows(h):
        return slice(h * HEAD, (h + 1) * HEAD)

    def pair_queries(block):
        return jnp.concatenate([block * pair_masks[0], block * pair_masks[1]], 0)

    def with_ones(v):
        return jnp.concatenate([v, ones[:, : v.shape[1]]], 0)

    def merge(lanes, top, total, heads):
        before = peak[:, lanes]
        after = jnp.maximum(before, top)
        old = jnp.exp2(before - after)
        new = jnp.exp2(top - after)
        den[:, lanes] = den[:, lanes] * old + new * total
        peak[:, lanes] = after
        for h in range(HEADS):
            rows = head_rows(h)
            acc[rows, lanes] = acc[rows, lanes] * old[h : h + 1] + heads(h) * new[h : h + 1]

    def run(units):
        waiting, active = list(units), []
        while waiting or active:
            if waiting:
                active.append(waiting.pop(0))
            active = [unit for unit in active if next(unit, None) is not None]

    def attend(keys, queries, values, done):
        s = nt(keys(), queries())
        yield True
        m = jnp.max(s, axis=0, keepdims=True)
        p = jnp.exp2(s - m).astype(BF16)
        yield True
        done(m, nn(with_ones(values()), p))

    def base_own(h):
        pairs = lanes_of(h // 2)

        def done(m, o):
            peak[h : h + 1, :] = m
            den[h : h + 1, :] = o[HEAD : HEAD + 1]
            acc[head_rows(h), :] = o[:HEAD]

        return attend(
            lambda: k0[:, pairs], lambda: q0[:, pairs] * pair_masks[h % 2], lambda: v0[head_rows(h), :], done
        )

    def project_side(buffer, slot):
        buffer[192:, :] = nn(halve[...], buffer[:BLOCK, :]).astype(BF16)
        kh[slot] = nn(buffer[...], wk[...]).astype(BF16)
        vh[slot] = nt(wvt[...], buffer[...]).astype(BF16)

    def side(slot, block):
        queries = pl.ds(pl.multiple_of(block * BLOCK, BLOCK), BLOCK)
        found = []
        units = [
            attend(
                lambda j=j: kh[slot, :BLOCK, lanes_of(j)],
                lambda j=j: pair_queries(q0[queries, lanes_of(j)]),
                lambda j=j: vh[slot, lanes_of(j), :BLOCK],
                lambda m, o: found.append((m, o)),
            )
            for j in range(HEADS // 2)
        ]
        return units, queries, found

    def level_one(j, missing, found):
        queries = pair_queries(ql[:BLOCK, lanes_of(j)])
        s = nt(kh[:, BLOCK:, lanes_of(j)].reshape(ROWS, BLOCK), queries)
        yield True
        near, far = s[:BLOCK], s[BLOCK:]
        m = jnp.maximum(jnp.max(near, axis=0, keepdims=True), jnp.max(far, axis=0, keepdims=True) - missing)
        p = jnp.concatenate([jnp.exp2(near - m).astype(BF16), jnp.exp2(far - (m + missing)).astype(BF16)], 0)
        yield True
        values = jnp.concatenate([vh[0, lanes_of(j), BLOCK:], vh[1, lanes_of(j), BLOCK:]], 1)
        found.append((m, nn(with_ones(values), p)))

    def by_head(part):
        tops = [m[:, lanes_of(h)] for m, _ in part for h in range(2)]
        totals = [o[BLOCK : BLOCK + 1, lanes_of(h)] for _, o in part for h in range(2)]
        sums = [o[head_rows(h), lanes_of(h)] for _, o in part for h in range(2)]
        return jnp.concatenate(tops, 0), jnp.concatenate(totals, 0), sums

    def off(missing):
        return jnp.where(missing, FAR, 0.0).astype(F32)

    everywhere = slice(0, ROWS)

    seen = {2: u2, 3: u3, 4: u4}

    def shape_of(level):
        queries = ROWS >> level
        together = min(HEADS, ROWS // queries)
        return queries, together, together * queries

    def look(level):
        queries = ROWS >> level
        for u in range(2):
            part = slice(u * ROWS, (u + 1) * ROWS)
            block = ql[START[level] : START[level] + queries, part]
            masked = [block * jnp.where(lane_head((1, ROWS), HEAD) == h, 1.0, 0.0).astype(BF16) for h in range(4)]
            rows = slice(u * 4 * queries, (u + 1) * 4 * queries)
            seen[level][rows, :] = nt(jnp.concatenate(masked, 0), wk[:, part]).astype(BF16)
            yield True

    def rows_of(level, whose):
        return half_of((h2, h3, h4)[level - 2], whose)[...]

    def values_of(whose):
        return nt(wvt[...], jnp.concatenate([rows_of(l, whose) for l in range(2, 5)], 0)).astype(BF16)

    scores = {}

    def coarse(level, index, count):
        queries, together, columns = shape_of(level)
        features = together * HEAD
        lanes = lanes_of(level - 2)
        off_left, off_right = off(index == 0), off(index == count - 1)
        column_head = lane_head((1, columns), queries)
        found = []

        def unit(u):
            part = slice(u * features, (u + 1) * features)
            s = [scores[level, u], nt(rows_of(level, 1 - core), seen[level][u * columns : (u + 1) * columns, :])]
            yield True
            left = [half[:64] for half in s]
            right = [half[64:] for half in s]
            m = jnp.maximum(
                jnp.max(jnp.maximum(*left), axis=0, keepdims=True) - off_left,
                jnp.max(jnp.maximum(*right), axis=0, keepdims=True) - off_right,
            )
            p = []
            for half in range(2):
                p.append(jnp.exp2(left[half] - (m + off_left)).astype(BF16))
                p.append(jnp.exp2(right[half] - (m + off_right)).astype(BF16))
            yield True
            values = jnp.concatenate([vd[0, part, lanes], vd[1, part, lanes]], 1)
            o = nn(with_ones(values), jnp.concatenate(p, 0))
            yield True
            own = [jnp.where(column_head == h, o[head_rows(h)], 0.0) for h in range(together)]
            row_head = iota((HEADS, columns), 0) == column_head + u * together
            found.append(
                spread_all(
                    jnp.concatenate(own, 0).astype(BF16),
                    jnp.where(row_head, m, 0.0),
                    jnp.where(row_head, o[features : features + 1], 0.0),
                    spreads[level][...],
                )
            )

        def gathered():
            def heads(h):
                u, inside = divmod(h, together)
                return found[u][0][head_rows(inside)]

            top = functools.reduce(jnp.add, [f[1] for f in found])
            total = functools.reduce(jnp.add, [f[2] for f in found])
            return top, total, heads, 2.0**level

        return [unit(u) for u in range(HEADS // together)], gathered

    landed(hnear, 0, 192, recv01.at[0])
    project_side(hnear, 0)
    units, near_lanes, base_near = side(0, 1 - core)
    mixed = [base_own(h) for h in range(HEADS)] + units
    for place_in_line, level in ((9, 4), (6, 3), (3, 2)):
        mixed.insert(place_in_line, look(level))
    run(mixed)
    top, total, near_sums = by_head(base_near)
    merge(near_lanes, top, total, lambda h: near_sums[h])

    landed_or_zero(there[0], hfar, 0, 192, recv01.at[1])
    h2[pl.ds(pl.multiple_of(mine(core), 64), 64), :] = nn(fold[...], hfar[:192, :]).astype(BF16)
    project_side(hfar, 1)
    missing = off(jnp.logical_not(there[0]))
    units, far_lanes, base_far = side(1, core)
    run(units)
    top, total, far_sums = by_head(base_far)
    merge(far_lanes, top - missing, total, lambda h: far_sums[h])

    landed_or_zero(there[1], h2, pl.multiple_of(mine(1 - core), 64), 64, recv_far.at[0])
    forward(h2, 0)
    finer(h2, odd, h3, 1 - odd)
    landed_or_zero(there[2], h3, pl.multiple_of(mine(1 - odd), 64), 64, recv_far.at[2])
    landed_or_zero(there[3], h3, pl.multiple_of(mine(odd) + odd * 32, 32), 32, recv_far.at[3])
    forward(h3, 1)
    finer(h3, second, h4, 1 - second)
    landed_or_zero(there[4], h4, pl.multiple_of(mine(1 - second), 64), 64, recv_far.at[4])
    landed_or_zero(there[5], h4, pl.multiple_of(mine(second) + second * 32, 32), 32, recv_far.at[5])
    forward(h4, 2)

    one = []
    run([level_one(j, missing, one) for j in range(HEADS // 2)])
    vd[0] = values_of(core)
    for l in range(4, 1, -1):
        _, together, columns = shape_of(l)
        for u in range(HEADS // together):
            scores[l, u] = nt(rows_of(l, core), seen[l][u * columns : (u + 1) * columns, :])
    top, total, sums = by_head(one)
    one_sums, top, total = spread_all(jnp.concatenate(sums, 0).astype(BF16), top, total, spread1[...])
    terms = [(top, total, lambda h: one_sums[head_rows(h)], 2.0)]
    for i, buffer in enumerate((h2, h3, h4)):
        landed(buffer, pl.multiple_of((1 - core) * BLOCK, BLOCK), BLOCK, recv_near.at[i])
    loads[4].wait()
    landed(deep, 0, 192 + 3 * BLOCK, send_sem.at[0])
    for i, (here, rows) in enumerate(zip(there, (192, 64, 64, 32, 64, 32))):
        pl.when(here)(lambda i=i, rows=rows: landed(deep, 0, rows, send_sem.at[i + 1]))

    vd[1] = values_of(1 - core)
    levels = [coarse(4, group, devices // 8), coarse(3, pair, devices // 4), coarse(2, chip, devices // 2)]
    run([unit for units, _ in levels for unit in units])
    terms += [gathered() for _, gathered in levels]

    before = peak[...]
    after = functools.reduce(jnp.maximum, [term[0] for term in terms], before)
    factors = [jnp.exp2(before - after)] + [weight * jnp.exp2(top - after) for top, _, _, weight in terms]
    lower = den[...] * factors[0]
    for factor, term in zip(factors[1:], terms):
        lower = lower + factor * term[1]
    inverse = 1.0 / lower
    factors = [factor * inverse for factor in factors]
    attended = []
    for h in range(HEADS):
        upper = acc[head_rows(h), :] * factors[0][h : h + 1]
        for factor, term in zip(factors[1:], terms):
            upper = upper + term[2](h) * factor[h : h + 1]
        attended.append(upper.astype(BF16))
    turned = nt(eye[...], jnp.concatenate(attended, 0)).astype(BF16)
    out_ref[...] = nn(turned, wo[...]).astype(BF16)


def solution(mesh):
    devices = mesh.shape["ctx"] * mesh.shape["node"]

    def local(tokens, w_query, w_key, w_value, w_out):
        square = pltpu.VMEM((WIDTH, WIDTH), BF16)
        tall = pltpu.VMEM((ROWS, WIDTH), BF16)
        return pl.pallas_call(
            functools.partial(kernel, devices),
            out_shape=jax.ShapeDtypeStruct((ROWS, WIDTH), BF16),
            in_specs=[pl.BlockSpec(memory_space=pltpu.HBM)] * 5,
            out_specs=pl.BlockSpec(memory_space=pltpu.VMEM),
            scratch_shapes=[
                tall,
                square,
                square,
                square,
                square,
                square,
                pltpu.VMEM((COARSE, WIDTH), BF16),
                tall,
                tall,
                pltpu.VMEM((3 * ROWS, WIDTH), BF16),
                tall,
                pltpu.VMEM((COARSE, WIDTH), BF16),
                tall,
                pltpu.VMEM((WIDTH, ROWS), BF16),
                pltpu.VMEM((2, ROWS, WIDTH), BF16),
                pltpu.VMEM((2, WIDTH, ROWS), BF16),
                square,
                tall,
                pltpu.VMEM((BLOCK, WIDTH), BF16),
                pltpu.VMEM((2, WIDTH, 3 * BLOCK), BF16),
                pltpu.VMEM((WIDTH, ROWS), F32),
                pltpu.VMEM((HEADS, ROWS), F32),
                pltpu.VMEM((HEADS, ROWS), F32),
                pltpu.VMEM((COARSE, ROWS), BF16),
                pltpu.VMEM((ROWS, ROWS), BF16),
                pltpu.VMEM((64, BLOCK), BF16),
                pltpu.VMEM((64, 192), BF16),
                pltpu.VMEM((BLOCK, ROWS), BF16),
                pltpu.VMEM((ROWS, ROWS), BF16),
                pltpu.VMEM((ROWS, ROWS), BF16),
                pltpu.VMEM((BLOCK, ROWS), BF16),
                pltpu.SemaphoreType.DMA((5,)),
                pltpu.SemaphoreType.DMA((7,)),
                pltpu.SemaphoreType.DMA((2,)),
                pltpu.SemaphoreType.DMA((6,)),
                pltpu.SemaphoreType.DMA((3,)),
            ],
            compiler_params=pltpu.CompilerParams(
                collective_id=0, has_side_effects=True, vmem_limit_bytes=40 * 2**20
            ),
            name="hierarchical_attention",
        )(*[pltpu.with_memory_space_constraint(a, pltpu.HBM) for a in (tokens, w_query, w_key, w_value, w_out)])

    placed = (P(("ctx", "node"), None), P(), P(), P(), P())
    return jax.shard_map(
        local, mesh=mesh, in_specs=placed, out_specs=P(("ctx", "node"), None), check_vma=False
    )
```

```python
import functools
import math

import jax
import jax.numpy as jnp
from jax import lax
from jax.experimental import pallas as pl
from jax.experimental.pallas import tpu as pltpu
from jax.sharding import PartitionSpec as P

HEADS = 8
HEAD = 64
WIDTH = HEADS * HEAD
BLOCK = 128
ROWS = 256
NODES = 8
FAR = 1e30
SCALE = math.log2(math.e) / math.sqrt(HEAD)
BF16 = jnp.bfloat16
F32 = jnp.float32
START = {1: 0, 2: 128, 3: 192, 4: 224}
COARSE = 240


def nn(a, b):
    return lax.dot_general(a, b, (((1,), (0,)), ((), ())), preferred_element_type=F32)


def nt(a, b):
    return lax.dot_general(a, b, (((1,), (1,)), ((), ())), preferred_element_type=F32)


def iota(shape, axis):
    return lax.broadcasted_iota(jnp.int32, shape, axis)


def averager(rows, columns, level):
    hit = iota((rows, columns), 0) == iota((rows, columns), 1) >> level
    return jnp.where(hit, 0.5**level, 0.0).astype(BF16)


def spreader(rows, queries, level):
    hit = (iota((rows, ROWS), 0) & (queries - 1)) == iota((rows, ROWS), 1) >> level
    return jnp.where(hit, 1.0, 0.0).astype(BF16)


def split(values):
    high = values.astype(BF16)
    rest = values - high.astype(F32)
    middle = rest.astype(BF16)
    return [high, middle, (rest - middle.astype(F32)).astype(BF16)]


def spread_all(sums, tops, totals, spread):
    rows = sums.shape[0]
    out = nn(jnp.concatenate([sums] + split(jnp.concatenate([tops, totals], 0)), 0), spread)
    stats = out[rows : rows + 16] + out[rows + 16 : rows + 32] + out[rows + 32 :]
    return out[:rows], stats[:8], stats[8:]


def lane_head(shape, width):
    return iota(shape, 1) >> (width.bit_length() - 1)


def kernel(
    devices, x_hbm, wq_hbm, wk_hbm, wv_hbm, wo_hbm, out_ref,
    x, wq, wk, wv, wo, wvt, t, hnear, hfar, deep, q0, ql, k0, v0, kh, vh, u2, u3, u4, vd, acc, peak, den,
    average, eye, halve, fold, spread1, spread2, spread3, spread4,
    load_sem, send_sem, recv01, recv_far, recv_near,
):
    me = lax.axis_index("ctx") * NODES + lax.axis_index("node")
    core = lax.rem(me, 2)
    chip = lax.div(me, 2)
    pair = lax.div(me, 4)
    group = lax.div(me, 8)

    def place(index):
        return {"ctx": lax.div(index, NODES), "node": lax.rem(index, NODES)}

    def exists(index):
        return jnp.logical_and(index >= 0, index < devices)

    loads = []
    for i, (source, kept) in enumerate(((x_hbm, x), (wq_hbm, wq), (wk_hbm, wk), (wv_hbm, wv), (wo_hbm, wo))):
        loads.append(pltpu.make_async_copy(source, kept, load_sem.at[i]))
    loads[0].start()

    twin = me + 1 - 2 * core
    beyond = me - 1 + 2 * core
    odd = lax.rem(chip, 2)
    two = me + 3 - 6 * core
    three = me + 6 - 12 * odd
    mate = me + 2 - 4 * odd
    four = [[8 * (group + s) + 2 * j + core for j in range(4)] for s in (1, -1)]
    there = [exists(target) for target in (beyond, two, three, four[0][0], four[1][0])]
    parties = [[beyond], [two], [three]] + four

    barrier = pltpu.get_barrier_semaphore()

    def signal(target):
        pl.semaphore_signal(barrier, inc=1, device_id=place(target), device_id_type=pl.DeviceIdType.MESH)

    expected = 2
    for here, targets in reversed(list(zip(there, parties))):
        expected = expected + jnp.where(here, len(targets), 0)
        pl.when(here)(lambda targets=targets: [signal(target) for target in targets] and None)
    signal(mate)
    signal(twin)
    for load in loads[1:]:
        load.start()

    h2, h3, h4 = (deep.at[pl.ds(i * ROWS, ROWS)] for i in range(3))
    for l in range(1, 5):
        average[START[l] : START[l] + (ROWS >> l), :] = averager(ROWS >> l, ROWS, l)
    loads[0].wait()
    t[...] = nn(average[...], x[...]).astype(BF16)

    eye[...] = averager(ROWS, ROWS, 0)
    halve[...] = averager(64, BLOCK, 1)
    fold[:32, :] = jnp.concatenate([averager(32, BLOCK, 2), jnp.zeros((32, 64), BF16)], 1)
    fold[32:, :] = jnp.concatenate([jnp.zeros((32, BLOCK), BF16), averager(32, 64, 1)], 1)
    spreads = {1: spread1, 2: spread2, 3: spread3, 4: spread4}
    for l in range(1, 5):
        spreads[l][...] = spreader(spreads[l].shape[0], ROWS >> l, l)
    for load in loads[1:4]:
        load.wait()
    q0[...] = (nn(x[...], wq[...]) * SCALE).astype(BF16)
    k0[...] = nn(x[...], wk[...]).astype(BF16)
    for i in range(2):
        wvt[i * ROWS : (i + 1) * ROWS, :] = nt(eye[...], wv[:, i * ROWS : (i + 1) * ROWS]).astype(BF16)
    ql[...] = nn(average[...], q0[...]).astype(BF16)
    v0[...] = nt(wvt[...], x[...]).astype(BF16)


    pl.semaphore_wait(barrier, expected)

    def send(source, target, landing, recv, sent):
        pltpu.make_async_remote_copy(
            src_ref=source,
            dst_ref=landing,
            send_sem=send_sem.at[sent],
            recv_sem=recv,
            device_id=place(target),
            device_id_type=pl.DeviceIdType.MESH,
        ).start()

    def mine(direction):
        return core * BLOCK + direction * 64

    def send_edge(target, half, landing, recv, sent):
        rows = pl.multiple_of(half * BLOCK, BLOCK)
        send(x_hbm.at[pl.ds(rows, BLOCK)], target, landing.at[pl.ds(0, BLOCK)], recv, sent)

    pl.when(there[0])(lambda: send_edge(beyond, core, hfar, recv01.at[1], 1))
    send_edge(twin, 1 - core, hnear, recv01.at[0], 0)

    def send_one_means(target, half, landing, recv, sent):
        means = pl.multiple_of((1 - half) * 64, 64)
        send(t.at[pl.ds(means, 64)], target, landing.at[pl.ds(BLOCK, 64)], recv, sent)

    @pl.when(there[0])
    def _():
        send_one_means(beyond, core, hfar, recv01.at[1], 1)

    @pl.when(there[1])
    def _():
        landing = h2.at[pl.ds(pl.multiple_of(BLOCK - core * 64, 64), 64)]
        send(t.at[pl.ds(START[2], 64)], two, landing, recv_far.at[0], 2)

    @pl.when(there[2])
    def _():
        landing = h3.at[pl.ds(pl.multiple_of(core * BLOCK + odd * 96, 32), 32)]
        send(t.at[pl.ds(START[3], 32)], three, landing, recv_far.at[1], 3)

    def send_four(targets, d):
        for target in targets:
            landing = h4.at[pl.ds(pl.multiple_of(mine(d) + lax.rem(chip, 4) * 16, 16), 16)]
            send(t.at[pl.ds(START[4], 16)], target, landing, recv_far.at[2 + d], 4 + d)

    pl.when(there[3])(lambda: send_four(four[0], 0))
    pl.when(there[4])(lambda: send_four(four[1], 1))
    send_one_means(twin, 1 - core, hnear, recv01.at[0], 0)

    def landed(buffer, start, rows, sem):
        region = buffer.at[pl.ds(start, rows)]
        pltpu.make_async_copy(region, region, sem).wait()

    def landed_or_zero(here, buffer, start, rows, sem):
        pl.when(here)(lambda: landed(buffer, start, rows, sem))

        @pl.when(jnp.logical_not(here))
        def _():
            buffer[pl.ds(start, rows), :] = jnp.zeros((rows, WIDTH), BF16)

    def half_of(buffer, whose):
        return buffer.at[pl.ds(pl.multiple_of(whose * BLOCK, BLOCK), BLOCK)]

    def forward(buffer, which):
        region = half_of(buffer, core)
        send(region, twin, region, recv_near.at[which], 0)

    ones = jnp.ones((16, ROWS), BF16)
    half = lane_head((1, BLOCK), HEAD)
    pair_masks = [jnp.where(half == h, 1.0, 0.0).astype(BF16) for h in range(2)]

    def lanes_of(j):
        return slice(j * BLOCK, (j + 1) * BLOCK)

    def head_rows(h):
        return slice(h * HEAD, (h + 1) * HEAD)

    def pair_queries(block):
        return jnp.concatenate([block * pair_masks[0], block * pair_masks[1]], 0)

    def with_ones(v):
        return jnp.concatenate([v, ones[:, : v.shape[1]]], 0)

    def merge(lanes, top, total, heads):
        before = peak[:, lanes]
        after = jnp.maximum(before, top)
        old = jnp.exp2(before - after)
        new = jnp.exp2(top - after)
        den[:, lanes] = den[:, lanes] * old + new * total
        peak[:, lanes] = after
        for h in range(HEADS):
            rows = head_rows(h)
            acc[rows, lanes] = acc[rows, lanes] * old[h : h + 1] + heads(h) * new[h : h + 1]

    def run(units):
        waiting, active = list(units), []
        while waiting or active:
            if waiting:
                active.append(waiting.pop(0))
            active = [unit for unit in active if next(unit, None) is not None]

    def attend(keys, queries, values, done):
        s = nt(keys(), queries())
        yield True
        m = jnp.max(s, axis=0, keepdims=True)
        p = jnp.exp2(s - m).astype(BF16)
        yield True
        done(m, nn(with_ones(values()), p))

    def base_own(h):
        pairs = lanes_of(h // 2)

        def done(m, o):
            peak[h : h + 1, :] = m
            den[h : h + 1, :] = o[HEAD : HEAD + 1]
            acc[head_rows(h), :] = o[:HEAD]

        return attend(
            lambda: k0[:, pairs], lambda: q0[:, pairs] * pair_masks[h % 2], lambda: v0[head_rows(h), :], done
        )

    def project_side(buffer, slot):
        buffer[192:, :] = nn(halve[...], buffer[:BLOCK, :]).astype(BF16)
        kh[slot] = nn(buffer[...], wk[...]).astype(BF16)
        vh[slot] = nt(wvt[...], buffer[...]).astype(BF16)

    def side(slot, block):
        queries = pl.ds(pl.multiple_of(block * BLOCK, BLOCK), BLOCK)
        found = []
        units = [
            attend(
                lambda j=j: kh[slot, :BLOCK, lanes_of(j)],
                lambda j=j: pair_queries(q0[queries, lanes_of(j)]),
                lambda j=j: vh[slot, lanes_of(j), :BLOCK],
                lambda m, o: found.append((m, o)),
            )
            for j in range(HEADS // 2)
        ]
        return units, queries, found

    def level_one(j, missing, found):
        queries = pair_queries(ql[:BLOCK, lanes_of(j)])
        s = nt(kh[:, BLOCK:, lanes_of(j)].reshape(ROWS, BLOCK), queries)
        yield True
        near, far = s[:BLOCK], s[BLOCK:]
        m = jnp.maximum(jnp.max(near, axis=0, keepdims=True), jnp.max(far, axis=0, keepdims=True) - missing)
        p = jnp.concatenate([jnp.exp2(near - m).astype(BF16), jnp.exp2(far - (m + missing)).astype(BF16)], 0)
        yield True
        values = jnp.concatenate([vh[0, lanes_of(j), BLOCK:], vh[1, lanes_of(j), BLOCK:]], 1)
        found.append((m, nn(with_ones(values), p)))

    def by_head(part):
        tops = [m[:, lanes_of(h)] for m, _ in part for h in range(2)]
        totals = [o[BLOCK : BLOCK + 1, lanes_of(h)] for _, o in part for h in range(2)]
        sums = [o[head_rows(h), lanes_of(h)] for _, o in part for h in range(2)]
        return jnp.concatenate(tops, 0), jnp.concatenate(totals, 0), sums

    def off(missing):
        return jnp.where(missing, FAR, 0.0).astype(F32)

    everywhere = slice(0, ROWS)

    seen = {2: u2, 3: u3, 4: u4}

    def shape_of(level):
        queries = ROWS >> level
        together = min(HEADS, ROWS // queries)
        return queries, together, together * queries

    def look(level):
        queries = ROWS >> level
        for u in range(2):
            part = slice(u * ROWS, (u + 1) * ROWS)
            block = ql[START[level] : START[level] + queries, part]
            masked = [block * jnp.where(lane_head((1, ROWS), HEAD) == h, 1.0, 0.0).astype(BF16) for h in range(4)]
            rows = slice(u * 4 * queries, (u + 1) * 4 * queries)
            seen[level][rows, :] = nt(jnp.concatenate(masked, 0), wk[:, part]).astype(BF16)
            yield True

    def rows_of(level, whose):
        return half_of((h2, h3, h4)[level - 2], whose)[...]

    def values_of(whose):
        return nt(wvt[...], jnp.concatenate([rows_of(l, whose) for l in range(2, 5)], 0)).astype(BF16)

    scores = {}

    def coarse(level, index, count):
        queries, together, columns = shape_of(level)
        features = together * HEAD
        lanes = lanes_of(level - 2)
        off_left, off_right = off(index == 0), off(index == count - 1)
        column_head = lane_head((1, columns), queries)
        found = []

        def unit(u):
            part = slice(u * features, (u + 1) * features)
            s = [scores[level, u], nt(rows_of(level, 1 - core), seen[level][u * columns : (u + 1) * columns, :])]
            yield True
            run_length = 32 if level == 3 else 64
            chunks = [half[i : i + run_length] for half in s for i in range(0, BLOCK, run_length)]
            m = jnp.maximum(
                jnp.max(functools.reduce(jnp.maximum, chunks[0::2]), axis=0, keepdims=True) - off_left,
                jnp.max(functools.reduce(jnp.maximum, chunks[1::2]), axis=0, keepdims=True) - off_right,
            )
            p = []
            for i, chunk in enumerate(chunks):
                p.append(jnp.exp2(chunk - (m + (off_right if i % 2 else off_left))).astype(BF16))
            yield True
            values = jnp.concatenate([vd[0, part, lanes], vd[1, part, lanes]], 1)
            o = nn(with_ones(values), jnp.concatenate(p, 0))
            yield True
            own = [jnp.where(column_head == h, o[head_rows(h)], 0.0) for h in range(together)]
            row_head = iota((HEADS, columns), 0) == column_head + u * together
            found.append(
                spread_all(
                    jnp.concatenate(own, 0).astype(BF16),
                    jnp.where(row_head, m, 0.0),
                    jnp.where(row_head, o[features : features + 1], 0.0),
                    spreads[level][...],
                )
            )

        def gathered():
            def heads(h):
                u, inside = divmod(h, together)
                return found[u][0][head_rows(inside)]

            top = functools.reduce(jnp.add, [f[1] for f in found])
            total = functools.reduce(jnp.add, [f[2] for f in found])
            return top, total, heads, 2.0**level

        return [unit(u) for u in range(HEADS // together)], gathered

    landed(hnear, 0, 192, recv01.at[0])
    project_side(hnear, 0)
    units, near_lanes, base_near = side(0, 1 - core)
    mixed = [base_own(h) for h in range(HEADS)] + units
    for place_in_line, level in ((9, 4), (6, 3), (3, 2)):
        mixed.insert(place_in_line, look(level))
    run(mixed)
    top, total, near_sums = by_head(base_near)
    merge(near_lanes, top, total, lambda h: near_sums[h])

    landed_or_zero(there[0], hfar, 0, 192, recv01.at[1])
    h2[pl.ds(pl.multiple_of(mine(core), 64), 64), :] = nn(fold[...], hfar[:192, :]).astype(BF16)
    project_side(hfar, 1)
    landed_or_zero(there[1], h2, pl.multiple_of(mine(1 - core), 64), 64, recv_far.at[0])
    forward(h2, 0)
    held = core * BLOCK + (1 - odd) * 64
    finer = nn(halve[:32, :64], h2[pl.ds(pl.multiple_of(mine(odd), 64), 64), :]).astype(BF16)
    h3[pl.ds(pl.multiple_of(held + odd * 32, 32), 32), :] = finer
    landed_or_zero(there[2], h3, pl.multiple_of(held + (1 - odd) * 32, 32), 32, recv_far.at[1])
    blocks = h3.at[pl.ds(pl.multiple_of(held, 64), 64)]
    send(blocks, mate, blocks, recv_far.at[4], 0)
    missing = off(jnp.logical_not(there[0]))
    units, far_lanes, base_far = side(1, core)
    run(units)
    top, total, far_sums = by_head(base_far)
    merge(far_lanes, top - missing, total, lambda h: far_sums[h])
    landed_or_zero(there[4], h4, pl.multiple_of(mine(0), 64), 64, recv_far.at[2])
    landed_or_zero(there[3], h4, pl.multiple_of(mine(1), 64), 64, recv_far.at[3])
    forward(h4, 2)
    landed(h3, pl.multiple_of(core * BLOCK + odd * 64, 64), 64, recv_far.at[4])
    forward(h3, 1)

    one = []
    run([level_one(j, missing, one) for j in range(HEADS // 2)])
    vd[0] = values_of(core)
    for l in range(4, 1, -1):
        _, together, columns = shape_of(l)
        for u in range(HEADS // together):
            scores[l, u] = nt(rows_of(l, core), seen[l][u * columns : (u + 1) * columns, :])
    top, total, sums = by_head(one)
    one_sums, top, total = spread_all(jnp.concatenate(sums, 0).astype(BF16), top, total, spread1[...])
    terms = [(top, total, lambda h: one_sums[head_rows(h)], 2.0)]
    for i, buffer in enumerate((h2, h3, h4)):
        landed(buffer, pl.multiple_of((1 - core) * BLOCK, BLOCK), BLOCK, recv_near.at[i])
    loads[4].wait()
    landed(deep, 0, 192 + 3 * BLOCK + 64, send_sem.at[0])
    for i, (here, rows) in enumerate(zip(there, (192, 64, 32, 64, 64))):
        pl.when(here)(lambda i=i, rows=rows: landed(deep, 0, rows, send_sem.at[i + 1]))

    vd[1] = values_of(1 - core)
    levels = [coarse(4, group, devices // 8), coarse(3, pair, devices // 4), coarse(2, chip, devices // 2)]
    run([unit for units, _ in levels for unit in units])
    terms += [gathered() for _, gathered in levels]

    before = peak[...]
    after = functools.reduce(jnp.maximum, [term[0] for term in terms], before)
    factors = [jnp.exp2(before - after)] + [weight * jnp.exp2(top - after) for top, _, _, weight in terms]
    lower = den[...] * factors[0]
    for factor, term in zip(factors[1:], terms):
        lower = lower + factor * term[1]
    inverse = 1.0 / lower
    factors = [factor * inverse for factor in factors]
    attended = []
    for h in range(HEADS):
        upper = acc[head_rows(h), :] * factors[0][h : h + 1]
        for factor, term in zip(factors[1:], terms):
            upper = upper + term[2](h) * factor[h : h + 1]
        attended.append(upper.astype(BF16))
    turned = nt(eye[...], jnp.concatenate(attended, 0)).astype(BF16)
    out_ref[...] = nn(turned, wo[...]).astype(BF16)


def solution(mesh):
    devices = mesh.shape["ctx"] * mesh.shape["node"]

    def local(tokens, w_query, w_key, w_value, w_out):
        square = pltpu.VMEM((WIDTH, WIDTH), BF16)
        tall = pltpu.VMEM((ROWS, WIDTH), BF16)
        return pl.pallas_call(
            functools.partial(kernel, devices),
            out_shape=jax.ShapeDtypeStruct((ROWS, WIDTH), BF16),
            in_specs=[pl.BlockSpec(memory_space=pltpu.HBM)] * 5,
            out_specs=pl.BlockSpec(memory_space=pltpu.VMEM),
            scratch_shapes=[
                tall,
                square,
                square,
                square,
                square,
                square,
                pltpu.VMEM((COARSE, WIDTH), BF16),
                tall,
                tall,
                pltpu.VMEM((3 * ROWS, WIDTH), BF16),
                tall,
                pltpu.VMEM((COARSE, WIDTH), BF16),
                tall,
                pltpu.VMEM((WIDTH, ROWS), BF16),
                pltpu.VMEM((2, ROWS, WIDTH), BF16),
                pltpu.VMEM((2, WIDTH, ROWS), BF16),
                square,
                tall,
                pltpu.VMEM((BLOCK, WIDTH), BF16),
                pltpu.VMEM((2, WIDTH, 3 * BLOCK), BF16),
                pltpu.VMEM((WIDTH, ROWS), F32),
                pltpu.VMEM((HEADS, ROWS), F32),
                pltpu.VMEM((HEADS, ROWS), F32),
                pltpu.VMEM((COARSE, ROWS), BF16),
                pltpu.VMEM((ROWS, ROWS), BF16),
                pltpu.VMEM((64, BLOCK), BF16),
                pltpu.VMEM((64, 192), BF16),
                pltpu.VMEM((BLOCK, ROWS), BF16),
                pltpu.VMEM((ROWS, ROWS), BF16),
                pltpu.VMEM((ROWS, ROWS), BF16),
                pltpu.VMEM((BLOCK, ROWS), BF16),
                pltpu.SemaphoreType.DMA((5,)),
                pltpu.SemaphoreType.DMA((7,)),
                pltpu.SemaphoreType.DMA((2,)),
                pltpu.SemaphoreType.DMA((6,)),
                pltpu.SemaphoreType.DMA((3,)),
            ],
            compiler_params=pltpu.CompilerParams(
                collective_id=0, has_side_effects=True, vmem_limit_bytes=40 * 2**20
            ),
            name="hierarchical_attention",
        )(*[pltpu.with_memory_space_constraint(a, pltpu.HBM) for a in (tokens, w_query, w_key, w_value, w_out)])

    placed = (P(("ctx", "node"), None), P(), P(), P(), P())
    return jax.shard_map(
        local, mesh=mesh, in_specs=placed, out_specs=P(("ctx", "node"), None), check_vma=False
    )
```

```python
import functools
import math

import jax
import jax.numpy as jnp
from jax import lax
from jax.experimental import pallas as pl
from jax.experimental.pallas import tpu as pltpu
from jax.sharding import PartitionSpec as P

HEADS = 8
HEAD = 64
WIDTH = HEADS * HEAD
BLOCK = 128
ROWS = 256
NODES = 8
FAR = 1e30
SCALE = math.log2(math.e) / math.sqrt(HEAD)
BF16 = jnp.bfloat16
F32 = jnp.float32
START = {1: 0, 2: 128, 3: 192, 4: 224}
COARSE = 240


def nn(a, b):
    return lax.dot_general(a, b, (((1,), (0,)), ((), ())), preferred_element_type=F32)


def nt(a, b):
    return lax.dot_general(a, b, (((1,), (1,)), ((), ())), preferred_element_type=F32)


def iota(shape, axis):
    return lax.broadcasted_iota(jnp.int32, shape, axis)


def averager(rows, columns, level):
    hit = iota((rows, columns), 0) == iota((rows, columns), 1) >> level
    return jnp.where(hit, 0.5**level, 0.0).astype(BF16)


def spreader(rows, queries, level):
    hit = (iota((rows, ROWS), 0) & (queries - 1)) == iota((rows, ROWS), 1) >> level
    return jnp.where(hit, 1.0, 0.0).astype(BF16)


def split(values):
    high = values.astype(BF16)
    rest = values - high.astype(F32)
    middle = rest.astype(BF16)
    return [high, middle, (rest - middle.astype(F32)).astype(BF16)]


def spread_all(sums, tops, totals, spread):
    rows = sums.shape[0]
    out = nn(jnp.concatenate([sums] + split(jnp.concatenate([tops, totals], 0)), 0), spread)
    stats = out[rows : rows + 16] + out[rows + 16 : rows + 32] + out[rows + 32 :]
    return out[:rows], stats[:8], stats[8:]


def lane_head(shape, width):
    return iota(shape, 1) >> (width.bit_length() - 1)


def kernel(
    devices, x_hbm, wq_hbm, wk_hbm, wv_hbm, wo_hbm, out_ref,
    x, wq, wk, wv, wo, wvt, t, hnear, hfar, deep, q0, ql, k0, v0, kh, vh, u2, u3, u4, vd, acc, peak, den,
    average, eye, halve, spread1, spread2, spread3, spread4,
    load_sem, send_sem, recv01, recv_far, recv_near,
):
    me = lax.axis_index("ctx") * NODES + lax.axis_index("node")
    core = lax.rem(me, 2)
    chip = lax.div(me, 2)
    pair = lax.div(me, 4)
    group = lax.div(me, 8)

    def place(index):
        return {"ctx": lax.div(index, NODES), "node": lax.rem(index, NODES)}

    def exists(index):
        return jnp.logical_and(index >= 0, index < devices)

    loads = []
    for i, (source, kept) in enumerate(((x_hbm, x), (wq_hbm, wq), (wk_hbm, wk), (wv_hbm, wv), (wo_hbm, wo))):
        loads.append(pltpu.make_async_copy(source, kept, load_sem.at[i]))
    loads[0].start()

    twin = me + 1 - 2 * core
    beyond = me - 1 + 2 * core
    odd = lax.rem(chip, 2)
    second = lax.rem(pair, 2)
    two = [me + 2, me - 2]
    three_ahead = [(me + 4 - 8 * odd, odd, 1), (me + 6 - 12 * odd, odd, 0)]
    three_behind = [(me - 4 + 8 * odd, 1 - odd, 0)]
    ahead = 8 * (group + 1 - 2 * second) + core
    behind = 8 * (group - 1 + 2 * second) + core
    four_ahead = [(ahead + 4 * second + 2 * j, second, 1) for j in range(2)]
    four_ahead += [(ahead + 4 * (1 - second) + 2 * j, second, 0) for j in range(2)]
    four_behind = [(behind + 4 * second + 2 * j, 1 - second, 0) for j in range(2)]
    there = [exists(beyond), exists(two[0]), exists(three_ahead[0][0]), exists(three_behind[0][0])]
    there += [exists(ahead), exists(behind), exists(two[1])]
    parties = [[beyond], two[:1]] + [[p[0] for p in ps] for ps in (three_ahead, three_behind, four_ahead, four_behind)] + [two[1:]]

    barrier = pltpu.get_barrier_semaphore()

    def signal(target):
        pl.semaphore_signal(barrier, inc=1, device_id=place(target), device_id_type=pl.DeviceIdType.MESH)

    expected = 1
    for here, targets in reversed(list(zip(there, parties))):
        expected = expected + jnp.where(here, len(targets), 0)
        pl.when(here)(lambda targets=targets: [signal(target) for target in targets] and None)
    signal(twin)
    for load in loads[1:]:
        load.start()

    h2, h3, h4 = (deep.at[pl.ds(i * ROWS, ROWS)] for i in range(3))
    for l in range(1, 5):
        average[START[l] : START[l] + (ROWS >> l), :] = averager(ROWS >> l, ROWS, l)
    loads[0].wait()
    t[...] = nn(average[...], x[...]).astype(BF16)

    eye[...] = averager(ROWS, ROWS, 0)
    halve[...] = averager(64, BLOCK, 1)
    spreads = {1: spread1, 2: spread2, 3: spread3, 4: spread4}
    for l in range(1, 5):
        spreads[l][...] = spreader(spreads[l].shape[0], ROWS >> l, l)
    for load in loads[1:4]:
        load.wait()
    q0[...] = (nn(x[...], wq[...]) * SCALE).astype(BF16)
    k0[...] = nn(x[...], wk[...]).astype(BF16)
    for i in range(2):
        wvt[i * ROWS : (i + 1) * ROWS, :] = nt(eye[...], wv[:, i * ROWS : (i + 1) * ROWS]).astype(BF16)
    ql[...] = nn(average[...], q0[...]).astype(BF16)
    v0[...] = nt(wvt[...], x[...]).astype(BF16)


    pl.semaphore_wait(barrier, expected)

    def send(source, target, landing, recv, sent):
        pltpu.make_async_remote_copy(
            src_ref=source,
            dst_ref=landing,
            send_sem=send_sem.at[sent],
            recv_sem=recv,
            device_id=place(target),
            device_id_type=pl.DeviceIdType.MESH,
        ).start()

    def mine(direction):
        return core * BLOCK + direction * 64

    def send_edge(target, half, landing, recv, sent):
        rows = pl.multiple_of(half * BLOCK, BLOCK)
        send(x_hbm.at[pl.ds(rows, BLOCK)], target, landing.at[pl.ds(0, BLOCK)], recv, sent)

    send_edge(twin, 1 - core, hnear, recv01.at[0], 0)

    def send_one_means(target, half, landing, recv, sent):
        means = pl.multiple_of((1 - half) * 64, 64)
        send(t.at[pl.ds(means, 64)], target, landing.at[pl.ds(BLOCK, 64)], recv, sent)

    send_one_means(twin, 1 - core, hnear, recv01.at[0], 0)

    def send_two(d, sent):
        landing = h2.at[pl.ds(pl.multiple_of(mine(d), 64), 64)]
        send(t.at[pl.ds(START[2], 64)], two[d], landing, recv_far.at[d], sent)

    pl.when(there[1])(lambda: send_two(0, 2))
    pl.when(there[6])(lambda: send_two(1, 7))

    def send_three(targets, sent):
        for target, d, short in targets:
            landing = h3.at[pl.ds(pl.multiple_of(mine(d) + odd * 32, 32), 32)]
            send(t.at[pl.ds(START[3], 32)], target, landing, recv_far.at[2 + short], sent)

    def send_four(targets, sent):
        for target, d, short in targets:
            landing = h4.at[pl.ds(pl.multiple_of(mine(d) + lax.rem(chip, 4) * 16, 16), 16)]
            send(t.at[pl.ds(START[4], 16)], target, landing, recv_far.at[4 + short], sent)

    pl.when(there[2])(lambda: send_three(three_ahead, 3))
    pl.when(there[3])(lambda: send_three(three_behind, 4))
    pl.when(there[4])(lambda: send_four(four_ahead, 5))
    pl.when(there[5])(lambda: send_four(four_behind, 6))

    @pl.when(there[0])
    def _():
        send_one_means(beyond, core, hfar, recv01.at[1], 1)
        send_edge(beyond, core, hfar, recv01.at[1], 1)

    def landed(buffer, start, rows, sem):
        region = buffer.at[pl.ds(start, rows)]
        pltpu.make_async_copy(region, region, sem).wait()

    def landed_or_zero(here, buffer, start, rows, sem):
        pl.when(here)(lambda: landed(buffer, start, rows, sem))

        @pl.when(jnp.logical_not(here))
        def _():
            buffer[pl.ds(start, rows), :] = jnp.zeros((rows, WIDTH), BF16)

    def half_of(buffer, whose):
        return buffer.at[pl.ds(pl.multiple_of(whose * BLOCK, BLOCK), BLOCK)]

    def forward(buffer, which):
        region = half_of(buffer, core)
        send(region, twin, region, recv_near.at[which], 0)

    def finer(source, d, target, inside):
        rows = source[pl.ds(pl.multiple_of(mine(d), 64), 64), :]
        means = nn(halve[:32, :64], rows).astype(BF16)
        target[pl.ds(pl.multiple_of(mine(d) + inside * 32, 32), 32), :] = means

    ones = jnp.ones((16, ROWS), BF16)
    half = lane_head((1, BLOCK), HEAD)
    pair_masks = [jnp.where(half == h, 1.0, 0.0).astype(BF16) for h in range(2)]

    def lanes_of(j):
        return slice(j * BLOCK, (j + 1) * BLOCK)

    def head_rows(h):
        return slice(h * HEAD, (h + 1) * HEAD)

    def pair_queries(block):
        return jnp.concatenate([block * pair_masks[0], block * pair_masks[1]], 0)

    def with_ones(v):
        return jnp.concatenate([v, ones[:, : v.shape[1]]], 0)

    def merge(lanes, top, total, heads):
        before = peak[:, lanes]
        after = jnp.maximum(before, top)
        old = jnp.exp2(before - after)
        new = jnp.exp2(top - after)
        den[:, lanes] = den[:, lanes] * old + new * total
        peak[:, lanes] = after
        for h in range(HEADS):
            rows = head_rows(h)
            acc[rows, lanes] = acc[rows, lanes] * old[h : h + 1] + heads(h) * new[h : h + 1]

    def run(units):
        waiting, active = list(units), []
        while waiting or active:
            if waiting:
                active.append(waiting.pop(0))
            active = [unit for unit in active if next(unit, None) is not None]

    def attend(keys, queries, values, done):
        s = nt(keys(), queries())
        yield True
        m = jnp.max(s, axis=0, keepdims=True)
        p = jnp.exp2(s - m).astype(BF16)
        yield True
        done(m, nn(with_ones(values()), p))

    def base_own(h):
        pairs = lanes_of(h // 2)

        def done(m, o):
            peak[h : h + 1, :] = m
            den[h : h + 1, :] = o[HEAD : HEAD + 1]
            acc[head_rows(h), :] = o[:HEAD]

        return attend(
            lambda: k0[:, pairs], lambda: q0[:, pairs] * pair_masks[h % 2], lambda: v0[head_rows(h), :], done
        )

    def project_side(buffer, slot):
        buffer[192:, :] = nn(halve[...], buffer[:BLOCK, :]).astype(BF16)
        kh[slot] = nn(buffer[...], wk[...]).astype(BF16)
        vh[slot] = nt(wvt[...], buffer[...]).astype(BF16)

    def side(slot, block):
        queries = pl.ds(pl.multiple_of(block * BLOCK, BLOCK), BLOCK)
        found = []
        units = [
            attend(
                lambda j=j: kh[slot, :BLOCK, lanes_of(j)],
                lambda j=j: pair_queries(q0[queries, lanes_of(j)]),
                lambda j=j: vh[slot, lanes_of(j), :BLOCK],
                lambda m, o: found.append((m, o)),
            )
            for j in range(HEADS // 2)
        ]
        return units, queries, found

    def level_one(j, missing, found):
        queries = pair_queries(ql[:BLOCK, lanes_of(j)])
        s = nt(kh[:, BLOCK:, lanes_of(j)].reshape(ROWS, BLOCK), queries)
        yield True
        near, far = s[:BLOCK], s[BLOCK:]
        m = jnp.maximum(jnp.max(near, axis=0, keepdims=True), jnp.max(far, axis=0, keepdims=True) - missing)
        p = jnp.concatenate([jnp.exp2(near - m).astype(BF16), jnp.exp2(far - (m + missing)).astype(BF16)], 0)
        yield True
        values = jnp.concatenate([vh[0, lanes_of(j), BLOCK:], vh[1, lanes_of(j), BLOCK:]], 1)
        found.append((m, nn(with_ones(values), p)))

    def by_head(part):
        tops = [m[:, lanes_of(h)] for m, _ in part for h in range(2)]
        totals = [o[BLOCK : BLOCK + 1, lanes_of(h)] for _, o in part for h in range(2)]
        sums = [o[head_rows(h), lanes_of(h)] for _, o in part for h in range(2)]
        return jnp.concatenate(tops, 0), jnp.concatenate(totals, 0), sums

    def off(missing):
        return jnp.where(missing, FAR, 0.0).astype(F32)

    everywhere = slice(0, ROWS)

    seen = {2: u2, 3: u3, 4: u4}

    def shape_of(level):
        queries = ROWS >> level
        together = min(HEADS, ROWS // queries)
        return queries, together, together * queries

    def look(level):
        queries = ROWS >> level
        for u in range(2):
            part = slice(u * ROWS, (u + 1) * ROWS)
            block = ql[START[level] : START[level] + queries, part]
            masked = [block * jnp.where(lane_head((1, ROWS), HEAD) == h, 1.0, 0.0).astype(BF16) for h in range(4)]
            rows = slice(u * 4 * queries, (u + 1) * 4 * queries)
            seen[level][rows, :] = nt(jnp.concatenate(masked, 0), wk[:, part]).astype(BF16)
            yield True

    def rows_of(level, whose):
        return half_of((h2, h3, h4)[level - 2], whose)[...]

    def values_of(whose):
        return nt(wvt[...], jnp.concatenate([rows_of(l, whose) for l in range(2, 5)], 0)).astype(BF16)

    scores = {}

    def coarse(level, index, count):
        queries, together, columns = shape_of(level)
        features = together * HEAD
        lanes = lanes_of(level - 2)
        off_left, off_right = off(index == 0), off(index == count - 1)
        column_head = lane_head((1, columns), queries)
        found = []

        def unit(u):
            part = slice(u * features, (u + 1) * features)
            s = [scores[level, u], nt(rows_of(level, 1 - core), seen[level][u * columns : (u + 1) * columns, :])]
            yield True
            left = [half[:64] for half in s]
            right = [half[64:] for half in s]
            m = jnp.maximum(
                jnp.max(jnp.maximum(*left), axis=0, keepdims=True) - off_left,
                jnp.max(jnp.maximum(*right), axis=0, keepdims=True) - off_right,
            )
            p = []
            for half in range(2):
                p.append(jnp.exp2(left[half] - (m + off_left)).astype(BF16))
                p.append(jnp.exp2(right[half] - (m + off_right)).astype(BF16))
            yield True
            values = jnp.concatenate([vd[0, part, lanes], vd[1, part, lanes]], 1)
            o = nn(with_ones(values), jnp.concatenate(p, 0))
            yield True
            own = [jnp.where(column_head == h, o[head_rows(h)], 0.0) for h in range(together)]
            row_head = iota((HEADS, columns), 0) == column_head + u * together
            found.append(
                spread_all(
                    jnp.concatenate(own, 0).astype(BF16),
                    jnp.where(row_head, m, 0.0),
                    jnp.where(row_head, o[features : features + 1], 0.0),
                    spreads[level][...],
                )
            )

        def gathered():
            def heads(h):
                u, inside = divmod(h, together)
                return found[u][0][head_rows(inside)]

            top = functools.reduce(jnp.add, [f[1] for f in found])
            total = functools.reduce(jnp.add, [f[2] for f in found])
            return top, total, heads, 2.0**level

        return [unit(u) for u in range(HEADS // together)], gathered

    landed(hnear, 0, 192, recv01.at[0])
    project_side(hnear, 0)
    units, near_lanes, base_near = side(0, 1 - core)
    mixed = [base_own(h) for h in range(HEADS)] + units
    for place_in_line, level in ((9, 4), (6, 3), (3, 2)):
        mixed.insert(place_in_line, look(level))
    run(mixed)
    top, total, near_sums = by_head(base_near)
    merge(near_lanes, top, total, lambda h: near_sums[h])

    landed_or_zero(there[6], h2, pl.multiple_of(mine(0), 64), 64, recv_far.at[0])
    landed_or_zero(there[1], h2, pl.multiple_of(mine(1), 64), 64, recv_far.at[1])
    forward(h2, 0)
    finer(h2, odd, h3, 1 - odd)
    landed_or_zero(there[2], h3, pl.multiple_of(mine(1 - odd), 64), 64, recv_far.at[2])
    landed_or_zero(there[3], h3, pl.multiple_of(mine(odd) + odd * 32, 32), 32, recv_far.at[3])
    forward(h3, 1)
    finer(h3, second, h4, 1 - second)
    landed_or_zero(there[4], h4, pl.multiple_of(mine(1 - second), 64), 64, recv_far.at[4])
    landed_or_zero(there[5], h4, pl.multiple_of(mine(second) + second * 32, 32), 32, recv_far.at[5])
    forward(h4, 2)

    vd[0] = values_of(core)
    for l in range(4, 1, -1):
        _, together, columns = shape_of(l)
        for u in range(HEADS // together):
            scores[l, u] = nt(rows_of(l, core), seen[l][u * columns : (u + 1) * columns, :])
    for i, buffer in enumerate((h2, h3, h4)):
        landed(buffer, pl.multiple_of((1 - core) * BLOCK, BLOCK), BLOCK, recv_near.at[i])
    vd[1] = values_of(1 - core)
    levels = [coarse(4, group, devices // 8), coarse(3, pair, devices // 4), coarse(2, chip, devices // 2)]
    run([unit for units, _ in levels for unit in units])
    terms = [gathered() for _, gathered in levels]

    landed_or_zero(there[0], hfar, 0, 192, recv01.at[1])
    loads[4].wait()
    landed(deep, 0, 192 + 3 * BLOCK, send_sem.at[0])
    for i, (here, rows) in enumerate(zip(there, (192, 64, 64, 32, 64, 32, 64))):
        pl.when(here)(lambda i=i, rows=rows: landed(deep, 0, rows, send_sem.at[i + 1]))
    project_side(hfar, 1)
    missing = off(jnp.logical_not(there[0]))
    units, far_lanes, base_far = side(1, core)
    one = []
    run(units + [level_one(j, missing, one) for j in range(HEADS // 2)])
    top, total, far_sums = by_head(base_far)
    merge(far_lanes, top - missing, total, lambda h: far_sums[h])
    top, total, sums = by_head(one)
    one_sums, top, total = spread_all(jnp.concatenate(sums, 0).astype(BF16), top, total, spread1[...])
    terms.append((top, total, lambda h: one_sums[head_rows(h)], 2.0))

    before = peak[...]
    after = functools.reduce(jnp.maximum, [term[0] for term in terms], before)
    factors = [jnp.exp2(before - after)] + [weight * jnp.exp2(top - after) for top, _, _, weight in terms]
    lower = den[...] * factors[0]
    for factor, term in zip(factors[1:], terms):
        lower = lower + factor * term[1]
    inverse = 1.0 / lower
    factors = [factor * inverse for factor in factors]
    attended = []
    for h in range(HEADS):
        upper = acc[head_rows(h), :] * factors[0][h : h + 1]
        for factor, term in zip(factors[1:], terms):
            upper = upper + term[2](h) * factor[h : h + 1]
        attended.append(upper.astype(BF16))
    turned = nt(eye[...], jnp.concatenate(attended, 0)).astype(BF16)
    out_ref[...] = nn(turned, wo[...]).astype(BF16)


def solution(mesh):
    devices = mesh.shape["ctx"] * mesh.shape["node"]

    def local(tokens, w_query, w_key, w_value, w_out):
        square = pltpu.VMEM((WIDTH, WIDTH), BF16)
        tall = pltpu.VMEM((ROWS, WIDTH), BF16)
        return pl.pallas_call(
            functools.partial(kernel, devices),
            out_shape=jax.ShapeDtypeStruct((ROWS, WIDTH), BF16),
            in_specs=[pl.BlockSpec(memory_space=pltpu.HBM)] * 5,
            out_specs=pl.BlockSpec(memory_space=pltpu.VMEM),
            scratch_shapes=[
                tall,
                square,
                square,
                square,
                square,
                square,
                pltpu.VMEM((COARSE, WIDTH), BF16),
                tall,
                tall,
                pltpu.VMEM((3 * ROWS, WIDTH), BF16),
                tall,
                pltpu.VMEM((COARSE, WIDTH), BF16),
                tall,
                pltpu.VMEM((WIDTH, ROWS), BF16),
                pltpu.VMEM((2, ROWS, WIDTH), BF16),
                pltpu.VMEM((2, WIDTH, ROWS), BF16),
                square,
                tall,
                pltpu.VMEM((BLOCK, WIDTH), BF16),
                pltpu.VMEM((2, WIDTH, 3 * BLOCK), BF16),
                pltpu.VMEM((WIDTH, ROWS), F32),
                pltpu.VMEM((HEADS, ROWS), F32),
                pltpu.VMEM((HEADS, ROWS), F32),
                pltpu.VMEM((COARSE, ROWS), BF16),
                pltpu.VMEM((ROWS, ROWS), BF16),
                pltpu.VMEM((64, BLOCK), BF16),
                pltpu.VMEM((BLOCK, ROWS), BF16),
                pltpu.VMEM((ROWS, ROWS), BF16),
                pltpu.VMEM((ROWS, ROWS), BF16),
                pltpu.VMEM((BLOCK, ROWS), BF16),
                pltpu.SemaphoreType.DMA((5,)),
                pltpu.SemaphoreType.DMA((8,)),
                pltpu.SemaphoreType.DMA((2,)),
                pltpu.SemaphoreType.DMA((6,)),
                pltpu.SemaphoreType.DMA((3,)),
            ],
            compiler_params=pltpu.CompilerParams(
                collective_id=0, has_side_effects=True, vmem_limit_bytes=40 * 2**20
            ),
            name="hierarchical_attention",
        )(*[pltpu.with_memory_space_constraint(a, pltpu.HBM) for a in (tokens, w_query, w_key, w_value, w_out)])

    placed = (P(("ctx", "node"), None), P(), P(), P(), P())
    return jax.shard_map(
        local, mesh=mesh, in_specs=placed, out_specs=P(("ctx", "node"), None), check_vma=False
    )
```

```python
import functools
import math

import jax
import jax.numpy as jnp
from jax import lax
from jax.experimental import pallas as pl
from jax.experimental.pallas import tpu as pltpu
from jax.sharding import PartitionSpec as P

HEADS = 8
HEAD = 64
WIDTH = HEADS * HEAD
BLOCK = 128
ROWS = 256
NODES = 8
FAR = 1e30
SCALE = math.log2(math.e) / math.sqrt(HEAD)
BF16 = jnp.bfloat16
F32 = jnp.float32
START = {1: 0, 2: 128, 3: 192, 4: 224}
COARSE = 240


def nn(a, b):
    return lax.dot_general(a, b, (((1,), (0,)), ((), ())), preferred_element_type=F32)


def nt(a, b):
    return lax.dot_general(a, b, (((1,), (1,)), ((), ())), preferred_element_type=F32)


def iota(shape, axis):
    return lax.broadcasted_iota(jnp.int32, shape, axis)


def averager(rows, columns, level):
    hit = iota((rows, columns), 0) == iota((rows, columns), 1) >> level
    return jnp.where(hit, 0.5**level, 0.0).astype(BF16)


def spreader(rows, queries, level):
    hit = (iota((rows, ROWS), 0) & (queries - 1)) == iota((rows, ROWS), 1) >> level
    return jnp.where(hit, 1.0, 0.0).astype(BF16)


def split(values):
    high = values.astype(BF16)
    rest = values - high.astype(F32)
    middle = rest.astype(BF16)
    return [high, middle, (rest - middle.astype(F32)).astype(BF16)]


def spread_all(sums, tops, totals, spread):
    rows = sums.shape[0]
    out = nn(jnp.concatenate([sums] + split(jnp.concatenate([tops, totals], 0)), 0), spread)
    stats = out[rows : rows + 16] + out[rows + 16 : rows + 32] + out[rows + 32 :]
    return out[:rows], stats[:8], stats[8:]


def lane_head(shape, width):
    return iota(shape, 1) >> (width.bit_length() - 1)


def kernel(
    devices, x_hbm, wq_hbm, wk_hbm, wv_hbm, wo_hbm, out_ref,
    x, wq, wk, wv, wo, wvt, t, hnear, hfar, deep, q0, ql, k0, v0, kh, vh, u2, u3, u4, vd, acc, peak, den,
    average, eye, halve, fold, spread1, spread2, spread3, spread4,
    load_sem, send_sem, recv01, recv_far, recv_near,
):
    me = lax.axis_index("ctx") * NODES + lax.axis_index("node")
    core = lax.rem(me, 2)
    chip = lax.div(me, 2)
    pair = lax.div(me, 4)
    group = lax.div(me, 8)

    def place(index):
        return {"ctx": lax.div(index, NODES), "node": lax.rem(index, NODES)}

    def exists(index):
        return jnp.logical_and(index >= 0, index < devices)

    loads = []
    for i, (source, kept) in enumerate(((x_hbm, x), (wq_hbm, wq), (wk_hbm, wk), (wv_hbm, wv), (wo_hbm, wo))):
        loads.append(pltpu.make_async_copy(source, kept, load_sem.at[i]))
    loads[0].start()

    twin = me + 1 - 2 * core
    beyond = me - 1 + 2 * core
    odd = lax.rem(chip, 2)
    second = lax.rem(pair, 2)
    two = me + 3 - 6 * core
    three_ahead = [(me + 4 - 8 * odd, odd, 1), (me + 6 - 12 * odd, odd, 0)]
    three_behind = [(me - 4 + 8 * odd, 1 - odd, 0)]
    ahead = 8 * (group + 1 - 2 * second) + core
    behind = 8 * (group - 1 + 2 * second) + core
    four_ahead = [(ahead + 4 * second + 2 * j, second, 1) for j in range(2)]
    four_ahead += [(ahead + 4 * (1 - second) + 2 * j, second, 0) for j in range(2)]
    four_behind = [(behind + 4 * second + 2 * j, 1 - second, 0) for j in range(2)]
    there = [exists(beyond), exists(two), exists(three_ahead[0][0]), exists(three_behind[0][0])]
    there += [exists(ahead), exists(behind)]
    parties = [[beyond], [two]] + [[p[0] for p in ps] for ps in (three_ahead, three_behind, four_ahead, four_behind)]

    barrier = pltpu.get_barrier_semaphore()

    def signal(target):
        pl.semaphore_signal(barrier, inc=1, device_id=place(target), device_id_type=pl.DeviceIdType.MESH)

    expected = 1
    for here, targets in reversed(list(zip(there, parties))):
        expected = expected + jnp.where(here, len(targets), 0)
        pl.when(here)(lambda targets=targets: [signal(target) for target in targets] and None)
    signal(twin)
    for load in loads[1:]:
        load.start()

    h2, h3, h4 = (deep.at[pl.ds(i * ROWS, ROWS)] for i in range(3))
    for l in range(1, 5):
        average[START[l] : START[l] + (ROWS >> l), :] = averager(ROWS >> l, ROWS, l)
    pl.semaphore_wait(barrier, expected)

    def send(source, target, landing, recv, sent):
        pltpu.make_async_remote_copy(
            src_ref=source,
            dst_ref=landing,
            send_sem=send_sem.at[sent],
            recv_sem=recv,
            device_id=place(target),
            device_id_type=pl.DeviceIdType.MESH,
        ).start()

    def mine(direction):
        return core * BLOCK + direction * 64

    def send_edge(target, half, landing, recv, sent):
        rows = pl.multiple_of(half * BLOCK, BLOCK)
        send(x_hbm.at[pl.ds(rows, BLOCK)], target, landing.at[pl.ds(0, BLOCK)], recv, sent)

    pl.when(there[0])(lambda: send_edge(beyond, core, hfar, recv01.at[1], 1))
    send_edge(twin, 1 - core, hnear, recv01.at[0], 0)

    loads[0].wait()
    t[...] = nn(average[...], x[...]).astype(BF16)

    def send_one_means(target, half, landing, recv, sent):
        means = pl.multiple_of((1 - half) * 64, 64)
        send(t.at[pl.ds(means, 64)], target, landing.at[pl.ds(BLOCK, 64)], recv, sent)

    @pl.when(there[0])
    def _():
        send_one_means(beyond, core, hfar, recv01.at[1], 1)

    @pl.when(there[1])
    def _():
        landing = h2.at[pl.ds(pl.multiple_of(BLOCK - core * 64, 64), 64)]
        send(t.at[pl.ds(START[2], 64)], two, landing, recv_far.at[0], 2)

    def send_three(targets, sent):
        for target, d, short in targets:
            landing = h3.at[pl.ds(pl.multiple_of(mine(d) + odd * 32, 32), 32)]
            send(t.at[pl.ds(START[3], 32)], target, landing, recv_far.at[2 + short], sent)

    def send_four(targets, sent):
        for target, d, short in targets:
            landing = h4.at[pl.ds(pl.multiple_of(mine(d) + lax.rem(chip, 4) * 16, 16), 16)]
            send(t.at[pl.ds(START[4], 16)], target, landing, recv_far.at[4 + short], sent)

    pl.when(there[2])(lambda: send_three(three_ahead, 3))
    pl.when(there[3])(lambda: send_three(three_behind, 4))
    pl.when(there[4])(lambda: send_four(four_ahead, 5))
    pl.when(there[5])(lambda: send_four(four_behind, 6))
    send_one_means(twin, 1 - core, hnear, recv01.at[0], 0)

    def landed(buffer, start, rows, sem):
        region = buffer.at[pl.ds(start, rows)]
        pltpu.make_async_copy(region, region, sem).wait()

    def landed_or_zero(here, buffer, start, rows, sem):
        pl.when(here)(lambda: landed(buffer, start, rows, sem))

        @pl.when(jnp.logical_not(here))
        def _():
            buffer[pl.ds(start, rows), :] = jnp.zeros((rows, WIDTH), BF16)

    def half_of(buffer, whose):
        return buffer.at[pl.ds(pl.multiple_of(whose * BLOCK, BLOCK), BLOCK)]

    def forward(buffer, which):
        region = half_of(buffer, core)
        send(region, twin, region, recv_near.at[which], 0)

    def finer(source, d, target, inside):
        rows = source[pl.ds(pl.multiple_of(mine(d), 64), 64), :]
        means = nn(halve[:32, :64], rows).astype(BF16)
        target[pl.ds(pl.multiple_of(mine(d) + inside * 32, 32), 32), :] = means

    ones = jnp.ones((16, ROWS), BF16)
    half = lane_head((1, BLOCK), HEAD)
    pair_masks = [jnp.where(half == h, 1.0, 0.0).astype(BF16) for h in range(2)]

    def lanes_of(j):
        return slice(j * BLOCK, (j + 1) * BLOCK)

    def head_rows(h):
        return slice(h * HEAD, (h + 1) * HEAD)

    def pair_queries(block):
        return jnp.concatenate([block * pair_masks[0], block * pair_masks[1]], 0)

    def with_ones(v):
        return jnp.concatenate([v, ones[:, : v.shape[1]]], 0)

    def merge(lanes, top, total, heads):
        before = peak[:, lanes]
        after = jnp.maximum(before, top)
        old = jnp.exp2(before - after)
        new = jnp.exp2(top - after)
        den[:, lanes] = den[:, lanes] * old + new * total
        peak[:, lanes] = after
        for h in range(HEADS):
            rows = head_rows(h)
            acc[rows, lanes] = acc[rows, lanes] * old[h : h + 1] + heads(h) * new[h : h + 1]

    def run(units):
        waiting, active = list(units), []
        while waiting or active:
            if waiting:
                active.append(waiting.pop(0))
            active = [unit for unit in active if next(unit, None) is not None]

    def attend(keys, queries, values, done):
        s = nt(keys(), queries())
        yield True
        m = jnp.max(s, axis=0, keepdims=True)
        p = jnp.exp2(s - m).astype(BF16)
        yield True
        done(m, nn(with_ones(values()), p))

    def base_own(h):
        pairs = lanes_of(h // 2)

        def done(m, o):
            peak[h : h + 1, :] = m
            den[h : h + 1, :] = o[HEAD : HEAD + 1]
            acc[head_rows(h), :] = o[:HEAD]

        return attend(
            lambda: k0[:, pairs], lambda: q0[:, pairs] * pair_masks[h % 2], lambda: v0[head_rows(h), :], done
        )

    def project_side(buffer, slot):
        buffer[192:, :] = nn(halve[...], buffer[:BLOCK, :]).astype(BF16)
        kh[slot] = nn(buffer[...], wk[...]).astype(BF16)
        vh[slot] = nt(wvt[...], buffer[...]).astype(BF16)

    def side(slot, block):
        queries = pl.ds(pl.multiple_of(block * BLOCK, BLOCK), BLOCK)
        found = []
        units = [
            attend(
                lambda j=j: kh[slot, :BLOCK, lanes_of(j)],
                lambda j=j: pair_queries(q0[queries, lanes_of(j)]),
                lambda j=j: vh[slot, lanes_of(j), :BLOCK],
                lambda m, o: found.append((m, o)),
            )
            for j in range(HEADS // 2)
        ]
        return units, queries, found

    def level_one(j, missing, found):
        queries = pair_queries(ql[:BLOCK, lanes_of(j)])
        s = nt(kh[:, BLOCK:, lanes_of(j)].reshape(ROWS, BLOCK), queries)
        yield True
        near, far = s[:BLOCK], s[BLOCK:]
        m = jnp.maximum(jnp.max(near, axis=0, keepdims=True), jnp.max(far, axis=0, keepdims=True) - missing)
        p = jnp.concatenate([jnp.exp2(near - m).astype(BF16), jnp.exp2(far - (m + missing)).astype(BF16)], 0)
        yield True
        values = jnp.concatenate([vh[0, lanes_of(j), BLOCK:], vh[1, lanes_of(j), BLOCK:]], 1)
        found.append((m, nn(with_ones(values), p)))

    def by_head(part):
        tops = [m[:, lanes_of(h)] for m, _ in part for h in range(2)]
        totals = [o[BLOCK : BLOCK + 1, lanes_of(h)] for _, o in part for h in range(2)]
        sums = [o[head_rows(h), lanes_of(h)] for _, o in part for h in range(2)]
        return jnp.concatenate(tops, 0), jnp.concatenate(totals, 0), sums

    def off(missing):
        return jnp.where(missing, FAR, 0.0).astype(F32)

    everywhere = slice(0, ROWS)

    seen = {2: u2, 3: u3, 4: u4}

    def shape_of(level):
        queries = ROWS >> level
        together = min(HEADS, ROWS // queries)
        return queries, together, together * queries

    def look(level):
        queries = ROWS >> level
        for u in range(2):
            part = slice(u * ROWS, (u + 1) * ROWS)
            block = ql[START[level] : START[level] + queries, part]
            masked = [block * jnp.where(lane_head((1, ROWS), HEAD) == h, 1.0, 0.0).astype(BF16) for h in range(4)]
            rows = slice(u * 4 * queries, (u + 1) * 4 * queries)
            seen[level][rows, :] = nt(jnp.concatenate(masked, 0), wk[:, part]).astype(BF16)
            yield True

    def rows_of(level, whose):
        return half_of((h2, h3, h4)[level - 2], whose)[...]

    def values_of(whose):
        return nt(wvt[...], jnp.concatenate([rows_of(l, whose) for l in range(2, 5)], 0)).astype(BF16)

    scores = {}

    def coarse(level, index, count):
        queries, together, columns = shape_of(level)
        features = together * HEAD
        lanes = lanes_of(level - 2)
        off_left, off_right = off(index == 0), off(index == count - 1)
        column_head = lane_head((1, columns), queries)
        found = []

        def unit(u):
            part = slice(u * features, (u + 1) * features)
            s = [scores[level, u], nt(rows_of(level, 1 - core), seen[level][u * columns : (u + 1) * columns, :])]
            yield True
            left = [half[:64] for half in s]
            right = [half[64:] for half in s]
            m = jnp.maximum(
                jnp.max(jnp.maximum(*left), axis=0, keepdims=True) - off_left,
                jnp.max(jnp.maximum(*right), axis=0, keepdims=True) - off_right,
            )
            p = []
            for half in range(2):
                p.append(jnp.exp2(left[half] - (m + off_left)).astype(BF16))
                p.append(jnp.exp2(right[half] - (m + off_right)).astype(BF16))
            yield True
            values = jnp.concatenate([vd[0, part, lanes], vd[1, part, lanes]], 1)
            o = nn(with_ones(values), jnp.concatenate(p, 0))
            yield True
            own = [jnp.where(column_head == h, o[head_rows(h)], 0.0) for h in range(together)]
            row_head = iota((HEADS, columns), 0) == column_head + u * together
            found.append(
                spread_all(
                    jnp.concatenate(own, 0).astype(BF16),
                    jnp.where(row_head, m, 0.0),
                    jnp.where(row_head, o[features : features + 1], 0.0),
                    spreads[level][...],
                )
            )

        def gathered():
            def heads(h):
                u, inside = divmod(h, together)
                return found[u][0][head_rows(inside)]

            top = functools.reduce(jnp.add, [f[1] for f in found])
            total = functools.reduce(jnp.add, [f[2] for f in found])
            return top, total, heads, 2.0**level

        return [unit(u) for u in range(HEADS // together)], gathered

    eye[...] = averager(ROWS, ROWS, 0)
    halve[...] = averager(64, BLOCK, 1)
    fold[:32, :] = jnp.concatenate([averager(32, BLOCK, 2), jnp.zeros((32, 64), BF16)], 1)
    fold[32:, :] = jnp.concatenate([jnp.zeros((32, BLOCK), BF16), averager(32, 64, 1)], 1)
    spreads = {1: spread1, 2: spread2, 3: spread3, 4: spread4}
    for l in range(1, 5):
        spreads[l][...] = spreader(spreads[l].shape[0], ROWS >> l, l)
    for load in loads[1:4]:
        load.wait()
    q0[...] = (nn(x[...], wq[...]) * SCALE).astype(BF16)
    k0[...] = nn(x[...], wk[...]).astype(BF16)
    for i in range(2):
        wvt[i * ROWS : (i + 1) * ROWS, :] = nt(eye[...], wv[:, i * ROWS : (i + 1) * ROWS]).astype(BF16)
    ql[...] = nn(average[...], q0[...]).astype(BF16)
    v0[...] = nt(wvt[...], x[...]).astype(BF16)

    mixed = [base_own(h) for h in range(HEADS)]
    for place_in_line, level in ((7, 4), (5, 3), (3, 2)):
        mixed.insert(place_in_line, look(level))
    run(mixed)

    landed(hnear, 0, 192, recv01.at[0])
    project_side(hnear, 0)
    units, near_lanes, base_near = side(0, 1 - core)
    run(units)
    top, total, near_sums = by_head(base_near)
    merge(near_lanes, top, total, lambda h: near_sums[h])

    landed_or_zero(there[0], hfar, 0, 192, recv01.at[1])
    h2[pl.ds(pl.multiple_of(mine(core), 64), 64), :] = nn(fold[...], hfar[:192, :]).astype(BF16)
    project_side(hfar, 1)
    missing = off(jnp.logical_not(there[0]))
    units, far_lanes, base_far = side(1, core)
    run(units)
    top, total, far_sums = by_head(base_far)
    merge(far_lanes, top - missing, total, lambda h: far_sums[h])

    landed_or_zero(there[1], h2, pl.multiple_of(mine(1 - core), 64), 64, recv_far.at[0])
    forward(h2, 0)
    finer(h2, odd, h3, 1 - odd)
    landed_or_zero(there[2], h3, pl.multiple_of(mine(1 - odd), 64), 64, recv_far.at[2])
    landed_or_zero(there[3], h3, pl.multiple_of(mine(odd) + odd * 32, 32), 32, recv_far.at[3])
    forward(h3, 1)
    finer(h3, second, h4, 1 - second)
    landed_or_zero(there[4], h4, pl.multiple_of(mine(1 - second), 64), 64, recv_far.at[4])
    landed_or_zero(there[5], h4, pl.multiple_of(mine(second) + second * 32, 32), 32, recv_far.at[5])
    forward(h4, 2)

    one = []
    run([level_one(j, missing, one) for j in range(HEADS // 2)])
    vd[0] = values_of(core)
    for l in range(4, 1, -1):
        _, together, columns = shape_of(l)
        for u in range(HEADS // together):
            scores[l, u] = nt(rows_of(l, core), seen[l][u * columns : (u + 1) * columns, :])
    top, total, sums = by_head(one)
    one_sums, top, total = spread_all(jnp.concatenate(sums, 0).astype(BF16), top, total, spread1[...])
    terms = [(top, total, lambda h: one_sums[head_rows(h)], 2.0)]
    for i, buffer in enumerate((h2, h3, h4)):
        landed(buffer, pl.multiple_of((1 - core) * BLOCK, BLOCK), BLOCK, recv_near.at[i])
    loads[4].wait()
    landed(deep, 0, 192 + 3 * BLOCK, send_sem.at[0])
    for i, (here, rows) in enumerate(zip(there, (192, 64, 64, 32, 64, 32))):
        pl.when(here)(lambda i=i, rows=rows: landed(deep, 0, rows, send_sem.at[i + 1]))

    vd[1] = values_of(1 - core)
    levels = [coarse(4, group, devices // 8), coarse(3, pair, devices // 4), coarse(2, chip, devices // 2)]
    run([unit for units, _ in levels for unit in units])
    terms += [gathered() for _, gathered in levels]

    before = peak[...]
    after = functools.reduce(jnp.maximum, [term[0] for term in terms], before)
    factors = [jnp.exp2(before - after)] + [weight * jnp.exp2(top - after) for top, _, _, weight in terms]
    lower = den[...] * factors[0]
    for factor, term in zip(factors[1:], terms):
        lower = lower + factor * term[1]
    inverse = 1.0 / lower
    factors = [factor * inverse for factor in factors]
    attended = []
    for h in range(HEADS):
        upper = acc[head_rows(h), :] * factors[0][h : h + 1]
        for factor, term in zip(factors[1:], terms):
            upper = upper + term[2](h) * factor[h : h + 1]
        attended.append(upper.astype(BF16))
    turned = nt(eye[...], jnp.concatenate(attended, 0)).astype(BF16)
    out_ref[...] = nn(turned, wo[...]).astype(BF16)


def solution(mesh):
    devices = mesh.shape["ctx"] * mesh.shape["node"]

    def local(tokens, w_query, w_key, w_value, w_out):
        square = pltpu.VMEM((WIDTH, WIDTH), BF16)
        tall = pltpu.VMEM((ROWS, WIDTH), BF16)
        return pl.pallas_call(
            functools.partial(kernel, devices),
            out_shape=jax.ShapeDtypeStruct((ROWS, WIDTH), BF16),
            in_specs=[pl.BlockSpec(memory_space=pltpu.HBM)] * 5,
            out_specs=pl.BlockSpec(memory_space=pltpu.VMEM),
            scratch_shapes=[
                tall,
                square,
                square,
                square,
                square,
                square,
                pltpu.VMEM((COARSE, WIDTH), BF16),
                tall,
                tall,
                pltpu.VMEM((3 * ROWS, WIDTH), BF16),
                tall,
                pltpu.VMEM((COARSE, WIDTH), BF16),
                tall,
                pltpu.VMEM((WIDTH, ROWS), BF16),
                pltpu.VMEM((2, ROWS, WIDTH), BF16),
                pltpu.VMEM((2, WIDTH, ROWS), BF16),
                square,
                tall,
                pltpu.VMEM((BLOCK, WIDTH), BF16),
                pltpu.VMEM((2, WIDTH, 3 * BLOCK), BF16),
                pltpu.VMEM((WIDTH, ROWS), F32),
                pltpu.VMEM((HEADS, ROWS), F32),
                pltpu.VMEM((HEADS, ROWS), F32),
                pltpu.VMEM((COARSE, ROWS), BF16),
                pltpu.VMEM((ROWS, ROWS), BF16),
                pltpu.VMEM((64, BLOCK), BF16),
                pltpu.VMEM((64, 192), BF16),
                pltpu.VMEM((BLOCK, ROWS), BF16),
                pltpu.VMEM((ROWS, ROWS), BF16),
                pltpu.VMEM((ROWS, ROWS), BF16),
                pltpu.VMEM((BLOCK, ROWS), BF16),
                pltpu.SemaphoreType.DMA((5,)),
                pltpu.SemaphoreType.DMA((7,)),
                pltpu.SemaphoreType.DMA((2,)),
                pltpu.SemaphoreType.DMA((6,)),
                pltpu.SemaphoreType.DMA((3,)),
            ],
            compiler_params=pltpu.CompilerParams(
                collective_id=0, has_side_effects=True, vmem_limit_bytes=40 * 2**20
            ),
            name="hierarchical_attention",
        )(*[pltpu.with_memory_space_constraint(a, pltpu.HBM) for a in (tokens, w_query, w_key, w_value, w_out)])

    placed = (P(("ctx", "node"), None), P(), P(), P(), P())
    return jax.shard_map(
        local, mesh=mesh, in_specs=placed, out_specs=P(("ctx", "node"), None), check_vma=False
    )
```
